128 devices in a mesh: dp: 8 (over x, core), fsdp: 16 (over z, y).
Axes of the slice: x: 4, y: 4, z: 4, core: 2. Of those that a mesh axis runs over, the one named last changes fastest.
Arguments:
- tokens: bfloat16 [512, 256, 768], P('fsdp', 'dp'), may hold values from -6 to 6
- cotangent: bfloat16 [512, 256, 768], P('fsdp', 'dp'), may hold values from -6 to 6
- perm: int32 [512], replicated, may hold values from 0 to 511, as said below
- lengths: int32 [512], P(('dp', 'fsdp')), may hold values from 32 to 256, as said below
- drop: int32 [512], P(('dp', 'fsdp')), may hold values 0 or 1
- w_query: bfloat16 [768, 768], P(('dp', 'fsdp')), may hold values from -0.21875 to 0.21875
- b_query: bfloat16 [768], P(('dp', 'fsdp')), may hold values from -3 to 3
- w_key: bfloat16 [768, 768], P(('dp', 'fsdp')), may hold values from -0.21875 to 0.21875
- w_value: bfloat16 [768, 768], P(('dp', 'fsdp')), may hold values from -0.21875 to 0.21875
- b_value: bfloat16 [768], P(('dp', 'fsdp')), may hold values from -3 to 3
- w_out: bfloat16 [768, 768], P(('dp', 'fsdp')), may hold values from -2 to 2
- b_out: bfloat16 [768], P(('dp', 'fsdp')), may hold values from -3 to 3
- norm1_gain: bfloat16 [768], P(('dp', 'fsdp')), may hold values from 0.5 to 1.5
- norm1_bias: bfloat16 [768], P(('dp', 'fsdp')), may hold values from -3 to 3
- w_inner: bfloat16 [768, 3072], P(('dp', 'fsdp')), may hold values from -0.21875 to 0.21875
- b_inner: bfloat16 [3072], P(('dp', 'fsdp')), may hold values from -3 to 3
- w_outer: bfloat16 [3072, 768], P(('dp', 'fsdp')), may hold values from -0.109375 to 0.109375
- b_outer: bfloat16 [768], P(('dp', 'fsdp')), may hold values from -3 to 3
- norm2_gain: bfloat16 [768], P(('dp', 'fsdp')), may hold values from 0.5 to 1.5
- norm2_bias: bfloat16 [768], P(('dp', 'fsdp')), may hold values from -3 to 3
Outputs:
- layer_out: bfloat16 [512, 256, 768], P('fsdp', 'dp')
- grad_tokens: bfloat16 [512, 256, 768], P('fsdp', 'dp')
- grad_w_query: float32 [768, 768], P(('dp', 'fsdp'))
- grad_b_query: float32 [768], P(('dp', 'fsdp'))
- grad_w_key: float32 [768, 768], P(('dp', 'fsdp'))
- grad_w_value: float32 [768, 768], P(('dp', 'fsdp'))
- grad_b_value: float32 [768], P(('dp', 'fsdp'))
- grad_w_out: float32 [768, 768], P(('dp', 'fsdp'))
- grad_b_out: float32 [768], P(('dp', 'fsdp'))
- grad_norm1_gain: float32 [768], P(('dp', 'fsdp'))
- grad_norm1_bias: float32 [768], P(('dp', 'fsdp'))
- grad_w_inner: float32 [768, 3072], P(('dp', 'fsdp'))
- grad_b_inner: float32 [3072], P(('dp', 'fsdp'))
- grad_w_outer: float32 [3072, 768], P(('dp', 'fsdp'))
- grad_b_outer: float32 [768], P(('dp', 'fsdp'))
- grad_norm2_gain: float32 [768], P(('dp', 'fsdp'))
- grad_norm2_bias: float32 [768], P(('dp', 'fsdp'))
The draws below stay inside these ranges and needn't reach their ends.
Inputs may be any that keep to these rules, and one draw needn't show every extreme that they name: `perm`: A permutation of the sequences. Dealt slot q = (a * 16 + b) * 4 + j, for dp index a and fsdp index b, holds an input sequence of b's range b * 32 to (b + 1) * 32 - 1. `lengths`: some sequence has 256 tokens and some has 32.
All inputs are finite; a program needn't handle non-finite values. No bound on the sum of `drop` on one device may be relied on, other than what follows from the above.
Results may differ from the reference program's by a relative error of at most 0.02.
Values may be sent and summed in bfloat16 or wider, within the bound.
No kernel may reach another device: no remote copies, remote signals or barrier semaphores. Data moves between devices by JAX's collectives and lax.ppermute only.
A program may use at most 256 MiB of HBM per device.

```python
import math
import jax
import jax.numpy as jnp
from jax import lax

D = 768
HEADS = 12
HEAD = 64
FF = 3072
SLOT = 256
SEQ_DEV = 4
SEQS = 512
BLOCK = 32


def draw_perm(key, part):
    shuffled = jax.random.permutation(key, SEQS).astype(jnp.int32)
    slot_ids = jnp.arange(SEQS, dtype=jnp.int32)
    ranked = jnp.argsort(slot_ids // BLOCK * SEQS + shuffled).astype(jnp.int32)
    fsdp_count = SEQS // BLOCK
    dp_index = slot_ids // (fsdp_count * SEQ_DEV)
    fsdp_index = slot_ids // SEQ_DEV % fsdp_count
    within = slot_ids % SEQ_DEV
    return ranked[fsdp_index * BLOCK + dp_index * SEQ_DEV + within]


def draw_lengths(key, part):
    drawn_lengths = jax.random.randint(jax.random.fold_in(key, 11), (SEQS,), SLOT // 8, SLOT + 1).astype(jnp.int32)
    long_slot = jax.random.randint(jax.random.fold_in(key, 12), (), 0, SEQS)
    short_slot = (long_slot + 1 + jax.random.randint(jax.random.fold_in(key, 13), (), 0, SEQS - 1)) % SEQS
    slot_ids = jnp.arange(SEQS, dtype=jnp.int32)
    drawn_lengths = jnp.where(slot_ids == long_slot, SLOT, drawn_lengths)
    drawn_lengths = jnp.where(slot_ids == short_slot, SLOT // 8, drawn_lengths)
    return drawn_lengths.astype(jnp.int32)


def plant(result, key, smallest, high):
    shape = result.shape
    index_at = [jax.random.randint(jax.random.fold_in(key, axis), (), 0, shape[axis]) for axis in range(len(shape))]
    result = result.at[tuple(index_at)].set(smallest)
    longest = shape.index(max(shape))
    index_at[longest] = (index_at[longest] + 1) % shape[longest]
    return result.at[tuple(index_at)].set(high)


def level_of(own_key, shape, cuts, least, high):
    def one(axis_at, shards_of):
        steps = jax.random.uniform(jax.random.fold_in(jax.random.fold_in(own_key, 6), axis_at), (shards_of,), jnp.float32, least / len(cuts), high / len(cuts))
        return jnp.repeat(jnp.exp(steps), shape[axis_at] // shards_of).reshape((-1,) + (1,) * (len(shape) - axis_at - 1))

    gain = one(*cuts[0])
    for cut in cuts[1:]:
        gain = gain * one(*cut)
    return gain


def centred(rng, dims, spread, bound, cuts=(), kind=jnp.bfloat16):
    entries = jax.random.normal(rng, dims, jnp.float32) * spread
    if len(cuts) > 0:
        entries = level_of(rng, dims, cuts, -0.22, 0.18) * entries
    return jnp.clip(entries, min=-bound, max=bound).astype(kind)


def setup_inputs(seed: int = 0) -> dict:
    key_list = jax.random.split(jax.random.key(seed), 21)
    tokens = centred(key_list[0], (SEQS, SLOT, D), 1.0, 6.0, ((0, 16), (1, 8)))
    cotangent = centred(key_list[1], (SEQS, SLOT, D), 1.0, 6.0, ((0, 16), (1, 8)))
    perm = draw_perm(jax.random.fold_in(key_list[20], 71), 0)
    lengths = draw_lengths(jax.random.fold_in(key_list[20], 71), 0)
    drop = plant((jax.random.randint(key_list[4], (SEQS,), 0, 4) < 1).astype(jnp.int32), jax.random.fold_in(key_list[4], 1), 0, 1)
    w_query = centred(key_list[5], (D, D), D ** -0.5, 0.21875, ((0, 128),))
    b_query = centred(key_list[6], (D,), 0.5, 3.0, ((0, 128),))
    w_key = centred(key_list[7], (D, D), D ** -0.5, 0.21875, ((0, 128),))
    w_value = centred(key_list[8], (D, D), D ** -0.5, 0.21875, ((0, 128),))
    b_value = centred(key_list[9], (D,), 0.5, 3.0, ((0, 128),))
    w_out = centred(key_list[10], (D, D), (D // 96) ** -0.5, 2.0, ((0, 128),))
    b_out = centred(key_list[11], (D,), 0.5, 3.0, ((0, 128),))
    norm1_gain = jnp.clip(1.0 + 0.1 * jax.random.normal(key_list[12], (D,), jnp.float32), 0.5, 1.5).astype(jnp.bfloat16)
    norm1_bias = centred(key_list[13], (D,), 0.5, 3.0, ((0, 128),))
    w_inner = centred(key_list[14], (D, FF), D ** -0.5, 0.21875, ((0, 128),))
    b_inner = centred(key_list[15], (FF,), 0.5, 3.0, ((0, 128),))
    w_outer = centred(key_list[16], (FF, D), FF ** -0.5, 0.109375, ((0, 128),))
    b_outer = centred(key_list[17], (D,), 0.5, 3.0, ((0, 128),))
    norm2_gain = jnp.clip(1.0 + 0.1 * jax.random.normal(key_list[18], (D,), jnp.float32), 0.5, 1.5).astype(jnp.bfloat16)
    norm2_bias = centred(key_list[19], (D,), 0.5, 3.0, ((0, 128),))
    return {"tokens": tokens, "cotangent": cotangent, "perm": perm, "lengths": lengths, "drop": drop, "w_query": w_query, "b_query": b_query, "w_key": w_key, "w_value": w_value, "b_value": b_value, "w_out": w_out, "b_out": b_out, "norm1_gain": norm1_gain, "norm1_bias": norm1_bias, "w_inner": w_inner, "b_inner": b_inner, "w_outer": w_outer, "b_outer": b_outer, "norm2_gain": norm2_gain, "norm2_bias": norm2_bias}


@jax.custom_vjp
def low(v):
    return lax.optimization_barrier(v.astype(jnp.bfloat16)).astype(jnp.float32)

@jax.custom_vjp
def low_back(v):
    return v

def low_keep(v):
    return (low(v), None)

def low_pass(kept, grad):
    return (grad,)

def back_keep(v):
    return (v, None)

def back_low(kept, grad):
    return (low(grad),)
low.defvjp(low_keep, low_pass)
low_back.defvjp(back_keep, back_low)
epsilon = 1e-05

def project(values, weight):
    return jnp.einsum('gsd,de->gse', values, weight, precision=lax.Precision.HIGHEST)

def layer_norm(values, norm_gain, offset):
    center = values - lax.optimization_barrier(jnp.mean(values, axis=-1, keepdims=True))
    variance = lax.optimization_barrier(jnp.mean(center * center, axis=-1, keepdims=True))
    return center * lax.rsqrt(variance + epsilon) * norm_gain + offset

def forward(params, inputs, seq_lens, drop_flags):
    w_query, b_query, w_key, w_value, b_value, w_out, b_out, norm1_gain, norm1_bias, w_inner, b_inner, w_outer, b_outer, norm2_gain, norm2_bias = params
    groups = inputs.shape[0]
    positions = jnp.arange(SLOT, dtype=jnp.int32)
    valid_rows = (positions[None, :] < seq_lens[:, None]).astype(jnp.float32)[:, :, None]
    key_mask = (positions[None, :] < seq_lens[:, None])[:, None, None, :]
    score_scale = HEAD ** (-0.5)
    queries = low(low_back(project(inputs, w_query) + b_query)).reshape(groups, SLOT, HEADS, HEAD)
    key_rows = low(low_back(project(inputs, w_key))).reshape(groups, SLOT, HEADS, HEAD)
    value_rows = low(low_back(project(inputs, w_value) + b_value)).reshape(groups, SLOT, HEADS, HEAD)
    raw_scores = low_back(jnp.einsum('gqhd,gkhd->ghqk', queries, key_rows, precision=lax.Precision.HIGHEST))
    scores = jnp.where(key_mask, raw_scores * score_scale, -1e+30)
    top_score = lax.optimization_barrier(jnp.max(scores, axis=-1, keepdims=True))
    expo = jnp.exp(scores - top_score)
    attn_probs = expo / lax.optimization_barrier(jnp.sum(expo, axis=-1, keepdims=True))
    probs_low = low(attn_probs)
    context = jnp.einsum('ghqk,gkhd->gqhd', probs_low, value_rows, precision=lax.Precision.HIGHEST)
    context = low(low_back(context.reshape(groups, SLOT, D)))
    attn_out = low_back(project(context, w_out) + b_out)
    hidden = layer_norm(inputs + attn_out, norm1_gain, norm1_bias)
    inner_pre = low_back(project(low(hidden), w_inner) + b_inner)
    activated = low(jax.nn.gelu(inner_pre, approximate=False))
    branch = low_back(project(activated, w_outer) + b_outer)
    normed = layer_norm(hidden + branch, norm2_gain, norm2_bias)
    kept = (drop_flags == 0)[:, None, None]
    return jnp.where(kept, normed, inputs) * valid_rows

def widen(array_in):
    return array_in.astype(jnp.float32)

def reference(tokens, cotangent, perm, lengths, drop, w_query, b_query, w_key, w_value, b_value, w_out, b_out, norm1_gain, norm1_bias, w_inner, b_inner, w_outer, b_outer, norm2_gain, norm2_bias):
    params = tuple(map(widen, (w_query, b_query, w_key, w_value, b_value, w_out, b_out, norm1_gain, norm1_bias, w_inner, b_inner, w_outer, b_outer, norm2_gain, norm2_bias)))
    seq_lens = jnp.zeros((SEQS,), jnp.int32).at[perm].set(lengths.astype(jnp.int32))
    drop_flags = jnp.zeros((SEQS,), jnp.int32).at[perm].set(drop.astype(jnp.int32))
    group_size = math.gcd(SEQS, max(1, 4096 // SLOT))
    group_count = SEQS // group_size
    inputs_all = tokens.astype(jnp.float32).reshape(group_count, group_size, SLOT, D)
    upstream_all = cotangent.astype(jnp.float32).reshape(group_count, group_size, SLOT, D)
    lens_all = seq_lens.reshape(group_count, group_size)
    drops_all = drop_flags.reshape(group_count, group_size)

    def one_group(totals, pieces):
        inputs, upstream, group_lens, group_drops = pieces

        def apply_layer(params_in, inputs_in):
            return forward(params_in, inputs_in, group_lens, group_drops)
        outputs, pullback = jax.vjp(apply_layer, params, inputs)
        grad_params, grad_inputs = pullback(upstream)
        totals = jax.tree.map(jnp.add, totals, grad_params)
        return (totals, (outputs, grad_inputs))
    initial = tuple(map(jnp.zeros_like, params))
    totals, (outputs, grad_inputs) = lax.scan(one_group, initial, (inputs_all, upstream_all, lens_all, drops_all))
    layer_out = outputs.reshape(SEQS, SLOT, D).astype(jnp.bfloat16)
    grad_tokens = grad_inputs.reshape(SEQS, SLOT, D).astype(jnp.bfloat16)
    return (layer_out, grad_tokens, totals[0], totals[1], totals[2], totals[3], totals[4], totals[5], totals[6], totals[7], totals[8], totals[9], totals[10], totals[11], totals[12], totals[13], totals[14])
```

```python
import jax
import jax.numpy as jnp
from jax import lax
from jax.sharding import Mesh
from jax.sharding import PartitionSpec as P

HEADS = 12
HEAD = 64
WIDTH = 768
FF = 3072
SLOT = 256
SEQ_DEV = 4
RING = 4
CORES = 2
PIECE = 32

epsilon = 1e-05
bf16 = jnp.bfloat16
f32 = jnp.float32


def norm_apply(values, norm_gain, offset):
    center = values - jnp.mean(values, axis=-1, keepdims=True)
    variance = jnp.mean(center * center, axis=-1, keepdims=True)
    return center * lax.rsqrt(variance + epsilon) * norm_gain + offset


def gelu_exact(values):
    return jax.nn.gelu(values, approximate=False)


def shift(value, axis, step):
    size = CORES if axis == "core" else RING
    return lax.ppermute(value, axis, [(i, (i + step) % size) for i in range(size)])


def at(value, index):
    return lax.dynamic_index_in_dim(value, index, 0, keepdims=False)


def gather_ring(value, axis):
    me = lax.axis_index(axis)
    out = jnp.broadcast_to(value[None], (RING,) + value.shape)
    for step in (1, 3, 2):
        out = lax.dynamic_update_index_in_dim(
            out, shift(value, axis, step), lax.rem(me + RING - step, RING), 0
        )
    return out


def gather_core(value):
    me = lax.axis_index("core")
    other = shift(value, "core", 1)
    return jnp.where(me == 0, jnp.stack([value, other]), jnp.stack([other, value]))


def scatter_ring(value, axis):
    me = lax.axis_index(axis)
    total = at(value, me).astype(f32)
    for step in (1, 3, 2):
        total += shift(at(value, lax.rem(me + step, RING)), axis, step).astype(f32)
    return total


def scatter_core(value):
    me = lax.axis_index("core")
    mine = lax.dynamic_index_in_dim(value, me, 1, keepdims=False)
    away = lax.dynamic_index_in_dim(value, 1 - me, 1, keepdims=False)
    return mine + shift(away.astype(bf16), "core", 1).astype(f32)


def deal(pieces):
    me_x = lax.axis_index("x")
    me_c = lax.axis_index("core")
    grid = pieces.reshape(RING, CORES, SEQ_DEV, PIECE, WIDTH)
    mine = lax.dynamic_index_in_dim(grid, me_c, 1, keepdims=False)
    away = lax.dynamic_index_in_dim(grid, 1 - me_c, 1, keepdims=False)
    both = jnp.stack([mine, shift(away, "core", 1)], axis=1)
    got = [at(both, me_x)] + [
        shift(at(both, lax.rem(me_x + d, RING)), "x", d) for d in (1, 2, 3)
    ]
    return jnp.stack(got)


def undeal(dealt):
    me_x = lax.axis_index("x")
    me_c = lax.axis_index("core")
    out = jnp.broadcast_to(dealt[0][None], (RING, CORES, SEQ_DEV, PIECE, WIDTH))
    for d in (1, 2, 3):
        out = lax.dynamic_update_index_in_dim(
            out, shift(dealt[d], "x", RING - d), lax.rem(me_x + d, RING), 0
        )
    same = out[:, 0]
    other = shift(out[:, 1], "core", 1)
    ordered = jnp.where(me_c == 0, jnp.stack([same, other], 1), jnp.stack([other, same], 1))
    return ordered.reshape(RING * CORES * SEQ_DEV, PIECE, WIDTH)


def body(
    tokens,
    cotangent,
    perm,
    lengths,
    drop,
    w_query,
    b_query,
    w_key,
    w_value,
    b_value,
    w_out,
    b_out,
    norm1_gain,
    norm1_bias,
    w_inner,
    b_inner,
    w_outer,
    b_outer,
    norm2_gain,
    norm2_bias,
):
    me_x = lax.axis_index("x")
    me_c = lax.axis_index("core")
    me_z = lax.axis_index("z")
    me_y = lax.axis_index("y")
    dealt_x = deal(tokens)
    small = [b_query, b_value, b_out, norm1_gain, norm1_bias, b_outer, norm2_gain, norm2_bias, b_inner]
    small = jnp.concatenate(small + [lengths.astype(bf16), drop.astype(bf16)])
    attn_piece = jnp.concatenate(
        [
            jnp.concatenate([w_query, w_key, w_value, w_out], axis=1),
            jnp.pad(small, (0, 4 * WIDTH - small.shape[0]))[None],
        ]
    )
    attn_y = gather_ring(attn_piece, "y")
    extras_y = jnp.pad(attn_y[:, 6, :96].reshape(1, 384), ((0, 23), (0, 0)))
    attn_y = jnp.concatenate([attn_y[:, :6].reshape(24, 4 * WIDTH), extras_y], axis=1)
    attn_xy = gather_ring(attn_y, "x")
    attn_zxy = gather_ring(attn_xy, "z")
    attn_all = gather_core(attn_zxy)
    attn_all = attn_all.transpose(2, 0, 1, 3, 4)
    attn_full = attn_all[..., : 4 * WIDTH].reshape(WIDTH, 4 * WIDTH)
    extras = attn_all[:, :, :, 0, 4 * WIDTH :].reshape(128, 96)
    (
        query_bias,
        value_bias,
        out_bias,
        gain1_full,
        bias1_full,
        outer_bias,
        gain2_full,
        bias2_full,
    ) = (extras[:, 6 * i : 6 * i + 6].reshape(WIDTH).astype(f32) for i in range(8))
    inner_bias = extras[:, 48:72].reshape(FF).astype(f32)
    slot_lengths = extras[:, 72:76].reshape(512).astype(f32)
    slot_drops = extras[:, 76:80].reshape(512).astype(f32)
    dealt_c = deal(cotangent)
    inner_y = gather_ring(w_inner, "y").reshape(24, FF)
    inner_zy = gather_ring(inner_y, "z").reshape(96, FF)
    inner_full = gather_core(gather_ring(inner_zy, "x")).transpose(1, 0, 2, 3).reshape(WIDTH, FF)
    outer_x = gather_ring(w_outer, "x")
    outer_zx = gather_ring(outer_x, "z")
    outer_all = gather_core(gather_ring(outer_zx, "y"))
    outer_full = outer_all.transpose(3, 0, 2, 1, 4, 5).reshape(FF, WIDTH)

    first = ((me_z * RING + me_y) * 8 + me_x * CORES + me_c) * SEQ_DEV
    wanted = first + jnp.arange(SEQ_DEV, dtype=jnp.int32)
    hit = (perm[None, :] == wanted[:, None]).astype(f32)
    my_lengths = jnp.sum(hit * slot_lengths[None], axis=1).astype(jnp.int32)
    my_drops = jnp.sum(hit * slot_drops[None], axis=1)
    steps = jnp.arange(RING, dtype=jnp.int32)
    from_x = lax.rem(me_x + RING - steps, RING)
    from_c = jnp.stack([me_c, 1 - me_c])
    positions = (
        (from_x[:, None, None] * CORES + from_c[None, :, None]) * PIECE
        + jnp.arange(PIECE, dtype=jnp.int32)[None, None, :]
    ).reshape(SLOT)

    row_count = SEQ_DEV * SLOT
    dealt_x = dealt_x.transpose(2, 0, 1, 3, 4).reshape(SEQ_DEV, SLOT, WIDTH)
    dealt_c = dealt_c.transpose(2, 0, 1, 3, 4).reshape(SEQ_DEV, SLOT, WIDTH)
    inputs_flat = dealt_x.reshape(row_count, WIDTH)
    is_valid = positions[None, :] < my_lengths[:, None]
    valid_rows = is_valid.astype(f32)[:, :, None]
    key_mask = is_valid[:, None, None, :]
    keep_seq = (my_drops == 0)[:, None, None]
    score_scale = HEAD ** (-0.5)
    head_shape = (SEQ_DEV, SLOT, HEADS, HEAD)
    zero_bias = jnp.zeros_like(query_bias)
    qkv = (
        jnp.dot(inputs_flat, attn_full[:, : 3 * WIDTH], preferred_element_type=f32)
        + jnp.concatenate([query_bias, zero_bias, value_bias])
    ).astype(bf16)
    out_full = attn_full[:, 3 * WIDTH :]
    queries = qkv[:, :WIDTH].reshape(head_shape)
    key_rows = qkv[:, WIDTH : 2 * WIDTH].reshape(head_shape)
    value_rows = qkv[:, 2 * WIDTH :].reshape(head_shape)
    raw_scores = jnp.einsum("sqhd,skhd->shqk", queries, key_rows, preferred_element_type=f32)
    scores = jnp.where(key_mask, raw_scores * score_scale, -1e30)
    top_score = jnp.max(scores, axis=-1, keepdims=True)
    expo = jnp.exp(scores - top_score)
    attn_probs = expo / jnp.sum(expo, axis=-1, keepdims=True)
    probs_low = attn_probs.astype(bf16)
    context = jnp.einsum("shqk,skhd->sqhd", probs_low, value_rows, preferred_element_type=f32)
    context = context.astype(bf16).reshape(row_count, WIDTH)
    attn_out = jnp.dot(context, out_full, preferred_element_type=f32) + out_bias
    hidden, norm1_pull = jax.vjp(
        norm_apply, inputs_flat.astype(f32) + attn_out, gain1_full, bias1_full
    )
    hidden_low = hidden.astype(bf16)
    inner_pre = jnp.dot(hidden_low, inner_full, preferred_element_type=f32) + inner_bias
    activated_wide, gelu_pull = jax.vjp(gelu_exact, inner_pre)
    activated = activated_wide.astype(bf16)
    branch = jnp.dot(activated, outer_full, preferred_element_type=f32) + outer_bias
    normed, norm2_pull = jax.vjp(norm_apply, hidden + branch, gain2_full, bias2_full)
    layer_rows = (
        jnp.where(keep_seq, normed.reshape(SEQ_DEV, SLOT, WIDTH), dealt_x.astype(f32)) * valid_rows
    )
    back_shape = (SEQ_DEV, RING, CORES, PIECE, WIDTH)
    layer_final = undeal(layer_rows.astype(bf16).reshape(back_shape).transpose(1, 2, 0, 3, 4))

    upstream = dealt_c.astype(f32) * valid_rows
    grad_normed = jnp.where(keep_seq, upstream, 0.0).reshape(row_count, WIDTH)
    d_sum2, grad_gain2, grad_bias2 = norm2_pull(grad_normed)
    d_branch = d_sum2.astype(bf16)
    grad_outer = jnp.einsum("nf,nd->fd", activated, d_branch, preferred_element_type=f32)
    grad_outer_bias = jnp.sum(d_branch.astype(f32), axis=0)
    d_activated = jnp.einsum("nd,fd->nf", d_branch, outer_full, preferred_element_type=f32)
    d_inner = gelu_pull(d_activated)[0].astype(bf16)
    grad_inner = jnp.einsum("nd,nf->df", hidden_low, d_inner, preferred_element_type=f32)
    grad_inner_bias = jnp.sum(d_inner.astype(f32), axis=0)
    d_hidden = d_sum2 + jnp.einsum("nf,df->nd", d_inner, inner_full, preferred_element_type=f32)

    inner_c = scatter_core(grad_inner.reshape(RING, CORES, RING, 24, FF)).astype(bf16)
    inner_z = scatter_ring(inner_c.transpose(1, 0, 2, 3), "z").astype(bf16)
    inner_x = scatter_ring(inner_z, "x").astype(bf16)
    inner_grad = scatter_ring(inner_x.reshape(RING, 6, FF), "y")
    outer_c = scatter_core(grad_outer.reshape(RING, CORES, RING, RING, 24, WIDTH)).astype(bf16)
    outer_y = scatter_ring(outer_c.transpose(2, 0, 1, 3, 4), "y").astype(bf16)
    outer_x = scatter_ring(outer_y, "x").astype(bf16)
    outer_grad = scatter_ring(outer_x, "z")

    d_sum1, grad_gain1, grad_bias1 = norm1_pull(d_hidden)
    d_attn = d_sum1.astype(bf16)
    grad_out = jnp.einsum("nc,nd->cd", context, d_attn, preferred_element_type=f32)
    grad_out_bias = jnp.sum(d_attn.astype(f32), axis=0)
    d_context = jnp.einsum("nd,cd->nc", d_attn, out_full, preferred_element_type=f32)
    d_context = d_context.astype(bf16).reshape(head_shape)
    d_probs = jnp.einsum("sqhd,skhd->shqk", d_context, value_rows, preferred_element_type=f32)
    d_values = jnp.einsum("shqk,sqhd->skhd", probs_low, d_context, preferred_element_type=f32)
    d_values = d_values.astype(bf16).reshape(row_count, WIDTH)
    d_scores = (
        attn_probs * (d_probs - jnp.sum(attn_probs * d_probs, axis=-1, keepdims=True)) * score_scale
    )
    d_scores = d_scores.astype(bf16)
    d_queries = jnp.einsum("shqk,skhd->sqhd", d_scores, key_rows, preferred_element_type=f32)
    d_queries = d_queries.astype(bf16).reshape(row_count, WIDTH)
    d_keys = jnp.einsum("shqk,sqhd->skhd", d_scores, queries, preferred_element_type=f32)
    d_keys = d_keys.astype(bf16).reshape(row_count, WIDTH)
    d_qkv = jnp.concatenate([d_queries, d_keys, d_values], axis=1)
    grad_qkv = jnp.einsum("nc,nd->cd", inputs_flat, d_qkv, preferred_element_type=f32)
    grad_query_bias = jnp.sum(d_queries.astype(f32), axis=0)
    grad_value_bias = jnp.sum(d_values.astype(f32), axis=0)
    d_inputs = d_sum1 + jnp.einsum(
        "nd,cd->nc", d_qkv, attn_full[:, : 3 * WIDTH], preferred_element_type=f32
    )
    grad_rows = jnp.where(keep_seq, d_inputs.reshape(SEQ_DEV, SLOT, WIDTH), upstream).astype(bf16)
    grad_final = undeal(grad_rows.reshape(back_shape).transpose(1, 2, 0, 3, 4))

    grad_small = [
        grad_query_bias,
        grad_value_bias,
        grad_out_bias,
        grad_gain1,
        grad_bias1,
        grad_outer_bias,
        grad_gain2,
        grad_bias2,
    ]
    grad_small = jnp.concatenate(
        [g.reshape(32, 24) for g in grad_small] + [grad_inner_bias.reshape(32, 96)], axis=1
    )
    grad_small = jnp.pad(grad_small, ((0, 0), (0, 96))).reshape(RING, CORES, RING, 1, 384)
    grad_small = jnp.pad(grad_small, ((0, 0), (0, 0), (0, 0), (0, 23), (0, 0)))
    grad_attn = jnp.concatenate([grad_qkv, grad_out], axis=1).reshape(
        RING, CORES, RING, 24, 4 * WIDTH
    )
    attn_c = scatter_core(jnp.concatenate([grad_attn, grad_small], axis=4)).astype(bf16)
    attn_z = scatter_ring(attn_c.transpose(1, 0, 2, 3), "z").astype(bf16)
    attn_x = scatter_ring(attn_z, "x").astype(bf16)
    vec = attn_x[0, 4 * WIDTH :]
    vec6 = vec[:192].reshape(8, RING, 6).transpose(1, 0, 2).reshape(RING, 48)
    vec24 = vec[192:288].reshape(RING, 24)
    vec = jnp.pad(jnp.concatenate([vec6, vec24], axis=1), ((0, 0), (0, 4 * WIDTH - 72)))
    last = jnp.concatenate([attn_x[:, : 4 * WIDTH].reshape(RING, 6, 4 * WIDTH), vec[:, None]], axis=1)
    attn_grad = scatter_ring(last, "y")
    parts = [attn_grad[:6, i * WIDTH : (i + 1) * WIDTH] for i in range(4)]
    bias_of = [attn_grad[6, 6 * i : 6 * i + 6] for i in range(8)]
    return (
        layer_final,
        grad_final,
        parts[0],
        bias_of[0],
        parts[1],
        parts[2],
        bias_of[1],
        parts[3],
        bias_of[2],
        bias_of[3],
        bias_of[4],
        inner_grad,
        attn_grad[6, 48:72],
        outer_grad,
        bias_of[5],
        bias_of[6],
        bias_of[7],
    )


def solution(mesh):
    chips = Mesh(mesh.devices.reshape(RING, CORES, RING, RING), ("x", "core", "z", "y"))
    dp = ("x", "core")
    fsdp = ("z", "y")
    every = P(dp + fsdp)
    rows = P(dp + fsdp, None)
    whole = P(fsdp, dp, None)
    return jax.shard_map(
        body,
        mesh=chips,
        in_specs=(
            whole, whole, P(), every, every,
            rows, every, rows, rows, every, rows, every, every, every,
            rows, every, rows, every, every, every,
        ),
        out_specs=(
            whole, whole,
            rows, every, rows, rows, every, rows, every, every, every,
            rows, every, rows, every, every, every,
        ),
        check_vma=False,
    )
```

```python
import functools
import jax
import jax.numpy as jnp
from jax import lax
from jax.experimental import pallas as pl
from jax.experimental.pallas import tpu as pltpu
from jax.sharding import Mesh
from jax.sharding import PartitionSpec as P

HEADS = 12
HEAD = 64
WIDTH = 768
FF = 3072
SLOT = 256
SEQ_DEV = 4
RING = 4
CORES = 2
PIECE = 32
ROWS = SEQ_DEV * SLOT
PAIR = 2 * HEAD
PACKED = 4 * WIDTH + 512
EXTRA = 256

epsilon = 1e-05
bf16 = jnp.bfloat16
f32 = jnp.float32
VMEM_LIMIT = 58 * 1024 * 1024

TN = (((0,), (0,)), ((), ()))
NT = (((1,), (1,)), ((), ()))


def mm(a, b):
    return jnp.dot(a, b, preferred_element_type=f32)


def mm_nt(a, b):
    return lax.dot_general(a, b, NT, preferred_element_type=f32)


def mm_tn(a, b):
    return lax.dot_general(a, b, TN, preferred_element_type=f32)


def slot_positions(ids, shape, axis):
    row = lax.broadcasted_iota(jnp.int32, shape, axis)
    from_x = lax.rem(ids[8] + RING - row // (CORES * PIECE), RING)
    away = lax.rem(row // PIECE, CORES)
    from_c = jnp.where(away == 1, 1 - ids[9], ids[9])
    return (from_x * CORES + from_c) * PIECE + lax.rem(row, PIECE)


def joined(refs):
    return jnp.concatenate([ref[...].reshape(CORES * PIECE, WIDTH) for ref in refs], axis=0)


def split_into(same, other, rows):
    for d in range(RING):
        start = d * CORES * PIECE
        same[d, 0] = rows[start : start + PIECE]
        other[d, 0] = rows[start + PIECE : start + 2 * PIECE]


def spread(values, width):
    total = 128 * width
    lane = lax.broadcasted_iota(jnp.int32, (128, total), 1)
    owner = lax.broadcasted_iota(jnp.int32, (128, total), 0)
    pick = lax.broadcasted_iota(jnp.int32, (width, total), 0)
    within = lax.rem(lax.broadcasted_iota(jnp.int32, (width, total), 1), width)
    repeated = mm(values, (pick == within).astype(bf16))
    return jnp.sum(jnp.where(lane // width == owner, repeated, 0.0), axis=0, keepdims=True)


def attention_forward(
    ids, x0, x1, x2, x3, w, extras, perm,
    xt_out, qkv_out, exp_out, norm_out, ctxt_out, sum_out, vec, bias_out,
):
    s = pl.program_id(0)

    @pl.when(s == 0)
    def _():
        for i in range(8):
            vec[i : i + 1] = spread(extras[:, 6 * i : 6 * i + 6], 6)
        bias_out[...] = spread(extras[:, 48:72], 24)

    x = joined((x0, x1, x2, x3))
    xt_out[...] = x.T
    q = ((mm(x, w[:, :WIDTH]) + vec[0:1]).astype(bf16).astype(f32) * HEAD**-0.5).astype(bf16)
    k = mm(x, w[:, WIDTH : 2 * WIDTH]).astype(bf16)
    v = (mm(x, w[:, 2 * WIDTH : 3 * WIDTH]) + vec[1:2]).astype(bf16)
    qkv_out[:, :WIDTH] = q
    qkv_out[:, WIDTH : 2 * WIDTH] = k
    qkv_out[:, 2 * WIDTH :] = v
    q_t = q.T
    v_t = v.T
    keys = slot_positions(ids, (SLOT, 1), 0).astype(f32)
    hit = perm[...] == ids[10] + s
    length = jnp.sum(jnp.where(hit, extras[:, 72:76].astype(f32), 0.0), keepdims=True)
    bias = jnp.where(keys < length, 0.0, -1e30)
    low = lax.broadcasted_iota(jnp.int32, (SLOT, PAIR), 1) < HEAD
    ctx_t = []
    for h in range(HEADS):
        p = h // 2 * PAIR
        k_pair = k[:, p : p + PAIR]
        k_one = jnp.where(low if h % 2 == 0 else ~low, k_pair, jnp.zeros_like(k_pair))
        scores = mm(k_one, q_t[p : p + PAIR]) + bias
        top = jnp.max(scores, axis=0, keepdims=True)
        expo = jnp.exp(scores - top)
        inverse = 1.0 / jnp.sum(expo, axis=0, keepdims=True)
        norm_out[0, h : h + 1, :] = inverse
        expo = expo.astype(bf16)
        exp_out[0, h] = expo
        ctx_t.append(mm(v_t[h * HEAD : (h + 1) * HEAD], expo) * inverse)
    ctx_t = jnp.concatenate(ctx_t, axis=0).astype(bf16)
    ctxt_out[...] = ctx_t
    sum_out[...] = x.astype(f32) + (mm(ctx_t.T, w[:, 3 * WIDTH : 4 * WIDTH]) + vec[2:3])


def row_mean(v):
    return jnp.mean(v, axis=-1, keepdims=True)


def normalised(z):
    center = z - row_mean(z)
    r = lax.rsqrt(row_mean(center * center) + epsilon)
    return center * r, r


def norm_back(dy, zhat, r, gain):
    e = dy * gain
    return r * (e - row_mean(e) - zhat * row_mean(e * zhat))


def col_sum(v):
    return jnp.sum(v, axis=0, keepdims=True)


FF_STEP = 768


def feed_forward(
    ids, sum1, x0, x1, x2, x3, c0, c1, c2, c3, w_in, w_out, vec, bias_in,
    same, other, hidt_out, actt_out, dbranch_out, dinner_out, dsum_out, dattn_out, vec_grad, bias_grad,
    slope,
):
    s = pl.program_id(0)

    @pl.when(s == 0)
    def _():
        vec_grad[...] = jnp.zeros_like(vec_grad)
        bias_grad[...] = jnp.zeros_like(bias_grad)

    zhat1, r1 = normalised(sum1[...])
    hidden = zhat1 * vec[3:4] + vec[4:5]
    hid_low = hidden.astype(bf16)
    hidt_out[...] = hid_low.T
    branch = jnp.broadcast_to(vec[5:6], (SLOT, WIDTH))
    for n in range(0, FF, FF_STEP):
        cols = slice(n, n + FF_STEP)
        inner = mm(hid_low, w_in[:, cols]) + bias_in[0:1, cols]
        half = 0.5 * lax.erf(inner * 0.7071067811865476) + 0.5
        bell = 0.3989422804014327 * jnp.exp(-0.5 * (inner * inner))
        act = (inner * half).astype(bf16)
        actt_out[cols, :] = act.T
        slope[:, cols] = (half + inner * bell).astype(bf16)
        branch += mm(act, w_out[cols, :])
    zhat2, r2 = normalised(hidden + branch)
    gain2 = vec[6:7]
    normed = zhat2 * gain2 + vec[7:8]
    valid = (slot_positions(ids, (SLOT, 1), 0) < ids[s]).astype(f32)
    keep = ids[4 + s] == 0
    x = joined((x0, x1, x2, x3)).astype(f32)
    split_into(same, other, (jnp.where(keep, normed, x) * valid).astype(bf16))
    upstream = joined((c0, c1, c2, c3)).astype(f32)
    dy = upstream * jnp.where(keep, valid, 0.0)
    vec_grad[1:2] += col_sum(dy * zhat2)
    vec_grad[2:3] += col_sum(dy)
    d_sum2 = norm_back(dy, zhat2, r2, gain2)
    d_branch = d_sum2.astype(bf16)
    dbranch_out[...] = d_branch
    vec_grad[0:1] += col_sum(d_branch.astype(f32))
    d_hidden = d_sum2
    for n in range(0, FF, FF_STEP):
        cols = slice(n, n + FF_STEP)
        d_act = mm_nt(d_branch, w_out[cols, :])
        d_inner = (d_act * slope[:, cols].astype(f32)).astype(bf16)
        dinner_out[:, cols] = d_inner
        bias_grad[0:1, cols] += col_sum(d_inner.astype(f32))
        d_hidden += mm_nt(d_inner, w_in[:, cols])
    vec_grad[3:4] += col_sum(d_hidden * zhat1)
    vec_grad[4:5] += col_sum(d_hidden)
    d_sum1 = norm_back(d_hidden, zhat1, r1, vec[3:4])
    dsum_out[...] = d_sum1
    d_attn = d_sum1.astype(bf16)
    dattn_out[...] = d_attn
    vec_grad[5:6] += col_sum(d_attn.astype(f32))


def attention_backward(
    ids, dsum, dattn, qkv, exp_in, norm_in, ctxt_in, c0, c1, c2, c3, w,
    same, other, dqkv_out, vec_grad,
):
    s = pl.program_id(0)

    @pl.when(s == 0)
    def _():
        vec_grad[...] = jnp.zeros_like(vec_grad)

    d_sum1 = dsum[...]
    dctx_t = mm_nt(dattn[...], w[:, 3 * WIDTH : 4 * WIDTH]).T
    ctx_t = ctxt_in[...].astype(f32)
    k_t = qkv[:, WIDTH : 2 * WIDTH].T
    scaled = []
    deltas = []
    for h in range(HEADS):
        rows = slice(h * HEAD, (h + 1) * HEAD)
        one = (dctx_t[rows] * norm_in[0, h : h + 1, :]).astype(bf16)
        scaled.append(one)
        deltas.append(col_sum(one.astype(f32) * ctx_t[rows]))
    dctx_t = jnp.concatenate(scaled, axis=0)
    dctx = dctx_t.T
    low = lax.broadcasted_iota(jnp.int32, (SLOT, PAIR), 1) < HEAD
    dq_t = []
    for p in range(0, WIDTH, PAIR):
        cols = slice(p, p + PAIR)
        q_pair = qkv[:, cols]
        v_pair = qkv[:, 2 * WIDTH + p : 2 * WIDTH + p + PAIR]
        dks = []
        dvs = []
        for half in range(2):
            h = p // HEAD + half
            v_one = jnp.where(low if half == 0 else ~low, v_pair, jnp.zeros_like(v_pair))
            d_probs = mm(v_one, dctx_t[cols]) - deltas[h]
            expo = exp_in[0, h]
            d_scores = (expo.astype(f32) * d_probs).astype(bf16)
            dvs.append(mm(expo, dctx[:, cols]))
            dks.append(mm(d_scores, q_pair))
            dq_t.append(mm(k_t[h * HEAD : (h + 1) * HEAD], d_scores))
        dqkv_out[:, WIDTH + p : WIDTH + p + PAIR] = jnp.where(low, dks[0], dks[1]).astype(bf16)
        dqkv_out[:, 2 * WIDTH + p : 2 * WIDTH + p + PAIR] = jnp.where(low, dvs[0], dvs[1]).astype(bf16)
    dq = (jnp.concatenate(dq_t, axis=0).T * HEAD**-0.5).astype(bf16)
    dqkv_out[:, :WIDTH] = dq
    vec_grad[0:1] += col_sum(dq.astype(f32))
    vec_grad[1:2] += col_sum(dqkv_out[:, 2 * WIDTH :].astype(f32))
    d_in = d_sum1 + mm_nt(dqkv_out[...], w[:, : 3 * WIDTH])
    valid = (slot_positions(ids, (SLOT, 1), 0) < ids[s]).astype(f32)
    upstream = joined((c0, c1, c2, c3)).astype(f32) * valid
    keep = ids[4 + s] == 0
    split_into(same, other, jnp.where(keep, d_in, upstream).astype(bf16))


def weight_grad(ids, left, right, out):
    rows = left[...].reshape(out.shape[0] * out.shape[1], ROWS)
    out[...] = mm(rows, right[...]).astype(bf16).reshape(out.shape)


def merge_rows(ids, own, r1, r2, r3, *outs):
    me = ids[12]
    values = [v[...].astype(f32) for v in (own, r1, r2, r3)]
    ordered = []
    for j in range(RING):
        step = lax.rem(me + RING - j, RING)
        value = values[0]
        for d in (1, 2, 3):
            value = jnp.where(step == d, values[d], value)
        ordered.append(value)
    (out,) = outs
    width = own.shape[1]
    out[:, :width] = jnp.concatenate([v[:6] for v in ordered], axis=0).astype(bf16)
    if out.shape[1] > width:
        row = jnp.concatenate([v[6:7, :128] for v in ordered], axis=1)
        first = lax.broadcasted_iota(jnp.int32, (24, 4 * 128), 0) == 0
        out[:, width:] = jnp.where(first, jnp.broadcast_to(row, (24, 4 * 128)), 0.0).astype(bf16)


def place_pieces(ids, p0, p1, p2, p3, out, sems):
    copies = []
    for d, piece in enumerate((p0, p1, p2, p3)):
        x = lax.rem(ids[8] + d, RING)
        for e in range(CORES):
            c = ids[9] if e == 0 else 1 - ids[9]
            copies.append(pltpu.make_async_copy(piece.at[e], out.at[x, c], sems.at[d, e]))
    for copy in copies:
        copy.start()
    for copy in copies:
        copy.wait()


def whole(shape):
    return pl.BlockSpec(shape, lambda s, ids: (0,) * len(shape), pipeline_mode=pl.Buffered(1))


PIECE_SPEC = pl.BlockSpec((CORES, 1, PIECE, WIDTH), lambda s, ids: (0, s, 0, 0))
PIECE_SHAPE = jax.ShapeDtypeStruct((CORES, SEQ_DEV, PIECE, WIDTH), bf16)


def by_rows(width):
    return pl.BlockSpec((SLOT, width), lambda s, ids: (s, 0))


def rows_of(width, kind):
    return jax.ShapeDtypeStruct((ROWS, width), kind)


EXP_SPEC = pl.BlockSpec((1, HEADS, SLOT, SLOT), lambda s, ids: (s, 0, 0, 0))
NORM_SPEC = pl.BlockSpec((1, 16, SLOT), lambda s, ids: (s, 0, 0))
RETURN_SPEC = pl.BlockSpec((RING, 1, PIECE, WIDTH), lambda s, ids: (0, s, 0, 0))
RETURN_SHAPE = jax.ShapeDtypeStruct((RING, SEQ_DEV, PIECE, WIDTH), bf16)


def by_columns(height):
    return pl.BlockSpec((height, SLOT), lambda s, ids: (0, s))


def columns_of(height):
    return jax.ShapeDtypeStruct((height, ROWS), bf16)


def run(kernel, grid, ins, outs, operands, name, flops, moved, scratch=()):
    return pl.pallas_call(
        kernel,
        grid_spec=pltpu.PrefetchScalarGridSpec(
            num_scalar_prefetch=1,
            grid=grid,
            in_specs=ins,
            out_specs=[spec for spec, _ in outs],
            scratch_shapes=list(scratch),
        ),
        out_shape=[shape for _, shape in outs],
        compiler_params=pltpu.CompilerParams(
            vmem_limit_bytes=VMEM_LIMIT, dimension_semantics=("arbitrary",) * len(grid)
        ),
        cost_estimate=pl.CostEstimate(flops=flops, bytes_accessed=moved, transcendentals=0),
        name=name,
    )(*operands)


def out_rows(width, kind):
    return (by_rows(width), rows_of(width, kind))


def out_columns(height):
    return (by_columns(height), columns_of(height))


def out_whole(shape):
    return (whole(shape), jax.ShapeDtypeStruct(shape, f32))


def call_forward(ids, pieces, w, extras, perm):
    return run(
        attention_forward,
        (SEQ_DEV,),
        [PIECE_SPEC] * 4 + [whole((WIDTH, PACKED)), whole((128, 128)), whole((128, 4))],
        [
            out_columns(WIDTH),
            out_rows(3 * WIDTH, bf16),
            (EXP_SPEC, jax.ShapeDtypeStruct((SEQ_DEV, HEADS, SLOT, SLOT), bf16)),
            (NORM_SPEC, jax.ShapeDtypeStruct((SEQ_DEV, 16, SLOT), f32)),
            out_columns(WIDTH),
            out_rows(WIDTH, f32),
            out_whole((8, WIDTH)),
            out_whole((1, FF)),
        ],
        (ids, *pieces, w, extras, perm),
        "attention_forward",
        22 * 10**9,
        22 * 10**6,
    )


def call_ffn(ids, sum1, pieces, cots, w_in, w_out, vec, bias_in):
    return run(
        feed_forward,
        (SEQ_DEV,),
        [by_rows(WIDTH)]
        + [PIECE_SPEC] * 8
        + [whole((WIDTH, FF)), whole((FF, WIDTH)), whole((8, WIDTH)), whole((1, FF))],
        [(RETURN_SPEC, RETURN_SHAPE)] * 2
        + [
            out_columns(WIDTH),
            out_columns(FF),
            out_rows(WIDTH, bf16),
            out_rows(FF, bf16),
            out_rows(WIDTH, f32),
            out_rows(WIDTH, bf16),
            out_whole((8, WIDTH)),
            out_whole((1, FF)),
        ],
        (ids, sum1, *pieces, *cots, w_in, w_out, vec, bias_in),
        "feed_forward",
        36 * 10**9,
        40 * 10**6,
        [pltpu.VMEM((SLOT, FF), bf16)],
    )


def call_backward(ids, dsum, dattn, qkv, expo, norm, ctx_t, cots, w):
    return run(
        attention_backward,
        (SEQ_DEV,),
        [by_rows(WIDTH), by_rows(WIDTH), by_rows(3 * WIDTH), EXP_SPEC, NORM_SPEC, by_columns(WIDTH)]
        + [PIECE_SPEC] * 4
        + [whole((WIDTH, PACKED))],
        [(RETURN_SPEC, RETURN_SHAPE)] * 2 + [out_rows(3 * WIDTH, bf16), out_whole((8, WIDTH))],
        (ids, dsum, dattn, qkv, expo, norm, ctx_t, *cots, w),
        "attention_backward",
        24 * 10**9,
        30 * 10**6,
    )


def call_grad(ids, left, right, away, x_block, step):
    rows = left.shape[0] // (RING * CORES)
    width = right.shape[1]
    left = left.reshape(RING, CORES, rows, ROWS)
    (out,) = run(
        weight_grad,
        (RING // x_block, width // step),
        [
            pl.BlockSpec((x_block, 1, rows, ROWS), lambda i, n, ids: (i, 1 - ids[9] if away else ids[9], 0, 0)),
            pl.BlockSpec((ROWS, step), lambda i, n, ids: (0, n)),
        ],
        [
            (
                pl.BlockSpec((x_block, rows, step), lambda i, n, ids: (i, 0, n)),
                jax.ShapeDtypeStruct((RING, rows, width), bf16),
            )
        ],
        (ids, left, right),
        "weight_grad",
        2 * RING * rows * ROWS * width,
        2 * (RING * rows * ROWS + ROWS * width + RING * rows * width),
    )
    return out


def call_merge(ids, pieces, width):
    shape = (8, pieces[0].shape[1])
    spec = pl.BlockSpec(shape, lambda i, ids: (0, 0))
    (out,) = run(
        merge_rows,
        (1,),
        [spec] * 4,
        [(pl.BlockSpec((24, width), lambda i, ids: (0, 0)), jax.ShapeDtypeStruct((24, width), bf16))],
        (ids, *pieces),
        "merge_rows",
        10**6,
        10**6,
    )
    return out


def call_place(ids, pieces):
    anywhere = pl.BlockSpec(memory_space=pl.ANY)
    shape = (RING, CORES, SEQ_DEV, PIECE, WIDTH)
    (out,) = run(
        place_pieces,
        (1,),
        [anywhere] * 4,
        [(anywhere, jax.ShapeDtypeStruct(shape, bf16))],
        (ids, *pieces),
        "place_pieces",
        10**6,
        3 * 10**6,
        [pltpu.SemaphoreType.DMA((RING, CORES))],
    )
    return out.reshape(RING * CORES * SEQ_DEV, PIECE, WIDTH)


def shift(value, axis, step):
    size = CORES if axis == "core" else RING
    return lax.ppermute(value, axis, [(i, (i + step) % size) for i in range(size)])


def at(value, index):
    return lax.dynamic_index_in_dim(value, index, 0, keepdims=False)


def gather_ring(value, axis):
    me = lax.axis_index(axis)
    out = jnp.broadcast_to(value[None], (RING,) + value.shape)
    for step in (1, 3, 2):
        out = lax.dynamic_update_index_in_dim(
            out, shift(value, axis, step), lax.rem(me + RING - step, RING), 0
        )
    return out


def gather_last(value, axis, out_shape, place):
    me = lax.axis_index(axis)
    core = lax.axis_index("core")
    out = jnp.zeros(out_shape, bf16)
    for step in (0, 1, 3, 2):
        piece = shift(value, axis, step) if step else value
        other = shift(piece, "core", 1)
        source = lax.rem(me + RING - step, RING)
        for part, c in ((piece, core), (other, 1 - core)):
            start = place(source, c)
            block = tuple(1 if isinstance(v, jax.Array) else n for v, n in zip(start, out_shape))
            start = [v if isinstance(v, jax.Array) else 0 for v in start]
            out = lax.dynamic_update_slice(out, part.reshape(block), start)
    return out


def hold(value, *others):
    return lax.optimization_barrier((value, *others))[0]


def send_ring(value, axis):
    me = lax.axis_index(axis)
    return [at(value, me)] + [
        shift(at(value, lax.rem(me + step, RING)), axis, step) for step in (1, 3, 2)
    ]


def total(parts):
    first, *rest = (part.astype(f32) for part in parts)
    return sum(rest, first)


def add_core(mine, away):
    return (mine.astype(f32) + away.astype(f32)).astype(bf16)


def deal(pieces):
    me_x = lax.axis_index("x")
    me_c = lax.axis_index("core")
    grid = pieces.reshape(RING, CORES, SEQ_DEV, PIECE, WIDTH)
    mine = lax.dynamic_index_in_dim(grid, me_c, 1, keepdims=False)
    away = lax.dynamic_index_in_dim(grid, 1 - me_c, 1, keepdims=False)
    both = jnp.stack([mine, shift(away, "core", 1)], axis=1)
    return [at(both, me_x)] + [shift(at(both, lax.rem(me_x + d, RING)), "x", d) for d in (1, 2, 3)]


def send_back(same, other):
    both = jnp.stack([same, shift(other, "core", 1)], axis=1)
    return [both[0]] + [shift(both[d], "x", RING - d) for d in (1, 2, 3)]


def vector_block(narrow, wide):
    groups = RING * CORES * RING
    row = narrow.reshape(-1, groups, RING, 6).transpose(1, 2, 0, 3).reshape(groups, 1, -1)
    rows = [jnp.pad(row, ((0, 0), (0, 0), (0, EXTRA - row.shape[2])))]
    if wide is not None:
        rows.append(jnp.pad(wide.reshape(groups, 1, 96), ((0, 0), (0, 0), (0, EXTRA - 96))))
    block = jnp.pad(jnp.concatenate(rows, axis=1), ((0, 0), (0, 24 - len(rows)), (0, 0)))
    block = block.reshape(RING, CORES, RING * 24, EXTRA).astype(bf16)
    me_c = lax.axis_index("core")
    mine = lax.dynamic_index_in_dim(block, me_c, 1, keepdims=False)
    away = lax.dynamic_index_in_dim(block, 1 - me_c, 1, keepdims=False)
    return mine, shift(away, "core", 1)


def last_rows(value, narrow, wide):
    width = value.shape[1] - EXTRA
    rows = value[:, :width].reshape(RING, 6, width)
    vectors = value[0, width:][: RING * narrow * 6].reshape(RING, narrow * 6)
    if wide:
        vectors = jnp.concatenate([vectors, value[1, width:][:96].reshape(RING, 24)], axis=1)
    vectors = jnp.pad(vectors, ((0, 0), (0, width - vectors.shape[1])))
    return jnp.concatenate([rows, vectors[:, None], jnp.zeros((RING, 1, width), bf16)], axis=1)


def body(
    tokens,
    cotangent,
    perm,
    lengths,
    drop,
    w_query,
    b_query,
    w_key,
    w_value,
    b_value,
    w_out,
    b_out,
    norm1_gain,
    norm1_bias,
    w_inner,
    b_inner,
    w_outer,
    b_outer,
    norm2_gain,
    norm2_bias,
):
    me_x = lax.axis_index("x")
    me_c = lax.axis_index("core")
    me_z = lax.axis_index("z")
    me_y = lax.axis_index("y")
    first = ((me_z * RING + me_y) * 8 + me_x * CORES + me_c) * SEQ_DEV
    places = jnp.stack([me_x, me_c, first, me_z, me_y]).astype(jnp.int32)
    places = jnp.pad(places, (8, 3))

    vectors = [b_query, b_value, b_out, norm1_gain, norm1_bias, b_outer, norm2_gain, norm2_bias, b_inner]
    vectors += [lengths.astype(bf16), drop.astype(bf16)]
    row = jnp.zeros((4 * WIDTH,), bf16)
    start = 0
    for vector in vectors:
        end = start + vector.shape[0]
        row += jnp.pad(vector, (start, 4 * WIDTH - end))
        start = end
    attn_piece = jnp.concatenate([w_query, w_key, w_value, w_out], axis=1)
    attn_piece = jnp.concatenate([attn_piece, row[None], jnp.zeros((1, 4 * WIDTH), bf16)])
    attn_y = [attn_piece] + [shift(attn_piece, "y", d) for d in (1, 2, 3)]
    dealt_x = deal(tokens)
    attn_y = call_merge(places, attn_y, PACKED)
    attn_xy = gather_ring(attn_y, "x")
    attn_all = gather_last(
        attn_xy, "z", (RING, CORES, RING, 24, PACKED), lambda z, c: (0, c, z, 0, 0)
    )
    attn_full = attn_all.reshape(WIDTH, PACKED)
    extras = attn_all[:, :, :, 0, 4 * WIDTH :].reshape(128, 128)

    inner_piece = hold(jnp.pad(w_inner, ((0, 2), (0, 0))), attn_y)
    inner_y = [inner_piece] + [shift(inner_piece, "y", d) for d in (1, 2, 3)]
    inner_y = call_merge(places, inner_y, FF)
    outer_z = gather_ring(hold(w_outer, attn_y), "z")
    inner_zy = gather_ring(inner_y, "z").reshape(96, FF)
    outer_xz = gather_ring(outer_z, "x")
    outer_full = gather_last(
        outer_xz, "y", (RING, CORES, RING, RING, 24, WIDTH), lambda y, c: (0, c, 0, y, 0, 0)
    ).reshape(FF, WIDTH)
    inner_full = gather_last(
        hold(inner_zy, attn_xy), "x", (RING, CORES, 96, FF), lambda x, c: (x, c, 0, 0)
    ).reshape(WIDTH, FF)
    dealt_c = deal(hold(cotangent, dealt_x[1], attn_xy))

    x_t, qkv, expo, norm, ctx_t, sum1, vec, inner_bias = call_forward(
        places, dealt_x, attn_full, extras, perm.reshape(128, 4)
    )

    slot_values = extras[:, 72:80].reshape(128, 2, 4).transpose(1, 0, 2).reshape(2, 512).astype(f32)
    wanted = first + jnp.arange(SEQ_DEV, dtype=jnp.int32)
    hit = (perm[None, :] == wanted[:, None]).astype(f32)
    found = jnp.sum(hit[None] * slot_values[:, None], axis=2).astype(jnp.int32)
    ids = jnp.concatenate([found.reshape(8), places[8:]])

    same, other, hid_t, act_t, d_branch, d_inner, d_sum1, d_attn, vec_grad, bias_grad = call_ffn(
        ids, sum1, dealt_x, dealt_c, inner_full, outer_full, vec, inner_bias
    )
    layer_back = send_back(same, other)

    outer_away = call_grad(ids, act_t, d_branch, True, 1, WIDTH)
    outer_core = shift(outer_away, "core", 1)
    outer_mine = call_grad(hold(ids, outer_away), act_t, d_branch, False, 1, WIDTH)
    outer_sum = add_core(outer_mine, outer_core).reshape(RING, RING, RING, 24, WIDTH)
    outer_parts = send_ring(outer_sum.transpose(2, 0, 1, 3, 4), "y")

    ids_inner = hold(ids, *outer_parts[:1])
    inner_away = jnp.concatenate(
        [
            call_grad(ids_inner, hid_t, d_inner, True, RING, WIDTH),
            call_grad(ids_inner, ctx_t, d_attn, True, RING, WIDTH),
        ],
        axis=2,
    )
    inner_core = shift(inner_away, "core", 1)
    ids_mine = hold(ids, inner_away)
    inner_mine = jnp.concatenate(
        [
            call_grad(ids_mine, hid_t, d_inner, False, RING, WIDTH),
            call_grad(ids_mine, ctx_t, d_attn, False, RING, WIDTH),
        ],
        axis=2,
    )
    vec_mine, vec_core = vector_block(vec_grad[:6], bias_grad)
    inner_sum = jnp.concatenate(
        [add_core(inner_mine, inner_core), add_core(vec_mine, vec_core)], axis=2
    )
    inner_width = inner_sum.shape[2]
    inner_sum = inner_sum.reshape(RING, RING, 24, inner_width).transpose(1, 0, 2, 3)
    inner_parts = send_ring(inner_sum, "z")

    d_sum1, d_attn = lax.optimization_barrier((d_sum1, d_attn, inner_parts[0]))[:2]
    grad_same, grad_other, d_qkv, qkv_vec = call_backward(
        ids, d_sum1, d_attn, qkv, expo, norm, ctx_t, dealt_c, attn_full
    )
    grad_back = send_back(grad_same, grad_other)

    inner_parts = [inner_parts[0]] + [hold(p, d_qkv) for p in inner_parts[1:]]
    outer_parts = [outer_parts[0]] + [hold(p, inner_away) for p in outer_parts[1:]]
    inner_z = total(inner_parts).astype(bf16)
    outer_y = total(outer_parts).astype(bf16)
    outer_y = outer_y.transpose(0, 2, 1, 3).reshape(RING, 24, RING * WIDTH)
    mid_parts = send_ring(jnp.concatenate([inner_z, outer_y], axis=2), "x")

    attn_away = call_grad(ids, x_t, d_qkv, True, RING, WIDTH)
    attn_core = shift(attn_away, "core", 1)
    attn_mine = call_grad(hold(ids, attn_away), x_t, d_qkv, False, RING, WIDTH)
    vec_mine, vec_core = vector_block(qkv_vec[:2], None)
    attn_sum = jnp.concatenate([add_core(attn_mine, attn_core), add_core(vec_mine, vec_core)], axis=2)
    attn_sum = attn_sum.reshape(RING, RING, 24, attn_sum.shape[2]).transpose(1, 0, 2, 3)
    attn_z = total(send_ring(attn_sum, "z")).astype(bf16)

    mid = total(mid_parts).astype(bf16)
    outer_grad = total(send_ring(mid[:, inner_width:].reshape(24, RING, WIDTH).transpose(1, 0, 2), "z"))
    inner_grad = total(send_ring(last_rows(mid[:, :inner_width], 6, True), "y"))
    attn_x = total(send_ring(attn_z, "x")).astype(bf16)
    attn_grad = total(send_ring(last_rows(attn_x, 2, False), "y"))
    layer_final = call_place(places, layer_back)
    grad_final = call_place(places, grad_back)
    inner_vecs = inner_grad[6, :36].reshape(6, 6)
    return (
        layer_final,
        grad_final,
        attn_grad[:6, :WIDTH],
        attn_grad[6, :6],
        attn_grad[:6, WIDTH : 2 * WIDTH],
        attn_grad[:6, 2 * WIDTH :],
        attn_grad[6, 6:12],
        inner_grad[:6, FF:],
        inner_vecs[5],
        inner_vecs[3],
        inner_vecs[4],
        inner_grad[:6, :FF],
        inner_grad[6, 36:60],
        outer_grad,
        inner_vecs[0],
        inner_vecs[1],
        inner_vecs[2],
    )


def solution(mesh):
    chips = Mesh(mesh.devices.reshape(RING, CORES, RING, RING), ("x", "core", "z", "y"))
    dp = ("x", "core")
    fsdp = ("z", "y")
    every = P(dp + fsdp)
    rows = P(dp + fsdp, None)
    whole_rows = P(fsdp, dp, None)
    return jax.shard_map(
        body,
        mesh=chips,
        in_specs=(
            whole_rows, whole_rows, P(), every, every,
            rows, every, rows, rows, every, rows, every, every, every,
            rows, every, rows, every, every, every,
        ),
        out_specs=(
            whole_rows, whole_rows,
            rows, every, rows, rows, every, rows, every, every, every,
            rows, every, rows, every, every, every,
        ),
        check_vma=False,
    )
```

```python
import functools
import jax
import jax.numpy as jnp
from jax import lax
from jax.experimental import pallas as pl
from jax.experimental.pallas import tpu as pltpu
from jax.sharding import Mesh
from jax.sharding import PartitionSpec as P

HEADS = 12
HEAD = 64
WIDTH = 768
FF = 3072
SLOT = 256
SEQ_DEV = 4
RING = 4
CORES = 2
PIECE = 32
ROWS = SEQ_DEV * SLOT
PAIR = 2 * HEAD
PACKED = 4 * WIDTH + 512

epsilon = 1e-05
bf16 = jnp.bfloat16
f32 = jnp.float32
VMEM_LIMIT = 58 * 1024 * 1024

TN = (((0,), (0,)), ((), ()))
NT = (((1,), (1,)), ((), ()))


def mm(a, b):
    return jnp.dot(a, b, preferred_element_type=f32)


def mm_nt(a, b):
    return lax.dot_general(a, b, NT, preferred_element_type=f32)


def mm_tn(a, b):
    return lax.dot_general(a, b, TN, preferred_element_type=f32)


def slot_positions(ids, shape, axis):
    row = lax.broadcasted_iota(jnp.int32, shape, axis)
    from_x = row // (CORES * PIECE)
    away = lax.rem(row // PIECE, CORES)
    from_c = jnp.where(away == 1, 1 - ids[9], ids[9])
    return (from_x * CORES + from_c) * PIECE + lax.rem(row, PIECE)


def joined(ref):
    return ref[...].reshape(SLOT, WIDTH)


def split_into(same, other, rows):
    for d in range(RING):
        start = d * CORES * PIECE
        same[d, 0] = rows[start : start + PIECE]
        other[d, 0] = rows[start + PIECE : start + 2 * PIECE]


def spread(extras, start, width):
    total = 128 * width
    group = lax.broadcasted_iota(jnp.int32, (32, total), 0)
    owner = lax.broadcasted_iota(jnp.int32, (32, total), 1) // width
    pick = lax.broadcasted_iota(jnp.int32, (width, total), 0)
    within = lax.rem(lax.broadcasted_iota(jnp.int32, (width, total), 1), width)
    chosen = (pick == within).astype(bf16)
    out = jnp.zeros((32, total), f32)
    for y in range(RING):
        values = extras[:, 128 * y + start : 128 * y + start + width].astype(bf16)
        out += jnp.where(owner == group * RING + y, mm(values, chosen), 0.0)
    return jnp.sum(out, axis=0, keepdims=True)


def gather_back(vectors):
    values = jnp.zeros((128, 128), f32)
    start = 0
    for vector in vectors:
        total = vector.shape[1]
        width = total // 128
        owner = lax.broadcasted_iota(jnp.int32, (128, total), 1) // width
        mine = owner == lax.broadcasted_iota(jnp.int32, (128, total), 0)
        within = lax.rem(lax.broadcasted_iota(jnp.int32, (total, 128), 0), width)
        column = lax.broadcasted_iota(jnp.int32, (total, 128), 1)
        spots = (column == within + start).astype(bf16)
        values += mm(jnp.where(mine, vector, 0.0).astype(bf16), spots)
        start += width
    row = lax.broadcasted_iota(jnp.int32, (WIDTH, 128), 0)
    device = lax.broadcasted_iota(jnp.int32, (WIDTH, 128), 1)
    within = lax.rem(row, 24)
    picks = (within < RING) & (row // 24 * RING + within == device)
    return mm(picks.astype(bf16), values.astype(bf16)).astype(bf16)


def attention_copies(ids, pieces, w, sems):
    copies = []
    for i, piece in enumerate(pieces):
        x = lax.rem(ids[8] + RING - i // 2, RING)
        c = ids[9] if i % 2 == 0 else 1 - ids[9]
        copies.append(pltpu.make_async_copy(piece, w.at[x, c], sems.at[i]))
    return copies


def columns(w, start, end):
    return w[:, :, :, start:end].reshape(WIDTH, end - start)


def attention_forward(
    ids, x_in, p0, p1, p2, p3, p4, p5, p6, p7, perm,
    xt_out, qkv_out, exp_out, norm_out, ctxt_out, sum_out, vec, bias_out, info,
    w, extras, sems,
):
    s = pl.program_id(0)

    @pl.when(s == 0)
    def _():
        copies = attention_copies(ids, (p0, p1, p2, p3, p4, p5, p6, p7), w, sems)
        for copy in copies:
            copy.start()
        for copy in copies:
            copy.wait()
        rows = columns(w, 4 * WIDTH, PACKED).astype(f32).reshape(32, 24, PACKED - 4 * WIDTH)
        extras[...] = jnp.sum(rows, axis=1)
        for i in range(8):
            vec[i : i + 1] = spread(extras, 6 * i, 6)
        bias_out[...] = spread(extras, 48, 24)

    length = jnp.zeros((1, 1), f32)
    dropped = jnp.zeros((1, 1), f32)
    for y in range(RING):
        hit = perm[:, RING * y : RING * y + 4] == ids[10] + s
        length += jnp.sum(jnp.where(hit, extras[:, 128 * y + 72 : 128 * y + 76], 0.0), keepdims=True)
        dropped += jnp.sum(jnp.where(hit, extras[:, 128 * y + 76 : 128 * y + 80], 0.0), keepdims=True)
    line = lax.broadcasted_iota(jnp.int32, (8, 128), 0)
    info[...] = jnp.where(line == s, length, jnp.where(line == s + 4, dropped, info[...]))

    x = joined(x_in)
    xt_out[...] = x.T
    q = ((mm(x, columns(w, 0, WIDTH)) + vec[0:1]).astype(bf16).astype(f32) * HEAD**-0.5).astype(bf16)
    k = mm(x, columns(w, WIDTH, 2 * WIDTH)).astype(bf16)
    v = (mm(x, columns(w, 2 * WIDTH, 3 * WIDTH)) + vec[1:2]).astype(bf16)
    qkv_out[:, :WIDTH] = q
    qkv_out[:, WIDTH : 2 * WIDTH] = k
    qkv_out[:, 2 * WIDTH :] = v
    q_t = q.T
    v_t = v.T
    keys = slot_positions(ids, (SLOT, 1), 0).astype(f32)
    bias = jnp.where(keys < length, 0.0, -1e30)
    low = lax.broadcasted_iota(jnp.int32, (SLOT, PAIR), 1) < HEAD
    ctx_t = []
    for h in range(HEADS):
        p = h // 2 * PAIR
        k_pair = k[:, p : p + PAIR]
        k_one = jnp.where(low if h % 2 == 0 else ~low, k_pair, jnp.zeros_like(k_pair))
        scores = mm(k_one, q_t[p : p + PAIR]) + bias
        top = jnp.max(scores, axis=0, keepdims=True)
        expo = jnp.exp(scores - top)
        inverse = 1.0 / jnp.sum(expo, axis=0, keepdims=True)
        norm_out[0, h : h + 1, :] = inverse
        expo = expo.astype(bf16)
        exp_out[0, h] = expo
        ctx_t.append(mm(v_t[h * HEAD : (h + 1) * HEAD], expo) * inverse)
    ctx_t = jnp.concatenate(ctx_t, axis=0).astype(bf16)
    ctxt_out[...] = ctx_t
    sum_out[...] = x.astype(f32) + (mm(ctx_t.T, columns(w, 3 * WIDTH, 4 * WIDTH)) + vec[2:3])


def row_mean(v):
    return jnp.mean(v, axis=-1, keepdims=True)


def normalised(z):
    center = z - row_mean(z)
    r = lax.rsqrt(row_mean(center * center) + epsilon)
    return center * r, r


def norm_back(dy, zhat, r, gain):
    e = dy * gain
    return r * (e - row_mean(e) - zhat * row_mean(e * zhat))


def col_sum(v):
    return jnp.sum(v, axis=0, keepdims=True)


FF_STEP = 768


def feed_forward(
    ids, sum1, x_in, c_in, i0, i1, i2, i3, j0, j1, j2, j3, vec, bias_in,
    same, other, hidt_out, actt_out, dbranch_out, dinner_out, dsum_out, dattn_out, vec_block,
    slope, vec_grad, bias_grad, w_in, w_out, in_sems, out_sems,
):
    s = pl.program_id(0)

    def copies():
        ins = []
        outs = []
        for i, (piece, late) in enumerate(zip((i0, i1, i2, i3), (j0, j1, j2, j3))):
            c = ids[9] if i % 2 == 0 else 1 - ids[9]
            z_half = ids[11] // 2 if i // 2 == 0 else 1 - ids[11] // 2
            y_half = ids[12] // 2 if i // 2 == 0 else 1 - ids[12] // 2
            for d in range(RING):
                x = lax.rem(ids[8] + RING - d, RING)
                ins.append(pltpu.make_async_copy(piece.at[d], w_in.at[x, c, z_half], in_sems.at[i, d]))
                for n in range(RING):
                    half = ids[11] // 2 if n // 2 == 0 else 1 - ids[11] // 2
                    target = w_out.at[x, c, 2 * half + n % 2, y_half]
                    outs.append(pltpu.make_async_copy(late.at[n, d], target, out_sems.at[i, d, n]))
        return ins, outs

    @pl.when(s == 0)
    def _():
        vec_grad[...] = jnp.zeros_like(vec_grad)
        bias_grad[...] = jnp.zeros_like(bias_grad)
        ins, outs = copies()
        for copy in ins + outs:
            copy.start()
        for copy in ins + outs:
            copy.wait()

    def inner_columns(start):
        return w_in[:, :, :, :, start : start + FF_STEP].reshape(WIDTH, FF_STEP)

    def outer_rows(start):
        x = start // (FF // RING)
        return w_out[x].reshape(FF // RING, WIDTH)

    zhat1, r1 = normalised(sum1[...])
    hidden = zhat1 * vec[3:4] + vec[4:5]
    hid_low = hidden.astype(bf16)
    hidt_out[...] = hid_low.T
    branch = jnp.broadcast_to(vec[5:6], (SLOT, WIDTH))
    for n in range(0, FF, FF_STEP):
        cols = slice(n, n + FF_STEP)
        inner = mm(hid_low, inner_columns(n)) + bias_in[0:1, cols]
        half = 0.5 * lax.erf(inner * 0.7071067811865476) + 0.5
        bell = 0.3989422804014327 * jnp.exp(-0.5 * (inner * inner))
        act = (inner * half).astype(bf16)
        actt_out[cols, :] = act.T
        slope[:, cols] = (half + inner * bell).astype(bf16)
        branch += mm(act, outer_rows(n))
    zhat2, r2 = normalised(hidden + branch)
    gain2 = vec[6:7]
    normed = zhat2 * gain2 + vec[7:8]
    valid = (slot_positions(ids, (SLOT, 1), 0) < ids[s]).astype(f32)
    keep = ids[4 + s] == 0
    x = joined(x_in).astype(f32)
    split_into(same, other, (jnp.where(keep, normed, x) * valid).astype(bf16))
    upstream = joined(c_in).astype(f32)
    dy = upstream * jnp.where(keep, valid, 0.0)
    vec_grad[1:2] += col_sum(dy * zhat2)
    vec_grad[2:3] += col_sum(dy)
    d_sum2 = norm_back(dy, zhat2, r2, gain2)
    d_branch = d_sum2.astype(bf16)
    dbranch_out[...] = d_branch
    vec_grad[0:1] += col_sum(d_branch.astype(f32))
    d_hidden = d_sum2
    for n in range(0, FF, FF_STEP):
        cols = slice(n, n + FF_STEP)
        d_act = mm_nt(d_branch, outer_rows(n))
        d_inner = (d_act * slope[:, cols].astype(f32)).astype(bf16)
        dinner_out[:, cols] = d_inner
        bias_grad[0:1, cols] += col_sum(d_inner.astype(f32))
        d_hidden += mm_nt(d_inner, inner_columns(n))
    vec_grad[3:4] += col_sum(d_hidden * zhat1)
    vec_grad[4:5] += col_sum(d_hidden)
    d_sum1 = norm_back(d_hidden, zhat1, r1, vec[3:4])
    dsum_out[...] = d_sum1
    d_attn = d_sum1.astype(bf16)
    dattn_out[...] = d_attn
    vec_grad[5:6] += col_sum(d_attn.astype(f32))

    @pl.when(s == SEQ_DEV - 1)
    def _():
        vec_block[...] = gather_back([vec_grad[i : i + 1] for i in range(6)] + [bias_grad[...]])


def attention_backward(
    ids, dsum, dattn, qkv, exp_in, norm_in, ctxt_in, c_in, p0, p1, p2, p3, p4, p5, p6, p7,
    same, other, dqkv_out, vec_block,
    w, vec_grad, sems,
):
    s = pl.program_id(0)

    @pl.when(s == 0)
    def _():
        vec_grad[...] = jnp.zeros_like(vec_grad)
        copies = attention_copies(ids, (p0, p1, p2, p3, p4, p5, p6, p7), w, sems)
        for copy in copies:
            copy.start()
        for copy in copies:
            copy.wait()

    d_sum1 = dsum[...]
    dctx_t = mm_nt(dattn[...], columns(w, 3 * WIDTH, 4 * WIDTH)).T
    ctx_t = ctxt_in[...].astype(f32)
    k_t = qkv[:, WIDTH : 2 * WIDTH].T
    scaled = []
    deltas = []
    for h in range(HEADS):
        rows = slice(h * HEAD, (h + 1) * HEAD)
        one = (dctx_t[rows] * norm_in[0, h : h + 1, :]).astype(bf16)
        scaled.append(one)
        deltas.append(col_sum(one.astype(f32) * ctx_t[rows]))
    dctx_t = jnp.concatenate(scaled, axis=0)
    dctx = dctx_t.T
    low = lax.broadcasted_iota(jnp.int32, (SLOT, PAIR), 1) < HEAD
    dq_t = []
    for p in range(0, WIDTH, PAIR):
        cols = slice(p, p + PAIR)
        q_pair = qkv[:, cols]
        v_pair = qkv[:, 2 * WIDTH + p : 2 * WIDTH + p + PAIR]
        dks = []
        dvs = []
        for half in range(2):
            h = p // HEAD + half
            v_one = jnp.where(low if half == 0 else ~low, v_pair, jnp.zeros_like(v_pair))
            d_probs = mm(v_one, dctx_t[cols]) - deltas[h]
            expo = exp_in[0, h]
            d_scores = (expo.astype(f32) * d_probs).astype(bf16)
            dvs.append(mm(expo, dctx[:, cols]))
            dks.append(mm(d_scores, q_pair))
            dq_t.append(mm(k_t[h * HEAD : (h + 1) * HEAD], d_scores))
        dqkv_out[:, WIDTH + p : WIDTH + p + PAIR] = jnp.where(low, dks[0], dks[1]).astype(bf16)
        dqkv_out[:, 2 * WIDTH + p : 2 * WIDTH + p + PAIR] = jnp.where(low, dvs[0], dvs[1]).astype(bf16)
    dq = (jnp.concatenate(dq_t, axis=0).T * HEAD**-0.5).astype(bf16)
    dqkv_out[:, :WIDTH] = dq
    vec_grad[0:1] += col_sum(dq.astype(f32))
    vec_grad[1:2] += col_sum(dqkv_out[:, 2 * WIDTH :].astype(f32))
    d_in = d_sum1 + mm_nt(dqkv_out[...], columns(w, 0, 3 * WIDTH))
    valid = (slot_positions(ids, (SLOT, 1), 0) < ids[s]).astype(f32)
    upstream = joined(c_in).astype(f32) * valid
    keep = ids[4 + s] == 0
    split_into(same, other, jnp.where(keep, d_in, upstream).astype(bf16))

    @pl.when(s == SEQ_DEV - 1)
    def _():
        vec_block[...] = gather_back([vec_grad[0:1], vec_grad[1:2]])


def weight_grad(ids, left, right, *refs):
    *tail, away, mine = refs
    value = mm(left[...], right[...]).astype(bf16)
    if tail:
        value = jnp.concatenate([value, tail[0][...]], axis=1)
    blocks, rows, _ = away.shape
    first = ids[9] == 0
    for x in range(blocks):
        even = value[2 * x * rows : (2 * x + 1) * rows]
        odd = value[(2 * x + 1) * rows : (2 * x + 2) * rows]
        away[x] = jnp.where(first, odd, even)
        mine[x] = jnp.where(first, even, odd)


def in_order(values, me):
    ordered = []
    for j in range(RING):
        step = lax.rem(me + RING - j, RING)
        value = values[0]
        for d in (1, 2, 3):
            value = jnp.where(step == d, values[d], value)
        ordered.append(value)
    return ordered


def merge_rows(ids, own, r1, r2, r3, attn_out, inner_out):
    ordered = in_order([v[...].astype(f32) for v in (own, r1, r2, r3)], ids[12])
    width = 4 * WIDTH
    rows = jnp.concatenate([v[:6] for v in ordered], axis=0).astype(bf16)
    attn_out[:, :width] = rows[:, :width]
    inner_out[...] = rows[:, width:]
    row = jnp.concatenate([v[6:7, :128] for v in ordered], axis=1)
    first = lax.broadcasted_iota(jnp.int32, (24, 4 * 128), 0) == 0
    attn_out[:, width:] = jnp.where(first, jnp.broadcast_to(row, (24, 4 * 128)), 0.0).astype(bf16)


def stack_rows(ids, own, r1, r2, r3, out):
    for d, piece in enumerate((own, r1, r2, r3)):
        out[lax.rem(ids[11] + RING - d, RING)] = piece[...]


def split_rows(ids, p0, p1, p2, p3, out):
    total = p0[...].astype(f32) + p1[...].astype(f32) + p2[...].astype(f32) + p3[...].astype(f32)
    width = out.shape[2]
    for y in range(RING):
        row = jnp.concatenate([total[y : y + 1, width:], jnp.zeros((1, width - 128), f32)], axis=1)
        rows = total[6 * y : 6 * y + 6, :width]
        out[y] = jnp.concatenate([rows, row, jnp.zeros((1, width), f32)], axis=0).astype(bf16)


def whole(shape):
    return pl.BlockSpec(shape, lambda s, ids: (0,) * len(shape), pipeline_mode=pl.Buffered(1))


DEALT_SPEC = pl.BlockSpec((RING, CORES, 1, PIECE, WIDTH), lambda s, ids: (0, 0, s, 0, 0))


def by_rows(width):
    return pl.BlockSpec((SLOT, width), lambda s, ids: (s, 0))


def rows_of(width, kind):
    return jax.ShapeDtypeStruct((ROWS, width), kind)


EXP_SPEC = pl.BlockSpec((1, HEADS, SLOT, SLOT), lambda s, ids: (s, 0, 0, 0))
NORM_SPEC = pl.BlockSpec((1, 16, SLOT), lambda s, ids: (s, 0, 0))
RETURN_SPEC = pl.BlockSpec((RING, 1, PIECE, WIDTH), lambda s, ids: (0, s, 0, 0))
RETURN_SHAPE = jax.ShapeDtypeStruct((RING, SEQ_DEV, PIECE, WIDTH), bf16)


def by_columns(height):
    return pl.BlockSpec((height, SLOT), lambda s, ids: (0, s))


def columns_of(height):
    return jax.ShapeDtypeStruct((height, ROWS), bf16)


def run(kernel, grid, ins, outs, operands, name, flops, moved, scratch=()):
    return pl.pallas_call(
        kernel,
        grid_spec=pltpu.PrefetchScalarGridSpec(
            num_scalar_prefetch=1,
            grid=grid,
            in_specs=ins,
            out_specs=[spec for spec, _ in outs],
            scratch_shapes=list(scratch),
        ),
        out_shape=[shape for _, shape in outs],
        compiler_params=pltpu.CompilerParams(
            vmem_limit_bytes=VMEM_LIMIT, dimension_semantics=("arbitrary",) * len(grid)
        ),
        cost_estimate=pl.CostEstimate(flops=flops, bytes_accessed=moved, transcendentals=0),
        name=name,
    )(*operands)


def out_rows(width, kind):
    return (by_rows(width), rows_of(width, kind))


def out_columns(height):
    return (by_columns(height), columns_of(height))


def out_whole(shape):
    return (whole(shape), jax.ShapeDtypeStruct(shape, f32))


ANYWHERE = pl.BlockSpec(memory_space=pl.ANY)
ATTENTION_SCRATCH = [pltpu.VMEM((RING, CORES, 96, PACKED), bf16)]


def call_forward(ids, dealt, weights, perm):
    return run(
        attention_forward,
        (SEQ_DEV,),
        [DEALT_SPEC] + [ANYWHERE] * 8 + [whole((32, 16))],
        [
            out_columns(WIDTH),
            out_rows(3 * WIDTH, bf16),
            (EXP_SPEC, jax.ShapeDtypeStruct((SEQ_DEV, HEADS, SLOT, SLOT), bf16)),
            (NORM_SPEC, jax.ShapeDtypeStruct((SEQ_DEV, 16, SLOT), f32)),
            out_columns(WIDTH),
            out_rows(WIDTH, f32),
            out_whole((8, WIDTH)),
            out_whole((1, FF)),
            out_whole((8, 128)),
        ],
        (ids, dealt, *weights, perm),
        "attention_forward",
        22 * 10**9,
        22 * 10**6,
        ATTENTION_SCRATCH + [pltpu.VMEM((32, PACKED - 4 * WIDTH), f32), pltpu.SemaphoreType.DMA((8,))],
    )


def call_ffn(ids, sum1, dealt, dealt_c, inner, outer, vec, bias_in):
    return run(
        feed_forward,
        (SEQ_DEV,),
        [by_rows(WIDTH)] + [DEALT_SPEC] * 2 + [ANYWHERE] * 8 + [whole((8, WIDTH)), whole((1, FF))],
        [(RETURN_SPEC, RETURN_SHAPE)] * 2
        + [
            out_columns(WIDTH),
            out_columns(FF),
            out_rows(WIDTH, bf16),
            out_rows(FF, bf16),
            out_rows(WIDTH, f32),
            out_rows(WIDTH, bf16),
            (whole((WIDTH, 128)), jax.ShapeDtypeStruct((WIDTH, 128), bf16)),
        ],
        (ids, sum1, dealt, dealt_c, *inner, *outer, vec, bias_in),
        "feed_forward",
        36 * 10**9,
        40 * 10**6,
        [
            pltpu.VMEM((SLOT, FF), bf16),
            pltpu.VMEM((8, WIDTH), f32),
            pltpu.VMEM((1, FF), f32),
            pltpu.VMEM((RING, CORES, 2, 48, FF), bf16),
            pltpu.VMEM((RING, CORES, RING, 2, 48, WIDTH), bf16),
            pltpu.SemaphoreType.DMA((RING, RING)),
            pltpu.SemaphoreType.DMA((RING, RING, RING)),
        ],
    )


def call_backward(ids, dsum, dattn, qkv, expo, norm, ctx_t, dealt_c, weights):
    return run(
        attention_backward,
        (SEQ_DEV,),
        [by_rows(WIDTH), by_rows(WIDTH), by_rows(3 * WIDTH), EXP_SPEC, NORM_SPEC, by_columns(WIDTH)]
        + [DEALT_SPEC]
        + [ANYWHERE] * 8,
        [(RETURN_SPEC, RETURN_SHAPE)] * 2
        + [
            out_rows(3 * WIDTH, bf16),
            (whole((WIDTH, 128)), jax.ShapeDtypeStruct((WIDTH, 128), bf16)),
        ],
        (ids, dsum, dattn, qkv, expo, norm, ctx_t, dealt_c, *weights),
        "attention_backward",
        24 * 10**9,
        30 * 10**6,
        ATTENTION_SCRATCH + [pltpu.VMEM((8, WIDTH), f32), pltpu.SemaphoreType.DMA((8,))],
    )


def call_grad(ids, left, right, blocks, step, tail=None):
    rows = left.shape[0] // (RING * CORES)
    width = right.shape[1]
    ins = [
        pl.BlockSpec((2 * blocks * rows, ROWS), lambda i, n, ids: (i, 0)),
        pl.BlockSpec((ROWS, step), lambda i, n, ids: (0, n)),
    ]
    operands = (ids, left, right)
    more = 0
    if tail is not None:
        more = tail.shape[1]
        ins.append(pl.BlockSpec((WIDTH, more), lambda i, n, ids: (0, 0)))
        operands += (tail,)
    out = (
        pl.BlockSpec((blocks, rows, step + more), lambda i, n, ids: (i, 0, n)),
        jax.ShapeDtypeStruct((RING, rows, width + more), bf16),
    )
    return run(
        weight_grad,
        (RING // blocks, width // step),
        ins,
        [out, out],
        operands,
        "weight_grad",
        3 * RING * CORES * rows * ROWS * width,
        2 * (RING * rows * ROWS + ROWS * width + RING * rows * width),
    )


def call_small(kernel, name, ids, pieces, *out_shapes):
    def full(shape):
        return pl.BlockSpec(shape, lambda i, ids: (0,) * len(shape))

    return run(
        kernel,
        (1,),
        [full(pieces[0].shape)] * 4,
        [(full(shape), jax.ShapeDtypeStruct(shape, bf16)) for shape in out_shapes],
        (ids, *pieces),
        name,
        10**6,
        3 * 10**6,
    )


def shift(value, axis, step):
    size = CORES if axis == "core" else RING
    return lax.ppermute(value, axis, [(i, (i + step) % size) for i in range(size)])


def swap(value, axis):
    return lax.ppermute(value, axis, [(i, i ^ 1) for i in range(RING)])


def at(value, index):
    return lax.dynamic_index_in_dim(value, index, 0, keepdims=False)


def arrivals(value, axis):
    return [value] + [shift(value, axis, step) for step in (1, 2, 3)]


def both_cores(pieces):
    return [part for piece in pieces for part in (piece, shift(piece, "core", 1))]


def paired(value, axis):
    other = swap(value, axis)
    even = lax.rem(lax.axis_index(axis), 2) == 0
    return jnp.where(even, value, other), jnp.where(even, other, value)


def hold(value, *others):
    return lax.optimization_barrier((value, *others))[0]


def send_ring(value, axis):
    me = lax.axis_index(axis)
    return [at(value, me)] + [
        shift(at(value, lax.rem(me + step, RING)), axis, step) for step in (1, 3, 2)
    ]


def total(parts):
    first, *rest = (part.astype(f32) for part in parts)
    return sum(rest, first)


def add_core(mine, away):
    return (mine.astype(f32) + away.astype(f32)).astype(bf16)


def over_x(value):
    return lax.all_to_all(value, "x", split_axis=0, concat_axis=0, tiled=True)


def pair_cores(pieces):
    me_c = lax.axis_index("core")
    grid = pieces.reshape(RING, CORES, SEQ_DEV, PIECE, WIDTH)
    mine = lax.dynamic_index_in_dim(grid, me_c, 1, keepdims=False)
    away = lax.dynamic_index_in_dim(grid, 1 - me_c, 1, keepdims=False)
    return jnp.stack([mine, shift(away, "core", 1)], axis=1)


def placed(value):
    first = lax.axis_index("core") == 0
    value = jnp.where(first, value, value[:, ::-1])
    return value.reshape(RING * CORES * SEQ_DEV, PIECE, WIDTH)


def body(
    tokens,
    cotangent,
    perm,
    lengths,
    drop,
    w_query,
    b_query,
    w_key,
    w_value,
    b_value,
    w_out,
    b_out,
    norm1_gain,
    norm1_bias,
    w_inner,
    b_inner,
    w_outer,
    b_outer,
    norm2_gain,
    norm2_bias,
):
    me_x = lax.axis_index("x")
    me_c = lax.axis_index("core")
    me_z = lax.axis_index("z")
    me_y = lax.axis_index("y")
    first = ((me_z * RING + me_y) * 8 + me_x * CORES + me_c) * SEQ_DEV
    places = jnp.stack([me_x, me_c, first, me_z, me_y]).astype(jnp.int32)
    places = jnp.pad(places, (8, 3))

    vectors = [b_query, b_value, b_out, norm1_gain, norm1_bias, b_outer, norm2_gain, norm2_bias, b_inner]
    vectors += [lengths.astype(bf16), drop.astype(bf16)]
    row = jnp.zeros((4 * WIDTH,), bf16)
    start = 0
    for vector in vectors:
        end = start + vector.shape[0]
        row += jnp.pad(vector, (start, 4 * WIDTH - end))
        start = end
    piece = jnp.concatenate([w_query, w_key, w_value, w_out, w_inner], axis=1)
    row = jnp.pad(row, (0, FF))
    piece = jnp.concatenate([piece, row[None], jnp.zeros((1, 4 * WIDTH + FF), bf16)])
    pieces_y = arrivals(piece, "y")
    cores_x = pair_cores(tokens)
    dealt_x = over_x(cores_x)
    attn_y, inner_y = call_small(merge_rows, "merge_rows", places, pieces_y, (24, PACKED), (24, FF))
    (attn_zy,) = call_small(
        stack_rows, "stack_rows", places, arrivals(hold(attn_y, cores_x), "z"), (RING, 24, PACKED)
    )
    attn_x = arrivals(attn_zy.reshape(96, PACKED), "x")
    attn_pieces = both_cores(attn_x)

    ffn_x = arrivals(jnp.concatenate([hold(inner_y, cores_x), w_outer], axis=1), "x")
    inner_x = jnp.stack([v[:, :FF] for v in ffn_x])
    outer_x = jnp.stack([v[:, FF:] for v in ffn_x])
    inner_z = jnp.concatenate(paired(hold(inner_x, attn_zy), "z"), axis=1)
    inner_pieces = both_cores([inner_z, shift(inner_z, "z", 2)])
    outer_y = jnp.concatenate(paired(hold(outer_x, attn_zy), "y"), axis=1)
    outer_z = jnp.stack(paired(outer_y, "z"))
    outer_z = jnp.concatenate([outer_z, shift(outer_z, "z", 2)])
    outer_pieces = both_cores([outer_z, shift(outer_z, "y", 2)])
    dealt_c = over_x(pair_cores(hold(cotangent, attn_x[1], dealt_x)))

    x_t, qkv, expo, norm, ctx_t, sum1, vec, inner_bias, info = call_forward(
        places, dealt_x, attn_pieces, perm.reshape(32, 16)
    )
    ids = jnp.concatenate([info[:, 0].astype(jnp.int32), places[8:]])

    inner_pieces = [hold(p, sum1) for p in inner_pieces]
    outer_pieces = [hold(p, sum1) for p in outer_pieces]
    same, other, hid_t, act_t, d_branch, d_inner, d_sum1, d_attn, vec_block = call_ffn(
        ids, sum1, dealt_x, dealt_c, inner_pieces, outer_pieces, vec, inner_bias
    )

    outer_away, outer_mine = call_grad(ids, act_t, d_branch, 1, WIDTH)
    outer_core = shift(outer_away, "core", 1)
    layer_cores = jnp.stack([same, shift(other, "core", 1)], axis=1)
    inner_away, inner_mine = call_grad(
        hold(ids, outer_away, layer_cores), hid_t, d_inner, RING, WIDTH
    )
    inner_core = shift(inner_away, "core", 1)
    layer_back = over_x(layer_cores)
    out_away, out_mine = call_grad(
        hold(ids, inner_away), ctx_t, d_attn, RING, WIDTH, vec_block
    )
    out_core = shift(out_away, "core", 1)
    outer_sum = add_core(outer_mine, outer_core).reshape(RING, RING, RING, 24, WIDTH)
    outer_sum = outer_sum.transpose(2, 0, 1, 3, 4)
    inner_sum = jnp.concatenate(
        [add_core(inner_mine, inner_core), add_core(out_mine, out_core)], axis=2
    )
    inner_width = inner_sum.shape[2]
    inner_sum = inner_sum.reshape(RING, RING, 24, inner_width).transpose(1, 0, 2, 3)
    inner_parts = send_ring(inner_sum, "z")
    outer_sum = hold(outer_sum, layer_back)
    outer_y = lax.all_to_all(outer_sum, "y", split_axis=0, concat_axis=0, tiled=True)

    d_sum1, d_attn = lax.optimization_barrier((d_sum1, d_attn, inner_parts[0], outer_sum))[:2]
    grad_same, grad_other, d_qkv, qkv_block = call_backward(
        ids, d_sum1, d_attn, qkv, expo, norm, ctx_t, dealt_c, attn_pieces
    )

    inner_z = total([inner_parts[0]] + [hold(p, d_qkv) for p in inner_parts[1:]]).astype(bf16)
    outer_y = jnp.sum(hold(outer_y, d_qkv).astype(f32), axis=0).astype(bf16)
    outer_y = outer_y.transpose(0, 2, 1, 3).reshape(RING, 24, RING * WIDTH)
    mid_parts = send_ring(jnp.concatenate([inner_z, outer_y], axis=2), "x")

    attn_away, attn_mine = call_grad(hold(ids, mid_parts[0]), x_t, d_qkv, RING, 3 * WIDTH, qkv_block)
    attn_core = shift(attn_away, "core", 1)
    attn_sum = add_core(attn_mine, attn_core)
    attn_sum = attn_sum.reshape(RING, RING, 24, attn_sum.shape[2]).transpose(1, 0, 2, 3)
    attn_parts = send_ring(attn_sum, "z")

    grad_same = hold(grad_same, attn_away)
    grad_cores = jnp.stack([grad_same, shift(hold(grad_other, attn_away), "core", 1)], axis=1)
    grad_back = over_x(hold(grad_cores, attn_parts[0]))
    mid_parts = [mid_parts[0]] + [hold(p, attn_parts[0]) for p in mid_parts[1:]]
    outer_x = total([p[:, inner_width:] for p in mid_parts]).astype(bf16)
    outer_x = jnp.stack([outer_x[:, z * WIDTH : (z + 1) * WIDTH] for z in range(RING)])
    outer_grad = total(send_ring(outer_x, "z"))
    (inner_y,) = call_small(
        split_rows, "split_rows", places, [p[:, :inner_width] for p in mid_parts], (RING, 8, inner_width - 128)
    )
    inner_grad = total(send_ring(inner_y, "y"))
    attn_x = send_ring(total(attn_parts).astype(bf16), "x")
    (attn_y,) = call_small(split_rows, "split_rows", places, attn_x, (RING, 8, 3 * WIDTH))
    attn_grad = total(send_ring(attn_y, "y"))
    layer_final = placed(layer_back)
    grad_final = placed(grad_back)
    inner_vecs = inner_grad[6, :36].reshape(6, 6)
    return (
        layer_final,
        grad_final,
        attn_grad[:6, :WIDTH],
        attn_grad[6, :6],
        attn_grad[:6, WIDTH : 2 * WIDTH],
        attn_grad[:6, 2 * WIDTH :],
        attn_grad[6, 6:12],
        inner_grad[:6, FF:],
        inner_vecs[5],
        inner_vecs[3],
        inner_vecs[4],
        inner_grad[:6, :FF],
        inner_grad[6, 36:60],
        outer_grad,
        inner_vecs[0],
        inner_vecs[1],
        inner_vecs[2],
    )


def solution(mesh):
    chips = Mesh(mesh.devices.reshape(RING, CORES, RING, RING), ("x", "core", "z", "y"))
    dp = ("x", "core")
    fsdp = ("z", "y")
    every = P(dp + fsdp)
    rows = P(dp + fsdp, None)
    whole_rows = P(fsdp, dp, None)
    return jax.shard_map(
        body,
        mesh=chips,
        in_specs=(
            whole_rows, whole_rows, P(), every, every,
            rows, every, rows, rows, every, rows, every, every, every,
            rows, every, rows, every, every, every,
        ),
        out_specs=(
            whole_rows, whole_rows,
            rows, every, rows, rows, every, rows, every, every, every,
            rows, every, rows, every, every, every,
        ),
        check_vma=False,
    )
```

```python
import functools
import jax
import jax.numpy as jnp
from jax import lax
from jax.experimental import pallas as pl
from jax.experimental.pallas import tpu as pltpu
from jax.sharding import Mesh
from jax.sharding import PartitionSpec as P

HEADS = 12
HEAD = 64
WIDTH = 768
FF = 3072
SLOT = 256
SEQ_DEV = 4
RING = 4
CORES = 2
PIECE = 32
ROWS = SEQ_DEV * SLOT
PAIR = 2 * HEAD
PACKED = 4 * WIDTH + 512

epsilon = 1e-05
bf16 = jnp.bfloat16
f32 = jnp.float32
VMEM_LIMIT = 58 * 1024 * 1024

TN = (((0,), (0,)), ((), ()))
NT = (((1,), (1,)), ((), ()))


def mm(a, b):
    return jnp.dot(a, b, preferred_element_type=f32)


def mm_nt(a, b):
    return lax.dot_general(a, b, NT, preferred_element_type=f32)


def mm_tn(a, b):
    return lax.dot_general(a, b, TN, preferred_element_type=f32)


def slot_positions(ids, shape, axis):
    row = lax.broadcasted_iota(jnp.int32, shape, axis)
    from_x = row // (CORES * PIECE)
    away = lax.rem(row // PIECE, CORES)
    from_c = jnp.where(away == 1, 1 - ids[9], ids[9])
    return (from_x * CORES + from_c) * PIECE + lax.rem(row, PIECE)


def joined(ref):
    return ref[...].reshape(SLOT, WIDTH)


def split_into(same, other, rows):
    for d in range(RING):
        start = d * CORES * PIECE
        same[d, 0] = rows[start : start + PIECE]
        other[d, 0] = rows[start + PIECE : start + 2 * PIECE]


def spread(extras, start, width):
    total = 128 * width
    group = lax.broadcasted_iota(jnp.int32, (32, total), 0)
    owner = lax.broadcasted_iota(jnp.int32, (32, total), 1) // width
    pick = lax.broadcasted_iota(jnp.int32, (width, total), 0)
    within = lax.rem(lax.broadcasted_iota(jnp.int32, (width, total), 1), width)
    chosen = (pick == within).astype(bf16)
    out = jnp.zeros((32, total), f32)
    for y in range(RING):
        values = extras[:, 128 * y + start : 128 * y + start + width].astype(bf16)
        out += jnp.where(owner == group * RING + y, mm(values, chosen), 0.0)
    return jnp.sum(out, axis=0, keepdims=True)


def gather_back(vectors):
    values = jnp.zeros((128, 128), f32)
    start = 0
    for vector in vectors:
        total = vector.shape[1]
        width = total // 128
        owner = lax.broadcasted_iota(jnp.int32, (128, total), 1) // width
        mine = owner == lax.broadcasted_iota(jnp.int32, (128, total), 0)
        within = lax.rem(lax.broadcasted_iota(jnp.int32, (total, 128), 0), width)
        column = lax.broadcasted_iota(jnp.int32, (total, 128), 1)
        spots = (column == within + start).astype(bf16)
        values += mm(jnp.where(mine, vector, 0.0).astype(bf16), spots)
        start += width
    row = lax.broadcasted_iota(jnp.int32, (WIDTH, 128), 0)
    device = lax.broadcasted_iota(jnp.int32, (WIDTH, 128), 1)
    within = lax.rem(row, 24)
    picks = (within < RING) & (row // 24 * RING + within == device)
    return mm(picks.astype(bf16), values.astype(bf16)).astype(bf16)


def attention_copies(ids, pieces, w, sems):
    copies = []
    for i, piece in enumerate(pieces):
        x = lax.rem(ids[8] + RING - i // 2, RING)
        c = ids[9] if i % 2 == 0 else 1 - ids[9]
        copies.append(pltpu.make_async_copy(piece, w.at[x, c], sems.at[i]))
    return copies


def columns(w, start, end):
    return w[:, :, :, start:end].reshape(WIDTH, end - start)


def attention_forward(
    ids, x_in, p0, p1, p2, p3, p4, p5, p6, p7, perm,
    xt_out, qkv_out, exp_out, norm_out, ctxt_out, sum_out, vec, bias_out, info,
    w, extras, sems,
):
    s = pl.program_id(0)

    @pl.when(s == 0)
    def _():
        copies = attention_copies(ids, (p0, p1, p2, p3, p4, p5, p6, p7), w, sems)
        for copy in copies:
            copy.start()
        for copy in copies:
            copy.wait()
        rows = columns(w, 4 * WIDTH, PACKED).astype(f32).reshape(32, 24, PACKED - 4 * WIDTH)
        extras[...] = jnp.sum(rows, axis=1)
        for i in range(8):
            vec[i : i + 1] = spread(extras, 6 * i, 6)
        bias_out[...] = spread(extras, 48, 24)

    length = jnp.zeros((1, 1), f32)
    dropped = jnp.zeros((1, 1), f32)
    for y in range(RING):
        hit = perm[:, RING * y : RING * y + 4] == ids[10] + s
        length += jnp.sum(jnp.where(hit, extras[:, 128 * y + 72 : 128 * y + 76], 0.0), keepdims=True)
        dropped += jnp.sum(jnp.where(hit, extras[:, 128 * y + 76 : 128 * y + 80], 0.0), keepdims=True)
    line = lax.broadcasted_iota(jnp.int32, (8, 128), 0)
    info[...] = jnp.where(line == s, length, jnp.where(line == s + 4, dropped, info[...]))

    x = joined(x_in)
    xt_out[...] = x.T
    q = ((mm(x, columns(w, 0, WIDTH)) + vec[0:1]).astype(bf16).astype(f32) * HEAD**-0.5).astype(bf16)
    k = mm(x, columns(w, WIDTH, 2 * WIDTH)).astype(bf16)
    v = (mm(x, columns(w, 2 * WIDTH, 3 * WIDTH)) + vec[1:2]).astype(bf16)
    qkv_out[:, :WIDTH] = q
    qkv_out[:, WIDTH : 2 * WIDTH] = k
    qkv_out[:, 2 * WIDTH :] = v
    q_t = q.T
    v_t = v.T
    keys = slot_positions(ids, (SLOT, 1), 0).astype(f32)
    bias = jnp.where(keys < length, 0.0, -1e30)
    low = lax.broadcasted_iota(jnp.int32, (SLOT, PAIR), 1) < HEAD
    ctx_t = []
    for h in range(HEADS):
        p = h // 2 * PAIR
        k_pair = k[:, p : p + PAIR]
        k_one = jnp.where(low if h % 2 == 0 else ~low, k_pair, jnp.zeros_like(k_pair))
        scores = mm(k_one, q_t[p : p + PAIR]) + bias
        top = jnp.max(scores, axis=0, keepdims=True)
        expo = jnp.exp(scores - top)
        inverse = 1.0 / jnp.sum(expo, axis=0, keepdims=True)
        norm_out[0, h : h + 1, :] = inverse
        expo = expo.astype(bf16)
        exp_out[0, h] = expo
        ctx_t.append(mm(v_t[h * HEAD : (h + 1) * HEAD], expo) * inverse)
    ctx_t = jnp.concatenate(ctx_t, axis=0).astype(bf16)
    ctxt_out[...] = ctx_t
    sum_out[...] = x.astype(f32) + (mm(ctx_t.T, columns(w, 3 * WIDTH, 4 * WIDTH)) + vec[2:3])


def row_mean(v):
    return jnp.mean(v, axis=-1, keepdims=True)


def normalised(z):
    center = z - row_mean(z)
    r = lax.rsqrt(row_mean(center * center) + epsilon)
    return center * r, r


def norm_back(dy, zhat, r, gain):
    e = dy * gain
    return r * (e - row_mean(e) - zhat * row_mean(e * zhat))


def col_sum(v):
    return jnp.sum(v, axis=0, keepdims=True)


FF_STEP = 768


def feed_forward(
    ids, sum1, x_in, c_in, i0, i1, i2, i3, j0, j1, j2, j3, vec, bias_in,
    same, other, hidt_out, actt_out, dbranch_out, dinner_out, dsum_out, dattn_out, vec_block,
    slope, vec_grad, bias_grad, w_in, w_out, in_sems, out_sems,
):
    s = pl.program_id(0)

    def copies():
        ins = []
        outs = []
        for i, (piece, late) in enumerate(zip((i0, i1, i2, i3), (j0, j1, j2, j3))):
            c = ids[9] if i % 2 == 0 else 1 - ids[9]
            z_half = ids[11] // 2 if i // 2 == 0 else 1 - ids[11] // 2
            y_half = ids[12] // 2 if i // 2 == 0 else 1 - ids[12] // 2
            for d in range(RING):
                x = lax.rem(ids[8] + RING - d, RING)
                ins.append(pltpu.make_async_copy(piece.at[d], w_in.at[x, c, z_half], in_sems.at[i, d]))
                for n in range(RING):
                    half = ids[11] // 2 if n // 2 == 0 else 1 - ids[11] // 2
                    target = w_out.at[x, c, 2 * half + n % 2, y_half]
                    outs.append(pltpu.make_async_copy(late.at[n, d], target, out_sems.at[i, d, n]))
        return ins, outs

    @pl.when(s == 0)
    def _():
        vec_grad[...] = jnp.zeros_like(vec_grad)
        bias_grad[...] = jnp.zeros_like(bias_grad)
        ins, outs = copies()
        for copy in ins + outs:
            copy.start()
        for copy in ins + outs:
            copy.wait()

    def inner_columns(start):
        return w_in[:, :, :, :, start : start + FF_STEP].reshape(WIDTH, FF_STEP)

    def outer_rows(start):
        x = start // (FF // RING)
        return w_out[x].reshape(FF // RING, WIDTH)

    zhat1, r1 = normalised(sum1[...])
    hidden = zhat1 * vec[3:4] + vec[4:5]
    hid_low = hidden.astype(bf16)
    hidt_out[...] = hid_low.T
    branch = jnp.broadcast_to(vec[5:6], (SLOT, WIDTH))
    for n in range(0, FF, FF_STEP):
        cols = slice(n, n + FF_STEP)
        inner = mm(hid_low, inner_columns(n)) + bias_in[0:1, cols]
        half = 0.5 * lax.erf(inner * 0.7071067811865476) + 0.5
        bell = 0.3989422804014327 * jnp.exp(-0.5 * (inner * inner))
        act = (inner * half).astype(bf16)
        actt_out[cols, :] = act.T
        slope[:, cols] = (half + inner * bell).astype(bf16)
        branch += mm(act, outer_rows(n))
    zhat2, r2 = normalised(hidden + branch)
    gain2 = vec[6:7]
    normed = zhat2 * gain2 + vec[7:8]
    valid = (slot_positions(ids, (SLOT, 1), 0) < ids[s]).astype(f32)
    keep = ids[4 + s] == 0
    x = joined(x_in).astype(f32)
    split_into(same, other, (jnp.where(keep, normed, x) * valid).astype(bf16))
    upstream = joined(c_in).astype(f32)
    dy = upstream * jnp.where(keep, valid, 0.0)
    vec_grad[1:2] += col_sum(dy * zhat2)
    vec_grad[2:3] += col_sum(dy)
    d_sum2 = norm_back(dy, zhat2, r2, gain2)
    d_branch = d_sum2.astype(bf16)
    dbranch_out[...] = d_branch
    vec_grad[0:1] += col_sum(d_branch.astype(f32))
    d_hidden = d_sum2
    for n in range(0, FF, FF_STEP):
        cols = slice(n, n + FF_STEP)
        d_act = mm_nt(d_branch, outer_rows(n))
        d_inner = (d_act * slope[:, cols].astype(f32)).astype(bf16)
        dinner_out[:, cols] = d_inner
        bias_grad[0:1, cols] += col_sum(d_inner.astype(f32))
        d_hidden += mm_nt(d_inner, inner_columns(n))
    vec_grad[3:4] += col_sum(d_hidden * zhat1)
    vec_grad[4:5] += col_sum(d_hidden)
    d_sum1 = norm_back(d_hidden, zhat1, r1, vec[3:4])
    dsum_out[...] = d_sum1
    d_attn = d_sum1.astype(bf16)
    dattn_out[...] = d_attn
    vec_grad[5:6] += col_sum(d_attn.astype(f32))

    @pl.when(s == SEQ_DEV - 1)
    def _():
        vec_block[...] = gather_back([vec_grad[i : i + 1] for i in range(6)] + [bias_grad[...]])


def attention_backward(
    ids, dsum, dattn, qkv, exp_in, norm_in, ctxt_in, c_in, p0, p1, p2, p3, p4, p5, p6, p7,
    same, other, dqkv_out, vec_block,
    w, vec_grad, sems,
):
    s = pl.program_id(0)

    @pl.when(s == 0)
    def _():
        vec_grad[...] = jnp.zeros_like(vec_grad)
        copies = attention_copies(ids, (p0, p1, p2, p3, p4, p5, p6, p7), w, sems)
        for copy in copies:
            copy.start()
        for copy in copies:
            copy.wait()

    d_sum1 = dsum[...]
    dctx_t = mm_nt(dattn[...], columns(w, 3 * WIDTH, 4 * WIDTH)).T
    ctx_t = ctxt_in[...].astype(f32)
    k_t = qkv[:, WIDTH : 2 * WIDTH].T
    scaled = []
    deltas = []
    for h in range(HEADS):
        rows = slice(h * HEAD, (h + 1) * HEAD)
        one = (dctx_t[rows] * norm_in[0, h : h + 1, :]).astype(bf16)
        scaled.append(one)
        deltas.append(col_sum(one.astype(f32) * ctx_t[rows]))
    dctx_t = jnp.concatenate(scaled, axis=0)
    dctx = dctx_t.T
    low = lax.broadcasted_iota(jnp.int32, (SLOT, PAIR), 1) < HEAD
    dq_t = []
    for p in range(0, WIDTH, PAIR):
        cols = slice(p, p + PAIR)
        q_pair = qkv[:, cols]
        v_pair = qkv[:, 2 * WIDTH + p : 2 * WIDTH + p + PAIR]
        dks = []
        dvs = []
        for half in range(2):
            h = p // HEAD + half
            v_one = jnp.where(low if half == 0 else ~low, v_pair, jnp.zeros_like(v_pair))
            d_probs = mm(v_one, dctx_t[cols]) - deltas[h]
            expo = exp_in[0, h]
            d_scores = (expo.astype(f32) * d_probs).astype(bf16)
            dvs.append(mm(expo, dctx[:, cols]))
            dks.append(mm(d_scores, q_pair))
            dq_t.append(mm(k_t[h * HEAD : (h + 1) * HEAD], d_scores))
        dqkv_out[:, WIDTH + p : WIDTH + p + PAIR] = jnp.where(low, dks[0], dks[1]).astype(bf16)
        dqkv_out[:, 2 * WIDTH + p : 2 * WIDTH + p + PAIR] = jnp.where(low, dvs[0], dvs[1]).astype(bf16)
    dq = (jnp.concatenate(dq_t, axis=0).T * HEAD**-0.5).astype(bf16)
    dqkv_out[:, :WIDTH] = dq
    vec_grad[0:1] += col_sum(dq.astype(f32))
    vec_grad[1:2] += col_sum(dqkv_out[:, 2 * WIDTH :].astype(f32))
    d_in = d_sum1 + mm_nt(dqkv_out[...], columns(w, 0, 3 * WIDTH))
    valid = (slot_positions(ids, (SLOT, 1), 0) < ids[s]).astype(f32)
    upstream = joined(c_in).astype(f32) * valid
    keep = ids[4 + s] == 0
    split_into(same, other, jnp.where(keep, d_in, upstream).astype(bf16))

    @pl.when(s == SEQ_DEV - 1)
    def _():
        vec_block[...] = gather_back([vec_grad[0:1], vec_grad[1:2]])


def weight_grad(ids, left, right, *refs):
    *tail, away, mine = refs
    value = mm(left[...], right[...]).astype(bf16)
    if tail:
        value = jnp.concatenate([value, tail[0][...]], axis=1)
    blocks, rows, _ = away.shape
    first = ids[9] == 0
    for x in range(blocks):
        even = value[2 * x * rows : (2 * x + 1) * rows]
        odd = value[(2 * x + 1) * rows : (2 * x + 2) * rows]
        away[x] = jnp.where(first, odd, even)
        mine[x] = jnp.where(first, even, odd)


def in_order(values, me):
    ordered = []
    for j in range(RING):
        step = lax.rem(me + RING - j, RING)
        value = values[0]
        for d in (1, 2, 3):
            value = jnp.where(step == d, values[d], value)
        ordered.append(value)
    return ordered


def merge_rows(ids, own, r1, r2, r3, attn_out, inner_out):
    ordered = in_order([v[...].astype(f32) for v in (own, r1, r2, r3)], ids[12])
    width = 4 * WIDTH
    rows = jnp.concatenate([v[:6] for v in ordered], axis=0).astype(bf16)
    attn_out[:, :width] = rows[:, :width]
    inner_out[...] = rows[:, width:]
    row = jnp.concatenate([v[6:7, :128] for v in ordered], axis=1)
    first = lax.broadcasted_iota(jnp.int32, (24, 4 * 128), 0) == 0
    attn_out[:, width:] = jnp.where(first, jnp.broadcast_to(row, (24, 4 * 128)), 0.0).astype(bf16)


def stack_rows(ids, own, r1, r2, r3, out):
    for d, piece in enumerate((own, r1, r2, r3)):
        out[lax.rem(ids[11] + RING - d, RING)] = piece[...]


def ahead(ids, axis, step):
    return lax.rem(ids[axis] + step, RING)


def sum_of(refs):
    total = refs[0][...].astype(f32)
    for ref in refs[1:]:
        total += ref[...].astype(f32)
    return total


def sum_blocks(ids, *refs):
    *parts, o0, o1, o2, o3, scratch = refs
    start = 0
    for mine, core in zip(parts[::2], parts[1::2]):
        end = start + mine.shape[2]
        scratch[:, :, start:end] = mine[...].astype(f32) + core[...].astype(f32)
        start = end
    for d, out in enumerate((o0, o1, o2, o3)):
        first = pl.multiple_of(ahead(ids, 11, d) * 24, 8)
        out[...] = scratch[:, pl.ds(first, 24), :].astype(bf16)


def sum_outer(ids, mine, core, out):
    for x in range(RING):
        total = (mine[x].astype(f32) + core[x].astype(f32))
        for z in range(RING):
            for y in range(RING):
                first = 96 * z + 24 * y
                out[y, x, z] = total[first : first + 24].astype(bf16)


def sum_first(ids, value, out):
    for x in range(RING):
        for z in range(RING):
            out[z, x] = sum_of([value.at[y, x, z] for y in range(RING)]).astype(bf16)


def split_rows(ids, p0, p1, p2, p3, o0, o1, o2, o3, scratch):
    width = o0.shape[2]
    for x in range(RING):
        total = p0[x].astype(f32) + p1[x].astype(f32) + p2[x].astype(f32) + p3[x].astype(f32)
        for y in range(RING):
            row = jnp.concatenate([total[y : y + 1, width:], jnp.zeros((1, width - 128), f32)], axis=1)
            rows = total[6 * y : 6 * y + 6, :width]
            scratch[y, x] = jnp.concatenate([rows, row, jnp.zeros((1, width), f32)], axis=0)
    for d, out in enumerate((o0, o1, o2, o3)):
        out[...] = scratch[ahead(ids, 12, d)].astype(bf16)


LAST = FF + WIDTH + 3 * WIDTH + 3 * WIDTH


def join_flows(ids, i0, i1, i2, i3, a0, a1, a2, a3, outer, o0, o1, o2, o3, scratch):
    scratch[:, :, : FF + WIDTH] = sum_of((i0, i1, i2, i3))
    scratch[:, :, FF + WIDTH : FF + 4 * WIDTH] = sum_of((a0, a1, a2, a3))
    for x in range(RING):
        total = sum_of([outer.at[z, x] for z in range(RING)])
        for k in range(3):
            start = FF + (4 + k) * WIDTH
            scratch[x, :, start : start + WIDTH] = total[8 * k : 8 * k + 8]
    for d, out in enumerate((o0, o1, o2, o3)):
        out[...] = scratch[ahead(ids, 8, d)].astype(bf16)


def stack_cores(ids, same, other, out):
    out[:, 0] = same[...]
    out[:, 1] = other[...]


def split_ffn(ids, p0, p1, p2, p3, inner, outer):
    for d, piece in enumerate((p0, p1, p2, p3)):
        inner[d] = piece[:, :FF]
        outer[d] = piece[:, FF:]


def write_grads(ids, p0, p1, p2, p3, query, key, value, out, inner, outer, vectors):
    total = sum_of((p0, p1, p2, p3))
    inner[...] = total[:6, :FF]
    out[...] = total[:6, FF : FF + WIDTH]
    start = FF + WIDTH
    query[...] = total[:6, start : start + WIDTH]
    key[...] = total[:6, start + WIDTH : start + 2 * WIDTH]
    value[...] = total[:6, start + 2 * WIDTH : start + 3 * WIDTH]
    vectors[...] = jnp.concatenate([total[6:7, :128], total[6:7, start : start + 128]], axis=0)
    start += 3 * WIDTH
    for k in range(3):
        outer[8 * k : 8 * k + 8] = total[:, start + k * WIDTH : start + (k + 1) * WIDTH]


def whole(shape):
    return pl.BlockSpec(shape, lambda s, ids: (0,) * len(shape), pipeline_mode=pl.Buffered(1))


DEALT_SPEC = pl.BlockSpec((RING, CORES, 1, PIECE, WIDTH), lambda s, ids: (0, 0, s, 0, 0))


def by_rows(width):
    return pl.BlockSpec((SLOT, width), lambda s, ids: (s, 0))


def rows_of(width, kind):
    return jax.ShapeDtypeStruct((ROWS, width), kind)


EXP_SPEC = pl.BlockSpec((1, HEADS, SLOT, SLOT), lambda s, ids: (s, 0, 0, 0))
NORM_SPEC = pl.BlockSpec((1, 16, SLOT), lambda s, ids: (s, 0, 0))
RETURN_SPEC = pl.BlockSpec((RING, 1, PIECE, WIDTH), lambda s, ids: (0, s, 0, 0))
RETURN_SHAPE = jax.ShapeDtypeStruct((RING, SEQ_DEV, PIECE, WIDTH), bf16)


def by_columns(height):
    return pl.BlockSpec((height, SLOT), lambda s, ids: (0, s))


def columns_of(height):
    return jax.ShapeDtypeStruct((height, ROWS), bf16)


def run(kernel, grid, ins, outs, operands, name, flops, moved, scratch=()):
    return pl.pallas_call(
        kernel,
        grid_spec=pltpu.PrefetchScalarGridSpec(
            num_scalar_prefetch=1,
            grid=grid,
            in_specs=ins,
            out_specs=[spec for spec, _ in outs],
            scratch_shapes=list(scratch),
        ),
        out_shape=[shape for _, shape in outs],
        compiler_params=pltpu.CompilerParams(
            vmem_limit_bytes=VMEM_LIMIT, dimension_semantics=("arbitrary",) * len(grid)
        ),
        cost_estimate=pl.CostEstimate(flops=flops, bytes_accessed=moved, transcendentals=0),
        name=name,
    )(*operands)


def out_rows(width, kind):
    return (by_rows(width), rows_of(width, kind))


def out_columns(height):
    return (by_columns(height), columns_of(height))


def out_whole(shape):
    return (whole(shape), jax.ShapeDtypeStruct(shape, f32))


ANYWHERE = pl.BlockSpec(memory_space=pl.ANY)
ATTENTION_SCRATCH = [pltpu.VMEM((RING, CORES, 96, PACKED), bf16)]


def call_forward(ids, dealt, weights, perm):
    return run(
        attention_forward,
        (SEQ_DEV,),
        [DEALT_SPEC] + [ANYWHERE] * 8 + [whole((32, 16))],
        [
            out_columns(WIDTH),
            out_rows(3 * WIDTH, bf16),
            (EXP_SPEC, jax.ShapeDtypeStruct((SEQ_DEV, HEADS, SLOT, SLOT), bf16)),
            (NORM_SPEC, jax.ShapeDtypeStruct((SEQ_DEV, 16, SLOT), f32)),
            out_columns(WIDTH),
            out_rows(WIDTH, f32),
            out_whole((8, WIDTH)),
            out_whole((1, FF)),
            out_whole((8, 128)),
        ],
        (ids, dealt, *weights, perm),
        "attention_forward",
        22 * 10**9,
        22 * 10**6,
        ATTENTION_SCRATCH + [pltpu.VMEM((32, PACKED - 4 * WIDTH), f32), pltpu.SemaphoreType.DMA((8,))],
    )


def call_ffn(ids, sum1, dealt, dealt_c, inner, outer, vec, bias_in):
    return run(
        feed_forward,
        (SEQ_DEV,),
        [by_rows(WIDTH)] + [DEALT_SPEC] * 2 + [ANYWHERE] * 8 + [whole((8, WIDTH)), whole((1, FF))],
        [(RETURN_SPEC, RETURN_SHAPE)] * 2
        + [
            out_columns(WIDTH),
            out_columns(FF),
            out_rows(WIDTH, bf16),
            out_rows(FF, bf16),
            out_rows(WIDTH, f32),
            out_rows(WIDTH, bf16),
            (whole((WIDTH, 128)), jax.ShapeDtypeStruct((WIDTH, 128), bf16)),
        ],
        (ids, sum1, dealt, dealt_c, *inner, *outer, vec, bias_in),
        "feed_forward",
        36 * 10**9,
        40 * 10**6,
        [
            pltpu.VMEM((SLOT, FF), bf16),
            pltpu.VMEM((8, WIDTH), f32),
            pltpu.VMEM((1, FF), f32),
            pltpu.VMEM((RING, CORES, 2, 48, FF), bf16),
            pltpu.VMEM((RING, CORES, RING, 2, 48, WIDTH), bf16),
            pltpu.SemaphoreType.DMA((RING, RING)),
            pltpu.SemaphoreType.DMA((RING, RING, RING)),
        ],
    )


def call_backward(ids, dsum, dattn, qkv, expo, norm, ctx_t, dealt_c, weights):
    return run(
        attention_backward,
        (SEQ_DEV,),
        [by_rows(WIDTH), by_rows(WIDTH), by_rows(3 * WIDTH), EXP_SPEC, NORM_SPEC, by_columns(WIDTH)]
        + [DEALT_SPEC]
        + [ANYWHERE] * 8,
        [(RETURN_SPEC, RETURN_SHAPE)] * 2
        + [
            out_rows(3 * WIDTH, bf16),
            (whole((WIDTH, 128)), jax.ShapeDtypeStruct((WIDTH, 128), bf16)),
        ],
        (ids, dsum, dattn, qkv, expo, norm, ctx_t, dealt_c, *weights),
        "attention_backward",
        24 * 10**9,
        30 * 10**6,
        ATTENTION_SCRATCH + [pltpu.VMEM((8, WIDTH), f32), pltpu.SemaphoreType.DMA((8,))],
    )


def call_grad(ids, left, right, blocks, step, tail=None):
    rows = left.shape[0] // (RING * CORES)
    width = right.shape[1]
    ins = [
        pl.BlockSpec((2 * blocks * rows, ROWS), lambda i, n, ids: (i, 0)),
        pl.BlockSpec((ROWS, step), lambda i, n, ids: (0, n)),
    ]
    operands = (ids, left, right)
    more = 0
    if tail is not None:
        more = tail.shape[1]
        ins.append(pl.BlockSpec((WIDTH, more), lambda i, n, ids: (0, 0)))
        operands += (tail,)
    out = (
        pl.BlockSpec((blocks, rows, step + more), lambda i, n, ids: (i, 0, n)),
        jax.ShapeDtypeStruct((RING, rows, width + more), bf16),
    )
    return run(
        weight_grad,
        (RING // blocks, width // step),
        ins,
        [out, out],
        operands,
        "weight_grad",
        3 * RING * CORES * rows * ROWS * width,
        2 * (RING * rows * ROWS + ROWS * width + RING * rows * width),
    )


def call_small(kernel, name, ids, pieces, *out_shapes, kind=bf16, scratch=()):
    def full(shape):
        return pl.BlockSpec(shape, lambda i, ids: (0,) * len(shape))

    return run(
        kernel,
        (1,),
        [full(piece.shape) for piece in pieces],
        [(full(shape), jax.ShapeDtypeStruct(shape, kind)) for shape in out_shapes],
        (ids, *pieces),
        name,
        10**6,
        6 * 10**6,
        [pltpu.VMEM(shape, f32) for shape in scratch],
    )


def shift(value, axis, step):
    size = CORES if axis == "core" else RING
    return lax.ppermute(value, axis, [(i, (i + step) % size) for i in range(size)])


def swap(value, axis):
    return lax.ppermute(value, axis, [(i, i ^ 1) for i in range(RING)])


def arrivals(value, axis):
    return [value] + [shift(value, axis, step) for step in (1, 2, 3)]


def both_cores(pieces):
    return [part for piece in pieces for part in (piece, shift(piece, "core", 1))]


def paired(value, axis):
    other = swap(value, axis)
    even = lax.rem(lax.axis_index(axis), 2) == 0
    return jnp.where(even, value, other), jnp.where(even, other, value)


def hold(value, *others):
    return lax.optimization_barrier((value, *others))[0]


def send_ring(parts, axis):
    return [parts[0]] + [shift(parts[step], axis, step) for step in (1, 2, 3)]


def over(value, axis):
    return lax.all_to_all(value, axis, split_axis=0, concat_axis=0, tiled=True)


def pair_cores(pieces):
    me_c = lax.axis_index("core")
    grid = pieces.reshape(RING, CORES, SEQ_DEV, PIECE, WIDTH)
    mine = lax.dynamic_index_in_dim(grid, me_c, 1, keepdims=False)
    away = lax.dynamic_index_in_dim(grid, 1 - me_c, 1, keepdims=False)
    return mine, shift(away, "core", 1)


def placed(value):
    first = lax.axis_index("core") == 0
    value = jnp.where(first, value, value[:, ::-1])
    return value.reshape(RING * CORES * SEQ_DEV, PIECE, WIDTH)


def body(
    tokens,
    cotangent,
    perm,
    lengths,
    drop,
    w_query,
    b_query,
    w_key,
    w_value,
    b_value,
    w_out,
    b_out,
    norm1_gain,
    norm1_bias,
    w_inner,
    b_inner,
    w_outer,
    b_outer,
    norm2_gain,
    norm2_bias,
):
    me_x = lax.axis_index("x")
    me_c = lax.axis_index("core")
    me_z = lax.axis_index("z")
    me_y = lax.axis_index("y")
    first = ((me_z * RING + me_y) * 8 + me_x * CORES + me_c) * SEQ_DEV
    places = jnp.stack([me_x, me_c, first, me_z, me_y]).astype(jnp.int32)
    places = jnp.pad(places, (8, 3))

    vectors = [b_query, b_value, b_out, norm1_gain, norm1_bias, b_outer, norm2_gain, norm2_bias, b_inner]
    vectors += [lengths.astype(bf16), drop.astype(bf16)]
    row = jnp.zeros((4 * WIDTH,), bf16)
    start = 0
    for vector in vectors:
        end = start + vector.shape[0]
        row += jnp.pad(vector, (start, 4 * WIDTH - end))
        start = end
    piece = jnp.concatenate([w_query, w_key, w_value, w_out, w_inner], axis=1)
    row = jnp.pad(row, (0, FF))
    piece = jnp.concatenate([piece, row[None], jnp.zeros((1, 4 * WIDTH + FF), bf16)])
    pieces_y = arrivals(piece, "y")
    dealt = (RING, CORES, SEQ_DEV, PIECE, WIDTH)
    (cores_x,) = call_small(stack_cores, "stack_cores", hold(places, piece), pair_cores(tokens), dealt)
    dealt_x = over(cores_x, "x")
    attn_y, inner_y = call_small(merge_rows, "merge_rows", places, pieces_y, (24, PACKED), (24, FF))
    (attn_zy,) = call_small(
        stack_rows, "stack_rows", places, arrivals(hold(attn_y, cores_x), "z"), (RING, 24, PACKED)
    )
    attn_x = arrivals(hold(attn_zy, dealt_x).reshape(96, PACKED), "x")
    attn_pieces = both_cores(attn_x)

    ffn_x = arrivals(jnp.concatenate([hold(inner_y, cores_x), w_outer], axis=1), "x")
    ffn_x[0] = hold(ffn_x[0], attn_zy)
    inner_x, outer_x = call_small(
        split_ffn, "split_ffn", places, ffn_x, (RING, 24, FF), (RING, 24, WIDTH)
    )
    inner_z = jnp.concatenate(paired(inner_x, "z"), axis=1)
    inner_far = shift(inner_z, "z", 2)
    outer_y = jnp.concatenate(paired(outer_x, "y"), axis=1)
    outer_z = jnp.stack(paired(outer_y, "z"))
    outer_z = jnp.concatenate([outer_z, shift(outer_z, "z", 2)])
    outer_far = shift(outer_z, "y", 2)
    (cores_c,) = call_small(
        stack_cores, "stack_cores", places, pair_cores(hold(cotangent, dealt_x)), dealt
    )
    dealt_c = over(hold(cores_c, attn_x[1]), "x")

    x_t, qkv, expo, norm, ctx_t, sum1, vec, inner_bias, info = call_forward(
        hold(places, cores_c), dealt_x, attn_pieces, perm.reshape(32, 16)
    )
    ids = jnp.concatenate([info[:, 0].astype(jnp.int32), places[8:]])

    inner_pieces = both_cores([inner_z, hold(inner_far, sum1)])
    outer_pieces = both_cores([outer_z, hold(outer_far, sum1)])
    same, other, hid_t, act_t, d_branch, d_inner, d_sum1, d_attn, vec_block = call_ffn(
        ids, sum1, dealt_x, dealt_c, inner_pieces, outer_pieces, vec, inner_bias
    )

    outer_away, outer_mine = call_grad(ids, act_t, d_branch, 1, WIDTH)
    outer_core = shift(outer_away, "core", 1)
    (layer_cores,) = call_small(
        stack_cores, "stack_cores", places, (same, hold(shift(other, "core", 1), outer_away)), dealt
    )
    layer_back = over(layer_cores, "x")
    inner_away, inner_mine = call_grad(
        hold(ids, outer_away, layer_cores), hid_t, d_inner, RING, WIDTH
    )
    inner_core = shift(inner_away, "core", 1)
    out_away, out_mine = call_grad(
        hold(ids, inner_away), ctx_t, d_attn, RING, WIDTH, vec_block
    )
    out_core = shift(out_away, "core", 1)
    (outer_sum,) = call_small(
        sum_outer, "sum_outer", places, (outer_mine, hold(outer_core, out_away, layer_back)),
        (RING, RING, RING, 24, WIDTH),
    )
    outer_y = over(outer_sum, "y")
    inner_width = FF + WIDTH + 128
    inner_parts = call_small(
        sum_blocks, "sum_blocks", hold(places, outer_sum), (inner_mine, inner_core, out_mine, out_core),
        *[(RING, 24, inner_width)] * 4, scratch=[(RING, 96, inner_width)],
    )
    inner_parts = send_ring(inner_parts, "z")

    d_sum1, d_attn = lax.optimization_barrier((d_sum1, d_attn, inner_parts[0], outer_sum))[:2]
    grad_same, grad_other, d_qkv, qkv_block = call_backward(
        ids, d_sum1, d_attn, qkv, expo, norm, ctx_t, dealt_c, attn_pieces
    )

    inner_parts = [hold(inner_parts[0], d_qkv)] + inner_parts[1:]
    inner_parts = call_small(
        split_rows, "split_rows", places, inner_parts, *[(RING, 8, FF + WIDTH)] * 4,
        scratch=[(RING, RING, 8, FF + WIDTH)],
    )
    inner_parts = send_ring(inner_parts, "y")
    (outer_z,) = call_small(
        sum_first, "sum_first", hold(places, d_qkv), (outer_y,), (RING, RING, 24, WIDTH)
    )
    attn_away, attn_mine = call_grad(
        hold(ids, inner_parts[0], outer_z), x_t, d_qkv, RING, 3 * WIDTH, qkv_block
    )
    outer_z = over(outer_z, "z")
    attn_core = shift(hold(attn_away, outer_z, *inner_parts[1:]), "core", 1)
    (grad_cores,) = call_small(
        stack_cores, "stack_cores", hold(places, attn_away), (grad_same, shift(grad_other, "core", 1)), dealt
    )
    attn_width = 3 * WIDTH + 128
    attn_parts = call_small(
        sum_blocks, "sum_blocks", hold(places, grad_cores), (attn_mine, attn_core),
        *[(RING, 24, attn_width)] * 4, scratch=[(RING, 96, attn_width)],
    )
    attn_parts = send_ring(attn_parts, "z")
    grad_back = over(grad_cores, "x")
    attn_parts = call_small(
        split_rows, "split_rows", places, attn_parts, *[(RING, 8, 3 * WIDTH)] * 4,
        scratch=[(RING, RING, 8, 3 * WIDTH)],
    )
    attn_parts = [attn_parts[0]] + [hold(p, grad_back) for p in attn_parts[1:]]
    attn_parts = send_ring(attn_parts, "y")
    last = call_small(
        join_flows, "join_flows", places, [*inner_parts, *attn_parts, outer_z], *[(8, LAST)] * 4,
        scratch=[(RING, 8, LAST)],
    )
    square = (6, WIDTH)
    grad_query, grad_key, grad_value, grad_out, grad_inner, grad_outer, vectors = call_small(
        write_grads, "write_grads", places, send_ring(last, "x"),
        square, square, square, square, (6, FF), (24, WIDTH), (2, 128), kind=f32,
    )
    layer_final = placed(hold(layer_back, last[0]))
    grad_final = placed(hold(grad_back, last[0]))
    ffn_vectors = [vectors[0, 6 * i : 6 * i + 6] for i in range(6)]
    return (
        layer_final,
        grad_final,
        grad_query,
        vectors[1, :6],
        grad_key,
        grad_value,
        vectors[1, 6:12],
        grad_out,
        ffn_vectors[5],
        ffn_vectors[3],
        ffn_vectors[4],
        grad_inner,
        vectors[0, 36:60],
        grad_outer,
        ffn_vectors[0],
        ffn_vectors[1],
        ffn_vectors[2],
    )


def solution(mesh):
    chips = Mesh(mesh.devices.reshape(RING, CORES, RING, RING), ("x", "core", "z", "y"))
    dp = ("x", "core")
    fsdp = ("z", "y")
    every = P(dp + fsdp)
    rows = P(dp + fsdp, None)
    whole_rows = P(fsdp, dp, None)
    return jax.shard_map(
        body,
        mesh=chips,
        in_specs=(
            whole_rows, whole_rows, P(), every, every,
            rows, every, rows, rows, every, rows, every, every, every,
            rows, every, rows, every, every, every,
        ),
        out_specs=(
            whole_rows, whole_rows,
            rows, every, rows, rows, every, rows, every, every, every,
            rows, every, rows, every, every, every,
        ),
        check_vma=False,
    )
```

```python
import functools
import jax
import jax.numpy as jnp
from jax import lax
from jax.experimental import pallas as pl
from jax.experimental.pallas import tpu as pltpu
from jax.sharding import Mesh
from jax.sharding import PartitionSpec as P

HEADS = 12
HEAD = 64
WIDTH = 768
FF = 3072
SLOT = 256
SEQ_DEV = 4
RING = 4
CORES = 2
PIECE = 32
GROUP = RING * CORES
ROWS = SEQ_DEV * SLOT
PAIR = 2 * HEAD
PACKED = 4 * WIDTH + 512

epsilon = 1e-05
bf16 = jnp.bfloat16
f32 = jnp.float32
VMEM_LIMIT = 58 * 1024 * 1024

TN = (((0,), (0,)), ((), ()))
NT = (((1,), (1,)), ((), ()))


def mm(a, b):
    return jnp.dot(a, b, preferred_element_type=f32)


def mm_nt(a, b):
    return lax.dot_general(a, b, NT, preferred_element_type=f32)


def mm_tn(a, b):
    return lax.dot_general(a, b, TN, preferred_element_type=f32)


def joined(ref):
    return ref[...].reshape(SLOT, WIDTH)


def spread(extras, start, width):
    total = 128 * width
    group = lax.broadcasted_iota(jnp.int32, (32, total), 0)
    owner = lax.broadcasted_iota(jnp.int32, (32, total), 1) // width
    pick = lax.broadcasted_iota(jnp.int32, (width, total), 0)
    within = lax.rem(lax.broadcasted_iota(jnp.int32, (width, total), 1), width)
    chosen = (pick == within).astype(bf16)
    out = jnp.zeros((32, total), f32)
    for y in range(RING):
        values = extras[:, 128 * y + start : 128 * y + start + width].astype(bf16)
        out += jnp.where(owner == group * RING + y, mm(values, chosen), 0.0)
    return jnp.sum(out, axis=0, keepdims=True)


def gather_back(vectors):
    values = jnp.zeros((128, 128), f32)
    start = 0
    for vector in vectors:
        total = vector.shape[1]
        width = total // 128
        owner = lax.broadcasted_iota(jnp.int32, (128, total), 1) // width
        mine = owner == lax.broadcasted_iota(jnp.int32, (128, total), 0)
        within = lax.rem(lax.broadcasted_iota(jnp.int32, (total, 128), 0), width)
        column = lax.broadcasted_iota(jnp.int32, (total, 128), 1)
        spots = (column == within + start).astype(bf16)
        values += mm(jnp.where(mine, vector, 0.0).astype(bf16), spots)
        start += width
    row = lax.broadcasted_iota(jnp.int32, (WIDTH, 128), 0)
    device = lax.broadcasted_iota(jnp.int32, (WIDTH, 128), 1)
    within = lax.rem(row, 24)
    picks = (within < RING) & (row // 24 * RING + within == device)
    return mm(picks.astype(bf16), values.astype(bf16)).astype(bf16)


def attention_copies(ids, pieces, w, sems):
    copies = []
    for i, piece in enumerate(pieces):
        x = lax.rem(ids[8] + RING - i // 2, RING)
        c = ids[9] if i % 2 == 0 else 1 - ids[9]
        copies.append(pltpu.make_async_copy(piece, w.at[x, c], sems.at[i]))
    return copies


def columns(w, start, end):
    return w[:, :, :, start:end].reshape(WIDTH, end - start)


def attention_forward(
    ids, x_in, p0, p1, p2, p3, p4, p5, p6, p7, perm,
    xt_out, qkv_out, exp_out, norm_out, ctxt_out, sum_out, vec, bias_out, info,
    w, extras, sems,
):
    s = pl.program_id(0)

    @pl.when(s == 0)
    def _():
        copies = attention_copies(ids, (p0, p1, p2, p3, p4, p5, p6, p7), w, sems)
        for copy in copies:
            copy.start()
        for copy in copies:
            copy.wait()
        rows = columns(w, 4 * WIDTH, PACKED).astype(f32).reshape(32, 24, PACKED - 4 * WIDTH)
        extras[...] = jnp.sum(rows, axis=1)
        for i in range(8):
            vec[i : i + 1] = spread(extras, 6 * i, 6)
        bias_out[...] = spread(extras, 48, 24)

    length = jnp.zeros((1, 1), f32)
    dropped = jnp.zeros((1, 1), f32)
    for y in range(RING):
        hit = perm[:, RING * y : RING * y + 4] == ids[10] + s
        length += jnp.sum(jnp.where(hit, extras[:, 128 * y + 72 : 128 * y + 76], 0.0), keepdims=True)
        dropped += jnp.sum(jnp.where(hit, extras[:, 128 * y + 76 : 128 * y + 80], 0.0), keepdims=True)
    line = lax.broadcasted_iota(jnp.int32, (8, 128), 0)
    info[...] = jnp.where(line == s, length, jnp.where(line == s + 4, dropped, info[...]))

    x = joined(x_in)
    xt_out[...] = x.T
    q = ((mm(x, columns(w, 0, WIDTH)) + vec[0:1]).astype(bf16).astype(f32) * HEAD**-0.5).astype(bf16)
    k = mm(x, columns(w, WIDTH, 2 * WIDTH)).astype(bf16)
    v = (mm(x, columns(w, 2 * WIDTH, 3 * WIDTH)) + vec[1:2]).astype(bf16)
    qkv_out[:, :WIDTH] = q
    qkv_out[:, WIDTH : 2 * WIDTH] = k
    qkv_out[:, 2 * WIDTH :] = v
    q_t = q.T
    v_t = v.T
    keys = lax.broadcasted_iota(jnp.int32, (SLOT, 1), 0).astype(f32)
    bias = jnp.where(keys < length, 0.0, -1e30)
    low = lax.broadcasted_iota(jnp.int32, (SLOT, PAIR), 1) < HEAD
    ctx_t = []
    for h in range(HEADS):
        p = h // 2 * PAIR
        k_pair = k[:, p : p + PAIR]
        k_one = jnp.where(low if h % 2 == 0 else ~low, k_pair, jnp.zeros_like(k_pair))
        scores = mm(k_one, q_t[p : p + PAIR]) + bias
        top = jnp.max(scores, axis=0, keepdims=True)
        expo = jnp.exp(scores - top)
        inverse = 1.0 / jnp.sum(expo, axis=0, keepdims=True)
        norm_out[0, h : h + 1, :] = inverse
        expo = expo.astype(bf16)
        exp_out[0, h] = expo
        ctx_t.append(mm(v_t[h * HEAD : (h + 1) * HEAD], expo) * inverse)
    ctx_t = jnp.concatenate(ctx_t, axis=0).astype(bf16)
    ctxt_out[...] = ctx_t
    sum_out[...] = x.astype(f32) + (mm(ctx_t.T, columns(w, 3 * WIDTH, 4 * WIDTH)) + vec[2:3])


def row_mean(v):
    return jnp.mean(v, axis=-1, keepdims=True)


def normalised(z):
    center = z - row_mean(z)
    r = lax.rsqrt(row_mean(center * center) + epsilon)
    return center * r, r


def norm_back(dy, zhat, r, gain):
    e = dy * gain
    return r * (e - row_mean(e) - zhat * row_mean(e * zhat))


def col_sum(v):
    return jnp.sum(v, axis=0, keepdims=True)


FF_STEP = 768


def feed_forward(
    ids, sum1, x_in, c_in, i0, i1, i2, i3, j0, j1, j2, j3, vec, bias_in,
    layer_out, hidt_out, actt_out, dbranch_out, dinner_out, dsum_out, dattn_out, vec_block,
    slope, vec_grad, bias_grad, w_in, w_out, in_sems, out_sems,
):
    s = pl.program_id(0)

    def copies():
        ins = []
        outs = []
        for i, (piece, late) in enumerate(zip((i0, i1, i2, i3), (j0, j1, j2, j3))):
            c = ids[9] if i % 2 == 0 else 1 - ids[9]
            z_half = ids[11] // 2 if i // 2 == 0 else 1 - ids[11] // 2
            y_half = ids[12] // 2 if i // 2 == 0 else 1 - ids[12] // 2
            for d in range(RING):
                x = lax.rem(ids[8] + RING - d, RING)
                ins.append(pltpu.make_async_copy(piece.at[d], w_in.at[x, c, z_half], in_sems.at[i, d]))
                for n in range(RING):
                    target = w_out.at[x, c, n, y_half]
                    outs.append(pltpu.make_async_copy(late.at[n, d], target, out_sems.at[i, d, n]))
        return ins, outs

    @pl.when(s == 0)
    def _():
        vec_grad[...] = jnp.zeros_like(vec_grad)
        bias_grad[...] = jnp.zeros_like(bias_grad)
        ins, outs = copies()
        for copy in ins + outs:
            copy.start()
        for copy in ins + outs:
            copy.wait()

    def inner_columns(start):
        return w_in[:, :, :, :, start : start + FF_STEP].reshape(WIDTH, FF_STEP)

    def outer_rows(start):
        x = start // (FF // RING)
        return w_out[x].reshape(FF // RING, WIDTH)

    zhat1, r1 = normalised(sum1[...])
    hidden = zhat1 * vec[3:4] + vec[4:5]
    hid_low = hidden.astype(bf16)
    hidt_out[...] = hid_low.T
    branch = jnp.broadcast_to(vec[5:6], (SLOT, WIDTH))
    for n in range(0, FF, FF_STEP):
        cols = slice(n, n + FF_STEP)
        inner = mm(hid_low, inner_columns(n)) + bias_in[0:1, cols]
        half = 0.5 * lax.erf(inner * 0.7071067811865476) + 0.5
        bell = 0.3989422804014327 * jnp.exp(-0.5 * (inner * inner))
        act = (inner * half).astype(bf16)
        actt_out[cols, :] = act.T
        slope[:, cols] = (half + inner * bell).astype(bf16)
        branch += mm(act, outer_rows(n))
    zhat2, r2 = normalised(hidden + branch)
    gain2 = vec[6:7]
    normed = zhat2 * gain2 + vec[7:8]
    valid = (lax.broadcasted_iota(jnp.int32, (SLOT, 1), 0) < ids[s]).astype(f32)
    keep = ids[4 + s] == 0
    x = joined(x_in).astype(f32)
    layer_out[...] = (jnp.where(keep, normed, x) * valid).astype(bf16)
    upstream = joined(c_in).astype(f32)
    dy = upstream * jnp.where(keep, valid, 0.0)
    vec_grad[1:2] += col_sum(dy * zhat2)
    vec_grad[2:3] += col_sum(dy)
    d_sum2 = norm_back(dy, zhat2, r2, gain2)
    d_branch = d_sum2.astype(bf16)
    dbranch_out[...] = d_branch
    vec_grad[0:1] += col_sum(d_branch.astype(f32))
    d_hidden = d_sum2
    for n in range(0, FF, FF_STEP):
        cols = slice(n, n + FF_STEP)
        d_act = mm_nt(d_branch, outer_rows(n))
        d_inner = (d_act * slope[:, cols].astype(f32)).astype(bf16)
        dinner_out[:, cols] = d_inner
        bias_grad[0:1, cols] += col_sum(d_inner.astype(f32))
        d_hidden += mm_nt(d_inner, inner_columns(n))
    vec_grad[3:4] += col_sum(d_hidden * zhat1)
    vec_grad[4:5] += col_sum(d_hidden)
    d_sum1 = norm_back(d_hidden, zhat1, r1, vec[3:4])
    dsum_out[...] = d_sum1
    d_attn = d_sum1.astype(bf16)
    dattn_out[...] = d_attn
    vec_grad[5:6] += col_sum(d_attn.astype(f32))

    @pl.when(s == SEQ_DEV - 1)
    def _():
        vec_block[...] = gather_back([vec_grad[i : i + 1] for i in range(6)] + [bias_grad[...]])


def attention_backward(
    ids, dsum, dattn, qkv, exp_in, norm_in, ctxt_in, c_in, layer_in, p0, p1, p2, p3, p4, p5, p6, p7,
    back_out, dqkv_out, vec_block,
    w, vec_grad, sems,
):
    s = pl.program_id(0)

    @pl.when(s == 0)
    def _():
        vec_grad[...] = jnp.zeros_like(vec_grad)
        copies = attention_copies(ids, (p0, p1, p2, p3, p4, p5, p6, p7), w, sems)
        for copy in copies:
            copy.start()
        for copy in copies:
            copy.wait()

    d_sum1 = dsum[...]
    dctx_t = mm_nt(dattn[...], columns(w, 3 * WIDTH, 4 * WIDTH)).T
    ctx_t = ctxt_in[...].astype(f32)
    k_t = qkv[:, WIDTH : 2 * WIDTH].T
    scaled = []
    deltas = []
    for h in range(HEADS):
        rows = slice(h * HEAD, (h + 1) * HEAD)
        one = (dctx_t[rows] * norm_in[0, h : h + 1, :]).astype(bf16)
        scaled.append(one)
        deltas.append(col_sum(one.astype(f32) * ctx_t[rows]))
    dctx_t = jnp.concatenate(scaled, axis=0)
    dctx = dctx_t.T
    low = lax.broadcasted_iota(jnp.int32, (SLOT, PAIR), 1) < HEAD
    dq_t = []
    for p in range(0, WIDTH, PAIR):
        cols = slice(p, p + PAIR)
        q_pair = qkv[:, cols]
        v_pair = qkv[:, 2 * WIDTH + p : 2 * WIDTH + p + PAIR]
        dks = []
        dvs = []
        for half in range(2):
            h = p // HEAD + half
            v_one = jnp.where(low if half == 0 else ~low, v_pair, jnp.zeros_like(v_pair))
            d_probs = mm(v_one, dctx_t[cols]) - deltas[h]
            expo = exp_in[0, h]
            d_scores = (expo.astype(f32) * d_probs).astype(bf16)
            dvs.append(mm(expo, dctx[:, cols]))
            dks.append(mm(d_scores, q_pair))
            dq_t.append(mm(k_t[h * HEAD : (h + 1) * HEAD], d_scores))
        dqkv_out[:, WIDTH + p : WIDTH + p + PAIR] = jnp.where(low, dks[0], dks[1]).astype(bf16)
        dqkv_out[:, 2 * WIDTH + p : 2 * WIDTH + p + PAIR] = jnp.where(low, dvs[0], dvs[1]).astype(bf16)
    dq = (jnp.concatenate(dq_t, axis=0).T * HEAD**-0.5).astype(bf16)
    dqkv_out[:, :WIDTH] = dq
    vec_grad[0:1] += col_sum(dq.astype(f32))
    vec_grad[1:2] += col_sum(dqkv_out[:, 2 * WIDTH :].astype(f32))
    d_in = d_sum1 + mm_nt(dqkv_out[...], columns(w, 0, 3 * WIDTH))
    valid = (lax.broadcasted_iota(jnp.int32, (SLOT, 1), 0) < ids[s]).astype(f32)
    upstream = joined(c_in).astype(f32) * valid
    keep = ids[4 + s] == 0
    grad = jnp.where(keep, d_in, upstream).astype(bf16)
    back_out[:, 0, 0] = layer_in[...].reshape(GROUP, PIECE, WIDTH)
    back_out[:, 1, 0] = grad.reshape(GROUP, PIECE, WIDTH)

    @pl.when(s == SEQ_DEV - 1)
    def _():
        vec_block[...] = gather_back([vec_grad[0:1], vec_grad[1:2]])


def weight_grad(ids, left, right, *refs):
    *tail, away, mine = refs
    value = mm(left[...], right[...]).astype(bf16)
    if tail:
        value = jnp.concatenate([value, tail[0][...]], axis=1)
    blocks, rows, _ = away.shape
    first = ids[9] == 0
    for x in range(blocks):
        even = value[2 * x * rows : (2 * x + 1) * rows]
        odd = value[(2 * x + 1) * rows : (2 * x + 2) * rows]
        away[x] = jnp.where(first, odd, even)
        mine[x] = jnp.where(first, even, odd)


def in_order(values, me):
    ordered = []
    for j in range(RING):
        step = lax.rem(me + RING - j, RING)
        value = values[0]
        for d in (1, 2, 3):
            value = jnp.where(step == d, values[d], value)
        ordered.append(value)
    return ordered


def merge_rows(ids, own, r1, r2, r3, attn_out, inner_out):
    ordered = in_order([v[...].astype(f32) for v in (own, r1, r2, r3)], ids[12])
    width = 4 * WIDTH
    rows = jnp.concatenate([v[:6] for v in ordered], axis=0).astype(bf16)
    attn_out[:, :width] = rows[:, :width]
    inner_out[...] = rows[:, width:]
    row = jnp.concatenate([v[6:7, :128] for v in ordered], axis=1)
    first = lax.broadcasted_iota(jnp.int32, (24, 4 * 128), 0) == 0
    attn_out[:, width:] = jnp.where(first, jnp.broadcast_to(row, (24, 4 * 128)), 0.0).astype(bf16)


def stack_rows(ids, own, r1, r2, r3, out):
    for d, piece in enumerate((own, r1, r2, r3)):
        out[lax.rem(ids[11] + RING - d, RING)] = piece[...]


def ahead(ids, axis, step):
    return lax.rem(ids[axis] + step, RING)


def sum_of(refs):
    total = refs[0][...].astype(f32)
    for ref in refs[1:]:
        total += ref[...].astype(f32)
    return total


def sum_blocks(ids, *refs):
    *parts, o0, o1, o2, o3, scratch = refs
    start = 0
    for mine, core in zip(parts[::2], parts[1::2]):
        end = start + mine.shape[2]
        scratch[:, start:end] = mine[0].astype(f32) + core[0].astype(f32)
        start = end
    for d, out in enumerate((o0, o1, o2, o3)):
        first = pl.multiple_of(ahead(ids, 11, d) * 24, 8)
        out[0] = scratch[pl.ds(first, 24), :].astype(bf16)


def sum_outer(ids, mine, core, out):
    total = mine[0].astype(f32) + core[0].astype(f32)
    for z in range(RING):
        for y in range(RING):
            first = 96 * z + 24 * y
            out[y, 0, z] = total[first : first + 24].astype(bf16)


def sum_first(ids, value, out):
    for z in range(RING):
        out[z, 0] = sum_of([value.at[y, 0, z] for y in range(RING)]).astype(bf16)


def split_rows(ids, p0, p1, p2, p3, o0, o1, o2, o3, scratch):
    width = o0.shape[2]
    total = sum_of([p.at[0] for p in (p0, p1, p2, p3)])
    for y in range(RING):
        row = jnp.concatenate([total[y : y + 1, width:], jnp.zeros((1, width - 128), f32)], axis=1)
        rows = total[6 * y : 6 * y + 6, :width]
        scratch[y] = jnp.concatenate([rows, row, jnp.zeros((1, width), f32)], axis=0)
    for d, out in enumerate((o0, o1, o2, o3)):
        out[0] = scratch[ahead(ids, 12, d)].astype(bf16)


LAST = FF + WIDTH + 3 * WIDTH + 3 * WIDTH


def join_flows(ids, i0, i1, i2, i3, a0, a1, a2, a3, outer, o0, o1, o2, o3, scratch):
    scratch[:, :, : FF + WIDTH] = sum_of((i0, i1, i2, i3))
    scratch[:, :, FF + WIDTH : FF + 4 * WIDTH] = sum_of((a0, a1, a2, a3))
    for x in range(RING):
        total = sum_of([outer.at[z, x] for z in range(RING)])
        for k in range(3):
            start = FF + (4 + k) * WIDTH
            scratch[x, :, start : start + WIDTH] = total[8 * k : 8 * k + 8]
    for d, out in enumerate((o0, o1, o2, o3)):
        out[...] = scratch[ahead(ids, 8, d)].astype(bf16)


def split_ffn(ids, p0, p1, p2, p3, inner, outer):
    for d, piece in enumerate((p0, p1, p2, p3)):
        inner[d] = piece[:, :FF]
        halves = [piece[:, FF + i * WIDTH : FF + (i + 1) * WIDTH].astype(f32) for i in range(2)]
        outer[d] = jnp.concatenate(halves, axis=0).astype(bf16)


def write_grads(ids, p0, p1, p2, p3, query, key, value, out, inner, outer, vectors):
    total = sum_of((p0, p1, p2, p3))
    inner[...] = total[:6, :FF]
    out[...] = total[:6, FF : FF + WIDTH]
    start = FF + WIDTH
    query[...] = total[:6, start : start + WIDTH]
    key[...] = total[:6, start + WIDTH : start + 2 * WIDTH]
    value[...] = total[:6, start + 2 * WIDTH : start + 3 * WIDTH]
    vectors[...] = jnp.concatenate([total[6:7, :128], total[6:7, start : start + 128]], axis=0)
    start += 3 * WIDTH
    for k in range(3):
        outer[8 * k : 8 * k + 8] = total[:, start + k * WIDTH : start + (k + 1) * WIDTH]


def whole(shape):
    return pl.BlockSpec(shape, lambda s, ids: (0,) * len(shape), pipeline_mode=pl.Buffered(1))


DEALT_SPEC = pl.BlockSpec((GROUP, 1, PIECE, WIDTH), lambda s, ids: (0, s, 0, 0))


def by_rows(width):
    return pl.BlockSpec((SLOT, width), lambda s, ids: (s, 0))


def rows_of(width, kind):
    return jax.ShapeDtypeStruct((ROWS, width), kind)


EXP_SPEC = pl.BlockSpec((1, HEADS, SLOT, SLOT), lambda s, ids: (s, 0, 0, 0))
NORM_SPEC = pl.BlockSpec((1, 16, SLOT), lambda s, ids: (s, 0, 0))
RETURN_SPEC = pl.BlockSpec((GROUP, 2, 1, PIECE, WIDTH), lambda s, ids: (0, 0, s, 0, 0))
RETURN_SHAPE = jax.ShapeDtypeStruct((GROUP, 2, SEQ_DEV, PIECE, WIDTH), bf16)


def by_columns(height):
    return pl.BlockSpec((height, SLOT), lambda s, ids: (0, s))


def columns_of(height):
    return jax.ShapeDtypeStruct((height, ROWS), bf16)


def run(kernel, grid, ins, outs, operands, name, flops, moved, scratch=()):
    return pl.pallas_call(
        kernel,
        grid_spec=pltpu.PrefetchScalarGridSpec(
            num_scalar_prefetch=1,
            grid=grid,
            in_specs=ins,
            out_specs=[spec for spec, _ in outs],
            scratch_shapes=list(scratch),
        ),
        out_shape=[shape for _, shape in outs],
        compiler_params=pltpu.CompilerParams(
            vmem_limit_bytes=VMEM_LIMIT, dimension_semantics=("arbitrary",) * len(grid)
        ),
        cost_estimate=pl.CostEstimate(flops=flops, bytes_accessed=moved, transcendentals=0),
        name=name,
    )(*operands)


def out_rows(width, kind):
    return (by_rows(width), rows_of(width, kind))


def out_columns(height):
    return (by_columns(height), columns_of(height))


def out_whole(shape):
    return (whole(shape), jax.ShapeDtypeStruct(shape, f32))


ANYWHERE = pl.BlockSpec(memory_space=pl.ANY)
ATTENTION_SCRATCH = [pltpu.VMEM((RING, CORES, 96, PACKED), bf16)]


def call_forward(ids, dealt, weights, perm):
    return run(
        attention_forward,
        (SEQ_DEV,),
        [DEALT_SPEC] + [ANYWHERE] * 8 + [whole((32, 16))],
        [
            out_columns(WIDTH),
            out_rows(3 * WIDTH, bf16),
            (EXP_SPEC, jax.ShapeDtypeStruct((SEQ_DEV, HEADS, SLOT, SLOT), bf16)),
            (NORM_SPEC, jax.ShapeDtypeStruct((SEQ_DEV, 16, SLOT), f32)),
            out_columns(WIDTH),
            out_rows(WIDTH, f32),
            out_whole((8, WIDTH)),
            out_whole((1, FF)),
            out_whole((8, 128)),
        ],
        (ids, dealt, *weights, perm),
        "attention_forward",
        22 * 10**9,
        22 * 10**6,
        ATTENTION_SCRATCH + [pltpu.VMEM((32, PACKED - 4 * WIDTH), f32), pltpu.SemaphoreType.DMA((8,))],
    )


def call_ffn(ids, sum1, dealt, dealt_c, inner, outer, vec, bias_in):
    return run(
        feed_forward,
        (SEQ_DEV,),
        [by_rows(WIDTH)] + [DEALT_SPEC] * 2 + [ANYWHERE] * 8 + [whole((8, WIDTH)), whole((1, FF))],
        [
            out_rows(WIDTH, bf16),
            out_columns(WIDTH),
            out_columns(FF),
            out_rows(WIDTH, bf16),
            out_rows(FF, bf16),
            out_rows(WIDTH, f32),
            out_rows(WIDTH, bf16),
            (whole((WIDTH, 128)), jax.ShapeDtypeStruct((WIDTH, 128), bf16)),
        ],
        (ids, sum1, dealt, dealt_c, *inner, *outer, vec, bias_in),
        "feed_forward",
        36 * 10**9,
        40 * 10**6,
        [
            pltpu.VMEM((SLOT, FF), bf16),
            pltpu.VMEM((8, WIDTH), f32),
            pltpu.VMEM((1, FF), f32),
            pltpu.VMEM((RING, CORES, 2, 48, FF), bf16),
            pltpu.VMEM((RING, CORES, RING, 2, 48, WIDTH), bf16),
            pltpu.SemaphoreType.DMA((RING, RING)),
            pltpu.SemaphoreType.DMA((RING, RING, RING)),
        ],
    )


def call_backward(ids, dsum, dattn, qkv, expo, norm, ctx_t, dealt_c, layer, weights):
    return run(
        attention_backward,
        (SEQ_DEV,),
        [by_rows(WIDTH), by_rows(WIDTH), by_rows(3 * WIDTH), EXP_SPEC, NORM_SPEC, by_columns(WIDTH)]
        + [DEALT_SPEC, by_rows(WIDTH)]
        + [ANYWHERE] * 8,
        [
            (RETURN_SPEC, RETURN_SHAPE),
            out_rows(3 * WIDTH, bf16),
            (whole((WIDTH, 128)), jax.ShapeDtypeStruct((WIDTH, 128), bf16)),
        ],
        (ids, dsum, dattn, qkv, expo, norm, ctx_t, dealt_c, layer, *weights),
        "attention_backward",
        24 * 10**9,
        30 * 10**6,
        ATTENTION_SCRATCH + [pltpu.VMEM((8, WIDTH), f32), pltpu.SemaphoreType.DMA((8,))],
    )


def call_grad(ids, left, right, blocks, step, tail=None):
    rows = left.shape[0] // (RING * CORES)
    width = right.shape[1]
    ins = [
        pl.BlockSpec((2 * blocks * rows, ROWS), lambda i, n, ids: (i, 0)),
        pl.BlockSpec((ROWS, step), lambda i, n, ids: (0, n)),
    ]
    operands = (ids, left, right)
    more = 0
    if tail is not None:
        more = tail.shape[1]
        ins.append(pl.BlockSpec((WIDTH, more), lambda i, n, ids: (0, 0)))
        operands += (tail,)
    out = (
        pl.BlockSpec((blocks, rows, step + more), lambda i, n, ids: (i, 0, n)),
        jax.ShapeDtypeStruct((RING, rows, width + more), bf16),
    )
    return run(
        weight_grad,
        (RING // blocks, width // step),
        ins,
        [out, out],
        operands,
        "weight_grad",
        3 * RING * CORES * rows * ROWS * width,
        2 * (RING * rows * ROWS + ROWS * width + RING * rows * width),
    )


def call_by_x(kernel, name, ids, pieces, at, out_shape, out_at, count, scratch=()):
    def one(shape, where):
        block = tuple(1 if i == where else n for i, n in enumerate(shape))
        return pl.BlockSpec(block, lambda x, ids: tuple(x if i == where else 0 for i in range(len(shape))))

    return run(
        kernel,
        (RING,),
        [one(piece.shape, at) for piece in pieces],
        [(one(out_shape, out_at), jax.ShapeDtypeStruct(out_shape, bf16))] * count,
        (ids, *pieces),
        name,
        10**6,
        8 * 10**6,
        [pltpu.VMEM(shape, f32) for shape in scratch],
    )


def call_small(kernel, name, ids, pieces, *out_shapes, kind=bf16, scratch=()):
    def full(shape):
        return pl.BlockSpec(shape, lambda i, ids: (0,) * len(shape))

    return run(
        kernel,
        (1,),
        [full(piece.shape) for piece in pieces],
        [(full(shape), jax.ShapeDtypeStruct(shape, kind)) for shape in out_shapes],
        (ids, *pieces),
        name,
        10**6,
        6 * 10**6,
        [pltpu.VMEM(shape, f32) for shape in scratch],
    )


def shift(value, axis, step):
    size = CORES if axis == "core" else RING
    return lax.ppermute(value, axis, [(i, (i + step) % size) for i in range(size)])


def swap(value, axis):
    return lax.ppermute(value, axis, [(i, i ^ 1) for i in range(RING)])


def arrivals(value, axis):
    return [value] + [shift(value, axis, step) for step in (1, 2, 3)]


def both_cores(pieces):
    return [part for piece in pieces for part in (piece, shift(piece, "core", 1))]


def paired(value, axis):
    return in_half(value, swap(value, axis), axis)


def in_half(value, other, axis):
    even = lax.rem(lax.axis_index(axis), 2) == 0
    return jnp.where(even, value, other), jnp.where(even, other, value)


def hold(value, *others):
    return lax.optimization_barrier((value, *others))[0]


def send_ring(parts, axis):
    return [parts[0]] + [shift(parts[step], axis, step) for step in (1, 2, 3)]


def over(value, axis):
    return lax.all_to_all(value, axis, split_axis=0, concat_axis=0, tiled=True)


def body(
    tokens,
    cotangent,
    perm,
    lengths,
    drop,
    w_query,
    b_query,
    w_key,
    w_value,
    b_value,
    w_out,
    b_out,
    norm1_gain,
    norm1_bias,
    w_inner,
    b_inner,
    w_outer,
    b_outer,
    norm2_gain,
    norm2_bias,
):
    me_x = lax.axis_index("x")
    me_c = lax.axis_index("core")
    me_z = lax.axis_index("z")
    me_y = lax.axis_index("y")
    first = ((me_z * RING + me_y) * 8 + me_x * CORES + me_c) * SEQ_DEV
    places = jnp.stack([me_x, me_c, first, me_z, me_y]).astype(jnp.int32)
    places = jnp.pad(places, (8, 3))

    vectors = [b_query, b_value, b_out, norm1_gain, norm1_bias, b_outer, norm2_gain, norm2_bias, b_inner]
    vectors += [lengths.astype(bf16), drop.astype(bf16)]
    row = jnp.zeros((4 * WIDTH,), bf16)
    start = 0
    for vector in vectors:
        end = start + vector.shape[0]
        row += jnp.pad(vector, (start, 4 * WIDTH - end))
        start = end
    piece = jnp.concatenate([w_query, w_key, w_value, w_out, w_inner], axis=1)
    row = jnp.pad(row, (0, FF))
    piece = jnp.concatenate([piece, row[None], jnp.zeros((1, 4 * WIDTH + FF), bf16)])
    pieces_y = arrivals(piece, "y")
    dp = ("x", "core")
    dealt = (GROUP, SEQ_DEV, PIECE, WIDTH)
    dealt_x = over(tokens.reshape(dealt), dp)
    attn_y, inner_y = call_small(merge_rows, "merge_rows", places, pieces_y, (24, PACKED), (24, FF))
    (attn_zy,) = call_small(
        stack_rows, "stack_rows", places, arrivals(attn_y, "z"), (RING, 24, PACKED)
    )

    outer_pair = paired(w_outer, "y")
    ffn_x = arrivals(jnp.concatenate([inner_y, *outer_pair], axis=1), "x")
    ffn_x[0] = hold(ffn_x[0], attn_zy)
    inner_x, outer_x = call_small(
        split_ffn, "split_ffn", places, ffn_x, (RING, 24, FF), (RING, 48, WIDTH)
    )
    attn_x = arrivals(hold(attn_zy, dealt_x, inner_x).reshape(96, PACKED), "x")
    attn_pieces = both_cores(attn_x)
    inner_z = swap(inner_x, "z")
    outer_z = over(jnp.broadcast_to(outer_x[None], (RING, RING, 48, WIDTH)), "z")
    inner_z = jnp.concatenate(in_half(inner_x, hold(inner_z, attn_x[1]), "z"), axis=1)
    inner_far = shift(inner_z, "z", 2)
    outer_z = hold(outer_z, attn_x[1])
    outer_far = shift(outer_z, "y", 2)
    dealt_c = over(hold(cotangent, attn_x[1]).reshape(dealt), dp)

    x_t, qkv, expo, norm, ctx_t, sum1, vec, inner_bias, info = call_forward(
        places, dealt_x, attn_pieces, perm.reshape(32, 16)
    )
    ids = jnp.concatenate([info[:, 0].astype(jnp.int32), places[8:]])

    inner_pieces = both_cores([inner_z, hold(inner_far, sum1)])
    outer_pieces = both_cores([outer_z, hold(outer_far, sum1)])
    layer, hid_t, act_t, d_branch, d_inner, d_sum1, d_attn, vec_block = call_ffn(
        ids, sum1, dealt_x, dealt_c, inner_pieces, outer_pieces, vec, inner_bias
    )

    outer_away, outer_mine = call_grad(ids, act_t, d_branch, 1, WIDTH)
    outer_core = shift(outer_away, "core", 1)
    inner_away, inner_mine = call_grad(hold(ids, outer_away), hid_t, d_inner, RING, WIDTH)
    inner_core = shift(inner_away, "core", 1)
    out_away, out_mine = call_grad(
        hold(ids, inner_away), ctx_t, d_attn, RING, WIDTH, vec_block
    )
    out_core = shift(out_away, "core", 1)
    (outer_sum,) = call_by_x(
        sum_outer, "sum_outer", places, (outer_mine, hold(outer_core, out_away)), 0,
        (RING, RING, RING, 24, WIDTH), 1, 1,
    )
    outer_y = over(outer_sum, "y")
    inner_width = FF + WIDTH + 128
    inner_parts = call_by_x(
        sum_blocks, "sum_blocks", hold(places, outer_sum), (inner_mine, inner_core, out_mine, out_core), 0,
        (RING, 24, inner_width), 0, RING, [(96, inner_width)],
    )
    inner_parts = send_ring(inner_parts, "z")

    d_sum1, d_attn = lax.optimization_barrier((d_sum1, d_attn, inner_parts[0], outer_sum))[:2]
    back, d_qkv, qkv_block = call_backward(
        ids, d_sum1, d_attn, qkv, expo, norm, ctx_t, dealt_c, layer, attn_pieces
    )

    inner_parts = [hold(inner_parts[0], d_qkv)] + inner_parts[1:]
    inner_parts = call_by_x(
        split_rows, "split_rows", places, inner_parts, 0, (RING, 8, FF + WIDTH), 0, RING, [(RING, 8, FF + WIDTH)]
    )
    (outer_z,) = call_by_x(
        sum_first, "sum_first", hold(places, d_qkv), (outer_y,), 1, (RING, RING, 24, WIDTH), 1, 1
    )
    attn_away, attn_mine = call_grad(
        hold(ids, inner_parts[0], outer_z), x_t, d_qkv, RING, 3 * WIDTH, qkv_block
    )
    outer_z = over(outer_z, "z")
    attn_core = shift(hold(attn_away, outer_z), "core", 1)
    attn_width = 3 * WIDTH + 128
    attn_parts = call_by_x(
        sum_blocks, "sum_blocks", places, (attn_mine, attn_core), 0,
        (RING, 24, attn_width), 0, RING, [(96, attn_width)],
    )
    inner_parts = [inner_parts[0]] + [hold(p, attn_parts[0]) for p in inner_parts[1:]]
    attn_parts = send_ring(attn_parts, "z")
    inner_parts = send_ring(inner_parts, "y")
    back = over(hold(back, attn_away), dp)
    attn_parts = call_by_x(
        split_rows, "split_rows", places, attn_parts, 0, (RING, 8, 3 * WIDTH), 0, RING, [(RING, 8, 3 * WIDTH)]
    )
    attn_parts = send_ring(attn_parts, "y")
    last = call_small(
        join_flows, "join_flows", places, [*inner_parts, *attn_parts, outer_z], *[(8, LAST)] * 4,
        scratch=[(RING, 8, LAST)],
    )
    square = (6, WIDTH)
    grad_query, grad_key, grad_value, grad_out, grad_inner, grad_outer, vectors = call_small(
        write_grads, "write_grads", places, send_ring(last, "x"),
        square, square, square, square, (6, FF), (24, WIDTH), (2, 128), kind=f32,
    )
    back = hold(back, last[0])
    layer_final = back[:, 0].reshape(GROUP * SEQ_DEV, PIECE, WIDTH)
    grad_final = back[:, 1].reshape(GROUP * SEQ_DEV, PIECE, WIDTH)
    ffn_vectors = [vectors[0, 6 * i : 6 * i + 6] for i in range(6)]
    return (
        layer_final,
        grad_final,
        grad_query,
        vectors[1, :6],
        grad_key,
        grad_value,
        vectors[1, 6:12],
        grad_out,
        ffn_vectors[5],
        ffn_vectors[3],
        ffn_vectors[4],
        grad_inner,
        vectors[0, 36:60],
        grad_outer,
        ffn_vectors[0],
        ffn_vectors[1],
        ffn_vectors[2],
    )


def solution(mesh):
    chips = Mesh(mesh.devices.reshape(RING, CORES, RING, RING), ("x", "core", "z", "y"))
    dp = ("x", "core")
    fsdp = ("z", "y")
    every = P(dp + fsdp)
    rows = P(dp + fsdp, None)
    whole_rows = P(fsdp, dp, None)
    return jax.shard_map(
        body,
        mesh=chips,
        in_specs=(
            whole_rows, whole_rows, P(), every, every,
            rows, every, rows, rows, every, rows, every, every, every,
            rows, every, rows, every, every, every,
        ),
        out_specs=(
            whole_rows, whole_rows,
            rows, every, rows, rows, every, rows, every, every, every,
            rows, every, rows, every, every, every,
        ),
        check_vma=False,
    )
```

```python
import functools
import jax
import jax.numpy as jnp
from jax import lax
from jax.experimental import pallas as pl
from jax.experimental.pallas import tpu as pltpu
from jax.sharding import Mesh
from jax.sharding import PartitionSpec as P

HEADS = 12
HEAD = 64
WIDTH = 768
FF = 3072
SLOT = 256
SEQ_DEV = 4
RING = 4
CORES = 2
PIECE = 32
GROUP = RING * CORES
ROWS = SEQ_DEV * SLOT
PAIR = 2 * HEAD
PACKED = 4 * WIDTH + 512

epsilon = 1e-05
bf16 = jnp.bfloat16
f32 = jnp.float32
VMEM_LIMIT = 58 * 1024 * 1024

TN = (((0,), (0,)), ((), ()))
NT = (((1,), (1,)), ((), ()))


def mm(a, b):
    return jnp.dot(a, b, preferred_element_type=f32)


def mm_nt(a, b):
    return lax.dot_general(a, b, NT, preferred_element_type=f32)


def mm_tn(a, b):
    return lax.dot_general(a, b, TN, preferred_element_type=f32)


def joined(ref):
    return ref[...].reshape(SLOT, WIDTH)


def spread(extras, start, width):
    total = 128 * width
    group = lax.broadcasted_iota(jnp.int32, (32, total), 0)
    owner = lax.broadcasted_iota(jnp.int32, (32, total), 1) // width
    pick = lax.broadcasted_iota(jnp.int32, (width, total), 0)
    within = lax.rem(lax.broadcasted_iota(jnp.int32, (width, total), 1), width)
    chosen = (pick == within).astype(bf16)
    out = jnp.zeros((32, total), f32)
    for y in range(RING):
        values = extras[:, 128 * y + start : 128 * y + start + width].astype(bf16)
        out += jnp.where(owner == group * RING + y, mm(values, chosen), 0.0)
    return jnp.sum(out, axis=0, keepdims=True)


def gather_back(vectors):
    values = jnp.zeros((128, 128), f32)
    start = 0
    for vector in vectors:
        total = vector.shape[1]
        width = total // 128
        owner = lax.broadcasted_iota(jnp.int32, (128, total), 1) // width
        mine = owner == lax.broadcasted_iota(jnp.int32, (128, total), 0)
        within = lax.rem(lax.broadcasted_iota(jnp.int32, (total, 128), 0), width)
        column = lax.broadcasted_iota(jnp.int32, (total, 128), 1)
        spots = (column == within + start).astype(bf16)
        values += mm(jnp.where(mine, vector, 0.0).astype(bf16), spots)
        start += width
    row = lax.broadcasted_iota(jnp.int32, (WIDTH, 128), 0)
    device = lax.broadcasted_iota(jnp.int32, (WIDTH, 128), 1)
    within = lax.rem(row, 24)
    picks = (within < RING) & (row // 24 * RING + within == device)
    return mm(picks.astype(bf16), values.astype(bf16)).astype(bf16)


def attention_copies(ids, pieces, w, sems):
    copies = []
    for i, piece in enumerate(pieces):
        x = lax.rem(ids[8] + RING - i // 2, RING)
        c = ids[9] if i % 2 == 0 else 1 - ids[9]
        copies.append(pltpu.make_async_copy(piece, w.at[x, c], sems.at[i]))
    return copies


def columns(w, start, end):
    return w[:, :, :, start:end].reshape(WIDTH, end - start)


def attention_forward(
    ids, x_in, p0, p1, p2, p3, p4, p5, p6, p7, perm,
    xt_out, qkv_out, exp_out, norm_out, ctxt_out, sum_out, vec, bias_out, info,
    w, extras, sems,
):
    s = pl.program_id(0)

    @pl.when(s == 0)
    def _():
        copies = attention_copies(ids, (p0, p1, p2, p3, p4, p5, p6, p7), w, sems)
        for copy in copies:
            copy.start()
        for copy in copies:
            copy.wait()
        rows = columns(w, 4 * WIDTH, PACKED).astype(f32).reshape(32, 24, PACKED - 4 * WIDTH)
        extras[...] = jnp.sum(rows, axis=1)
        for i in range(8):
            vec[i : i + 1] = spread(extras, 6 * i, 6)
        bias_out[...] = spread(extras, 48, 24)

    length = jnp.zeros((1, 1), f32)
    dropped = jnp.zeros((1, 1), f32)
    for y in range(RING):
        hit = perm[:, RING * y : RING * y + 4] == ids[10] + s
        length += jnp.sum(jnp.where(hit, extras[:, 128 * y + 72 : 128 * y + 76], 0.0), keepdims=True)
        dropped += jnp.sum(jnp.where(hit, extras[:, 128 * y + 76 : 128 * y + 80], 0.0), keepdims=True)
    line = lax.broadcasted_iota(jnp.int32, (8, 128), 0)
    info[...] = jnp.where(line == s, length, jnp.where(line == s + 4, dropped, info[...]))

    x = joined(x_in)
    xt_out[...] = x.T
    q = ((mm(x, columns(w, 0, WIDTH)) + vec[0:1]).astype(bf16).astype(f32) * HEAD**-0.5).astype(bf16)
    k = mm(x, columns(w, WIDTH, 2 * WIDTH)).astype(bf16)
    v = (mm(x, columns(w, 2 * WIDTH, 3 * WIDTH)) + vec[1:2]).astype(bf16)
    qkv_out[:, :WIDTH] = q
    qkv_out[:, WIDTH : 2 * WIDTH] = k
    qkv_out[:, 2 * WIDTH :] = v
    q_t = q.T
    v_t = v.T
    keys = lax.broadcasted_iota(jnp.int32, (SLOT, 1), 0).astype(f32)
    bias = jnp.where(keys < length, 0.0, -1e30)
    low = lax.broadcasted_iota(jnp.int32, (SLOT, PAIR), 1) < HEAD
    ctx_t = []
    for h in range(HEADS):
        p = h // 2 * PAIR
        k_pair = k[:, p : p + PAIR]
        k_one = jnp.where(low if h % 2 == 0 else ~low, k_pair, jnp.zeros_like(k_pair))
        scores = mm(k_one, q_t[p : p + PAIR]) + bias
        top = jnp.max(scores, axis=0, keepdims=True)
        expo = jnp.exp(scores - top)
        inverse = 1.0 / jnp.sum(expo, axis=0, keepdims=True)
        norm_out[0, h : h + 1, :] = inverse
        expo = expo.astype(bf16)
        exp_out[0, h] = expo
        ctx_t.append(mm(v_t[h * HEAD : (h + 1) * HEAD], expo) * inverse)
    ctx_t = jnp.concatenate(ctx_t, axis=0).astype(bf16)
    ctxt_out[...] = ctx_t
    sum_out[...] = x.astype(f32) + (mm(ctx_t.T, columns(w, 3 * WIDTH, 4 * WIDTH)) + vec[2:3])


def row_mean(v):
    return jnp.mean(v, axis=-1, keepdims=True)


def normalised(z):
    center = z - row_mean(z)
    r = lax.rsqrt(row_mean(center * center) + epsilon)
    return center * r, r


def norm_back(dy, zhat, r, gain):
    e = dy * gain
    return r * (e - row_mean(e) - zhat * row_mean(e * zhat))


def col_sum(v):
    return jnp.sum(v, axis=0, keepdims=True)


FF_STEP = 768


def feed_forward(
    ids, sum1, x_in, c_in, i0, i1, i2, i3, j0, j1, j2, j3, vec, bias_in,
    layer_out, hidt_out, actt_out, dbranch_out, dinner_out, dsum_out, dattn_out, vec_block,
    slope, vec_grad, bias_grad, w_in, w_out, in_sems, out_sems,
):
    s = pl.program_id(0)

    def copies():
        ins = []
        outs = []
        for i, (piece, late) in enumerate(zip((i0, i1, i2, i3), (j0, j1, j2, j3))):
            c = ids[9] if i % 2 == 0 else 1 - ids[9]
            z_half = ids[11] // 2 if i // 2 == 0 else 1 - ids[11] // 2
            y_half = ids[12] // 2 if i // 2 == 0 else 1 - ids[12] // 2
            for d in range(RING):
                x = lax.rem(ids[8] + RING - d, RING)
                ins.append(pltpu.make_async_copy(piece.at[d], w_in.at[x, c, z_half], in_sems.at[i, d]))
                for n in range(RING):
                    target = w_out.at[x, c, n, y_half]
                    outs.append(pltpu.make_async_copy(late.at[n, d], target, out_sems.at[i, d, n]))
        return ins, outs

    @pl.when(s == 0)
    def _():
        vec_grad[...] = jnp.zeros_like(vec_grad)
        bias_grad[...] = jnp.zeros_like(bias_grad)
        ins, outs = copies()
        for copy in ins + outs:
            copy.start()
        for copy in ins + outs:
            copy.wait()

    def inner_columns(start):
        return w_in[:, :, :, :, start : start + FF_STEP].reshape(WIDTH, FF_STEP)

    def outer_rows(start):
        x = start // (FF // RING)
        return w_out[x].reshape(FF // RING, WIDTH)

    zhat1, r1 = normalised(sum1[...])
    hidden = zhat1 * vec[3:4] + vec[4:5]
    hid_low = hidden.astype(bf16)
    hidt_out[...] = hid_low.T
    branch = jnp.broadcast_to(vec[5:6], (SLOT, WIDTH))
    for n in range(0, FF, FF_STEP):
        cols = slice(n, n + FF_STEP)
        inner = mm(hid_low, inner_columns(n)) + bias_in[0:1, cols]
        half = 0.5 * lax.erf(inner * 0.7071067811865476) + 0.5
        bell = 0.3989422804014327 * jnp.exp(-0.5 * (inner * inner))
        act = (inner * half).astype(bf16)
        actt_out[cols, :] = act.T
        slope[:, cols] = (half + inner * bell).astype(bf16)
        branch += mm(act, outer_rows(n))
    zhat2, r2 = normalised(hidden + branch)
    gain2 = vec[6:7]
    normed = zhat2 * gain2 + vec[7:8]
    valid = (lax.broadcasted_iota(jnp.int32, (SLOT, 1), 0) < ids[s]).astype(f32)
    keep = ids[4 + s] == 0
    x = joined(x_in).astype(f32)
    layer_out[...] = (jnp.where(keep, normed, x) * valid).astype(bf16)
    upstream = joined(c_in).astype(f32)
    dy = upstream * jnp.where(keep, valid, 0.0)
    vec_grad[1:2] += col_sum(dy * zhat2)
    vec_grad[2:3] += col_sum(dy)
    d_sum2 = norm_back(dy, zhat2, r2, gain2)
    d_branch = d_sum2.astype(bf16)
    dbranch_out[...] = d_branch
    vec_grad[0:1] += col_sum(d_branch.astype(f32))
    d_hidden = d_sum2
    for n in range(0, FF, FF_STEP):
        cols = slice(n, n + FF_STEP)
        d_act = mm_nt(d_branch, outer_rows(n))
        d_inner = (d_act * slope[:, cols].astype(f32)).astype(bf16)
        dinner_out[:, cols] = d_inner
        bias_grad[0:1, cols] += col_sum(d_inner.astype(f32))
        d_hidden += mm_nt(d_inner, inner_columns(n))
    vec_grad[3:4] += col_sum(d_hidden * zhat1)
    vec_grad[4:5] += col_sum(d_hidden)
    d_sum1 = norm_back(d_hidden, zhat1, r1, vec[3:4])
    dsum_out[...] = d_sum1
    d_attn = d_sum1.astype(bf16)
    dattn_out[...] = d_attn
    vec_grad[5:6] += col_sum(d_attn.astype(f32))

    @pl.when(s == SEQ_DEV - 1)
    def _():
        vec_block[...] = gather_back([vec_grad[i : i + 1] for i in range(6)] + [bias_grad[...]])


def attention_backward(
    ids, dsum, dattn, qkv, exp_in, norm_in, ctxt_in, c_in, layer_in, p0, p1, p2, p3, p4, p5, p6, p7,
    back_out, dqkv_out, vec_block,
    w, vec_grad, sems,
):
    s = pl.program_id(0)

    @pl.when(s == 0)
    def _():
        vec_grad[...] = jnp.zeros_like(vec_grad)
        copies = attention_copies(ids, (p0, p1, p2, p3, p4, p5, p6, p7), w, sems)
        for copy in copies:
            copy.start()
        for copy in copies:
            copy.wait()

    d_sum1 = dsum[...]
    dctx_t = mm_nt(dattn[...], columns(w, 3 * WIDTH, 4 * WIDTH)).T
    ctx_t = ctxt_in[...].astype(f32)
    k_t = qkv[:, WIDTH : 2 * WIDTH].T
    scaled = []
    deltas = []
    for h in range(HEADS):
        rows = slice(h * HEAD, (h + 1) * HEAD)
        one = (dctx_t[rows] * norm_in[0, h : h + 1, :]).astype(bf16)
        scaled.append(one)
        deltas.append(col_sum(one.astype(f32) * ctx_t[rows]))
    dctx_t = jnp.concatenate(scaled, axis=0)
    dctx = dctx_t.T
    low = lax.broadcasted_iota(jnp.int32, (SLOT, PAIR), 1) < HEAD
    dq_t = []
    for p in range(0, WIDTH, PAIR):
        cols = slice(p, p + PAIR)
        q_pair = qkv[:, cols]
        v_pair = qkv[:, 2 * WIDTH + p : 2 * WIDTH + p + PAIR]
        dks = []
        dvs = []
        for half in range(2):
            h = p // HEAD + half
            v_one = jnp.where(low if half == 0 else ~low, v_pair, jnp.zeros_like(v_pair))
            d_probs = mm(v_one, dctx_t[cols]) - deltas[h]
            expo = exp_in[0, h]
            d_scores = (expo.astype(f32) * d_probs).astype(bf16)
            dvs.append(mm(expo, dctx[:, cols]))
            dks.append(mm(d_scores, q_pair))
            dq_t.append(mm(k_t[h * HEAD : (h + 1) * HEAD], d_scores))
        dqkv_out[:, WIDTH + p : WIDTH + p + PAIR] = jnp.where(low, dks[0], dks[1]).astype(bf16)
        dqkv_out[:, 2 * WIDTH + p : 2 * WIDTH + p + PAIR] = jnp.where(low, dvs[0], dvs[1]).astype(bf16)
    dq = (jnp.concatenate(dq_t, axis=0).T * HEAD**-0.5).astype(bf16)
    dqkv_out[:, :WIDTH] = dq
    vec_grad[0:1] += col_sum(dq.astype(f32))
    vec_grad[1:2] += col_sum(dqkv_out[:, 2 * WIDTH :].astype(f32))
    d_in = d_sum1 + mm_nt(dqkv_out[...], columns(w, 0, 3 * WIDTH))
    valid = (lax.broadcasted_iota(jnp.int32, (SLOT, 1), 0) < ids[s]).astype(f32)
    upstream = joined(c_in).astype(f32) * valid
    keep = ids[4 + s] == 0
    grad = jnp.where(keep, d_in, upstream).astype(bf16)
    back_out[:, 0, 0] = layer_in[...].reshape(GROUP, PIECE, WIDTH)
    back_out[:, 1, 0] = grad.reshape(GROUP, PIECE, WIDTH)

    @pl.when(s == SEQ_DEV - 1)
    def _():
        vec_block[...] = gather_back([vec_grad[0:1], vec_grad[1:2]])


def weight_grad(ids, left, right, *refs):
    *tail, away, mine = refs
    value = mm(left[...], right[...]).astype(bf16)
    if tail:
        value = jnp.concatenate([value, tail[0][...]], axis=1)
    blocks, rows, _ = away.shape
    first = ids[9] == 0
    for x in range(blocks):
        even = value[2 * x * rows : (2 * x + 1) * rows]
        odd = value[(2 * x + 1) * rows : (2 * x + 2) * rows]
        away[x] = jnp.where(first, odd, even)
        mine[x] = jnp.where(first, even, odd)


def in_order(values, me):
    ordered = []
    for j in range(RING):
        step = lax.rem(me + RING - j, RING)
        value = values[0]
        for d in (1, 2, 3):
            value = jnp.where(step == d, values[d], value)
        ordered.append(value)
    return ordered


def merge_rows(ids, own, r1, r2, r3, attn_out, inner_out):
    ordered = in_order([v[...].astype(f32) for v in (own, r1, r2, r3)], ids[12])
    width = 4 * WIDTH
    rows = jnp.concatenate([v[:6] for v in ordered], axis=0).astype(bf16)
    attn_out[:, :width] = rows[:, :width]
    inner_out[...] = rows[:, width:]
    row = jnp.concatenate([v[6:7, :128] for v in ordered], axis=1)
    first = lax.broadcasted_iota(jnp.int32, (24, 4 * 128), 0) == 0
    attn_out[:, width:] = jnp.where(first, jnp.broadcast_to(row, (24, 4 * 128)), 0.0).astype(bf16)


def stack_rows(ids, own, r1, r2, r3, out):
    for d, piece in enumerate((own, r1, r2, r3)):
        out[lax.rem(ids[11] + RING - d, RING)] = piece[...]


def ahead(ids, axis, step):
    return lax.rem(ids[axis] + step, RING)


def sum_of(refs):
    total = refs[0][...].astype(f32)
    for ref in refs[1:]:
        total += ref[...].astype(f32)
    return total


def sum_blocks(ids, *refs):
    *parts, o0, o1, o2, o3, scratch = refs
    start = 0
    for mine, core in zip(parts[::2], parts[1::2]):
        end = start + mine.shape[2]
        scratch[:, start:end] = mine[0].astype(f32) + core[0].astype(f32)
        start = end
    for d, out in enumerate((o0, o1, o2, o3)):
        first = pl.multiple_of(ahead(ids, 11, d) * 24, 8)
        out[0] = scratch[pl.ds(first, 24), :].astype(bf16)


def sum_outer(ids, mine, core, out):
    total = mine[0].astype(f32) + core[0].astype(f32)
    for z in range(RING):
        for y in range(RING):
            first = 96 * z + 24 * y
            out[y, 0, z] = total[first : first + 24].astype(bf16)


def sum_first(ids, value, out):
    for z in range(RING):
        out[z, 0] = sum_of([value.at[y, 0, z] for y in range(RING)]).astype(bf16)


def split_rows(ids, p0, p1, p2, p3, o0, o1, o2, o3, scratch):
    width = o0.shape[2]
    total = sum_of([p.at[0] for p in (p0, p1, p2, p3)])
    for y in range(RING):
        row = jnp.concatenate([total[y : y + 1, width:], jnp.zeros((1, width - 128), f32)], axis=1)
        rows = total[6 * y : 6 * y + 6, :width]
        scratch[y] = jnp.concatenate([rows, row, jnp.zeros((1, width), f32)], axis=0)
    for d, out in enumerate((o0, o1, o2, o3)):
        out[0] = scratch[ahead(ids, 12, d)].astype(bf16)


LAST = FF + WIDTH + 3 * WIDTH + 3 * WIDTH


def join_flows(ids, i0, i1, i2, i3, a0, a1, a2, a3, outer, o0, o1, o2, o3, scratch):
    scratch[:, :, : FF + WIDTH] = sum_of((i0, i1, i2, i3))
    scratch[:, :, FF + WIDTH : FF + 4 * WIDTH] = sum_of((a0, a1, a2, a3))
    for x in range(RING):
        total = sum_of([outer.at[z, x] for z in range(RING)])
        for k in range(3):
            start = FF + (4 + k) * WIDTH
            scratch[x, :, start : start + WIDTH] = total[8 * k : 8 * k + 8]
    for d, out in enumerate((o0, o1, o2, o3)):
        out[...] = scratch[ahead(ids, 8, d)].astype(bf16)


def split_ffn(ids, p0, p1, p2, p3, inner, outer):
    for d, piece in enumerate((p0, p1, p2, p3)):
        inner[d] = piece[:, :FF]
        halves = [piece[:, FF + i * WIDTH : FF + (i + 1) * WIDTH].astype(f32) for i in range(2)]
        outer[d] = jnp.concatenate(halves, axis=0).astype(bf16)


def write_grads(ids, p0, p1, p2, p3, query, key, value, out, inner, outer, vectors):
    total = sum_of((p0, p1, p2, p3))
    inner[...] = total[:6, :FF]
    out[...] = total[:6, FF : FF + WIDTH]
    start = FF + WIDTH
    query[...] = total[:6, start : start + WIDTH]
    key[...] = total[:6, start + WIDTH : start + 2 * WIDTH]
    value[...] = total[:6, start + 2 * WIDTH : start + 3 * WIDTH]
    vectors[...] = jnp.concatenate([total[6:7, :128], total[6:7, start : start + 128]], axis=0)
    start += 3 * WIDTH
    for k in range(3):
        outer[8 * k : 8 * k + 8] = total[:, start + k * WIDTH : start + (k + 1) * WIDTH]


def whole(shape):
    return pl.BlockSpec(shape, lambda s, ids: (0,) * len(shape), pipeline_mode=pl.Buffered(1))


DEALT_SPEC = pl.BlockSpec((GROUP, 1, PIECE, WIDTH), lambda s, ids: (0, s, 0, 0))


def by_rows(width):
    return pl.BlockSpec((SLOT, width), lambda s, ids: (s, 0))


def rows_of(width, kind):
    return jax.ShapeDtypeStruct((ROWS, width), kind)


EXP_SPEC = pl.BlockSpec((1, HEADS, SLOT, SLOT), lambda s, ids: (s, 0, 0, 0))
NORM_SPEC = pl.BlockSpec((1, 16, SLOT), lambda s, ids: (s, 0, 0))
RETURN_SPEC = pl.BlockSpec((GROUP, 2, 1, PIECE, WIDTH), lambda s, ids: (0, 0, s, 0, 0))
RETURN_SHAPE = jax.ShapeDtypeStruct((GROUP, 2, SEQ_DEV, PIECE, WIDTH), bf16)


def by_columns(height):
    return pl.BlockSpec((height, SLOT), lambda s, ids: (0, s))


def columns_of(height):
    return jax.ShapeDtypeStruct((height, ROWS), bf16)


def run(kernel, grid, ins, outs, operands, name, flops, moved, scratch=()):
    return pl.pallas_call(
        kernel,
        grid_spec=pltpu.PrefetchScalarGridSpec(
            num_scalar_prefetch=1,
            grid=grid,
            in_specs=ins,
            out_specs=[spec for spec, _ in outs],
            scratch_shapes=list(scratch),
        ),
        out_shape=[shape for _, shape in outs],
        compiler_params=pltpu.CompilerParams(
            vmem_limit_bytes=VMEM_LIMIT, dimension_semantics=("arbitrary",) * len(grid)
        ),
        cost_estimate=pl.CostEstimate(flops=flops, bytes_accessed=moved, transcendentals=0),
        name=name,
    )(*operands)


def out_rows(width, kind):
    return (by_rows(width), rows_of(width, kind))


def out_columns(height):
    return (by_columns(height), columns_of(height))


def out_whole(shape):
    return (whole(shape), jax.ShapeDtypeStruct(shape, f32))


ANYWHERE = pl.BlockSpec(memory_space=pl.ANY)
ATTENTION_SCRATCH = [pltpu.VMEM((RING, CORES, 96, PACKED), bf16)]


def call_forward(ids, dealt, weights, perm):
    return run(
        attention_forward,
        (SEQ_DEV,),
        [DEALT_SPEC] + [ANYWHERE] * 8 + [whole((32, 16))],
        [
            out_columns(WIDTH),
            out_rows(3 * WIDTH, bf16),
            (EXP_SPEC, jax.ShapeDtypeStruct((SEQ_DEV, HEADS, SLOT, SLOT), bf16)),
            (NORM_SPEC, jax.ShapeDtypeStruct((SEQ_DEV, 16, SLOT), f32)),
            out_columns(WIDTH),
            out_rows(WIDTH, f32),
            out_whole((8, WIDTH)),
            out_whole((1, FF)),
            out_whole((8, 128)),
        ],
        (ids, dealt, *weights, perm),
        "attention_forward",
        22 * 10**9,
        22 * 10**6,
        ATTENTION_SCRATCH + [pltpu.VMEM((32, PACKED - 4 * WIDTH), f32), pltpu.SemaphoreType.DMA((8,))],
    )


def call_ffn(ids, sum1, dealt, dealt_c, inner, outer, vec, bias_in):
    return run(
        feed_forward,
        (SEQ_DEV,),
        [by_rows(WIDTH)] + [DEALT_SPEC] * 2 + [ANYWHERE] * 8 + [whole((8, WIDTH)), whole((1, FF))],
        [
            out_rows(WIDTH, bf16),
            out_columns(WIDTH),
            out_columns(FF),
            out_rows(WIDTH, bf16),
            out_rows(FF, bf16),
            out_rows(WIDTH, f32),
            out_rows(WIDTH, bf16),
            (whole((WIDTH, 128)), jax.ShapeDtypeStruct((WIDTH, 128), bf16)),
        ],
        (ids, sum1, dealt, dealt_c, *inner, *outer, vec, bias_in),
        "feed_forward",
        36 * 10**9,
        40 * 10**6,
        [
            pltpu.VMEM((SLOT, FF), bf16),
            pltpu.VMEM((8, WIDTH), f32),
            pltpu.VMEM((1, FF), f32),
            pltpu.VMEM((RING, CORES, 2, 48, FF), bf16),
            pltpu.VMEM((RING, CORES, RING, 2, 48, WIDTH), bf16),
            pltpu.SemaphoreType.DMA((RING, RING)),
            pltpu.SemaphoreType.DMA((RING, RING, RING)),
        ],
    )


def call_backward(ids, dsum, dattn, qkv, expo, norm, ctx_t, dealt_c, layer, weights):
    return run(
        attention_backward,
        (SEQ_DEV,),
        [by_rows(WIDTH), by_rows(WIDTH), by_rows(3 * WIDTH), EXP_SPEC, NORM_SPEC, by_columns(WIDTH)]
        + [DEALT_SPEC, by_rows(WIDTH)]
        + [ANYWHERE] * 8,
        [
            (RETURN_SPEC, RETURN_SHAPE),
            out_rows(3 * WIDTH, bf16),
            (whole((WIDTH, 128)), jax.ShapeDtypeStruct((WIDTH, 128), bf16)),
        ],
        (ids, dsum, dattn, qkv, expo, norm, ctx_t, dealt_c, layer, *weights),
        "attention_backward",
        24 * 10**9,
        30 * 10**6,
        ATTENTION_SCRATCH + [pltpu.VMEM((8, WIDTH), f32), pltpu.SemaphoreType.DMA((8,))],
    )


def call_grad(ids, left, right, blocks, step, tail=None):
    rows = left.shape[0] // (RING * CORES)
    width = right.shape[1]
    ins = [
        pl.BlockSpec((2 * blocks * rows, ROWS), lambda i, n, ids: (i, 0)),
        pl.BlockSpec((ROWS, step), lambda i, n, ids: (0, n)),
    ]
    operands = (ids, left, right)
    more = 0
    if tail is not None:
        more = tail.shape[1]
        ins.append(pl.BlockSpec((WIDTH, more), lambda i, n, ids: (0, 0)))
        operands += (tail,)
    out = (
        pl.BlockSpec((blocks, rows, step + more), lambda i, n, ids: (i, 0, n)),
        jax.ShapeDtypeStruct((RING, rows, width + more), bf16),
    )
    return run(
        weight_grad,
        (RING // blocks, width // step),
        ins,
        [out, out],
        operands,
        "weight_grad",
        3 * RING * CORES * rows * ROWS * width,
        2 * (RING * rows * ROWS + ROWS * width + RING * rows * width),
    )


def call_by_x(kernel, name, ids, pieces, at, out_shape, out_at, count, scratch=()):
    def one(shape, where):
        block = tuple(1 if i == where else n for i, n in enumerate(shape))
        return pl.BlockSpec(block, lambda x, ids: tuple(x if i == where else 0 for i in range(len(shape))))

    return run(
        kernel,
        (RING,),
        [one(piece.shape, at) for piece in pieces],
        [(one(out_shape, out_at), jax.ShapeDtypeStruct(out_shape, bf16))] * count,
        (ids, *pieces),
        name,
        10**6,
        8 * 10**6,
        [pltpu.VMEM(shape, f32) for shape in scratch],
    )


def call_small(kernel, name, ids, pieces, *out_shapes, kind=bf16, scratch=()):
    def full(shape):
        return pl.BlockSpec(shape, lambda i, ids: (0,) * len(shape))

    return run(
        kernel,
        (1,),
        [full(piece.shape) for piece in pieces],
        [(full(shape), jax.ShapeDtypeStruct(shape, kind)) for shape in out_shapes],
        (ids, *pieces),
        name,
        10**6,
        6 * 10**6,
        [pltpu.VMEM(shape, f32) for shape in scratch],
    )


def shift(value, axis, step):
    size = CORES if axis == "core" else RING
    return lax.ppermute(value, axis, [(i, (i + step) % size) for i in range(size)])


def swap(value, axis):
    return lax.ppermute(value, axis, [(i, i ^ 1) for i in range(RING)])


def arrivals(value, axis):
    return [value] + [shift(value, axis, step) for step in (1, 2, 3)]


def both_cores(pieces):
    return [part for piece in pieces for part in (piece, shift(piece, "core", 1))]


def paired(value, axis):
    return in_half(value, swap(value, axis), axis)


def in_half(value, other, axis):
    even = lax.rem(lax.axis_index(axis), 2) == 0
    return jnp.where(even, value, other), jnp.where(even, other, value)


def hold(value, *others):
    return lax.optimization_barrier((value, *others))[0]


def send_ring(parts, axis):
    return [parts[0]] + [shift(parts[step], axis, step) for step in (1, 2, 3)]


def over(value, axis):
    return lax.all_to_all(value, axis, split_axis=0, concat_axis=0, tiled=True)


def body(
    tokens,
    cotangent,
    perm,
    lengths,
    drop,
    w_query,
    b_query,
    w_key,
    w_value,
    b_value,
    w_out,
    b_out,
    norm1_gain,
    norm1_bias,
    w_inner,
    b_inner,
    w_outer,
    b_outer,
    norm2_gain,
    norm2_bias,
):
    me_x = lax.axis_index("x")
    me_c = lax.axis_index("core")
    me_z = lax.axis_index("z")
    me_y = lax.axis_index("y")
    first = ((me_z * RING + me_y) * 8 + me_x * CORES + me_c) * SEQ_DEV
    places = jnp.stack([me_x, me_c, first, me_z, me_y]).astype(jnp.int32)
    places = jnp.pad(places, (8, 3))

    vectors = [b_query, b_value, b_out, norm1_gain, norm1_bias, b_outer, norm2_gain, norm2_bias, b_inner]
    vectors += [lengths.astype(bf16), drop.astype(bf16)]
    row = jnp.zeros((4 * WIDTH,), bf16)
    start = 0
    for vector in vectors:
        end = start + vector.shape[0]
        row += jnp.pad(vector, (start, 4 * WIDTH - end))
        start = end
    piece = jnp.concatenate([w_query, w_key, w_value, w_out, w_inner], axis=1)
    row = jnp.pad(row, (0, FF))
    piece = jnp.concatenate([piece, row[None], jnp.zeros((1, 4 * WIDTH + FF), bf16)])
    pieces_y = arrivals(piece, "y")
    dp = ("x", "core")
    dealt = (GROUP, SEQ_DEV, PIECE, WIDTH)
    dealt_x = over(hold(tokens, piece).reshape(dealt), dp)
    attn_y, inner_y = call_small(merge_rows, "merge_rows", places, pieces_y, (24, PACKED), (24, FF))
    (attn_zy,) = call_small(
        stack_rows, "stack_rows", places, arrivals(attn_y, "z"), (RING, 24, PACKED)
    )

    outer_pair = paired(w_outer, "y")
    ffn_x = arrivals(jnp.concatenate([hold(inner_y, dealt_x), *outer_pair], axis=1), "x")
    inner_x, outer_x = call_small(
        split_ffn, "split_ffn", places, ffn_x, (RING, 24, FF), (RING, 48, WIDTH)
    )
    attn_x = arrivals(hold(attn_zy, dealt_x).reshape(96, PACKED), "x")
    attn_pieces = both_cores(attn_x)
    inner_z = swap(inner_x, "z")
    outer_z = over(jnp.broadcast_to(outer_x[None], (RING, RING, 48, WIDTH)), "z")
    inner_z = jnp.concatenate(in_half(inner_x, hold(inner_z, attn_x[1]), "z"), axis=1)
    inner_far = shift(inner_z, "z", 2)
    outer_z = hold(outer_z, attn_x[1])
    outer_far = shift(outer_z, "y", 2)
    dealt_c = over(hold(cotangent, attn_x[1]).reshape(dealt), dp)

    x_t, qkv, expo, norm, ctx_t, sum1, vec, inner_bias, info = call_forward(
        places, dealt_x, attn_pieces, perm.reshape(32, 16)
    )
    ids = jnp.concatenate([info[:, 0].astype(jnp.int32), places[8:]])

    inner_pieces = both_cores([hold(inner_z, sum1), hold(inner_far, sum1)])
    outer_pieces = both_cores([hold(outer_z, sum1), hold(outer_far, sum1)])
    layer, hid_t, act_t, d_branch, d_inner, d_sum1, d_attn, vec_block = call_ffn(
        ids, sum1, dealt_x, dealt_c, inner_pieces, outer_pieces, vec, inner_bias
    )

    outer_away, outer_mine = call_grad(ids, act_t, d_branch, 1, WIDTH)
    outer_core = shift(outer_away, "core", 1)
    inner_away, inner_mine = call_grad(hold(ids, outer_away), hid_t, d_inner, RING, WIDTH)
    inner_core = shift(inner_away, "core", 1)
    out_away, out_mine = call_grad(
        hold(ids, inner_away), ctx_t, d_attn, RING, WIDTH, vec_block
    )
    out_core = shift(out_away, "core", 1)
    inner_width = FF + WIDTH + 128
    inner_parts = call_by_x(
        sum_blocks, "sum_blocks", places, (inner_mine, inner_core, out_mine, out_core), 0,
        (RING, 24, inner_width), 0, RING, [(96, inner_width)],
    )
    (outer_sum,) = call_by_x(
        sum_outer, "sum_outer", hold(places, inner_parts[0]), (outer_mine, hold(outer_core, out_away)), 0,
        (RING, RING, RING, 24, WIDTH), 1, 1,
    )
    inner_parts = send_ring(inner_parts, "z")
    outer_y = over(outer_sum, "y")

    d_sum1, d_attn = lax.optimization_barrier((d_sum1, d_attn, inner_parts[0], outer_sum))[:2]
    back, d_qkv, qkv_block = call_backward(
        ids, d_sum1, d_attn, qkv, expo, norm, ctx_t, dealt_c, layer, attn_pieces
    )

    attn_away, attn_mine = call_grad(hold(ids, *inner_parts[1:]), x_t, d_qkv, RING, 3 * WIDTH, qkv_block)
    attn_core = shift(attn_away, "core", 1)
    (outer_z,) = call_by_x(
        sum_first, "sum_first", hold(places, attn_away), (hold(outer_y, attn_away),), 1,
        (RING, RING, 24, WIDTH), 1, 1,
    )
    attn_width = 3 * WIDTH + 128
    attn_parts = call_by_x(
        sum_blocks, "sum_blocks", hold(places, outer_z), (attn_mine, attn_core), 0,
        (RING, 24, attn_width), 0, RING, [(96, attn_width)],
    )
    outer_z = over(outer_z, "z")
    attn_first = attn_parts[0]
    attn_parts = send_ring(attn_parts, "z")
    back = over(hold(back, outer_z, attn_first), dp)

    inner_parts = [hold(inner_parts[0], attn_first)] + [hold(p, attn_away) for p in inner_parts[1:]]
    inner_parts = call_by_x(
        split_rows, "split_rows", places, inner_parts, 0, (RING, 8, FF + WIDTH), 0, RING, [(RING, 8, FF + WIDTH)]
    )
    attn_parts = call_by_x(
        split_rows, "split_rows", hold(places, inner_parts[0]), attn_parts, 0,
        (RING, 8, 3 * WIDTH), 0, RING, [(RING, 8, 3 * WIDTH)],
    )
    inner_parts = send_ring(inner_parts, "y")
    attn_parts = send_ring(attn_parts, "y")
    last = call_small(
        join_flows, "join_flows", places, [*inner_parts, *attn_parts, outer_z], *[(8, LAST)] * 4,
        scratch=[(RING, 8, LAST)],
    )
    square = (6, WIDTH)
    grad_query, grad_key, grad_value, grad_out, grad_inner, grad_outer, vectors = call_small(
        write_grads, "write_grads", places, send_ring(last, "x"),
        square, square, square, square, (6, FF), (24, WIDTH), (2, 128), kind=f32,
    )
    back = hold(back, last[0])
    layer_final = back[:, 0].reshape(GROUP * SEQ_DEV, PIECE, WIDTH)
    grad_final = back[:, 1].reshape(GROUP * SEQ_DEV, PIECE, WIDTH)
    ffn_vectors = [vectors[0, 6 * i : 6 * i + 6] for i in range(6)]
    return (
        layer_final,
        grad_final,
        grad_query,
        vectors[1, :6],
        grad_key,
        grad_value,
        vectors[1, 6:12],
        grad_out,
        ffn_vectors[5],
        ffn_vectors[3],
        ffn_vectors[4],
        grad_inner,
        vectors[0, 36:60],
        grad_outer,
        ffn_vectors[0],
        ffn_vectors[1],
        ffn_vectors[2],
    )


def solution(mesh):
    chips = Mesh(mesh.devices.reshape(RING, CORES, RING, RING), ("x", "core", "z", "y"))
    dp = ("x", "core")
    fsdp = ("z", "y")
    every = P(dp + fsdp)
    rows = P(dp + fsdp, None)
    whole_rows = P(fsdp, dp, None)
    return jax.shard_map(
        body,
        mesh=chips,
        in_specs=(
            whole_rows, whole_rows, P(), every, every,
            rows, every, rows, rows, every, rows, every, every, every,
            rows, every, rows, every, every, every,
        ),
        out_specs=(
            whole_rows, whole_rows,
            rows, every, rows, rows, every, rows, every, every, every,
            rows, every, rows, every, every, every,
        ),
        check_vma=False,
    )
```

```python
import functools
import jax
import jax.numpy as jnp
from jax import lax
from jax.experimental import pallas as pl
from jax.experimental.pallas import tpu as pltpu
from jax.sharding import Mesh
from jax.sharding import PartitionSpec as P

HEADS = 12
HEAD = 64
WIDTH = 768
FF = 3072
SLOT = 256
SEQ_DEV = 4
RING = 4
CORES = 2
PIECE = 32
GROUP = RING * CORES
ROWS = SEQ_DEV * SLOT
PAIR = 2 * HEAD
PACKED = 4 * WIDTH + 512

epsilon = 1e-05
bf16 = jnp.bfloat16
f32 = jnp.float32
VMEM_LIMIT = 58 * 1024 * 1024

TN = (((0,), (0,)), ((), ()))
NT = (((1,), (1,)), ((), ()))


def mm(a, b):
    return jnp.dot(a, b, preferred_element_type=f32)


def mm_nt(a, b):
    return lax.dot_general(a, b, NT, preferred_element_type=f32)


def mm_tn(a, b):
    return lax.dot_general(a, b, TN, preferred_element_type=f32)


def joined(ref):
    return ref[...].reshape(SLOT, WIDTH)


def spread(extras, start, width):
    total = 128 * width
    group = lax.broadcasted_iota(jnp.int32, (32, total), 0)
    owner = lax.broadcasted_iota(jnp.int32, (32, total), 1) // width
    pick = lax.broadcasted_iota(jnp.int32, (width, total), 0)
    within = lax.rem(lax.broadcasted_iota(jnp.int32, (width, total), 1), width)
    chosen = (pick == within).astype(bf16)
    out = jnp.zeros((32, total), f32)
    for y in range(RING):
        values = extras[:, 128 * y + start : 128 * y + start + width].astype(bf16)
        out += jnp.where(owner == group * RING + y, mm(values, chosen), 0.0)
    return jnp.sum(out, axis=0, keepdims=True)


def gather_back(vectors):
    values = jnp.zeros((128, 128), f32)
    start = 0
    for vector in vectors:
        total = vector.shape[1]
        width = total // 128
        owner = lax.broadcasted_iota(jnp.int32, (128, total), 1) // width
        mine = owner == lax.broadcasted_iota(jnp.int32, (128, total), 0)
        within = lax.rem(lax.broadcasted_iota(jnp.int32, (total, 128), 0), width)
        column = lax.broadcasted_iota(jnp.int32, (total, 128), 1)
        spots = (column == within + start).astype(bf16)
        values += mm(jnp.where(mine, vector, 0.0).astype(bf16), spots)
        start += width
    row = lax.broadcasted_iota(jnp.int32, (WIDTH, 128), 0)
    device = lax.broadcasted_iota(jnp.int32, (WIDTH, 128), 1)
    within = lax.rem(row, 24)
    picks = (within < RING) & (row // 24 * RING + within == device)
    return mm(picks.astype(bf16), values.astype(bf16)).astype(bf16)


def attention_copies(ids, pieces, w, sems):
    copies = []
    for i, piece in enumerate(pieces):
        x = lax.rem(ids[8] + RING - i // 2, RING)
        c = ids[9] if i % 2 == 0 else 1 - ids[9]
        copies.append(pltpu.make_async_copy(piece, w.at[x, c], sems.at[i]))
    return copies


def columns(w, start, end):
    return w[:, :, :, start:end].reshape(WIDTH, end - start)


def attention_forward(
    ids, x_in, p0, p1, p2, p3, p4, p5, p6, p7, perm,
    xt_out, qkv_out, exp_out, norm_out, ctxt_out, sum_out, vec, bias_out, info,
    w, extras, sems,
):
    s = pl.program_id(0)

    @pl.when(s == 0)
    def _():
        copies = attention_copies(ids, (p0, p1, p2, p3, p4, p5, p6, p7), w, sems)
        for copy in copies:
            copy.start()
        for copy in copies:
            copy.wait()
        rows = columns(w, 4 * WIDTH, PACKED).astype(f32).reshape(32, 24, PACKED - 4 * WIDTH)
        extras[...] = jnp.sum(rows, axis=1)
        for i in range(8):
            vec[i : i + 1] = spread(extras, 6 * i, 6)
        bias_out[...] = spread(extras, 48, 24)

    length = jnp.zeros((1, 1), f32)
    dropped = jnp.zeros((1, 1), f32)
    for y in range(RING):
        hit = perm[:, RING * y : RING * y + 4] == ids[10] + s
        length += jnp.sum(jnp.where(hit, extras[:, 128 * y + 72 : 128 * y + 76], 0.0), keepdims=True)
        dropped += jnp.sum(jnp.where(hit, extras[:, 128 * y + 76 : 128 * y + 80], 0.0), keepdims=True)
    line = lax.broadcasted_iota(jnp.int32, (8, 128), 0)
    info[...] = jnp.where(line == s, length, jnp.where(line == s + 4, dropped, info[...]))

    x = joined(x_in)
    xt_out[...] = x.T
    q = ((mm(x, columns(w, 0, WIDTH)) + vec[0:1]).astype(bf16).astype(f32) * HEAD**-0.5).astype(bf16)
    k = mm(x, columns(w, WIDTH, 2 * WIDTH)).astype(bf16)
    v = (mm(x, columns(w, 2 * WIDTH, 3 * WIDTH)) + vec[1:2]).astype(bf16)
    qkv_out[:, :WIDTH] = q
    qkv_out[:, WIDTH : 2 * WIDTH] = k
    qkv_out[:, 2 * WIDTH :] = v
    q_t = q.T
    v_t = v.T
    keys = lax.broadcasted_iota(jnp.int32, (SLOT, 1), 0).astype(f32)
    bias = jnp.where(keys < length, 0.0, -1e30)
    low = lax.broadcasted_iota(jnp.int32, (SLOT, PAIR), 1) < HEAD
    ctx_t = []
    for h in range(HEADS):
        p = h // 2 * PAIR
        k_pair = k[:, p : p + PAIR]
        k_one = jnp.where(low if h % 2 == 0 else ~low, k_pair, jnp.zeros_like(k_pair))
        scores = mm(k_one, q_t[p : p + PAIR]) + bias
        top = jnp.max(scores, axis=0, keepdims=True)
        expo = jnp.exp(scores - top)
        inverse = 1.0 / jnp.sum(expo, axis=0, keepdims=True)
        norm_out[0, h : h + 1, :] = inverse
        expo = expo.astype(bf16)
        exp_out[0, h] = expo
        ctx_t.append(mm(v_t[h * HEAD : (h + 1) * HEAD], expo) * inverse)
    ctx_t = jnp.concatenate(ctx_t, axis=0).astype(bf16)
    ctxt_out[...] = ctx_t
    sum_out[...] = x.astype(f32) + (mm(ctx_t.T, columns(w, 3 * WIDTH, 4 * WIDTH)) + vec[2:3])


def row_mean(v):
    return jnp.mean(v, axis=-1, keepdims=True)


def normalised(z):
    center = z - row_mean(z)
    r = lax.rsqrt(row_mean(center * center) + epsilon)
    return center * r, r


def norm_back(dy, zhat, r, gain):
    e = dy * gain
    return r * (e - row_mean(e) - zhat * row_mean(e * zhat))


def col_sum(v):
    return jnp.sum(v, axis=0, keepdims=True)


FF_STEP = 768
FF_STEPS = FF // FF_STEP


def cut_cores(ids, value, away, mine):
    blocks, rows, _ = away.shape
    first = ids[9] == 0
    for x in range(blocks):
        even = value[2 * x * rows : (2 * x + 1) * rows]
        odd = value[(2 * x + 1) * rows : (2 * x + 2) * rows]
        away[x] = jnp.where(first, odd, even)
        mine[x] = jnp.where(first, even, odd)


def feed_forward(
    ids, sum1, x_in, c_in, ctx_t, i0, i1, i2, i3, j0, j1, j2, j3, vec, bias_in,
    layer_out, dsum_out, dattn_out, outer_away, outer_mine, inner_away, inner_mine, out_away, out_mine,
    slope, vec_grad, bias_grad, w_in, w_out, hid_t, act_t, d_branches, d_inners, d_attns, in_sems, out_sems,
):
    s = pl.program_id(0)

    @pl.when(s == 0)
    def _():
        vec_grad[...] = jnp.zeros_like(vec_grad)
        bias_grad[...] = jnp.zeros_like(bias_grad)
        copies = []
        for i, (piece, late) in enumerate(zip((i0, i1, i2, i3), (j0, j1, j2, j3))):
            c = ids[9] if i % 2 == 0 else 1 - ids[9]
            z_half = ids[11] // 2 if i // 2 == 0 else 1 - ids[11] // 2
            y_half = ids[12] // 2 if i // 2 == 0 else 1 - ids[12] // 2
            for d in range(RING):
                x = lax.rem(ids[8] + RING - d, RING)
                copies.append(pltpu.make_async_copy(piece.at[d], w_in.at[x, c, z_half], in_sems.at[i, d]))
                for n in range(RING):
                    target = w_out.at[x, c, n, y_half]
                    copies.append(pltpu.make_async_copy(late.at[n, d], target, out_sems.at[i, d, n]))
        for copy in copies:
            copy.start()
        for copy in copies:
            copy.wait()

    def inner_columns(n):
        return w_in[:, :, :, :, n * FF_STEP : (n + 1) * FF_STEP].reshape(WIDTH, FF_STEP)

    def outer_rows(n):
        return w_out[n].reshape(FF_STEP, WIDTH)

    @pl.when(s < SEQ_DEV)
    def _():
        zhat1, r1 = normalised(sum1[...])
        hidden = zhat1 * vec[3:4] + vec[4:5]
        hid_low = hidden.astype(bf16)
        hid_t[s] = hid_low.T
        branch = jnp.broadcast_to(vec[5:6], (SLOT, WIDTH))
        for n in range(FF_STEPS):
            cols = slice(n * FF_STEP, (n + 1) * FF_STEP)
            inner = mm(hid_low, inner_columns(n)) + bias_in[0:1, cols]
            half = 0.5 * lax.erf(inner * 0.7071067811865476) + 0.5
            bell = 0.3989422804014327 * jnp.exp(-0.5 * (inner * inner))
            act = (inner * half).astype(bf16)
            act_t[s, cols, :] = act.T
            slope[:, cols] = (half + inner * bell).astype(bf16)
            branch += mm(act, outer_rows(n))
        zhat2, r2 = normalised(hidden + branch)
        gain2 = vec[6:7]
        normed = zhat2 * gain2 + vec[7:8]
        valid = (lax.broadcasted_iota(jnp.int32, (SLOT, 1), 0) < ids[s]).astype(f32)
        keep = ids[4 + s] == 0
        x = joined(x_in).astype(f32)
        layer_out[...] = (jnp.where(keep, normed, x) * valid).astype(bf16)
        dy = joined(c_in).astype(f32) * jnp.where(keep, valid, 0.0)
        vec_grad[1:2] += col_sum(dy * zhat2)
        vec_grad[2:3] += col_sum(dy)
        d_sum2 = norm_back(dy, zhat2, r2, gain2)
        d_branch = d_sum2.astype(bf16)
        d_branches[s] = d_branch
        vec_grad[0:1] += col_sum(d_branch.astype(f32))
        d_hidden = d_sum2
        for n in range(FF_STEPS):
            cols = slice(n * FF_STEP, (n + 1) * FF_STEP)
            d_act = mm_nt(d_branch, outer_rows(n))
            d_inner = (d_act * slope[:, cols].astype(f32)).astype(bf16)
            d_inners[s, n] = d_inner
            bias_grad[0:1, cols] += col_sum(d_inner.astype(f32))
            d_hidden += mm_nt(d_inner, inner_columns(n))
        vec_grad[3:4] += col_sum(d_hidden * zhat1)
        vec_grad[4:5] += col_sum(d_hidden)
        d_sum1 = norm_back(d_hidden, zhat1, r1, vec[3:4])
        dsum_out[...] = d_sum1
        d_attn = d_sum1.astype(bf16)
        dattn_out[...] = d_attn
        d_attns[s] = d_attn
        vec_grad[5:6] += col_sum(d_attn.astype(f32))

    @pl.when((s >= SEQ_DEV) & (s < SEQ_DEV + RING))
    def _():
        rows = pl.ds(pl.multiple_of((s - SEQ_DEV) * FF_STEP, FF_STEP), FF_STEP)
        value = mm(act_t[0, rows, :], d_branches[0])
        for i in range(1, SEQ_DEV):
            value += mm(act_t[i, rows, :], d_branches[i])
        cut_cores(ids, value.astype(bf16), outer_away, outer_mine)

    @pl.when((s >= SEQ_DEV + RING) & (s < SEQ_DEV + RING + FF_STEPS))
    def _():
        n = s - SEQ_DEV - RING
        value = mm(hid_t[0], d_inners[0, n])
        for i in range(1, SEQ_DEV):
            value += mm(hid_t[i], d_inners[i, n])
        cut_cores(ids, value.astype(bf16), inner_away, inner_mine)

    @pl.when(s == SEQ_DEV + RING + FF_STEPS)
    def _():
        value = mm(ctx_t[:, :SLOT], d_attns[0])
        for i in range(1, SEQ_DEV):
            value += mm(ctx_t[:, i * SLOT : (i + 1) * SLOT], d_attns[i])
        block = gather_back([vec_grad[i : i + 1] for i in range(6)] + [bias_grad[...]])
        cut_cores(ids, jnp.concatenate([value.astype(bf16), block], axis=1), out_away, out_mine)


def attention_backward(
    ids, dsum, dattn, qkv, exp_in, norm_in, ctxt_in, x_t, c_in, layer_in, p0, p1, p2, p3, p4, p5, p6, p7,
    back_out, attn_away, attn_mine,
    w, vec_grad, d_qkv, sems,
):
    s = pl.program_id(0)

    @pl.when(s == 0)
    def _():
        vec_grad[...] = jnp.zeros_like(vec_grad)
        copies = attention_copies(ids, (p0, p1, p2, p3, p4, p5, p6, p7), w, sems)
        for copy in copies:
            copy.start()
        for copy in copies:
            copy.wait()

    @pl.when(s < SEQ_DEV)
    def _():
        d_sum1 = dsum[...]
        dctx_t = mm_nt(dattn[...], columns(w, 3 * WIDTH, 4 * WIDTH)).T
        ctx_t = ctxt_in[...].astype(f32)
        k_t = qkv[:, WIDTH : 2 * WIDTH].T
        scaled = []
        deltas = []
        for h in range(HEADS):
            rows = slice(h * HEAD, (h + 1) * HEAD)
            one = (dctx_t[rows] * norm_in[0, h : h + 1, :]).astype(bf16)
            scaled.append(one)
            deltas.append(col_sum(one.astype(f32) * ctx_t[rows]))
        dctx_t = jnp.concatenate(scaled, axis=0)
        dctx = dctx_t.T
        low = lax.broadcasted_iota(jnp.int32, (SLOT, PAIR), 1) < HEAD
        dq_t = []
        for p in range(0, WIDTH, PAIR):
            cols = slice(p, p + PAIR)
            q_pair = qkv[:, cols]
            v_pair = qkv[:, 2 * WIDTH + p : 2 * WIDTH + p + PAIR]
            dks = []
            dvs = []
            for half in range(2):
                h = p // HEAD + half
                v_one = jnp.where(low if half == 0 else ~low, v_pair, jnp.zeros_like(v_pair))
                d_probs = mm(v_one, dctx_t[cols]) - deltas[h]
                expo = exp_in[0, h]
                d_scores = (expo.astype(f32) * d_probs).astype(bf16)
                dvs.append(mm(expo, dctx[:, cols]))
                dks.append(mm(d_scores, q_pair))
                dq_t.append(mm(k_t[h * HEAD : (h + 1) * HEAD], d_scores))
            d_qkv[s, 1, :, cols] = jnp.where(low, dks[0], dks[1]).astype(bf16)
            d_qkv[s, 2, :, cols] = jnp.where(low, dvs[0], dvs[1]).astype(bf16)
        dq = (jnp.concatenate(dq_t, axis=0).T * HEAD**-0.5).astype(bf16)
        d_qkv[s, 0] = dq
        vec_grad[0:1] += col_sum(dq.astype(f32))
        vec_grad[1:2] += col_sum(d_qkv[s, 2].astype(f32))
        d_in = d_sum1
        for n in range(3):
            d_in += mm_nt(d_qkv[s, n], columns(w, n * WIDTH, (n + 1) * WIDTH))
        valid = (lax.broadcasted_iota(jnp.int32, (SLOT, 1), 0) < ids[s]).astype(f32)
        upstream = joined(c_in).astype(f32) * valid
        keep = ids[4 + s] == 0
        grad = jnp.where(keep, d_in, upstream).astype(bf16)
        back_out[:, 0, 0] = layer_in[...].reshape(GROUP, PIECE, WIDTH)
        back_out[:, 1, 0] = grad.reshape(GROUP, PIECE, WIDTH)

    @pl.when(s == SEQ_DEV)
    def _():
        values = []
        for n in range(3):
            value = mm(x_t[:, :SLOT], d_qkv[0, n])
            for i in range(1, SEQ_DEV):
                value += mm(x_t[:, i * SLOT : (i + 1) * SLOT], d_qkv[i, n])
            values.append(value.astype(bf16))
        values.append(gather_back([vec_grad[0:1], vec_grad[1:2]]))
        cut_cores(ids, jnp.concatenate(values, axis=1), attn_away, attn_mine)


def in_order(values, me):
    ordered = []
    for j in range(RING):
        step = lax.rem(me + RING - j, RING)
        value = values[0]
        for d in (1, 2, 3):
            value = jnp.where(step == d, values[d], value)
        ordered.append(value)
    return ordered


def pack_rows(ids, query, key, value, out, inner, row, packed):
    for i, ref in enumerate((query, key, value, out)):
        block = jnp.concatenate([ref[...].astype(f32), jnp.zeros((2, WIDTH), f32)], axis=0)
        if i == 0:
            line = lax.broadcasted_iota(jnp.int32, (8, WIDTH), 0)
            block = jnp.where(line == 6, row[...].astype(f32), block)
        packed[:, i * WIDTH : (i + 1) * WIDTH] = block.astype(bf16)
    block = jnp.concatenate([inner[...].astype(f32), jnp.zeros((2, FF), f32)], axis=0)
    packed[:, 4 * WIDTH :] = block.astype(bf16)


def merge_rows(ids, own, r1, r2, r3, attn_out, inner_out):
    ordered = in_order([v[...].astype(f32) for v in (own, r1, r2, r3)], ids[12])
    width = 4 * WIDTH
    rows = jnp.concatenate([v[:6] for v in ordered], axis=0).astype(bf16)
    attn_out[:, :width] = rows[:, :width]
    inner_out[...] = rows[:, width:]
    row = jnp.concatenate([v[6:7, :128] for v in ordered], axis=1)
    first = lax.broadcasted_iota(jnp.int32, (24, 4 * 128), 0) == 0
    attn_out[:, width:] = jnp.where(first, jnp.broadcast_to(row, (24, 4 * 128)), 0.0).astype(bf16)


def stack_rows(ids, own, r1, r2, r3, out):
    for d, piece in enumerate((own, r1, r2, r3)):
        out[lax.rem(ids[11] + RING - d, RING)] = piece[...]


def ahead(ids, axis, step):
    return lax.rem(ids[axis] + step, RING)


def sum_of(refs):
    total = refs[0][...].astype(f32)
    for ref in refs[1:]:
        total += ref[...].astype(f32)
    return total


def sum_blocks(ids, *refs):
    *parts, o0, o1, o2, o3, scratch = refs
    start = 0
    for mine, core in zip(parts[::2], parts[1::2]):
        end = start + mine.shape[2]
        scratch[:, start:end] = mine[0].astype(f32) + core[0].astype(f32)
        start = end
    for d, out in enumerate((o0, o1, o2, o3)):
        first = pl.multiple_of(ahead(ids, 11, d) * 24, 8)
        out[0] = scratch[pl.ds(first, 24), :].astype(bf16)


def sum_attention(ids, outer, mine, core, o0, o1, o2, o3, scratch):
    scratch[...] = mine[0].astype(f32) + core[0].astype(f32)
    for d, out in enumerate((o0, o1, o2, o3)):
        z = ahead(ids, 11, d)
        first = pl.multiple_of(z * 24, 8)
        out[0, :, : scratch.shape[1]] = scratch[pl.ds(first, 24), :].astype(bf16)
        out[0, :, scratch.shape[1] :] = outer[0, z]


def sum_outer(ids, mine, core, out):
    total = mine[0].astype(f32) + core[0].astype(f32)
    for z in range(RING):
        for y in range(RING):
            first = 96 * z + 24 * y
            out[y, 0, z] = total[first : first + 24].astype(bf16)


def sum_first(ids, value, out):
    for z in range(RING):
        out[0, z] = sum_of([value.at[y, 0, z] for y in range(RING)]).astype(bf16)


def split_rows(ids, p0, p1, p2, p3, o0, o1, o2, o3, *refs):
    *rest, scratch = refs
    width = o0.shape[2]
    total = sum_of([p.at[0] for p in (p0, p1, p2, p3)])
    if rest:
        rest[0][0] = total[:, width + 128 :].astype(bf16)
    for y in range(RING):
        vectors = total[y : y + 1, width : width + 128]
        row = jnp.concatenate([vectors, jnp.zeros((1, width - 128), f32)], axis=1)
        rows = total[6 * y : 6 * y + 6, :width]
        scratch[y] = jnp.concatenate([rows, row, jnp.zeros((1, width), f32)], axis=0)
    for d, out in enumerate((o0, o1, o2, o3)):
        out[0] = scratch[ahead(ids, 12, d)].astype(bf16)


LAST = FF + WIDTH + 3 * WIDTH + 3 * WIDTH


def join_flows(ids, i0, i1, i2, i3, a0, a1, a2, a3, outer, o0, o1, o2, o3, scratch):
    scratch[:, :, : FF + WIDTH] = sum_of((i0, i1, i2, i3))
    scratch[:, :, FF + WIDTH : FF + 4 * WIDTH] = sum_of((a0, a1, a2, a3))
    for x in range(RING):
        total = outer[x].astype(f32)
        for k in range(3):
            start = FF + (4 + k) * WIDTH
            scratch[x, :, start : start + WIDTH] = total[8 * k : 8 * k + 8]
    for d, out in enumerate((o0, o1, o2, o3)):
        out[...] = scratch[ahead(ids, 8, d)].astype(bf16)


def split_ffn(ids, p0, p1, p2, p3, inner, outer):
    for d, piece in enumerate((p0, p1, p2, p3)):
        inner[d] = piece[:, :FF]
        halves = [piece[:, FF + i * WIDTH : FF + (i + 1) * WIDTH].astype(f32) for i in range(2)]
        outer[d] = jnp.concatenate(halves, axis=0).astype(bf16)


def write_grads(ids, p0, p1, p2, p3, query, key, value, out, inner, outer, vectors):
    total = sum_of((p0, p1, p2, p3))
    inner[...] = total[:6, :FF]
    out[...] = total[:6, FF : FF + WIDTH]
    start = FF + WIDTH
    query[...] = total[:6, start : start + WIDTH]
    key[...] = total[:6, start + WIDTH : start + 2 * WIDTH]
    value[...] = total[:6, start + 2 * WIDTH : start + 3 * WIDTH]
    vectors[...] = jnp.concatenate([total[6:7, :128], total[6:7, start : start + 128]], axis=0)
    start += 3 * WIDTH
    for k in range(3):
        outer[8 * k : 8 * k + 8] = total[:, start + k * WIDTH : start + (k + 1) * WIDTH]


def whole(shape):
    return pl.BlockSpec(shape, lambda s, ids: (0,) * len(shape), pipeline_mode=pl.Buffered(1))


def sequence(s):
    return jnp.minimum(s, SEQ_DEV - 1)


DEALT_SPEC = pl.BlockSpec((GROUP, 1, PIECE, WIDTH), lambda s, ids: (0, sequence(s), 0, 0))


def by_rows(width):
    return pl.BlockSpec((SLOT, width), lambda s, ids: (sequence(s), 0))


def rows_of(width, kind):
    return jax.ShapeDtypeStruct((ROWS, width), kind)


EXP_SPEC = pl.BlockSpec((1, HEADS, SLOT, SLOT), lambda s, ids: (sequence(s), 0, 0, 0))
NORM_SPEC = pl.BlockSpec((1, 16, SLOT), lambda s, ids: (sequence(s), 0, 0))
RETURN_SPEC = pl.BlockSpec((GROUP, 2, 1, PIECE, WIDTH), lambda s, ids: (0, 0, sequence(s), 0, 0))
RETURN_SHAPE = jax.ShapeDtypeStruct((GROUP, 2, SEQ_DEV, PIECE, WIDTH), bf16)


def by_columns(height):
    return pl.BlockSpec((height, SLOT), lambda s, ids: (0, sequence(s)))


def columns_of(height):
    return jax.ShapeDtypeStruct((height, ROWS), bf16)


def run(kernel, grid, ins, outs, operands, name, flops, moved, scratch=()):
    return pl.pallas_call(
        kernel,
        grid_spec=pltpu.PrefetchScalarGridSpec(
            num_scalar_prefetch=1,
            grid=grid,
            in_specs=ins,
            out_specs=[spec for spec, _ in outs],
            scratch_shapes=list(scratch),
        ),
        out_shape=[shape for _, shape in outs],
        compiler_params=pltpu.CompilerParams(
            vmem_limit_bytes=VMEM_LIMIT, dimension_semantics=("arbitrary",) * len(grid)
        ),
        cost_estimate=pl.CostEstimate(flops=flops, bytes_accessed=moved, transcendentals=0),
        name=name,
    )(*operands)


def out_rows(width, kind):
    return (by_rows(width), rows_of(width, kind))


def out_columns(height):
    return (by_columns(height), columns_of(height))


def out_whole(shape):
    return (whole(shape), jax.ShapeDtypeStruct(shape, f32))


ANYWHERE = pl.BlockSpec(memory_space=pl.ANY)
ATTENTION_SCRATCH = [pltpu.VMEM((RING, CORES, 96, PACKED), bf16)]


def call_forward(ids, dealt, weights, perm):
    return run(
        attention_forward,
        (SEQ_DEV,),
        [DEALT_SPEC] + [ANYWHERE] * 8 + [whole((32, 16))],
        [
            out_columns(WIDTH),
            out_rows(3 * WIDTH, bf16),
            (EXP_SPEC, jax.ShapeDtypeStruct((SEQ_DEV, HEADS, SLOT, SLOT), bf16)),
            (NORM_SPEC, jax.ShapeDtypeStruct((SEQ_DEV, 16, SLOT), f32)),
            out_columns(WIDTH),
            out_rows(WIDTH, f32),
            out_whole((8, WIDTH)),
            out_whole((1, FF)),
            out_whole((8, 128)),
        ],
        (ids, dealt, *weights, perm),
        "attention_forward",
        22 * 10**9,
        22 * 10**6,
        ATTENTION_SCRATCH + [pltpu.VMEM((32, PACKED - 4 * WIDTH), f32), pltpu.SemaphoreType.DMA((8,))],
    )


def halves(block, shape, where):
    return [(pl.BlockSpec(block, lambda s, ids: where(s)), jax.ShapeDtypeStruct(shape, bf16))] * 2


def call_ffn(ids, sum1, dealt, dealt_c, ctx_t, inner, outer, vec, bias_in):
    outer_rows = FF // GROUP
    inner_rows = WIDTH // GROUP
    first = SEQ_DEV
    second = first + RING
    return run(
        feed_forward,
        (second + FF_STEPS + 1,),
        [by_rows(WIDTH)]
        + [DEALT_SPEC] * 2
        + [whole((WIDTH, ROWS))]
        + [ANYWHERE] * 8
        + [whole((8, WIDTH)), whole((1, FF))],
        [out_rows(WIDTH, bf16), out_rows(WIDTH, f32), out_rows(WIDTH, bf16)]
        + halves(
            (1, outer_rows, WIDTH), (RING, outer_rows, WIDTH), lambda s: (jnp.clip(s - first, 0, RING - 1), 0, 0)
        )
        + halves(
            (RING, inner_rows, FF_STEP),
            (RING, inner_rows, FF),
            lambda s: (0, 0, jnp.clip(s - second, 0, FF_STEPS - 1)),
        )
        + halves((RING, inner_rows, WIDTH + 128), (RING, inner_rows, WIDTH + 128), lambda s: (0, 0, 0)),
        (ids, sum1, dealt, dealt_c, ctx_t, *inner, *outer, vec, bias_in),
        "feed_forward",
        50 * 10**9,
        40 * 10**6,
        [
            pltpu.VMEM((SLOT, FF), bf16),
            pltpu.VMEM((8, WIDTH), f32),
            pltpu.VMEM((1, FF), f32),
            pltpu.VMEM((RING, CORES, 2, 48, FF), bf16),
            pltpu.VMEM((RING, CORES, RING, 2, 48, WIDTH), bf16),
            pltpu.VMEM((SEQ_DEV, WIDTH, SLOT), bf16),
            pltpu.VMEM((SEQ_DEV, FF, SLOT), bf16),
            pltpu.VMEM((SEQ_DEV, SLOT, WIDTH), bf16),
            pltpu.VMEM((SEQ_DEV, FF_STEPS, SLOT, FF_STEP), bf16),
            pltpu.VMEM((SEQ_DEV, SLOT, WIDTH), bf16),
            pltpu.SemaphoreType.DMA((RING, RING)),
            pltpu.SemaphoreType.DMA((RING, RING, RING)),
        ],
    )


def call_backward(ids, dsum, dattn, qkv, expo, norm, ctx_t, x_t, dealt_c, layer, weights):
    block = (RING, WIDTH // GROUP, 3 * WIDTH + 128)
    return run(
        attention_backward,
        (SEQ_DEV + 1,),
        [by_rows(WIDTH), by_rows(WIDTH), by_rows(3 * WIDTH), EXP_SPEC, NORM_SPEC, by_columns(WIDTH)]
        + [whole((WIDTH, ROWS)), DEALT_SPEC, by_rows(WIDTH)]
        + [ANYWHERE] * 8,
        [(RETURN_SPEC, RETURN_SHAPE)] + halves(block, block, lambda s: (0, 0, 0)),
        (ids, dsum, dattn, qkv, expo, norm, ctx_t, x_t, dealt_c, layer, *weights),
        "attention_backward",
        28 * 10**9,
        30 * 10**6,
        ATTENTION_SCRATCH
        + [
            pltpu.VMEM((8, WIDTH), f32),
            pltpu.VMEM((SEQ_DEV, 3, SLOT, WIDTH), bf16),
            pltpu.SemaphoreType.DMA((8,)),
        ],
    )


def call_by_x(kernel, name, ids, pieces, at, out_shapes, out_at, scratch):
    count = len(out_shapes)

    def every_x(ids, *refs):
        ins, outs, rest = refs[: len(pieces)], refs[len(pieces) :][:count], refs[len(pieces) + count :]
        for x in range(RING):
            one = (pl.ds(x, 1),)
            kernel(
                ids,
                *[ref.at[(slice(None),) * at + one] for ref in ins],
                *[ref.at[(slice(None),) * out_at + one] for ref in outs],
                *rest,
            )

    return call_small(every_x, name, ids, pieces, *out_shapes, scratch=scratch)


def call_small(kernel, name, ids, pieces, *out_shapes, kind=bf16, scratch=()):
    def full(shape):
        return pl.BlockSpec(shape, lambda i, ids: (0,) * len(shape))

    return run(
        kernel,
        (1,),
        [full(piece.shape) for piece in pieces],
        [(full(shape), jax.ShapeDtypeStruct(shape, kind)) for shape in out_shapes],
        (ids, *pieces),
        name,
        10**6,
        6 * 10**6,
        [pltpu.VMEM(shape, f32) for shape in scratch],
    )


def shift(value, axis, step):
    size = CORES if axis == "core" else RING
    return lax.ppermute(value, axis, [(i, (i + step) % size) for i in range(size)])


def swap(value, axis):
    return lax.ppermute(value, axis, [(i, i ^ 1) for i in range(RING)])


def arrivals(value, axis):
    return [value] + [shift(value, axis, step) for step in (1, 2, 3)]


def both_cores(pieces):
    return [part for piece in pieces for part in (piece, shift(piece, "core", 1))]


def paired(value, axis):
    return in_half(value, swap(value, axis), axis)


def in_half(value, other, axis):
    even = lax.rem(lax.axis_index(axis), 2) == 0
    return jnp.where(even, value, other), jnp.where(even, other, value)


def hold(value, *others):
    return lax.optimization_barrier((value, *others))[0]


def send_ring(parts, axis):
    return [parts[0]] + [shift(parts[step], axis, step) for step in (1, 2, 3)]


def over(value, axis):
    return lax.all_to_all(value, axis, split_axis=0, concat_axis=0, tiled=True)


def body(
    tokens,
    cotangent,
    perm,
    lengths,
    drop,
    w_query,
    b_query,
    w_key,
    w_value,
    b_value,
    w_out,
    b_out,
    norm1_gain,
    norm1_bias,
    w_inner,
    b_inner,
    w_outer,
    b_outer,
    norm2_gain,
    norm2_bias,
):
    me_x = lax.axis_index("x")
    me_c = lax.axis_index("core")
    me_z = lax.axis_index("z")
    me_y = lax.axis_index("y")
    first = ((me_z * RING + me_y) * 8 + me_x * CORES + me_c) * SEQ_DEV
    places = jnp.stack([me_x, me_c, first, me_z, me_y]).astype(jnp.int32)
    places = jnp.pad(places, (8, 3))

    vectors = [b_query, b_value, b_out, norm1_gain, norm1_bias, b_outer, norm2_gain, norm2_bias, b_inner]
    vectors += [lengths.astype(bf16), drop.astype(bf16)]
    row = jnp.zeros((WIDTH,), bf16)
    start = 0
    for vector in vectors:
        end = start + vector.shape[0]
        row += jnp.pad(vector, (start, WIDTH - end))
        start = end
    (piece,) = call_small(
        pack_rows, "pack_rows", places, (w_query, w_key, w_value, w_out, w_inner, row[None]), (8, 4 * WIDTH + FF)
    )
    pieces_y = arrivals(piece, "y")
    dp = ("x", "core")
    dealt = (GROUP, SEQ_DEV, PIECE, WIDTH)
    dealt_x = over(tokens.reshape(dealt), dp)
    attn_y, inner_y = call_small(merge_rows, "merge_rows", places, pieces_y, (24, PACKED), (24, FF))
    (attn_zy,) = call_small(
        stack_rows, "stack_rows", places, arrivals(attn_y, "z"), (RING, 24, PACKED)
    )

    outer_pair = paired(w_outer, "y")
    ffn_x = arrivals(jnp.concatenate([hold(inner_y, dealt_x), *outer_pair], axis=1), "x")
    inner_x, outer_x = call_small(
        split_ffn, "split_ffn", places, ffn_x, (RING, 24, FF), (RING, 48, WIDTH)
    )
    attn_x = arrivals(hold(attn_zy, dealt_x).reshape(96, PACKED), "x")
    attn_pieces = both_cores(attn_x)
    inner_z = swap(inner_x, "z")
    outer_z = over(jnp.broadcast_to(outer_x[None], (RING, RING, 48, WIDTH)), "z")
    inner_z = jnp.concatenate(in_half(inner_x, hold(inner_z, attn_x[1]), "z"), axis=1)
    inner_far = shift(inner_z, "z", 2)
    outer_z = hold(outer_z, attn_x[1])
    outer_far = shift(outer_z, "y", 2)
    dealt_c = over(hold(cotangent, attn_x[1]).reshape(dealt), dp)

    x_t, qkv, expo, norm, ctx_t, sum1, vec, inner_bias, info = call_forward(
        places, dealt_x, attn_pieces, perm.reshape(32, 16)
    )
    ids = jnp.concatenate([info[:, 0].astype(jnp.int32), places[8:]])

    inner_pieces = both_cores([hold(inner_z, sum1), hold(inner_far, sum1)])
    outer_pieces = both_cores([hold(outer_z, sum1), hold(outer_far, sum1)])
    (
        layer, d_sum1, d_attn, outer_away, outer_mine, inner_away, inner_mine, out_away, out_mine
    ) = call_ffn(ids, sum1, dealt_x, dealt_c, ctx_t, inner_pieces, outer_pieces, vec, inner_bias)

    inner_core = shift(inner_away, "core", 1)
    out_core = shift(out_away, "core", 1)
    outer_core = shift(outer_away, "core", 1)
    inner_width = FF + WIDTH + 128
    inner_parts = call_by_x(
        sum_blocks, "sum_blocks", places, (inner_mine, inner_core, out_mine, out_core), 0,
        [(RING, 24, inner_width)] * RING, 0, [(96, inner_width)],
    )
    (outer_sum,) = call_by_x(
        sum_outer, "sum_outer", hold(places, inner_parts[0]), (outer_mine, outer_core), 0,
        [(RING, RING, RING, 24, WIDTH)], 1, [],
    )
    inner_parts = send_ring(inner_parts, "z")
    outer_y = over(outer_sum, "y")

    d_sum1, d_attn = lax.optimization_barrier((d_sum1, d_attn, inner_parts[0], outer_sum))[:2]
    back, attn_away, attn_mine = call_backward(
        ids, d_sum1, d_attn, qkv, expo, norm, ctx_t, x_t, dealt_c, layer, attn_pieces
    )

    attn_core = shift(hold(attn_away, outer_y, *inner_parts[1:]), "core", 1)
    (outer_z,) = call_by_x(
        sum_first, "sum_first", hold(places, attn_away), (hold(outer_y, attn_away),), 1,
        [(RING, RING, 24, WIDTH)], 0, [],
    )
    attn_width = 3 * WIDTH + 128
    attn_parts = call_by_x(
        sum_attention, "sum_attention", places, (outer_z, attn_mine, attn_core), 0,
        [(RING, 24, attn_width + WIDTH)] * RING, 0, [(96, attn_width)],
    )
    attn_first = attn_parts[0]
    attn_parts = send_ring(attn_parts, "z")
    back = over(hold(back, outer_z), dp)

    inner_parts = [hold(p, attn_first) for p in inner_parts]
    inner_parts = call_by_x(
        split_rows, "split_rows", places, inner_parts, 0,
        [(RING, 8, FF + WIDTH)] * RING, 0, [(RING, 8, FF + WIDTH)],
    )
    *attn_parts, outer_z = call_by_x(
        split_rows, "split_rows", hold(places, inner_parts[0]), attn_parts, 0,
        [(RING, 8, 3 * WIDTH)] * RING + [(RING, 24, WIDTH)], 0, [(RING, 8, 3 * WIDTH)],
    )
    inner_parts = send_ring(inner_parts, "y")
    attn_parts = send_ring(attn_parts, "y")
    last = call_small(
        join_flows, "join_flows", places, [*inner_parts, *attn_parts, outer_z], *[(8, LAST)] * 4,
        scratch=[(RING, 8, LAST)],
    )
    back = hold(back, last[0])
    layer_final = back[:, 0].reshape(GROUP * SEQ_DEV, PIECE, WIDTH)
    grad_final = back[:, 1].reshape(GROUP * SEQ_DEV, PIECE, WIDTH)
    square = (6, WIDTH)
    grad_query, grad_key, grad_value, grad_out, grad_inner, grad_outer, vectors = call_small(
        write_grads, "write_grads", hold(places, layer_final), send_ring(last, "x"),
        square, square, square, square, (6, FF), (24, WIDTH), (2, 128), kind=f32,
    )
    ffn_vectors = [vectors[0, 6 * i : 6 * i + 6] for i in range(6)]
    return (
        layer_final,
        grad_final,
        grad_query,
        vectors[1, :6],
        grad_key,
        grad_value,
        vectors[1, 6:12],
        grad_out,
        ffn_vectors[5],
        ffn_vectors[3],
        ffn_vectors[4],
        grad_inner,
        vectors[0, 36:60],
        grad_outer,
        ffn_vectors[0],
        ffn_vectors[1],
        ffn_vectors[2],
    )


def solution(mesh):
    chips = Mesh(mesh.devices.reshape(RING, CORES, RING, RING), ("x", "core", "z", "y"))
    dp = ("x", "core")
    fsdp = ("z", "y")
    every = P(dp + fsdp)
    rows = P(dp + fsdp, None)
    whole_rows = P(fsdp, dp, None)
    return jax.shard_map(
        body,
        mesh=chips,
        in_specs=(
            whole_rows, whole_rows, P(), every, every,
            rows, every, rows, rows, every, rows, every, every, every,
            rows, every, rows, every, every, every,
        ),
        out_specs=(
            whole_rows, whole_rows,
            rows, every, rows, rows, every, rows, every, every, every,
            rows, every, rows, every, every, every,
        ),
        check_vma=False,
    )
```

```python
import functools
import jax
import jax.numpy as jnp
from jax import lax
from jax.experimental import pallas as pl
from jax.experimental.pallas import tpu as pltpu
from jax.sharding import Mesh
from jax.sharding import PartitionSpec as P

HEADS = 12
HEAD = 64
WIDTH = 768
FF = 3072
SLOT = 256
SEQ_DEV = 4
RING = 4
CORES = 2
PIECE = 32
GROUP = RING * CORES
ROWS = SEQ_DEV * SLOT
PAIR = 2 * HEAD
PACKED = 3 * WIDTH + 512
MIXED = WIDTH + FF

epsilon = 1e-05
bf16 = jnp.bfloat16
f32 = jnp.float32
VMEM_LIMIT = 58 * 1024 * 1024

TN = (((0,), (0,)), ((), ()))
NT = (((1,), (1,)), ((), ()))


def mm(a, b):
    return jnp.dot(a, b, preferred_element_type=f32)


def mm_nt(a, b):
    return lax.dot_general(a, b, NT, preferred_element_type=f32)


def mm_tn(a, b):
    return lax.dot_general(a, b, TN, preferred_element_type=f32)


def joined(ref):
    return ref[...].reshape(SLOT, WIDTH)


def spread(extras, start, width):
    total = 128 * width
    group = lax.broadcasted_iota(jnp.int32, (32, total), 0)
    owner = lax.broadcasted_iota(jnp.int32, (32, total), 1) // width
    pick = lax.broadcasted_iota(jnp.int32, (width, total), 0)
    within = lax.rem(lax.broadcasted_iota(jnp.int32, (width, total), 1), width)
    chosen = (pick == within).astype(bf16)
    out = jnp.zeros((32, total), f32)
    for y in range(RING):
        values = extras[:, 128 * y + start : 128 * y + start + width].astype(bf16)
        out += jnp.where(owner == group * RING + y, mm(values, chosen), 0.0)
    return jnp.sum(out, axis=0, keepdims=True)


def gather_back(vectors):
    values = jnp.zeros((128, 128), f32)
    start = 0
    for vector in vectors:
        total = vector.shape[1]
        width = total // 128
        owner = lax.broadcasted_iota(jnp.int32, (128, total), 1) // width
        mine = owner == lax.broadcasted_iota(jnp.int32, (128, total), 0)
        within = lax.rem(lax.broadcasted_iota(jnp.int32, (total, 128), 0), width)
        column = lax.broadcasted_iota(jnp.int32, (total, 128), 1)
        spots = (column == within + start).astype(bf16)
        values += mm(jnp.where(mine, vector, 0.0).astype(bf16), spots)
        start += width
    row = lax.broadcasted_iota(jnp.int32, (WIDTH, 128), 0)
    device = lax.broadcasted_iota(jnp.int32, (WIDTH, 128), 1)
    within = lax.rem(row, 24)
    picks = (within < RING) & (row // 24 * RING + within == device)
    return mm(picks.astype(bf16), values.astype(bf16)).astype(bf16)


def attention_copies(ids, pieces, w, sems):
    copies = []
    for i, piece in enumerate(pieces):
        x = lax.rem(ids[8] + RING - i // 2, RING)
        c = ids[9] if i % 2 == 0 else 1 - ids[9]
        copies.append(pltpu.make_async_copy(piece, w.at[x, c], sems.at[i]))
    return copies


def half_of(ids, i):
    c = ids[9] if i % 2 == 0 else 1 - ids[9]
    return c, ids[11] // 2 if i // 2 == 0 else 1 - ids[11] // 2


def columns(w, start, end):
    return w[:, :, :, start:end].reshape(WIDTH, end - start)


def attention_forward(
    ids, x_in, p0, p1, p2, p3, p4, p5, p6, p7, perm,
    xt_out, qkv_out, exp_out, norm_out, ctxt_out, vec, bias_out, info,
    w, extras, sems,
):
    s = pl.program_id(0)

    @pl.when(s == 0)
    def _():
        copies = attention_copies(ids, (p0, p1, p2, p3, p4, p5, p6, p7), w, sems)
        for copy in copies:
            copy.start()
        for copy in copies:
            copy.wait()
        rows = columns(w, 3 * WIDTH, PACKED).astype(f32).reshape(32, 24, PACKED - 3 * WIDTH)
        extras[...] = jnp.sum(rows, axis=1)
        for i in range(8):
            vec[i : i + 1] = spread(extras, 6 * i, 6)
        bias_out[...] = spread(extras, 48, 24)

    length = jnp.zeros((1, 1), f32)
    dropped = jnp.zeros((1, 1), f32)
    for y in range(RING):
        hit = perm[:, RING * y : RING * y + 4] == ids[10] + s
        length += jnp.sum(jnp.where(hit, extras[:, 128 * y + 72 : 128 * y + 76], 0.0), keepdims=True)
        dropped += jnp.sum(jnp.where(hit, extras[:, 128 * y + 76 : 128 * y + 80], 0.0), keepdims=True)
    line = lax.broadcasted_iota(jnp.int32, (8, 128), 0)
    info[...] = jnp.where(line == s, length, jnp.where(line == s + 4, dropped, info[...]))

    x = joined(x_in)
    xt_out[...] = x.T
    q = ((mm(x, columns(w, 0, WIDTH)) + vec[0:1]).astype(bf16).astype(f32) * HEAD**-0.5).astype(bf16)
    k = mm(x, columns(w, WIDTH, 2 * WIDTH)).astype(bf16)
    v = (mm(x, columns(w, 2 * WIDTH, 3 * WIDTH)) + vec[1:2]).astype(bf16)
    qkv_out[:, :WIDTH] = q
    qkv_out[:, WIDTH : 2 * WIDTH] = k
    qkv_out[:, 2 * WIDTH :] = v
    q_t = q.T
    v_t = v.T
    keys = lax.broadcasted_iota(jnp.int32, (SLOT, 1), 0).astype(f32)
    bias = jnp.where(keys < length, 0.0, -1e30)
    low = lax.broadcasted_iota(jnp.int32, (SLOT, PAIR), 1) < HEAD
    ctx_t = []
    for h in range(HEADS):
        p = h // 2 * PAIR
        k_pair = k[:, p : p + PAIR]
        k_one = jnp.where(low if h % 2 == 0 else ~low, k_pair, jnp.zeros_like(k_pair))
        scores = mm(k_one, q_t[p : p + PAIR]) + bias
        top = jnp.max(scores, axis=0, keepdims=True)
        expo = jnp.exp(scores - top)
        inverse = 1.0 / jnp.sum(expo, axis=0, keepdims=True)
        norm_out[0, h : h + 1, :] = inverse
        expo = expo.astype(bf16)
        exp_out[0, h] = expo
        ctx_t.append(mm(v_t[h * HEAD : (h + 1) * HEAD], expo) * inverse)
    ctx_t = jnp.concatenate(ctx_t, axis=0).astype(bf16)
    ctxt_out[...] = ctx_t


def row_mean(v):
    return jnp.mean(v, axis=-1, keepdims=True)


def normalised(z):
    center = z - row_mean(z)
    r = lax.rsqrt(row_mean(center * center) + epsilon)
    return center * r, r


def norm_back(dy, zhat, r, gain):
    e = dy * gain
    return r * (e - row_mean(e) - zhat * row_mean(e * zhat))


def col_sum(v):
    return jnp.sum(v, axis=0, keepdims=True)


FF_STEP = 768
FF_STEPS = FF // FF_STEP


def cut_cores(ids, value, away, mine):
    blocks, rows, _ = away.shape
    first = ids[9] == 0
    for x in range(blocks):
        even = value[2 * x * rows : (2 * x + 1) * rows]
        odd = value[(2 * x + 1) * rows : (2 * x + 2) * rows]
        away[x] = jnp.where(first, odd, even)
        mine[x] = jnp.where(first, even, odd)


def feed_forward(
    ids, x_in, c_in, ctx_t, i0, i1, i2, i3, j0, j1, j2, j3, vec, bias_in,
    layer_out, dsum_out, dattn_out, outer_away, outer_mine, inner_away, inner_mine, out_away, out_mine,
    slope, vec_grad, bias_grad, w_in, w_out, hid_t, act_t, d_branches, d_inners, d_attns, in_sems, out_sems,
):
    s = pl.program_id(0)

    @pl.when(s == 0)
    def _():
        vec_grad[...] = jnp.zeros_like(vec_grad)
        bias_grad[...] = jnp.zeros_like(bias_grad)
        copies = []
        for i, (piece, late) in enumerate(zip((i0, i1, i2, i3), (j0, j1, j2, j3))):
            c, z_half = half_of(ids, i)
            y_half = ids[12] // 2 if i // 2 == 0 else 1 - ids[12] // 2
            for d in range(RING):
                x = lax.rem(ids[8] + RING - d, RING)
                copies.append(pltpu.make_async_copy(piece.at[d], w_in.at[x, c, z_half], in_sems.at[i, d]))
                for n in range(RING):
                    target = w_out.at[x, c, n, y_half]
                    copies.append(pltpu.make_async_copy(late.at[n, d], target, out_sems.at[i, d, n]))
        for copy in copies:
            copy.start()
        for copy in copies:
            copy.wait()

    def inner_columns(n):
        return w_in[:, :, :, :, WIDTH + n * FF_STEP : WIDTH + (n + 1) * FF_STEP].reshape(WIDTH, FF_STEP)

    def outer_rows(n):
        return w_out[n].reshape(FF_STEP, WIDTH)

    @pl.when(s < SEQ_DEV)
    def _():
        x = joined(x_in).astype(f32)
        context = ctx_t[:, pl.ds(pl.multiple_of(s * SLOT, SLOT), SLOT)].T
        attn_out = mm(context, w_in[:, :, :, :, :WIDTH].reshape(WIDTH, WIDTH)) + vec[2:3]
        zhat1, r1 = normalised(x + attn_out)
        hidden = zhat1 * vec[3:4] + vec[4:5]
        hid_low = hidden.astype(bf16)
        hid_t[s] = hid_low.T
        branch = jnp.broadcast_to(vec[5:6], (SLOT, WIDTH))
        for n in range(FF_STEPS):
            cols = slice(n * FF_STEP, (n + 1) * FF_STEP)
            inner = mm(hid_low, inner_columns(n)) + bias_in[0:1, cols]
            half = 0.5 * lax.erf(inner * 0.7071067811865476) + 0.5
            bell = 0.3989422804014327 * jnp.exp(-0.5 * (inner * inner))
            act = (inner * half).astype(bf16)
            act_t[s, cols, :] = act.T
            slope[:, cols] = (half + inner * bell).astype(bf16)
            branch += mm(act, outer_rows(n))
        zhat2, r2 = normalised(hidden + branch)
        gain2 = vec[6:7]
        normed = zhat2 * gain2 + vec[7:8]
        valid = (lax.broadcasted_iota(jnp.int32, (SLOT, 1), 0) < ids[s]).astype(f32)
        keep = ids[4 + s] == 0
        layer_out[...] = (jnp.where(keep, normed, x) * valid).astype(bf16)
        dy = joined(c_in).astype(f32) * jnp.where(keep, valid, 0.0)
        vec_grad[1:2] += col_sum(dy * zhat2)
        vec_grad[2:3] += col_sum(dy)
        d_sum2 = norm_back(dy, zhat2, r2, gain2)
        d_branch = d_sum2.astype(bf16)
        d_branches[s] = d_branch
        vec_grad[0:1] += col_sum(d_branch.astype(f32))
        d_hidden = d_sum2
        for n in range(FF_STEPS):
            cols = slice(n * FF_STEP, (n + 1) * FF_STEP)
            d_act = mm_nt(d_branch, outer_rows(n))
            d_inner = (d_act * slope[:, cols].astype(f32)).astype(bf16)
            d_inners[s, n] = d_inner
            bias_grad[0:1, cols] += col_sum(d_inner.astype(f32))
            d_hidden += mm_nt(d_inner, inner_columns(n))
        vec_grad[3:4] += col_sum(d_hidden * zhat1)
        vec_grad[4:5] += col_sum(d_hidden)
        d_sum1 = norm_back(d_hidden, zhat1, r1, vec[3:4])
        dsum_out[...] = d_sum1
        d_attn = d_sum1.astype(bf16)
        dattn_out[...] = d_attn
        d_attns[s] = d_attn
        vec_grad[5:6] += col_sum(d_attn.astype(f32))

    @pl.when((s >= SEQ_DEV) & (s < SEQ_DEV + RING))
    def _():
        rows = pl.ds(pl.multiple_of((s - SEQ_DEV) * FF_STEP, FF_STEP), FF_STEP)
        value = mm(act_t[0, rows, :], d_branches[0])
        for i in range(1, SEQ_DEV):
            value += mm(act_t[i, rows, :], d_branches[i])
        cut_cores(ids, value.astype(bf16), outer_away, outer_mine)

    @pl.when((s >= SEQ_DEV + RING) & (s < SEQ_DEV + RING + FF_STEPS))
    def _():
        n = s - SEQ_DEV - RING
        value = mm(hid_t[0], d_inners[0, n])
        for i in range(1, SEQ_DEV):
            value += mm(hid_t[i], d_inners[i, n])
        cut_cores(ids, value.astype(bf16), inner_away, inner_mine)

    @pl.when(s == SEQ_DEV + RING + FF_STEPS)
    def _():
        value = mm(ctx_t[:, :SLOT], d_attns[0])
        for i in range(1, SEQ_DEV):
            value += mm(ctx_t[:, i * SLOT : (i + 1) * SLOT], d_attns[i])
        block = gather_back([vec_grad[i : i + 1] for i in range(6)] + [bias_grad[...]])
        cut_cores(ids, jnp.concatenate([value.astype(bf16), block], axis=1), out_away, out_mine)


def attention_backward(
    ids, dsum, dattn, qkv, exp_in, norm_in, ctxt_in, x_t, c_in, layer_in, p0, p1, p2, p3, p4, p5, p6, p7, i0, i1, i2, i3,
    back_out, attn_away, attn_mine,
    w, w_out, vec_grad, d_qkv, sems, out_sems,
):
    s = pl.program_id(0)

    @pl.when(s == 0)
    def _():
        vec_grad[...] = jnp.zeros_like(vec_grad)
        copies = attention_copies(ids, (p0, p1, p2, p3, p4, p5, p6, p7), w, sems)
        for i, piece in enumerate((i0, i1, i2, i3)):
            c, z_half = half_of(ids, i)
            for d in range(RING):
                x = lax.rem(ids[8] + RING - d, RING)
                source = piece.at[d, :, pl.ds(0, WIDTH)]
                copies.append(pltpu.make_async_copy(source, w_out.at[x, c, z_half], out_sems.at[i, d]))
        for copy in copies:
            copy.start()
        for copy in copies:
            copy.wait()

    @pl.when(s < SEQ_DEV)
    def _():
        d_sum1 = dsum[...]
        dctx_t = mm_nt(dattn[...], w_out[...].reshape(WIDTH, WIDTH)).T
        ctx_t = ctxt_in[...].astype(f32)
        k_t = qkv[:, WIDTH : 2 * WIDTH].T
        scaled = []
        deltas = []
        for h in range(HEADS):
            rows = slice(h * HEAD, (h + 1) * HEAD)
            one = (dctx_t[rows] * norm_in[0, h : h + 1, :]).astype(bf16)
            scaled.append(one)
            deltas.append(col_sum(one.astype(f32) * ctx_t[rows]))
        dctx_t = jnp.concatenate(scaled, axis=0)
        dctx = dctx_t.T
        low = lax.broadcasted_iota(jnp.int32, (SLOT, PAIR), 1) < HEAD
        dq_t = []
        for p in range(0, WIDTH, PAIR):
            cols = slice(p, p + PAIR)
            q_pair = qkv[:, cols]
            v_pair = qkv[:, 2 * WIDTH + p : 2 * WIDTH + p + PAIR]
            dks = []
            dvs = []
            for half in range(2):
                h = p // HEAD + half
                v_one = jnp.where(low if half == 0 else ~low, v_pair, jnp.zeros_like(v_pair))
                d_probs = mm(v_one, dctx_t[cols]) - deltas[h]
                expo = exp_in[0, h]
                d_scores = (expo.astype(f32) * d_probs).astype(bf16)
                dvs.append(mm(expo, dctx[:, cols]))
                dks.append(mm(d_scores, q_pair))
                dq_t.append(mm(k_t[h * HEAD : (h + 1) * HEAD], d_scores))
            d_qkv[s, 1, :, cols] = jnp.where(low, dks[0], dks[1]).astype(bf16)
            d_qkv[s, 2, :, cols] = jnp.where(low, dvs[0], dvs[1]).astype(bf16)
        dq = (jnp.concatenate(dq_t, axis=0).T * HEAD**-0.5).astype(bf16)
        d_qkv[s, 0] = dq
        vec_grad[0:1] += col_sum(dq.astype(f32))
        vec_grad[1:2] += col_sum(d_qkv[s, 2].astype(f32))
        d_in = d_sum1
        for n in range(3):
            d_in += mm_nt(d_qkv[s, n], columns(w, n * WIDTH, (n + 1) * WIDTH))
        valid = (lax.broadcasted_iota(jnp.int32, (SLOT, 1), 0) < ids[s]).astype(f32)
        upstream = joined(c_in).astype(f32) * valid
        keep = ids[4 + s] == 0
        grad = jnp.where(keep, d_in, upstream).astype(bf16)
        back_out[:, 0, 0] = layer_in[...].reshape(GROUP, PIECE, WIDTH)
        back_out[:, 1, 0] = grad.reshape(GROUP, PIECE, WIDTH)

    @pl.when(s == SEQ_DEV)
    def _():
        values = []
        for n in range(3):
            value = mm(x_t[:, :SLOT], d_qkv[0, n])
            for i in range(1, SEQ_DEV):
                value += mm(x_t[:, i * SLOT : (i + 1) * SLOT], d_qkv[i, n])
            values.append(value.astype(bf16))
        values.append(gather_back([vec_grad[0:1], vec_grad[1:2]]))
        cut_cores(ids, jnp.concatenate(values, axis=1), attn_away, attn_mine)


def in_order(values, me):
    ordered = []
    for j in range(RING):
        step = lax.rem(me + RING - j, RING)
        value = values[0]
        for d in (1, 2, 3):
            value = jnp.where(step == d, values[d], value)
        ordered.append(value)
    return ordered


def pack_rows(ids, query, key, value, out, inner, row, packed):
    for i, ref in enumerate((query, key, value, out)):
        block = jnp.concatenate([ref[...].astype(f32), jnp.zeros((2, WIDTH), f32)], axis=0)
        if i == 0:
            line = lax.broadcasted_iota(jnp.int32, (8, WIDTH), 0)
            block = jnp.where(line == 6, row[...].astype(f32), block)
        packed[:, i * WIDTH : (i + 1) * WIDTH] = block.astype(bf16)
    block = jnp.concatenate([inner[...].astype(f32), jnp.zeros((2, FF), f32)], axis=0)
    packed[:, 4 * WIDTH :] = block.astype(bf16)


def merge_rows(ids, own, r1, r2, r3, attn_out, inner_out):
    ordered = in_order([v[...].astype(f32) for v in (own, r1, r2, r3)], ids[12])
    width = 3 * WIDTH
    rows = jnp.concatenate([v[:6] for v in ordered], axis=0).astype(bf16)
    attn_out[:, :width] = rows[:, :width]
    inner_out[...] = rows[:, width:]
    row = jnp.concatenate([v[6:7, :128] for v in ordered], axis=1)
    first = lax.broadcasted_iota(jnp.int32, (24, 4 * 128), 0) == 0
    attn_out[:, width:] = jnp.where(first, jnp.broadcast_to(row, (24, 4 * 128)), 0.0).astype(bf16)


def stack_rows(ids, own, r1, r2, r3, out):
    for d, piece in enumerate((own, r1, r2, r3)):
        out[lax.rem(ids[11] + RING - d, RING)] = piece[...]


def ahead(ids, axis, step):
    return lax.rem(ids[axis] + step, RING)


def sum_of(refs):
    total = refs[0][...].astype(f32)
    for ref in refs[1:]:
        total += ref[...].astype(f32)
    return total


def sum_blocks(ids, *refs):
    *parts, o0, o1, o2, o3, scratch = refs
    start = 0
    for mine, core in zip(parts[::2], parts[1::2]):
        end = start + mine.shape[2]
        scratch[:, start:end] = mine[0].astype(f32) + core[0].astype(f32)
        start = end
    for d, out in enumerate((o0, o1, o2, o3)):
        first = pl.multiple_of(ahead(ids, 11, d) * 24, 8)
        out[0] = scratch[pl.ds(first, 24), :].astype(bf16)


def sum_attention(ids, outer, mine, core, o0, o1, o2, o3, scratch):
    scratch[...] = mine[0].astype(f32) + core[0].astype(f32)
    for d, out in enumerate((o0, o1, o2, o3)):
        z = ahead(ids, 11, d)
        first = pl.multiple_of(z * 24, 8)
        out[0, :, : scratch.shape[1]] = scratch[pl.ds(first, 24), :].astype(bf16)
        out[0, :, scratch.shape[1] :] = outer[0, z]


def sum_outer(ids, mine, core, out):
    total = mine[0].astype(f32) + core[0].astype(f32)
    for z in range(RING):
        for y in range(RING):
            first = 96 * z + 24 * y
            out[y, 0, z] = total[first : first + 24].astype(bf16)


def sum_first(ids, value, out):
    for z in range(RING):
        out[0, z] = sum_of([value.at[y, 0, z] for y in range(RING)]).astype(bf16)


def split_rows(ids, p0, p1, p2, p3, o0, o1, o2, o3, *refs):
    *rest, scratch = refs
    width = o0.shape[2]
    total = sum_of([p.at[0] for p in (p0, p1, p2, p3)])
    if rest:
        rest[0][0] = total[:, width + 128 :].astype(bf16)
    for y in range(RING):
        vectors = total[y : y + 1, width : width + 128]
        row = jnp.concatenate([vectors, jnp.zeros((1, width - 128), f32)], axis=1)
        rows = total[6 * y : 6 * y + 6, :width]
        scratch[y] = jnp.concatenate([rows, row, jnp.zeros((1, width), f32)], axis=0)
    for d, out in enumerate((o0, o1, o2, o3)):
        out[0] = scratch[ahead(ids, 12, d)].astype(bf16)


LAST = FF + WIDTH + 3 * WIDTH + 3 * WIDTH


def join_flows(ids, i0, i1, i2, i3, a0, a1, a2, a3, outer, o0, o1, o2, o3, scratch):
    scratch[:, :, : FF + WIDTH] = sum_of((i0, i1, i2, i3))
    scratch[:, :, FF + WIDTH : FF + 4 * WIDTH] = sum_of((a0, a1, a2, a3))
    for x in range(RING):
        total = outer[x].astype(f32)
        for k in range(3):
            start = FF + (4 + k) * WIDTH
            scratch[x, :, start : start + WIDTH] = total[8 * k : 8 * k + 8]
    for d, out in enumerate((o0, o1, o2, o3)):
        out[...] = scratch[ahead(ids, 8, d)].astype(bf16)


def split_ffn(ids, p0, p1, p2, p3, inner, outer):
    for d, piece in enumerate((p0, p1, p2, p3)):
        inner[d] = piece[:, :MIXED]
        halves = [piece[:, MIXED + i * WIDTH : MIXED + (i + 1) * WIDTH].astype(f32) for i in range(2)]
        outer[d] = jnp.concatenate(halves, axis=0).astype(bf16)


def write_grads(ids, p0, p1, p2, p3, query, key, value, out, inner, outer, vectors):
    total = sum_of((p0, p1, p2, p3))
    inner[...] = total[:6, :FF]
    out[...] = total[:6, FF : FF + WIDTH]
    start = FF + WIDTH
    query[...] = total[:6, start : start + WIDTH]
    key[...] = total[:6, start + WIDTH : start + 2 * WIDTH]
    value[...] = total[:6, start + 2 * WIDTH : start + 3 * WIDTH]
    vectors[...] = jnp.concatenate([total[6:7, :128], total[6:7, start : start + 128]], axis=0)
    start += 3 * WIDTH
    for k in range(3):
        outer[8 * k : 8 * k + 8] = total[:, start + k * WIDTH : start + (k + 1) * WIDTH]


def whole(shape):
    return pl.BlockSpec(shape, lambda s, ids: (0,) * len(shape), pipeline_mode=pl.Buffered(1))


def sequence(s):
    return jnp.minimum(s, SEQ_DEV - 1)


DEALT_SPEC = pl.BlockSpec((GROUP, 1, PIECE, WIDTH), lambda s, ids: (0, sequence(s), 0, 0))


def by_rows(width):
    return pl.BlockSpec((SLOT, width), lambda s, ids: (sequence(s), 0))


def rows_of(width, kind):
    return jax.ShapeDtypeStruct((ROWS, width), kind)


EXP_SPEC = pl.BlockSpec((1, HEADS, SLOT, SLOT), lambda s, ids: (sequence(s), 0, 0, 0))
NORM_SPEC = pl.BlockSpec((1, 16, SLOT), lambda s, ids: (sequence(s), 0, 0))
RETURN_SPEC = pl.BlockSpec((GROUP, 2, 1, PIECE, WIDTH), lambda s, ids: (0, 0, sequence(s), 0, 0))
RETURN_SHAPE = jax.ShapeDtypeStruct((GROUP, 2, SEQ_DEV, PIECE, WIDTH), bf16)


def by_columns(height):
    return pl.BlockSpec((height, SLOT), lambda s, ids: (0, sequence(s)))


def columns_of(height):
    return jax.ShapeDtypeStruct((height, ROWS), bf16)


def run(kernel, grid, ins, outs, operands, name, flops, moved, scratch=()):
    return pl.pallas_call(
        kernel,
        grid_spec=pltpu.PrefetchScalarGridSpec(
            num_scalar_prefetch=1,
            grid=grid,
            in_specs=ins,
            out_specs=[spec for spec, _ in outs],
            scratch_shapes=list(scratch),
        ),
        out_shape=[shape for _, shape in outs],
        compiler_params=pltpu.CompilerParams(
            vmem_limit_bytes=VMEM_LIMIT, dimension_semantics=("arbitrary",) * len(grid)
        ),
        cost_estimate=pl.CostEstimate(flops=flops, bytes_accessed=moved, transcendentals=0),
        name=name,
    )(*operands)


def out_rows(width, kind):
    return (by_rows(width), rows_of(width, kind))


def out_columns(height):
    return (by_columns(height), columns_of(height))


def out_whole(shape):
    return (whole(shape), jax.ShapeDtypeStruct(shape, f32))


ANYWHERE = pl.BlockSpec(memory_space=pl.ANY)
ATTENTION_SCRATCH = [pltpu.VMEM((RING, CORES, 96, PACKED), bf16)]


def call_forward(ids, dealt, weights, perm):
    return run(
        attention_forward,
        (SEQ_DEV,),
        [DEALT_SPEC] + [ANYWHERE] * 8 + [whole((32, 16))],
        [
            out_columns(WIDTH),
            out_rows(3 * WIDTH, bf16),
            (EXP_SPEC, jax.ShapeDtypeStruct((SEQ_DEV, HEADS, SLOT, SLOT), bf16)),
            (NORM_SPEC, jax.ShapeDtypeStruct((SEQ_DEV, 16, SLOT), f32)),
            out_columns(WIDTH),
            out_whole((8, WIDTH)),
            out_whole((1, FF)),
            out_whole((8, 128)),
        ],
        (ids, dealt, *weights, perm),
        "attention_forward",
        22 * 10**9,
        22 * 10**6,
        ATTENTION_SCRATCH + [pltpu.VMEM((32, PACKED - 3 * WIDTH), f32), pltpu.SemaphoreType.DMA((8,))],
    )


def halves(block, shape, where):
    return [(pl.BlockSpec(block, lambda s, ids: where(s)), jax.ShapeDtypeStruct(shape, bf16))] * 2


def call_ffn(ids, dealt, dealt_c, ctx_t, inner, outer, vec, bias_in):
    outer_rows = FF // GROUP
    inner_rows = WIDTH // GROUP
    first = SEQ_DEV
    second = first + RING
    return run(
        feed_forward,
        (second + FF_STEPS + 1,),
        [DEALT_SPEC] * 2
        + [whole((WIDTH, ROWS))]
        + [ANYWHERE] * 8
        + [whole((8, WIDTH)), whole((1, FF))],
        [out_rows(WIDTH, bf16), out_rows(WIDTH, f32), out_rows(WIDTH, bf16)]
        + halves(
            (1, outer_rows, WIDTH), (RING, outer_rows, WIDTH), lambda s: (jnp.clip(s - first, 0, RING - 1), 0, 0)
        )
        + halves(
            (RING, inner_rows, FF_STEP),
            (RING, inner_rows, FF),
            lambda s: (0, 0, jnp.clip(s - second, 0, FF_STEPS - 1)),
        )
        + halves((RING, inner_rows, WIDTH + 128), (RING, inner_rows, WIDTH + 128), lambda s: (0, 0, 0)),
        (ids, dealt, dealt_c, ctx_t, *inner, *outer, vec, bias_in),
        "feed_forward",
        50 * 10**9,
        40 * 10**6,
        [
            pltpu.VMEM((SLOT, FF), bf16),
            pltpu.VMEM((8, WIDTH), f32),
            pltpu.VMEM((1, FF), f32),
            pltpu.VMEM((RING, CORES, 2, 48, MIXED), bf16),
            pltpu.VMEM((RING, CORES, RING, 2, 48, WIDTH), bf16),
            pltpu.VMEM((SEQ_DEV, WIDTH, SLOT), bf16),
            pltpu.VMEM((SEQ_DEV, FF, SLOT), bf16),
            pltpu.VMEM((SEQ_DEV, SLOT, WIDTH), bf16),
            pltpu.VMEM((SEQ_DEV, FF_STEPS, SLOT, FF_STEP), bf16),
            pltpu.VMEM((SEQ_DEV, SLOT, WIDTH), bf16),
            pltpu.SemaphoreType.DMA((RING, RING)),
            pltpu.SemaphoreType.DMA((RING, RING, RING)),
        ],
    )


def call_backward(ids, dsum, dattn, qkv, expo, norm, ctx_t, x_t, dealt_c, layer, weights, inner):
    block = (RING, WIDTH // GROUP, 3 * WIDTH + 128)
    return run(
        attention_backward,
        (SEQ_DEV + 1,),
        [by_rows(WIDTH), by_rows(WIDTH), by_rows(3 * WIDTH), EXP_SPEC, NORM_SPEC, by_columns(WIDTH)]
        + [whole((WIDTH, ROWS)), DEALT_SPEC, by_rows(WIDTH)]
        + [ANYWHERE] * 12,
        [(RETURN_SPEC, RETURN_SHAPE)] + halves(block, block, lambda s: (0, 0, 0)),
        (ids, dsum, dattn, qkv, expo, norm, ctx_t, x_t, dealt_c, layer, *weights, *inner),
        "attention_backward",
        28 * 10**9,
        30 * 10**6,
        ATTENTION_SCRATCH
        + [
            pltpu.VMEM((RING, CORES, 2, 48, WIDTH), bf16),
            pltpu.VMEM((8, WIDTH), f32),
            pltpu.VMEM((SEQ_DEV, 3, SLOT, WIDTH), bf16),
            pltpu.SemaphoreType.DMA((8,)),
            pltpu.SemaphoreType.DMA((RING, RING)),
        ],
    )


def call_by_x(kernel, name, ids, pieces, at, out_shapes, out_at, scratch):
    count = len(out_shapes)

    def every_x(ids, *refs):
        ins, outs, rest = refs[: len(pieces)], refs[len(pieces) :][:count], refs[len(pieces) + count :]
        for x in range(RING):
            one = (pl.ds(x, 1),)
            kernel(
                ids,
                *[ref.at[(slice(None),) * at + one] for ref in ins],
                *[ref.at[(slice(None),) * out_at + one] for ref in outs],
                *rest,
            )

    return call_small(every_x, name, ids, pieces, *out_shapes, scratch=scratch)


def call_small(kernel, name, ids, pieces, *out_shapes, kind=bf16, scratch=()):
    def full(shape):
        return pl.BlockSpec(shape, lambda i, ids: (0,) * len(shape))

    return run(
        kernel,
        (1,),
        [full(piece.shape) for piece in pieces],
        [(full(shape), jax.ShapeDtypeStruct(shape, kind)) for shape in out_shapes],
        (ids, *pieces),
        name,
        10**6,
        6 * 10**6,
        [pltpu.VMEM(shape, f32) for shape in scratch],
    )


def shift(value, axis, step):
    size = CORES if axis == "core" else RING
    return lax.ppermute(value, axis, [(i, (i + step) % size) for i in range(size)])


def swap(value, axis):
    return lax.ppermute(value, axis, [(i, i ^ 1) for i in range(RING)])


def arrivals(value, axis):
    return [value] + [shift(value, axis, step) for step in (1, 2, 3)]


def both_cores(pieces):
    return [part for piece in pieces for part in (piece, shift(piece, "core", 1))]


def paired(value, axis):
    return in_half(value, swap(value, axis), axis)


def in_half(value, other, axis):
    even = lax.rem(lax.axis_index(axis), 2) == 0
    return jnp.where(even, value, other), jnp.where(even, other, value)


def hold(value, *others):
    return lax.optimization_barrier((value, *others))[0]


def send_ring(parts, axis):
    return [parts[0]] + [shift(parts[step], axis, step) for step in (1, 2, 3)]


def over(value, axis):
    return lax.all_to_all(value, axis, split_axis=0, concat_axis=0, tiled=True)


def body(
    tokens,
    cotangent,
    perm,
    lengths,
    drop,
    w_query,
    b_query,
    w_key,
    w_value,
    b_value,
    w_out,
    b_out,
    norm1_gain,
    norm1_bias,
    w_inner,
    b_inner,
    w_outer,
    b_outer,
    norm2_gain,
    norm2_bias,
):
    me_x = lax.axis_index("x")
    me_c = lax.axis_index("core")
    me_z = lax.axis_index("z")
    me_y = lax.axis_index("y")
    first = ((me_z * RING + me_y) * 8 + me_x * CORES + me_c) * SEQ_DEV
    places = jnp.stack([me_x, me_c, first, me_z, me_y]).astype(jnp.int32)
    places = jnp.pad(places, (8, 3))

    vectors = [b_query, b_value, b_out, norm1_gain, norm1_bias, b_outer, norm2_gain, norm2_bias, b_inner]
    vectors += [lengths.astype(bf16), drop.astype(bf16)]
    row = jnp.zeros((WIDTH,), bf16)
    start = 0
    for vector in vectors:
        end = start + vector.shape[0]
        row += jnp.pad(vector, (start, WIDTH - end))
        start = end
    (piece,) = call_small(
        pack_rows, "pack_rows", places, (w_query, w_key, w_value, w_out, w_inner, row[None]), (8, 4 * WIDTH + FF)
    )
    pieces_y = arrivals(piece, "y")
    dp = ("x", "core")
    dealt = (GROUP, SEQ_DEV, PIECE, WIDTH)
    dealt_x = over(tokens.reshape(dealt), dp)
    attn_y, inner_y = call_small(merge_rows, "merge_rows", places, pieces_y, (24, PACKED), (24, MIXED))
    (attn_zy,) = call_small(
        stack_rows, "stack_rows", places, arrivals(attn_y, "z"), (RING, 24, PACKED)
    )

    outer_pair = paired(w_outer, "y")
    ffn_x = arrivals(jnp.concatenate([hold(inner_y, dealt_x), *outer_pair], axis=1), "x")
    ffn_x[0] = hold(ffn_x[0], attn_zy)
    inner_x, outer_x = call_small(
        split_ffn, "split_ffn", places, ffn_x, (RING, 24, MIXED), (RING, 48, WIDTH)
    )
    attn_x = arrivals(hold(attn_zy, dealt_x).reshape(96, PACKED), "x")
    attn_pieces = both_cores(attn_x)
    inner_z = swap(inner_x, "z")
    outer_z = over(jnp.broadcast_to(outer_x[None], (RING, RING, 48, WIDTH)), "z")
    inner_z = jnp.concatenate(in_half(inner_x, hold(inner_z, attn_x[1]), "z"), axis=1)
    inner_far = shift(inner_z, "z", 2)
    outer_z = hold(outer_z, attn_x[1])
    outer_far = shift(outer_z, "y", 2)
    dealt_c = over(hold(cotangent, attn_x[1]).reshape(dealt), dp)

    x_t, qkv, expo, norm, ctx_t, vec, inner_bias, info = call_forward(
        places, dealt_x, attn_pieces, perm.reshape(32, 16)
    )
    ids = jnp.concatenate([info[:, 0].astype(jnp.int32), places[8:]])

    inner_pieces = both_cores([hold(inner_z, ctx_t, dealt_c), hold(inner_far, ctx_t)])
    outer_pieces = both_cores([hold(outer_z, ctx_t), hold(outer_far, ctx_t)])
    (
        layer, d_sum1, d_attn, outer_away, outer_mine, inner_away, inner_mine, out_away, out_mine
    ) = call_ffn(ids, dealt_x, dealt_c, ctx_t, inner_pieces, outer_pieces, vec, inner_bias)

    inner_core = shift(inner_away, "core", 1)
    out_core = shift(out_away, "core", 1)
    outer_core = shift(hold(outer_away, out_core), "core", 1)
    inner_width = FF + WIDTH + 128
    inner_parts = call_by_x(
        sum_blocks, "sum_blocks", places, (inner_mine, inner_core, out_mine, out_core), 0,
        [(RING, 24, inner_width)] * RING, 0, [(96, inner_width)],
    )
    (outer_sum,) = call_by_x(
        sum_outer, "sum_outer", hold(places, inner_parts[0]), (outer_mine, outer_core), 0,
        [(RING, RING, RING, 24, WIDTH)], 1, [],
    )
    inner_parts = send_ring(inner_parts, "z")
    outer_y = over(outer_sum, "y")

    d_sum1, d_attn = lax.optimization_barrier((d_sum1, d_attn, inner_parts[0], outer_sum))[:2]
    back, attn_away, attn_mine = call_backward(
        ids, d_sum1, d_attn, qkv, expo, norm, ctx_t, x_t, dealt_c, layer, attn_pieces, inner_pieces
    )

    attn_core = shift(hold(attn_away, outer_y, *inner_parts[1:]), "core", 1)
    (outer_z,) = call_by_x(
        sum_first, "sum_first", hold(places, attn_away), (hold(outer_y, attn_away),), 1,
        [(RING, RING, 24, WIDTH)], 0, [],
    )
    attn_width = 3 * WIDTH + 128
    attn_parts = call_by_x(
        sum_attention, "sum_attention", places, (outer_z, attn_mine, attn_core), 0,
        [(RING, 24, attn_width + WIDTH)] * RING, 0, [(96, attn_width)],
    )
    attn_first = attn_parts[0]
    attn_parts = send_ring(attn_parts, "z")
    back = over(hold(back, outer_z), dp)

    inner_parts = [hold(p, attn_first) for p in inner_parts]
    inner_parts = call_by_x(
        split_rows, "split_rows", places, inner_parts, 0,
        [(RING, 8, FF + WIDTH)] * RING, 0, [(RING, 8, FF + WIDTH)],
    )
    *attn_parts, outer_z = call_by_x(
        split_rows, "split_rows", hold(places, inner_parts[0]), attn_parts, 0,
        [(RING, 8, 3 * WIDTH)] * RING + [(RING, 24, WIDTH)], 0, [(RING, 8, 3 * WIDTH)],
    )
    inner_parts = send_ring(inner_parts, "y")
    attn_parts = send_ring(attn_parts, "y")
    last = call_small(
        join_flows, "join_flows", places, [*inner_parts, *attn_parts, outer_z], *[(8, LAST)] * 4,
        scratch=[(RING, 8, LAST)],
    )
    back = hold(back, last[0])
    layer_final = back[:, 0].reshape(GROUP * SEQ_DEV, PIECE, WIDTH)
    grad_final = back[:, 1].reshape(GROUP * SEQ_DEV, PIECE, WIDTH)
    square = (6, WIDTH)
    grad_query, grad_key, grad_value, grad_out, grad_inner, grad_outer, vectors = call_small(
        write_grads, "write_grads", hold(places, layer_final), send_ring(last, "x"),
        square, square, square, square, (6, FF), (24, WIDTH), (2, 128), kind=f32,
    )
    ffn_vectors = [vectors[0, 6 * i : 6 * i + 6] for i in range(6)]
    return (
        layer_final,
        grad_final,
        grad_query,
        vectors[1, :6],
        grad_key,
        grad_value,
        vectors[1, 6:12],
        grad_out,
        ffn_vectors[5],
        ffn_vectors[3],
        ffn_vectors[4],
        grad_inner,
        vectors[0, 36:60],
        grad_outer,
        ffn_vectors[0],
        ffn_vectors[1],
        ffn_vectors[2],
    )


def solution(mesh):
    chips = Mesh(mesh.devices.reshape(RING, CORES, RING, RING), ("x", "core", "z", "y"))
    dp = ("x", "core")
    fsdp = ("z", "y")
    every = P(dp + fsdp)
    rows = P(dp + fsdp, None)
    whole_rows = P(fsdp, dp, None)
    return jax.shard_map(
        body,
        mesh=chips,
        in_specs=(
            whole_rows, whole_rows, P(), every, every,
            rows, every, rows, rows, every, rows, every, every, every,
            rows, every, rows, every, every, every,
        ),
        out_specs=(
            whole_rows, whole_rows,
            rows, every, rows, rows, every, rows, every, every, every,
            rows, every, rows, every, every, every,
        ),
        check_vma=False,
    )
```

```python
import functools
import jax
import jax.numpy as jnp
from jax import lax
from jax.experimental import pallas as pl
from jax.experimental.pallas import tpu as pltpu
from jax.sharding import Mesh
from jax.sharding import PartitionSpec as P

HEADS = 12
HEAD = 64
WIDTH = 768
FF = 3072
SLOT = 256
SEQ_DEV = 4
RING = 4
CORES = 2
PIECE = 32
GROUP = RING * CORES
ROWS = SEQ_DEV * SLOT
PAIR = 2 * HEAD
PACKED = 3 * WIDTH + 512
MIXED = WIDTH + FF

epsilon = 1e-05
bf16 = jnp.bfloat16
f32 = jnp.float32
MIB = 1024 * 1024

TN = (((0,), (0,)), ((), ()))
NT = (((1,), (1,)), ((), ()))


def mm(a, b):
    return jnp.dot(a, b, preferred_element_type=f32)


def mm_nt(a, b):
    return lax.dot_general(a, b, NT, preferred_element_type=f32)


def mm_tn(a, b):
    return lax.dot_general(a, b, TN, preferred_element_type=f32)


def joined(ref):
    return ref[...].reshape(SLOT, WIDTH)


def spread(extras, start, width):
    total = 128 * width
    group = lax.broadcasted_iota(jnp.int32, (32, total), 0)
    owner = lax.broadcasted_iota(jnp.int32, (32, total), 1) // width
    pick = lax.broadcasted_iota(jnp.int32, (width, total), 0)
    within = lax.rem(lax.broadcasted_iota(jnp.int32, (width, total), 1), width)
    chosen = (pick == within).astype(bf16)
    out = jnp.zeros((32, total), f32)
    for y in range(RING):
        values = extras[:, 128 * y + start : 128 * y + start + width].astype(bf16)
        out += jnp.where(owner == group * RING + y, mm(values, chosen), 0.0)
    return jnp.sum(out, axis=0, keepdims=True)


def gather_back(vectors):
    values = jnp.zeros((128, 128), f32)
    start = 0
    for vector in vectors:
        total = vector.shape[1]
        width = total // 128
        owner = lax.broadcasted_iota(jnp.int32, (128, total), 1) // width
        mine = owner == lax.broadcasted_iota(jnp.int32, (128, total), 0)
        within = lax.rem(lax.broadcasted_iota(jnp.int32, (total, 128), 0), width)
        column = lax.broadcasted_iota(jnp.int32, (total, 128), 1)
        spots = (column == within + start).astype(bf16)
        values += mm(jnp.where(mine, vector, 0.0).astype(bf16), spots)
        start += width
    row = lax.broadcasted_iota(jnp.int32, (WIDTH, 128), 0)
    device = lax.broadcasted_iota(jnp.int32, (WIDTH, 128), 1)
    within = lax.rem(row, 24)
    picks = (within < RING) & (row // 24 * RING + within == device)
    return mm(picks.astype(bf16), values.astype(bf16)).astype(bf16)


def attention_copies(ids, pieces, w, sems):
    copies = []
    for i, piece in enumerate(pieces):
        x = lax.rem(ids[8] + RING - i // 2, RING)
        c = ids[9] if i % 2 == 0 else 1 - ids[9]
        copies.append(pltpu.make_async_copy(piece, w.at[x, c], sems.at[i]))
    return copies


def half_of(ids, i):
    c = ids[9] if i % 2 == 0 else 1 - ids[9]
    return c, ids[11] // 2 if i // 2 == 0 else 1 - ids[11] // 2


def columns(w, start, end):
    return w[:, :, :, start:end].reshape(WIDTH, end - start)


def attention_forward(
    ids, x_in, p0, p1, p2, p3, p4, p5, p6, p7, perm,
    xt_out, qkv_out, exp_out, norm_out, ctxt_out, vec, bias_out, info,
    w, extras, sems,
):
    s = pl.program_id(0)

    @pl.when(s == 0)
    def _():
        copies = attention_copies(ids, (p0, p1, p2, p3, p4, p5, p6, p7), w, sems)
        for copy in copies:
            copy.start()
        for copy in copies:
            copy.wait()
        rows = columns(w, 3 * WIDTH, PACKED).astype(f32).reshape(32, 24, PACKED - 3 * WIDTH)
        extras[...] = jnp.sum(rows, axis=1)
        for i in range(8):
            vec[i : i + 1] = spread(extras, 6 * i, 6)
        bias_out[...] = spread(extras, 48, 24)

    length = jnp.zeros((1, 1), f32)
    dropped = jnp.zeros((1, 1), f32)
    for y in range(RING):
        hit = perm[:, RING * y : RING * y + 4] == ids[10] + s
        length += jnp.sum(jnp.where(hit, extras[:, 128 * y + 72 : 128 * y + 76], 0.0), keepdims=True)
        dropped += jnp.sum(jnp.where(hit, extras[:, 128 * y + 76 : 128 * y + 80], 0.0), keepdims=True)
    line = lax.broadcasted_iota(jnp.int32, (8, 128), 0)
    info[...] = jnp.where(line == s, length, jnp.where(line == s + 4, dropped, info[...]))

    x = joined(x_in)
    xt_out[...] = x.T
    q = ((mm(x, columns(w, 0, WIDTH)) + vec[0:1]).astype(bf16).astype(f32) * HEAD**-0.5).astype(bf16)
    k = mm(x, columns(w, WIDTH, 2 * WIDTH)).astype(bf16)
    v = (mm(x, columns(w, 2 * WIDTH, 3 * WIDTH)) + vec[1:2]).astype(bf16)
    qkv_out[:, :WIDTH] = q
    qkv_out[:, WIDTH : 2 * WIDTH] = k
    qkv_out[:, 2 * WIDTH :] = v
    q_t = q.T
    v_t = v.T
    keys = lax.broadcasted_iota(jnp.int32, (SLOT, 1), 0).astype(f32)
    bias = jnp.where(keys < length, 0.0, -1e30)
    low = lax.broadcasted_iota(jnp.int32, (SLOT, PAIR), 1) < HEAD
    ctx_t = []
    for h in range(HEADS):
        p = h // 2 * PAIR
        k_pair = k[:, p : p + PAIR]
        k_one = jnp.where(low if h % 2 == 0 else ~low, k_pair, jnp.zeros_like(k_pair))
        scores = mm(k_one, q_t[p : p + PAIR]) + bias
        top = jnp.max(scores, axis=0, keepdims=True)
        expo = jnp.exp(scores - top)
        inverse = 1.0 / jnp.sum(expo, axis=0, keepdims=True)
        norm_out[0, h : h + 1, :] = inverse
        expo = expo.astype(bf16)
        exp_out[0, h] = expo
        ctx_t.append(mm(v_t[h * HEAD : (h + 1) * HEAD], expo) * inverse)
    ctx_t = jnp.concatenate(ctx_t, axis=0).astype(bf16)
    ctxt_out[...] = ctx_t


def row_mean(v):
    return jnp.mean(v, axis=-1, keepdims=True)


def normalised(z):
    center = z - row_mean(z)
    r = lax.rsqrt(row_mean(center * center) + epsilon)
    return center * r, r


def norm_back(dy, zhat, r, gain):
    e = dy * gain
    return r * (e - row_mean(e) - zhat * row_mean(e * zhat))


def col_sum(v):
    return jnp.sum(v, axis=0, keepdims=True)


FF_STEP = 768
FF_STEPS = FF // FF_STEP


def cut_cores(ids, value, away, mine):
    blocks, rows, _ = away.shape
    first = ids[9] == 0
    for x in range(blocks):
        even = value[2 * x * rows : (2 * x + 1) * rows]
        odd = value[(2 * x + 1) * rows : (2 * x + 2) * rows]
        away[x] = jnp.where(first, odd, even)
        mine[x] = jnp.where(first, even, odd)


def feed_forward(
    ids, x_in, c_in, ctx_t, i0, i1, i2, i3, j0, j1, j2, j3, vec, bias_in,
    layer_out, dsum_out, dattn_out, outer_away, outer_mine, inner_away, inner_mine, out_away, out_mine,
    slope, vec_grad, bias_grad, w_in, w_out, hid_t, act_t, d_branches, d_inners, d_attns, in_sems, out_sems,
):
    s = pl.program_id(0)

    @pl.when(s == 0)
    def _():
        vec_grad[...] = jnp.zeros_like(vec_grad)
        bias_grad[...] = jnp.zeros_like(bias_grad)
        copies = []
        for i, (piece, late) in enumerate(zip((i0, i1, i2, i3), (j0, j1, j2, j3))):
            c, z_half = half_of(ids, i)
            y_half = ids[12] // 2 if i // 2 == 0 else 1 - ids[12] // 2
            for d in range(RING):
                x = lax.rem(ids[8] + RING - d, RING)
                copies.append(pltpu.make_async_copy(piece.at[d], w_in.at[x, c, z_half], in_sems.at[i, d]))
                for n in range(RING):
                    target = w_out.at[x, c, n, y_half]
                    copies.append(pltpu.make_async_copy(late.at[n, d], target, out_sems.at[i, d, n]))
        for copy in copies:
            copy.start()
        for copy in copies:
            copy.wait()

    def inner_columns(n):
        return w_in[:, :, :, :, WIDTH + n * FF_STEP : WIDTH + (n + 1) * FF_STEP].reshape(WIDTH, FF_STEP)

    def outer_rows(n):
        return w_out[n].reshape(FF_STEP, WIDTH)

    @pl.when(s < SEQ_DEV)
    def _():
        x = joined(x_in).astype(f32)
        context = ctx_t[:, pl.ds(pl.multiple_of(s * SLOT, SLOT), SLOT)].T
        attn_out = mm(context, w_in[:, :, :, :, :WIDTH].reshape(WIDTH, WIDTH)) + vec[2:3]
        zhat1, r1 = normalised(x + attn_out)
        hidden = zhat1 * vec[3:4] + vec[4:5]
        hid_low = hidden.astype(bf16)
        hid_t[s] = hid_low.T
        branch = jnp.broadcast_to(vec[5:6], (SLOT, WIDTH))
        for n in range(FF_STEPS):
            cols = slice(n * FF_STEP, (n + 1) * FF_STEP)
            inner = mm(hid_low, inner_columns(n)) + bias_in[0:1, cols]
            half = 0.5 * lax.erf(inner * 0.7071067811865476) + 0.5
            bell = 0.3989422804014327 * jnp.exp(-0.5 * (inner * inner))
            act = (inner * half).astype(bf16)
            act_t[s, cols, :] = act.T
            slope[:, cols] = (half + inner * bell).astype(bf16)
            branch += mm(act, outer_rows(n))
        zhat2, r2 = normalised(hidden + branch)
        gain2 = vec[6:7]
        normed = zhat2 * gain2 + vec[7:8]
        valid = (lax.broadcasted_iota(jnp.int32, (SLOT, 1), 0) < ids[s]).astype(f32)
        keep = ids[4 + s] == 0
        layer_out[...] = (jnp.where(keep, normed, x) * valid).astype(bf16)
        dy = joined(c_in).astype(f32) * jnp.where(keep, valid, 0.0)
        vec_grad[1:2] += col_sum(dy * zhat2)
        vec_grad[2:3] += col_sum(dy)
        d_sum2 = norm_back(dy, zhat2, r2, gain2)
        d_branch = d_sum2.astype(bf16)
        d_branches[s] = d_branch
        vec_grad[0:1] += col_sum(d_branch.astype(f32))
        d_hidden = d_sum2
        for n in range(FF_STEPS):
            cols = slice(n * FF_STEP, (n + 1) * FF_STEP)
            d_act = mm_nt(d_branch, outer_rows(n))
            d_inner = (d_act * slope[:, cols].astype(f32)).astype(bf16)
            d_inners[s, n] = d_inner
            bias_grad[0:1, cols] += col_sum(d_inner.astype(f32))
            d_hidden += mm_nt(d_inner, inner_columns(n))
        vec_grad[3:4] += col_sum(d_hidden * zhat1)
        vec_grad[4:5] += col_sum(d_hidden)
        d_sum1 = norm_back(d_hidden, zhat1, r1, vec[3:4])
        dsum_out[...] = d_sum1
        d_attn = d_sum1.astype(bf16)
        dattn_out[...] = d_attn
        d_attns[s] = d_attn
        vec_grad[5:6] += col_sum(d_attn.astype(f32))

    @pl.when((s >= SEQ_DEV) & (s < SEQ_DEV + RING))
    def _():
        rows = pl.ds(pl.multiple_of((s - SEQ_DEV) * FF_STEP, FF_STEP), FF_STEP)
        value = mm(act_t[0, rows, :], d_branches[0])
        for i in range(1, SEQ_DEV):
            value += mm(act_t[i, rows, :], d_branches[i])
        cut_cores(ids, value.astype(bf16), outer_away, outer_mine)

    @pl.when((s >= SEQ_DEV + RING) & (s < SEQ_DEV + RING + FF_STEPS))
    def _():
        n = s - SEQ_DEV - RING
        value = mm(hid_t[0], d_inners[0, n])
        for i in range(1, SEQ_DEV):
            value += mm(hid_t[i], d_inners[i, n])
        cut_cores(ids, value.astype(bf16), inner_away, inner_mine)

    @pl.when(s == SEQ_DEV + RING + FF_STEPS)
    def _():
        value = mm(ctx_t[:, :SLOT], d_attns[0])
        for i in range(1, SEQ_DEV):
            value += mm(ctx_t[:, i * SLOT : (i + 1) * SLOT], d_attns[i])
        block = gather_back([vec_grad[i : i + 1] for i in range(6)] + [bias_grad[...]])
        cut_cores(ids, jnp.concatenate([value.astype(bf16), block], axis=1), out_away, out_mine)


def attention_backward(
    ids, dsum, dattn, qkv, exp_in, norm_in, ctxt_in, x_t, c_in, layer_in, p0, p1, p2, p3, p4, p5, p6, p7, i0, i1, i2, i3,
    back_out, attn_away, attn_mine,
    w, w_out, vec_grad, d_qkv, sems, out_sems,
):
    s = pl.program_id(0)

    @pl.when(s == 0)
    def _():
        vec_grad[...] = jnp.zeros_like(vec_grad)
        copies = attention_copies(ids, (p0, p1, p2, p3, p4, p5, p6, p7), w, sems)
        for i, piece in enumerate((i0, i1, i2, i3)):
            c, z_half = half_of(ids, i)
            for d in range(RING):
                x = lax.rem(ids[8] + RING - d, RING)
                source = piece.at[d, :, pl.ds(0, WIDTH)]
                copies.append(pltpu.make_async_copy(source, w_out.at[x, c, z_half], out_sems.at[i, d]))
        for copy in copies:
            copy.start()
        for copy in copies:
            copy.wait()

    @pl.when(s < SEQ_DEV)
    def _():
        d_sum1 = dsum[...]
        dctx_t = mm_nt(dattn[...], w_out[...].reshape(WIDTH, WIDTH)).T
        ctx_t = ctxt_in[...].astype(f32)
        k_t = qkv[:, WIDTH : 2 * WIDTH].T
        scaled = []
        deltas = []
        for h in range(HEADS):
            rows = slice(h * HEAD, (h + 1) * HEAD)
            one = (dctx_t[rows] * norm_in[0, h : h + 1, :]).astype(bf16)
            scaled.append(one)
            deltas.append(col_sum(one.astype(f32) * ctx_t[rows]))
        dctx_t = jnp.concatenate(scaled, axis=0)
        dctx = dctx_t.T
        low = lax.broadcasted_iota(jnp.int32, (SLOT, PAIR), 1) < HEAD
        dq_t = []
        for p in range(0, WIDTH, PAIR):
            cols = slice(p, p + PAIR)
            q_pair = qkv[:, cols]
            v_pair = qkv[:, 2 * WIDTH + p : 2 * WIDTH + p + PAIR]
            dks = []
            dvs = []
            for half in range(2):
                h = p // HEAD + half
                v_one = jnp.where(low if half == 0 else ~low, v_pair, jnp.zeros_like(v_pair))
                d_probs = mm(v_one, dctx_t[cols]) - deltas[h]
                expo = exp_in[0, h]
                d_scores = (expo.astype(f32) * d_probs).astype(bf16)
                dvs.append(mm(expo, dctx[:, cols]))
                dks.append(mm(d_scores, q_pair))
                dq_t.append(mm(k_t[h * HEAD : (h + 1) * HEAD], d_scores))
            d_qkv[s, 1, :, cols] = jnp.where(low, dks[0], dks[1]).astype(bf16)
            d_qkv[s, 2, :, cols] = jnp.where(low, dvs[0], dvs[1]).astype(bf16)
        dq = (jnp.concatenate(dq_t, axis=0).T * HEAD**-0.5).astype(bf16)
        d_qkv[s, 0] = dq
        vec_grad[0:1] += col_sum(dq.astype(f32))
        vec_grad[1:2] += col_sum(d_qkv[s, 2].astype(f32))
        d_in = d_sum1
        for n in range(3):
            d_in += mm_nt(d_qkv[s, n], columns(w, n * WIDTH, (n + 1) * WIDTH))
        valid = (lax.broadcasted_iota(jnp.int32, (SLOT, 1), 0) < ids[s]).astype(f32)
        upstream = joined(c_in).astype(f32) * valid
        keep = ids[4 + s] == 0
        grad = jnp.where(keep, d_in, upstream).astype(bf16)
        back_out[:, 0, 0] = layer_in[...].reshape(GROUP, PIECE, WIDTH)
        back_out[:, 1, 0] = grad.reshape(GROUP, PIECE, WIDTH)

    @pl.when(s == SEQ_DEV)
    def _():
        values = []
        for n in range(3):
            value = mm(x_t[:, :SLOT], d_qkv[0, n])
            for i in range(1, SEQ_DEV):
                value += mm(x_t[:, i * SLOT : (i + 1) * SLOT], d_qkv[i, n])
            values.append(value.astype(bf16))
        values.append(gather_back([vec_grad[0:1], vec_grad[1:2]]))
        cut_cores(ids, jnp.concatenate(values, axis=1), attn_away, attn_mine)


def in_order(values, me):
    ordered = []
    for j in range(RING):
        step = lax.rem(me + RING - j, RING)
        value = values[0]
        for d in (1, 2, 3):
            value = jnp.where(step == d, values[d], value)
        ordered.append(value)
    return ordered


def pack_rows(ids, query, key, value, out, inner, row, packed):
    for i, ref in enumerate((query, key, value, out)):
        block = jnp.concatenate([ref[...].astype(f32), jnp.zeros((2, WIDTH), f32)], axis=0)
        if i == 0:
            line = lax.broadcasted_iota(jnp.int32, (8, WIDTH), 0)
            block = jnp.where(line == 6, row[...].astype(f32), block)
        packed[:, i * WIDTH : (i + 1) * WIDTH] = block.astype(bf16)
    block = jnp.concatenate([inner[...].astype(f32), jnp.zeros((2, FF), f32)], axis=0)
    packed[:, 4 * WIDTH :] = block.astype(bf16)


def merge_rows(ids, own, r1, r2, r3, attn_out, inner_out):
    ordered = in_order([v[...].astype(f32) for v in (own, r1, r2, r3)], ids[12])
    width = 3 * WIDTH
    rows = jnp.concatenate([v[:6] for v in ordered], axis=0).astype(bf16)
    attn_out[:, :width] = rows[:, :width]
    inner_out[...] = rows[:, width:]
    row = jnp.concatenate([v[6:7, :128] for v in ordered], axis=1)
    first = lax.broadcasted_iota(jnp.int32, (24, 4 * 128), 0) == 0
    attn_out[:, width:] = jnp.where(first, jnp.broadcast_to(row, (24, 4 * 128)), 0.0).astype(bf16)


def stack_rows(ids, own, r1, r2, r3, out):
    for d, piece in enumerate((own, r1, r2, r3)):
        out[lax.rem(ids[11] + RING - d, RING)] = piece[...]


def ahead(ids, axis, step):
    return lax.rem(ids[axis] + step, RING)


def sum_of(refs):
    total = refs[0][...].astype(f32)
    for ref in refs[1:]:
        total += ref[...].astype(f32)
    return total


def sum_blocks(ids, *refs):
    *parts, o0, o1, o2, o3, scratch = refs
    start = 0
    for mine, core in zip(parts[::2], parts[1::2]):
        end = start + mine.shape[2]
        scratch[:, start:end] = mine[0].astype(f32) + core[0].astype(f32)
        start = end
    for d, out in enumerate((o0, o1, o2, o3)):
        first = pl.multiple_of(ahead(ids, 11, d) * 24, 8)
        out[0] = scratch[pl.ds(first, 24), :].astype(bf16)


def sum_attention(ids, outer, mine, core, o0, o1, o2, o3, scratch):
    scratch[...] = mine[0].astype(f32) + core[0].astype(f32)
    for d, out in enumerate((o0, o1, o2, o3)):
        z = ahead(ids, 11, d)
        first = pl.multiple_of(z * 24, 8)
        out[0, :, : scratch.shape[1]] = scratch[pl.ds(first, 24), :].astype(bf16)
        out[0, :, scratch.shape[1] :] = outer[0, z]


def sum_outer(ids, mine, core, out):
    total = mine[0].astype(f32) + core[0].astype(f32)
    for z in range(RING):
        for y in range(RING):
            first = 96 * z + 24 * y
            out[y, 0, z] = total[first : first + 24].astype(bf16)


def sum_first(ids, value, out):
    for z in range(RING):
        out[0, z] = sum_of([value.at[y, 0, z] for y in range(RING)]).astype(bf16)


def split_rows(ids, p0, p1, p2, p3, o0, o1, o2, o3, *refs):
    *rest, scratch = refs
    width = o0.shape[2]
    total = sum_of([p.at[0] for p in (p0, p1, p2, p3)])
    if rest:
        rest[0][0] = total[:, width + 128 :].astype(bf16)
    for y in range(RING):
        vectors = total[y : y + 1, width : width + 128]
        row = jnp.concatenate([vectors, jnp.zeros((1, width - 128), f32)], axis=1)
        rows = total[6 * y : 6 * y + 6, :width]
        scratch[y] = jnp.concatenate([rows, row, jnp.zeros((1, width), f32)], axis=0)
    for d, out in enumerate((o0, o1, o2, o3)):
        out[0] = scratch[ahead(ids, 12, d)].astype(bf16)


LAST = FF + WIDTH + 3 * WIDTH + 3 * WIDTH


def join_flows(ids, i0, i1, i2, i3, a0, a1, a2, a3, outer, o0, o1, o2, o3, scratch):
    scratch[:, :, : FF + WIDTH] = sum_of((i0, i1, i2, i3))
    scratch[:, :, FF + WIDTH : FF + 4 * WIDTH] = sum_of((a0, a1, a2, a3))
    for x in range(RING):
        total = outer[x].astype(f32)
        for k in range(3):
            start = FF + (4 + k) * WIDTH
            scratch[x, :, start : start + WIDTH] = total[8 * k : 8 * k + 8]
    for d, out in enumerate((o0, o1, o2, o3)):
        out[...] = scratch[ahead(ids, 8, d)].astype(bf16)


def split_ffn(ids, p0, p1, p2, p3, inner, outer):
    for d, piece in enumerate((p0, p1, p2, p3)):
        inner[d] = piece[:, :MIXED]
        halves = [piece[:, MIXED + i * WIDTH : MIXED + (i + 1) * WIDTH].astype(f32) for i in range(2)]
        outer[d] = jnp.concatenate(halves, axis=0).astype(bf16)


def write_grads(ids, p0, p1, p2, p3, query, key, value, out, inner, outer, vectors):
    total = sum_of((p0, p1, p2, p3))
    inner[...] = total[:6, :FF]
    out[...] = total[:6, FF : FF + WIDTH]
    start = FF + WIDTH
    query[...] = total[:6, start : start + WIDTH]
    key[...] = total[:6, start + WIDTH : start + 2 * WIDTH]
    value[...] = total[:6, start + 2 * WIDTH : start + 3 * WIDTH]
    vectors[...] = jnp.concatenate([total[6:7, :128], total[6:7, start : start + 128]], axis=0)
    start += 3 * WIDTH
    for k in range(3):
        outer[8 * k : 8 * k + 8] = total[:, start + k * WIDTH : start + (k + 1) * WIDTH]


def whole(shape):
    return pl.BlockSpec(shape, lambda s, ids: (0,) * len(shape), pipeline_mode=pl.Buffered(1))


def sequence(s):
    return jnp.minimum(s, SEQ_DEV - 1)


DEALT_SPEC = pl.BlockSpec((GROUP, 1, PIECE, WIDTH), lambda s, ids: (0, sequence(s), 0, 0))


def by_rows(width):
    return pl.BlockSpec((SLOT, width), lambda s, ids: (sequence(s), 0))


def rows_of(width, kind):
    return jax.ShapeDtypeStruct((ROWS, width), kind)


EXP_SPEC = pl.BlockSpec((1, HEADS, SLOT, SLOT), lambda s, ids: (sequence(s), 0, 0, 0))
NORM_SPEC = pl.BlockSpec((1, 16, SLOT), lambda s, ids: (sequence(s), 0, 0))
RETURN_SPEC = pl.BlockSpec((GROUP, 2, 1, PIECE, WIDTH), lambda s, ids: (0, 0, sequence(s), 0, 0))
RETURN_SHAPE = jax.ShapeDtypeStruct((GROUP, 2, SEQ_DEV, PIECE, WIDTH), bf16)


def by_columns(height):
    return pl.BlockSpec((height, SLOT), lambda s, ids: (0, sequence(s)))


def columns_of(height):
    return jax.ShapeDtypeStruct((height, ROWS), bf16)


def run(kernel, grid, ins, outs, operands, name, flops, moved, scratch, limit):
    return pl.pallas_call(
        kernel,
        grid_spec=pltpu.PrefetchScalarGridSpec(
            num_scalar_prefetch=1,
            grid=grid,
            in_specs=ins,
            out_specs=[spec for spec, _ in outs],
            scratch_shapes=list(scratch),
        ),
        out_shape=[shape for _, shape in outs],
        compiler_params=pltpu.CompilerParams(
            vmem_limit_bytes=limit * MIB, dimension_semantics=("arbitrary",) * len(grid)
        ),
        cost_estimate=pl.CostEstimate(flops=flops, bytes_accessed=moved, transcendentals=0),
        name=name,
    )(*operands)


def out_rows(width, kind):
    return (by_rows(width), rows_of(width, kind))


def out_columns(height):
    return (by_columns(height), columns_of(height))


def out_whole(shape):
    return (whole(shape), jax.ShapeDtypeStruct(shape, f32))


ANYWHERE = pl.BlockSpec(memory_space=pl.ANY)
ATTENTION_SCRATCH = [pltpu.VMEM((RING, CORES, 96, PACKED), bf16)]


def call_forward(ids, dealt, weights, perm):
    return run(
        attention_forward,
        (SEQ_DEV,),
        [DEALT_SPEC] + [ANYWHERE] * 8 + [whole((32, 16))],
        [
            out_columns(WIDTH),
            out_rows(3 * WIDTH, bf16),
            (EXP_SPEC, jax.ShapeDtypeStruct((SEQ_DEV, HEADS, SLOT, SLOT), bf16)),
            (NORM_SPEC, jax.ShapeDtypeStruct((SEQ_DEV, 16, SLOT), f32)),
            out_columns(WIDTH),
            out_whole((8, WIDTH)),
            out_whole((1, FF)),
            out_whole((8, 128)),
        ],
        (ids, dealt, *weights, perm),
        "attention_forward",
        22 * 10**9,
        22 * 10**6,
        ATTENTION_SCRATCH + [pltpu.VMEM((32, PACKED - 3 * WIDTH), f32), pltpu.SemaphoreType.DMA((8,))],
        28,
    )


def halves(block, shape, where):
    return [(pl.BlockSpec(block, lambda s, ids: where(s)), jax.ShapeDtypeStruct(shape, bf16))] * 2


def call_ffn(ids, dealt, dealt_c, ctx_t, inner, outer, vec, bias_in):
    outer_rows = FF // GROUP
    inner_rows = WIDTH // GROUP
    first = SEQ_DEV
    second = first + RING
    return run(
        feed_forward,
        (second + FF_STEPS + 1,),
        [DEALT_SPEC] * 2
        + [whole((WIDTH, ROWS))]
        + [ANYWHERE] * 8
        + [whole((8, WIDTH)), whole((1, FF))],
        [out_rows(WIDTH, bf16), out_rows(WIDTH, f32), out_rows(WIDTH, bf16)]
        + halves(
            (1, outer_rows, WIDTH), (RING, outer_rows, WIDTH), lambda s: (jnp.clip(s - first, 0, RING - 1), 0, 0)
        )
        + halves(
            (RING, inner_rows, FF_STEP),
            (RING, inner_rows, FF),
            lambda s: (0, 0, jnp.clip(s - second, 0, FF_STEPS - 1)),
        )
        + halves((RING, inner_rows, WIDTH + 128), (RING, inner_rows, WIDTH + 128), lambda s: (0, 0, 0)),
        (ids, dealt, dealt_c, ctx_t, *inner, *outer, vec, bias_in),
        "feed_forward",
        50 * 10**9,
        40 * 10**6,
        [
            pltpu.VMEM((SLOT, FF), bf16),
            pltpu.VMEM((8, WIDTH), f32),
            pltpu.VMEM((1, FF), f32),
            pltpu.VMEM((RING, CORES, 2, 48, MIXED), bf16),
            pltpu.VMEM((RING, CORES, RING, 2, 48, WIDTH), bf16),
            pltpu.VMEM((SEQ_DEV, WIDTH, SLOT), bf16),
            pltpu.VMEM((SEQ_DEV, FF, SLOT), bf16),
            pltpu.VMEM((SEQ_DEV, SLOT, WIDTH), bf16),
            pltpu.VMEM((SEQ_DEV, FF_STEPS, SLOT, FF_STEP), bf16),
            pltpu.VMEM((SEQ_DEV, SLOT, WIDTH), bf16),
            pltpu.SemaphoreType.DMA((RING, RING)),
            pltpu.SemaphoreType.DMA((RING, RING, RING)),
        ],
        54,
    )


def call_backward(ids, dsum, dattn, qkv, expo, norm, ctx_t, x_t, dealt_c, layer, weights, inner):
    block = (RING, WIDTH // GROUP, 3 * WIDTH + 128)
    return run(
        attention_backward,
        (SEQ_DEV + 1,),
        [by_rows(WIDTH), by_rows(WIDTH), by_rows(3 * WIDTH), EXP_SPEC, NORM_SPEC, by_columns(WIDTH)]
        + [whole((WIDTH, ROWS)), DEALT_SPEC, by_rows(WIDTH)]
        + [ANYWHERE] * 12,
        [(RETURN_SPEC, RETURN_SHAPE)] + halves(block, block, lambda s: (0, 0, 0)),
        (ids, dsum, dattn, qkv, expo, norm, ctx_t, x_t, dealt_c, layer, *weights, *inner),
        "attention_backward",
        28 * 10**9,
        30 * 10**6,
        ATTENTION_SCRATCH
        + [
            pltpu.VMEM((RING, CORES, 2, 48, WIDTH), bf16),
            pltpu.VMEM((8, WIDTH), f32),
            pltpu.VMEM((SEQ_DEV, 3, SLOT, WIDTH), bf16),
            pltpu.SemaphoreType.DMA((8,)),
            pltpu.SemaphoreType.DMA((RING, RING)),
        ],
        36,
    )


def call_by_x(kernel, name, ids, pieces, at, out_shapes, out_at, scratch):
    count = len(out_shapes)

    def every_x(ids, *refs):
        ins, outs, rest = refs[: len(pieces)], refs[len(pieces) :][:count], refs[len(pieces) + count :]
        for x in range(RING):
            one = (pl.ds(x, 1),)
            kernel(
                ids,
                *[ref.at[(slice(None),) * at + one] for ref in ins],
                *[ref.at[(slice(None),) * out_at + one] for ref in outs],
                *rest,
            )

    return call_small(every_x, name, ids, pieces, *out_shapes, scratch=scratch)


def call_small(kernel, name, ids, pieces, *out_shapes, kind=bf16, scratch=()):
    def full(shape):
        return pl.BlockSpec(shape, lambda i, ids: (0,) * len(shape))

    return run(
        kernel,
        (1,),
        [full(piece.shape) for piece in pieces],
        [(full(shape), jax.ShapeDtypeStruct(shape, kind)) for shape in out_shapes],
        (ids, *pieces),
        name,
        10**6,
        6 * 10**6,
        [pltpu.VMEM(shape, f32) for shape in scratch],
        30,
    )


def shift(value, axis, step):
    size = CORES if axis == "core" else RING
    return lax.ppermute(value, axis, [(i, (i + step) % size) for i in range(size)])


def swap(value, axis):
    return lax.ppermute(value, axis, [(i, i ^ 1) for i in range(RING)])


def arrivals(value, axis):
    return [value] + [shift(value, axis, step) for step in (1, 2, 3)]


def both_cores(pieces):
    return [part for piece in pieces for part in (piece, shift(piece, "core", 1))]


def paired(value, axis):
    return in_half(value, swap(value, axis), axis)


def in_half(value, other, axis):
    even = lax.rem(lax.axis_index(axis), 2) == 0
    return jnp.where(even, value, other), jnp.where(even, other, value)


def hold(value, *others):
    return lax.optimization_barrier((value, *others))[0]


def send_ring(parts, axis):
    return [parts[0]] + [shift(parts[step], axis, step) for step in (1, 2, 3)]


def over(value, axis):
    return lax.all_to_all(value, axis, split_axis=0, concat_axis=0, tiled=True)


def body(
    tokens,
    cotangent,
    perm,
    lengths,
    drop,
    w_query,
    b_query,
    w_key,
    w_value,
    b_value,
    w_out,
    b_out,
    norm1_gain,
    norm1_bias,
    w_inner,
    b_inner,
    w_outer,
    b_outer,
    norm2_gain,
    norm2_bias,
):
    me_x = lax.axis_index("x")
    me_c = lax.axis_index("core")
    me_z = lax.axis_index("z")
    me_y = lax.axis_index("y")
    first = ((me_z * RING + me_y) * 8 + me_x * CORES + me_c) * SEQ_DEV
    places = jnp.stack([me_x, me_c, first, me_z, me_y]).astype(jnp.int32)
    places = jnp.pad(places, (8, 3))

    vectors = [b_query, b_value, b_out, norm1_gain, norm1_bias, b_outer, norm2_gain, norm2_bias, b_inner]
    vectors += [lengths.astype(bf16), drop.astype(bf16)]
    row = jnp.zeros((WIDTH,), bf16)
    start = 0
    for vector in vectors:
        end = start + vector.shape[0]
        row += jnp.pad(vector, (start, WIDTH - end))
        start = end
    (piece,) = call_small(
        pack_rows, "pack_rows", places, (w_query, w_key, w_value, w_out, w_inner, row[None]), (8, 4 * WIDTH + FF)
    )
    pieces_y = arrivals(piece, "y")
    dp = ("x", "core")
    dealt = (GROUP, SEQ_DEV, PIECE, WIDTH)
    dealt_x = over(tokens.reshape(dealt), dp)
    attn_y, inner_y = call_small(merge_rows, "merge_rows", places, pieces_y, (24, PACKED), (24, MIXED))
    (attn_zy,) = call_small(
        stack_rows, "stack_rows", places, arrivals(attn_y, "z"), (RING, 24, PACKED)
    )

    outer_pair = paired(w_outer, "y")
    ffn_x = arrivals(jnp.concatenate([hold(inner_y, dealt_x), *outer_pair], axis=1), "x")
    ffn_x[0] = hold(ffn_x[0], attn_zy)
    inner_x, outer_x = call_small(
        split_ffn, "split_ffn", places, ffn_x, (RING, 24, MIXED), (RING, 48, WIDTH)
    )
    attn_x = arrivals(hold(attn_zy, dealt_x).reshape(96, PACKED), "x")
    attn_pieces = both_cores(attn_x)
    inner_z = swap(inner_x, "z")
    outer_z = over(jnp.broadcast_to(outer_x[None], (RING, RING, 48, WIDTH)), "z")
    inner_z = jnp.concatenate(in_half(inner_x, hold(inner_z, attn_x[1]), "z"), axis=1)
    inner_far = shift(inner_z, "z", 2)
    outer_z = hold(outer_z, attn_x[1])
    outer_far = shift(outer_z, "y", 2)
    dealt_c = over(hold(cotangent, attn_x[1]).reshape(dealt), dp)

    x_t, qkv, expo, norm, ctx_t, vec, inner_bias, info = call_forward(
        places, dealt_x, attn_pieces, perm.reshape(32, 16)
    )
    ids = jnp.concatenate([info[:, 0].astype(jnp.int32), places[8:]])

    inner_pieces = both_cores([hold(inner_z, ctx_t, dealt_c), hold(inner_far, ctx_t)])
    outer_pieces = both_cores([hold(outer_z, ctx_t), hold(outer_far, ctx_t)])
    (
        layer, d_sum1, d_attn, outer_away, outer_mine, inner_away, inner_mine, out_away, out_mine
    ) = call_ffn(ids, dealt_x, dealt_c, ctx_t, inner_pieces, outer_pieces, vec, inner_bias)

    inner_core = shift(inner_away, "core", 1)
    out_core = shift(out_away, "core", 1)
    outer_core = shift(hold(outer_away, out_core), "core", 1)
    inner_width = FF + WIDTH + 128
    inner_parts = call_by_x(
        sum_blocks, "sum_blocks", places, (inner_mine, inner_core, out_mine, out_core), 0,
        [(RING, 24, inner_width)] * RING, 0, [(96, inner_width)],
    )
    (outer_sum,) = call_by_x(
        sum_outer, "sum_outer", hold(places, inner_parts[0]), (outer_mine, outer_core), 0,
        [(RING, RING, RING, 24, WIDTH)], 1, [],
    )
    inner_parts = send_ring(inner_parts, "z")
    outer_y = over(outer_sum, "y")

    d_sum1, d_attn = lax.optimization_barrier((d_sum1, d_attn, inner_parts[0], outer_sum))[:2]
    back, attn_away, attn_mine = call_backward(
        ids, d_sum1, d_attn, qkv, expo, norm, ctx_t, x_t, dealt_c, layer, attn_pieces, inner_pieces
    )

    attn_core = shift(hold(attn_away, outer_y, *inner_parts[1:]), "core", 1)
    (outer_z,) = call_by_x(
        sum_first, "sum_first", hold(places, attn_away), (hold(outer_y, attn_away),), 1,
        [(RING, RING, 24, WIDTH)], 0, [],
    )
    attn_width = 3 * WIDTH + 128
    attn_parts = call_by_x(
        sum_attention, "sum_attention", places, (outer_z, attn_mine, attn_core), 0,
        [(RING, 24, attn_width + WIDTH)] * RING, 0, [(96, attn_width)],
    )
    attn_first = attn_parts[0]
    attn_parts = send_ring(attn_parts, "z")
    back = over(hold(back, outer_z), dp)

    inner_parts = [hold(p, attn_first) for p in inner_parts]
    inner_parts = call_by_x(
        split_rows, "split_rows", places, inner_parts, 0,
        [(RING, 8, FF + WIDTH)] * RING, 0, [(RING, 8, FF + WIDTH)],
    )
    *attn_parts, outer_z = call_by_x(
        split_rows, "split_rows", hold(places, inner_parts[0]), attn_parts, 0,
        [(RING, 8, 3 * WIDTH)] * RING + [(RING, 24, WIDTH)], 0, [(RING, 8, 3 * WIDTH)],
    )
    inner_parts = send_ring(inner_parts, "y")
    attn_parts = send_ring(attn_parts, "y")
    last = call_small(
        join_flows, "join_flows", places, [*inner_parts, *attn_parts, outer_z], *[(8, LAST)] * 4,
        scratch=[(RING, 8, LAST)],
    )
    back = hold(back, last[0])
    layer_final = back[:, 0].reshape(GROUP * SEQ_DEV, PIECE, WIDTH)
    grad_final = back[:, 1].reshape(GROUP * SEQ_DEV, PIECE, WIDTH)
    square = (6, WIDTH)
    grad_query, grad_key, grad_value, grad_out, grad_inner, grad_outer, vectors = call_small(
        write_grads, "write_grads", hold(places, layer_final), send_ring(last, "x"),
        square, square, square, square, (6, FF), (24, WIDTH), (2, 128), kind=f32,
    )
    ffn_vectors = [vectors[0, 6 * i : 6 * i + 6] for i in range(6)]
    return (
        layer_final,
        grad_final,
        grad_query,
        vectors[1, :6],
        grad_key,
        grad_value,
        vectors[1, 6:12],
        grad_out,
        ffn_vectors[5],
        ffn_vectors[3],
        ffn_vectors[4],
        grad_inner,
        vectors[0, 36:60],
        grad_outer,
        ffn_vectors[0],
        ffn_vectors[1],
        ffn_vectors[2],
    )


def solution(mesh):
    chips = Mesh(mesh.devices.reshape(RING, CORES, RING, RING), ("x", "core", "z", "y"))
    dp = ("x", "core")
    fsdp = ("z", "y")
    every = P(dp + fsdp)
    rows = P(dp + fsdp, None)
    whole_rows = P(fsdp, dp, None)
    return jax.shard_map(
        body,
        mesh=chips,
        in_specs=(
            whole_rows, whole_rows, P(), every, every,
            rows, every, rows, rows, every, rows, every, every, every,
            rows, every, rows, every, every, every,
        ),
        out_specs=(
            whole_rows, whole_rows,
            rows, every, rows, rows, every, rows, every, every, every,
            rows, every, rows, every, every, every,
        ),
        check_vma=False,
    )
```

```python
import functools
import jax
import jax.numpy as jnp
from jax import lax
from jax.experimental import pallas as pl
from jax.experimental.pallas import tpu as pltpu
from jax.sharding import Mesh
from jax.sharding import PartitionSpec as P

HEADS = 12
HEAD = 64
WIDTH = 768
FF = 3072
SLOT = 256
SEQ_DEV = 4
RING = 4
CORES = 2
PIECE = 32
GROUP = RING * CORES
ROWS = SEQ_DEV * SLOT
PAIR = 2 * HEAD
PACKED = 3 * WIDTH + 512
MIXED = WIDTH + FF

epsilon = 1e-05
bf16 = jnp.bfloat16
f32 = jnp.float32
MIB = 1024 * 1024

TN = (((0,), (0,)), ((), ()))
NT = (((1,), (1,)), ((), ()))


def mm(a, b):
    return jnp.dot(a, b, preferred_element_type=f32)


def mm_nt(a, b):
    return lax.dot_general(a, b, NT, preferred_element_type=f32)


def mm_tn(a, b):
    return lax.dot_general(a, b, TN, preferred_element_type=f32)


def joined(ref):
    return ref[...].reshape(SLOT, WIDTH)


def spread(extras, start, width):
    total = 128 * width
    group = lax.broadcasted_iota(jnp.int32, (32, total), 0)
    owner = lax.broadcasted_iota(jnp.int32, (32, total), 1) // width
    pick = lax.broadcasted_iota(jnp.int32, (width, total), 0)
    within = lax.rem(lax.broadcasted_iota(jnp.int32, (width, total), 1), width)
    chosen = (pick == within).astype(bf16)
    out = jnp.zeros((32, total), f32)
    for y in range(RING):
        values = extras[:, 128 * y + start : 128 * y + start + width].astype(bf16)
        out += jnp.where(owner == group * RING + y, mm(values, chosen), 0.0)
    return jnp.sum(out, axis=0, keepdims=True)


def gather_back(vectors):
    values = jnp.zeros((128, 128), f32)
    start = 0
    for vector in vectors:
        total = vector.shape[1]
        width = total // 128
        owner = lax.broadcasted_iota(jnp.int32, (128, total), 1) // width
        mine = owner == lax.broadcasted_iota(jnp.int32, (128, total), 0)
        within = lax.rem(lax.broadcasted_iota(jnp.int32, (total, 128), 0), width)
        column = lax.broadcasted_iota(jnp.int32, (total, 128), 1)
        spots = (column == within + start).astype(bf16)
        values += mm(jnp.where(mine, vector, 0.0).astype(bf16), spots)
        start += width
    row = lax.broadcasted_iota(jnp.int32, (WIDTH, 128), 0)
    device = lax.broadcasted_iota(jnp.int32, (WIDTH, 128), 1)
    within = lax.rem(row, 24)
    picks = (within < RING) & (row // 24 * RING + within == device)
    return mm(picks.astype(bf16), values.astype(bf16)).astype(bf16)


def attention_copies(ids, pieces, w, sems):
    copies = []
    for i, piece in enumerate(pieces):
        x = lax.rem(ids[8] + RING - i // 2, RING)
        c = ids[9] if i % 2 == 0 else 1 - ids[9]
        copies.append(pltpu.make_async_copy(piece, w.at[x, c], sems.at[i]))
    return copies


def half_of(ids, i):
    c = ids[9] if i % 2 == 0 else 1 - ids[9]
    return c, ids[11] // 2 if i // 2 == 0 else 1 - ids[11] // 2


def columns(w, start, end):
    return w[:, :, :, start:end].reshape(WIDTH, end - start)


def attention_forward(
    ids, x_in, p0, p1, p2, p3, p4, p5, p6, p7, perm,
    xt_out, qkv_out, exp_out, norm_out, ctxt_out, vec, bias_out, info,
    w, extras, sems,
):
    s = pl.program_id(0)

    @pl.when(s == 0)
    def _():
        copies = attention_copies(ids, (p0, p1, p2, p3, p4, p5, p6, p7), w, sems)
        for copy in copies:
            copy.start()
        for copy in copies:
            copy.wait()
        rows = columns(w, 3 * WIDTH, PACKED).astype(f32).reshape(32, 24, PACKED - 3 * WIDTH)
        extras[...] = jnp.sum(rows, axis=1)
        for i in range(8):
            vec[i : i + 1] = spread(extras, 6 * i, 6)
        bias_out[...] = spread(extras, 48, 24)

    length = jnp.zeros((1, 1), f32)
    dropped = jnp.zeros((1, 1), f32)
    for y in range(RING):
        hit = perm[:, RING * y : RING * y + 4] == ids[10] + s
        length += jnp.sum(jnp.where(hit, extras[:, 128 * y + 72 : 128 * y + 76], 0.0), keepdims=True)
        dropped += jnp.sum(jnp.where(hit, extras[:, 128 * y + 76 : 128 * y + 80], 0.0), keepdims=True)
    line = lax.broadcasted_iota(jnp.int32, (8, 128), 0)
    info[...] = jnp.where(line == s, length, jnp.where(line == s + 4, dropped, info[...]))

    x = joined(x_in)
    xt_out[...] = x.T
    q = ((mm(x, columns(w, 0, WIDTH)) + vec[0:1]).astype(bf16).astype(f32) * HEAD**-0.5).astype(bf16)
    k = mm(x, columns(w, WIDTH, 2 * WIDTH)).astype(bf16)
    v = (mm(x, columns(w, 2 * WIDTH, 3 * WIDTH)) + vec[1:2]).astype(bf16)
    qkv_out[:, :WIDTH] = q
    qkv_out[:, WIDTH : 2 * WIDTH] = k
    qkv_out[:, 2 * WIDTH :] = v
    q_t = q.T
    v_t = v.T
    keys = lax.broadcasted_iota(jnp.int32, (SLOT, 1), 0).astype(f32)
    bias = jnp.where(keys < length, 0.0, -1e30)
    low = lax.broadcasted_iota(jnp.int32, (SLOT, PAIR), 1) < HEAD
    ctx_t = []
    for h in range(HEADS):
        p = h // 2 * PAIR
        k_pair = k[:, p : p + PAIR]
        k_one = jnp.where(low if h % 2 == 0 else ~low, k_pair, jnp.zeros_like(k_pair))
        scores = mm(k_one, q_t[p : p + PAIR]) + bias
        top = jnp.max(scores, axis=0, keepdims=True)
        expo = jnp.exp(scores - top)
        inverse = 1.0 / jnp.sum(expo, axis=0, keepdims=True)
        norm_out[0, h : h + 1, :] = inverse
        expo = expo.astype(bf16)
        exp_out[0, h] = expo
        ctx_t.append(mm(v_t[h * HEAD : (h + 1) * HEAD], expo) * inverse)
    ctx_t = jnp.concatenate(ctx_t, axis=0).astype(bf16)
    ctxt_out[...] = ctx_t


def row_mean(v):
    return jnp.mean(v, axis=-1, keepdims=True)


def normalised(z):
    center = z - row_mean(z)
    r = lax.rsqrt(row_mean(center * center) + epsilon)
    return center * r, r


def norm_back(dy, zhat, r, gain):
    e = dy * gain
    return r * (e - row_mean(e) - zhat * row_mean(e * zhat))


def col_sum(v):
    return jnp.sum(v, axis=0, keepdims=True)


FF_STEP = 768
FF_STEPS = FF // FF_STEP


def cut_cores(ids, value, away, mine):
    blocks, rows, _ = away.shape
    first = ids[9] == 0
    for x in range(blocks):
        even = value[2 * x * rows : (2 * x + 1) * rows]
        odd = value[(2 * x + 1) * rows : (2 * x + 2) * rows]
        away[x] = jnp.where(first, odd, even)
        mine[x] = jnp.where(first, even, odd)


def feed_forward(
    ids, x_in, c_in, ctx_t, i0, i1, i2, i3, j0, j1, j2, j3, vec, bias_in,
    layer_out, dsum_out, dattn_out, outer_away, outer_mine, inner_away, inner_mine, out_away, out_mine,
    slope, vec_grad, bias_grad, w_in, w_out, hid_t, act_t, d_branches, d_inners, d_attns, in_sems, out_sems,
):
    s = pl.program_id(0)

    @pl.when(s == 0)
    def _():
        vec_grad[...] = jnp.zeros_like(vec_grad)
        bias_grad[...] = jnp.zeros_like(bias_grad)
        copies = []
        for i, (piece, late) in enumerate(zip((i0, i1, i2, i3), (j0, j1, j2, j3))):
            c, z_half = half_of(ids, i)
            y_half = ids[12] // 2 if i // 2 == 0 else 1 - ids[12] // 2
            for d in range(RING):
                x = lax.rem(ids[8] + RING - d, RING)
                copies.append(pltpu.make_async_copy(piece.at[d], w_in.at[x, c, z_half], in_sems.at[i, d]))
                for n in range(RING):
                    target = w_out.at[x, c, n, y_half]
                    copies.append(pltpu.make_async_copy(late.at[n, d], target, out_sems.at[i, d, n]))
        for copy in copies:
            copy.start()
        for copy in copies:
            copy.wait()

    def inner_columns(n):
        return w_in[:, :, :, :, WIDTH + n * FF_STEP : WIDTH + (n + 1) * FF_STEP].reshape(WIDTH, FF_STEP)

    def outer_rows(n):
        return w_out[n].reshape(FF_STEP, WIDTH)

    @pl.when(s < SEQ_DEV)
    def _():
        x = joined(x_in).astype(f32)
        context = ctx_t[:, pl.ds(pl.multiple_of(s * SLOT, SLOT), SLOT)].T
        attn_out = mm(context, w_in[:, :, :, :, :WIDTH].reshape(WIDTH, WIDTH)) + vec[2:3]
        zhat1, r1 = normalised(x + attn_out)
        hidden = zhat1 * vec[3:4] + vec[4:5]
        hid_low = hidden.astype(bf16)
        hid_t[s] = hid_low.T
        branch = jnp.broadcast_to(vec[5:6], (SLOT, WIDTH))
        for n in range(FF_STEPS):
            cols = slice(n * FF_STEP, (n + 1) * FF_STEP)
            inner = mm(hid_low, inner_columns(n)) + bias_in[0:1, cols]
            half = 0.5 * lax.erf(inner * 0.7071067811865476) + 0.5
            bell = 0.3989422804014327 * jnp.exp(-0.5 * (inner * inner))
            act = (inner * half).astype(bf16)
            act_t[s, cols, :] = act.T
            slope[:, cols] = (half + inner * bell).astype(bf16)
            branch += mm(act, outer_rows(n))
        zhat2, r2 = normalised(hidden + branch)
        gain2 = vec[6:7]
        normed = zhat2 * gain2 + vec[7:8]
        valid = (lax.broadcasted_iota(jnp.int32, (SLOT, 1), 0) < ids[s]).astype(f32)
        keep = ids[4 + s] == 0
        layer_out[...] = (jnp.where(keep, normed, x) * valid).astype(bf16)
        dy = joined(c_in).astype(f32) * jnp.where(keep, valid, 0.0)
        vec_grad[1:2] += col_sum(dy * zhat2)
        vec_grad[2:3] += col_sum(dy)
        d_sum2 = norm_back(dy, zhat2, r2, gain2)
        d_branch = d_sum2.astype(bf16)
        d_branches[s] = d_branch
        vec_grad[0:1] += col_sum(d_branch.astype(f32))
        d_hidden = d_sum2
        for n in range(FF_STEPS):
            cols = slice(n * FF_STEP, (n + 1) * FF_STEP)
            d_act = mm_nt(d_branch, outer_rows(n))
            d_inner = (d_act * slope[:, cols].astype(f32)).astype(bf16)
            d_inners[s, n] = d_inner
            bias_grad[0:1, cols] += col_sum(d_inner.astype(f32))
            d_hidden += mm_nt(d_inner, inner_columns(n))
        vec_grad[3:4] += col_sum(d_hidden * zhat1)
        vec_grad[4:5] += col_sum(d_hidden)
        d_sum1 = norm_back(d_hidden, zhat1, r1, vec[3:4])
        dsum_out[...] = d_sum1
        d_attn = d_sum1.astype(bf16)
        dattn_out[...] = d_attn
        d_attns[s] = d_attn
        vec_grad[5:6] += col_sum(d_attn.astype(f32))

    @pl.when((s >= SEQ_DEV) & (s < SEQ_DEV + RING))
    def _():
        rows = pl.ds(pl.multiple_of((s - SEQ_DEV) * FF_STEP, FF_STEP), FF_STEP)
        value = mm(act_t[0, rows, :], d_branches[0])
        for i in range(1, SEQ_DEV):
            value += mm(act_t[i, rows, :], d_branches[i])
        cut_cores(ids, value.astype(bf16), outer_away, outer_mine)

    @pl.when((s >= SEQ_DEV + RING) & (s < SEQ_DEV + RING + FF_STEPS))
    def _():
        n = s - SEQ_DEV - RING
        value = mm(hid_t[0], d_inners[0, n])
        for i in range(1, SEQ_DEV):
            value += mm(hid_t[i], d_inners[i, n])
        cut_cores(ids, value.astype(bf16), inner_away, inner_mine)

    @pl.when(s == SEQ_DEV + RING + FF_STEPS)
    def _():
        value = mm(ctx_t[:, :SLOT], d_attns[0])
        for i in range(1, SEQ_DEV):
            value += mm(ctx_t[:, i * SLOT : (i + 1) * SLOT], d_attns[i])
        block = gather_back([vec_grad[i : i + 1] for i in range(6)] + [bias_grad[...]])
        cut_cores(ids, jnp.concatenate([value.astype(bf16), block], axis=1), out_away, out_mine)


def attention_backward(
    ids, dsum, dattn, qkv, exp_in, norm_in, ctxt_in, x_t, c_in, layer_in, p0, p1, p2, p3, p4, p5, p6, p7, i0, i1, i2, i3,
    back_out, attn_away, attn_mine,
    w, w_out, vec_grad, d_qkv, sems, out_sems,
):
    s = pl.program_id(0)

    @pl.when(s == 0)
    def _():
        vec_grad[...] = jnp.zeros_like(vec_grad)
        copies = attention_copies(ids, (p0, p1, p2, p3, p4, p5, p6, p7), w, sems)
        for i, piece in enumerate((i0, i1, i2, i3)):
            c, z_half = half_of(ids, i)
            for d in range(RING):
                x = lax.rem(ids[8] + RING - d, RING)
                source = piece.at[d, :, pl.ds(0, WIDTH)]
                copies.append(pltpu.make_async_copy(source, w_out.at[x, c, z_half], out_sems.at[i, d]))
        for copy in copies:
            copy.start()
        for copy in copies:
            copy.wait()

    @pl.when(s < SEQ_DEV)
    def _():
        d_sum1 = dsum[...]
        dctx_t = mm_nt(dattn[...], w_out[...].reshape(WIDTH, WIDTH)).T
        ctx_t = ctxt_in[...].astype(f32)
        k_t = qkv[:, WIDTH : 2 * WIDTH].T
        scaled = []
        deltas = []
        for h in range(HEADS):
            rows = slice(h * HEAD, (h + 1) * HEAD)
            one = (dctx_t[rows] * norm_in[0, h : h + 1, :]).astype(bf16)
            scaled.append(one)
            deltas.append(col_sum(one.astype(f32) * ctx_t[rows]))
        dctx_t = jnp.concatenate(scaled, axis=0)
        dctx = dctx_t.T
        low = lax.broadcasted_iota(jnp.int32, (SLOT, PAIR), 1) < HEAD
        dq_t = []
        for p in range(0, WIDTH, PAIR):
            cols = slice(p, p + PAIR)
            q_pair = qkv[:, cols]
            v_pair = qkv[:, 2 * WIDTH + p : 2 * WIDTH + p + PAIR]
            dks = []
            dvs = []
            for half in range(2):
                h = p // HEAD + half
                v_one = jnp.where(low if half == 0 else ~low, v_pair, jnp.zeros_like(v_pair))
                d_probs = mm(v_one, dctx_t[cols]) - deltas[h]
                expo = exp_in[0, h]
                d_scores = (expo.astype(f32) * d_probs).astype(bf16)
                dvs.append(mm(expo, dctx[:, cols]))
                dks.append(mm(d_scores, q_pair))
                dq_t.append(mm(k_t[h * HEAD : (h + 1) * HEAD], d_scores))
            d_qkv[s, 1, :, cols] = jnp.where(low, dks[0], dks[1]).astype(bf16)
            d_qkv[s, 2, :, cols] = jnp.where(low, dvs[0], dvs[1]).astype(bf16)
        dq = (jnp.concatenate(dq_t, axis=0).T * HEAD**-0.5).astype(bf16)
        d_qkv[s, 0] = dq
        vec_grad[0:1] += col_sum(dq.astype(f32))
        vec_grad[1:2] += col_sum(d_qkv[s, 2].astype(f32))
        d_in = d_sum1
        for n in range(3):
            d_in += mm_nt(d_qkv[s, n], columns(w, n * WIDTH, (n + 1) * WIDTH))
        valid = (lax.broadcasted_iota(jnp.int32, (SLOT, 1), 0) < ids[s]).astype(f32)
        upstream = joined(c_in).astype(f32) * valid
        keep = ids[4 + s] == 0
        grad = jnp.where(keep, d_in, upstream).astype(bf16)
        back_out[:, 0, 0] = layer_in[...].reshape(GROUP, PIECE, WIDTH)
        back_out[:, 1, 0] = grad.reshape(GROUP, PIECE, WIDTH)

    @pl.when(s == SEQ_DEV)
    def _():
        values = []
        for n in range(3):
            value = mm(x_t[:, :SLOT], d_qkv[0, n])
            for i in range(1, SEQ_DEV):
                value += mm(x_t[:, i * SLOT : (i + 1) * SLOT], d_qkv[i, n])
            values.append(value.astype(bf16))
        values.append(gather_back([vec_grad[0:1], vec_grad[1:2]]))
        cut_cores(ids, jnp.concatenate(values, axis=1), attn_away, attn_mine)


def in_order(values, me):
    ordered = []
    for j in range(RING):
        step = lax.rem(me + RING - j, RING)
        value = values[0]
        for d in (1, 2, 3):
            value = jnp.where(step == d, values[d], value)
        ordered.append(value)
    return ordered


def pack_rows(ids, query, key, value, out, inner, row, packed):
    for i, ref in enumerate((query, key, value, out)):
        block = jnp.concatenate([ref[...].astype(f32), jnp.zeros((2, WIDTH), f32)], axis=0)
        if i == 0:
            line = lax.broadcasted_iota(jnp.int32, (8, WIDTH), 0)
            block = jnp.where(line == 6, row[...].astype(f32), block)
        packed[:, i * WIDTH : (i + 1) * WIDTH] = block.astype(bf16)
    block = jnp.concatenate([inner[...].astype(f32), jnp.zeros((2, FF), f32)], axis=0)
    packed[:, 4 * WIDTH :] = block.astype(bf16)


def merge_rows(ids, own, r1, r2, r3, attn_out, inner_out):
    ordered = in_order([v[...].astype(f32) for v in (own, r1, r2, r3)], ids[12])
    width = 3 * WIDTH
    rows = jnp.concatenate([v[:6] for v in ordered], axis=0).astype(bf16)
    attn_out[:, :width] = rows[:, :width]
    inner_out[...] = rows[:, width:]
    row = jnp.concatenate([v[6:7, :128] for v in ordered], axis=1)
    first = lax.broadcasted_iota(jnp.int32, (24, 4 * 128), 0) == 0
    attn_out[:, width:] = jnp.where(first, jnp.broadcast_to(row, (24, 4 * 128)), 0.0).astype(bf16)


def stack_rows(ids, own, r1, r2, r3, out):
    for d, piece in enumerate((own, r1, r2, r3)):
        out[lax.rem(ids[11] + RING - d, RING)] = piece[...]


def ahead(ids, axis, step):
    return lax.rem(ids[axis] + step, RING)


def sum_of(refs):
    total = refs[0][...].astype(f32)
    for ref in refs[1:]:
        total += ref[...].astype(f32)
    return total


def sum_blocks(ids, *refs):
    *parts, o0, o1, o2, o3, scratch = refs
    start = 0
    for mine, core in zip(parts[::2], parts[1::2]):
        end = start + mine.shape[2]
        scratch[:, start:end] = mine[0].astype(f32) + core[0].astype(f32)
        start = end
    for d, out in enumerate((o0, o1, o2, o3)):
        first = pl.multiple_of(ahead(ids, 11, d) * 24, 8)
        out[0] = scratch[pl.ds(first, 24), :].astype(bf16)


def sum_attention(ids, outer, mine, core, o0, o1, o2, o3, scratch):
    scratch[...] = mine[0].astype(f32) + core[0].astype(f32)
    for d, out in enumerate((o0, o1, o2, o3)):
        z = ahead(ids, 11, d)
        first = pl.multiple_of(z * 24, 8)
        out[0, :, : scratch.shape[1]] = scratch[pl.ds(first, 24), :].astype(bf16)
        out[0, :, scratch.shape[1] :] = outer[0, z]


def sum_outer(ids, mine, core, out):
    total = mine[0].astype(f32) + core[0].astype(f32)
    for z in range(RING):
        for y in range(RING):
            first = 96 * z + 24 * y
            out[y, 0, z] = total[first : first + 24].astype(bf16)


def sum_first(ids, value, out):
    for z in range(RING):
        out[0, z] = sum_of([value.at[y, 0, z] for y in range(RING)]).astype(bf16)


def split_rows(ids, p0, p1, p2, p3, o0, o1, o2, o3, *refs):
    *rest, scratch = refs
    width = o0.shape[2]
    total = sum_of([p.at[0] for p in (p0, p1, p2, p3)])
    if rest:
        rest[0][0] = total[:, width + 128 :].astype(bf16)
    for y in range(RING):
        vectors = total[y : y + 1, width : width + 128]
        row = jnp.concatenate([vectors, jnp.zeros((1, width - 128), f32)], axis=1)
        rows = total[6 * y : 6 * y + 6, :width]
        scratch[y] = jnp.concatenate([rows, row, jnp.zeros((1, width), f32)], axis=0)
    for d, out in enumerate((o0, o1, o2, o3)):
        out[0] = scratch[ahead(ids, 12, d)].astype(bf16)


LAST = FF + WIDTH + 3 * WIDTH + 3 * WIDTH


def join_flows(ids, i0, i1, i2, i3, a0, a1, a2, a3, outer, o0, o1, o2, o3, scratch):
    scratch[:, :, : FF + WIDTH] = sum_of((i0, i1, i2, i3))
    scratch[:, :, FF + WIDTH : FF + 4 * WIDTH] = sum_of((a0, a1, a2, a3))
    for x in range(RING):
        total = outer[x].astype(f32)
        for k in range(3):
            start = FF + (4 + k) * WIDTH
            scratch[x, :, start : start + WIDTH] = total[8 * k : 8 * k + 8]
    for d, out in enumerate((o0, o1, o2, o3)):
        out[...] = scratch[ahead(ids, 8, d)].astype(bf16)


def split_ffn(ids, p0, p1, p2, p3, inner, outer):
    for d, piece in enumerate((p0, p1, p2, p3)):
        inner[d] = piece[:, :MIXED]
        halves = [piece[:, MIXED + i * WIDTH : MIXED + (i + 1) * WIDTH].astype(f32) for i in range(2)]
        outer[d] = jnp.concatenate(halves, axis=0).astype(bf16)


def write_grads(ids, p0, p1, p2, p3, query, key, value, out, inner, outer, vectors):
    total = sum_of((p0, p1, p2, p3))
    inner[...] = total[:6, :FF]
    out[...] = total[:6, FF : FF + WIDTH]
    start = FF + WIDTH
    query[...] = total[:6, start : start + WIDTH]
    key[...] = total[:6, start + WIDTH : start + 2 * WIDTH]
    value[...] = total[:6, start + 2 * WIDTH : start + 3 * WIDTH]
    vectors[...] = jnp.concatenate([total[6:7, :128], total[6:7, start : start + 128]], axis=0)
    start += 3 * WIDTH
    for k in range(3):
        outer[8 * k : 8 * k + 8] = total[:, start + k * WIDTH : start + (k + 1) * WIDTH]


def whole(shape):
    return pl.BlockSpec(shape, lambda s, ids: (0,) * len(shape), pipeline_mode=pl.Buffered(1))


def sequence(s):
    return jnp.minimum(s, SEQ_DEV - 1)


DEALT_SPEC = pl.BlockSpec((GROUP, 1, PIECE, WIDTH), lambda s, ids: (0, sequence(s), 0, 0))


def by_rows(width):
    return pl.BlockSpec((SLOT, width), lambda s, ids: (sequence(s), 0))


def rows_of(width, kind):
    return jax.ShapeDtypeStruct((ROWS, width), kind)


EXP_SPEC = pl.BlockSpec((1, HEADS, SLOT, SLOT), lambda s, ids: (sequence(s), 0, 0, 0))
NORM_SPEC = pl.BlockSpec((1, 16, SLOT), lambda s, ids: (sequence(s), 0, 0))
RETURN_SPEC = pl.BlockSpec((GROUP, 2, 1, PIECE, WIDTH), lambda s, ids: (0, 0, sequence(s), 0, 0))
RETURN_SHAPE = jax.ShapeDtypeStruct((GROUP, 2, SEQ_DEV, PIECE, WIDTH), bf16)


def by_columns(height):
    return pl.BlockSpec((height, SLOT), lambda s, ids: (0, sequence(s)))


def columns_of(height):
    return jax.ShapeDtypeStruct((height, ROWS), bf16)


def run(kernel, grid, ins, outs, operands, name, flops, moved, scratch, limit):
    return pl.pallas_call(
        kernel,
        grid_spec=pltpu.PrefetchScalarGridSpec(
            num_scalar_prefetch=1,
            grid=grid,
            in_specs=ins,
            out_specs=[spec for spec, _ in outs],
            scratch_shapes=list(scratch),
        ),
        out_shape=[shape for _, shape in outs],
        compiler_params=pltpu.CompilerParams(
            vmem_limit_bytes=limit * MIB, dimension_semantics=("arbitrary",) * len(grid)
        ),
        cost_estimate=pl.CostEstimate(flops=flops, bytes_accessed=moved, transcendentals=0),
        name=name,
    )(*operands)


def out_rows(width, kind):
    return (by_rows(width), rows_of(width, kind))


def out_columns(height):
    return (by_columns(height), columns_of(height))


def out_whole(shape):
    return (whole(shape), jax.ShapeDtypeStruct(shape, f32))


ANYWHERE = pl.BlockSpec(memory_space=pl.ANY)
ATTENTION_SCRATCH = [pltpu.VMEM((RING, CORES, 96, PACKED), bf16)]


def call_forward(ids, dealt, weights, perm):
    return run(
        attention_forward,
        (SEQ_DEV,),
        [DEALT_SPEC] + [ANYWHERE] * 8 + [whole((32, 16))],
        [
            out_columns(WIDTH),
            out_rows(3 * WIDTH, bf16),
            (EXP_SPEC, jax.ShapeDtypeStruct((SEQ_DEV, HEADS, SLOT, SLOT), bf16)),
            (NORM_SPEC, jax.ShapeDtypeStruct((SEQ_DEV, 16, SLOT), f32)),
            out_columns(WIDTH),
            out_whole((8, WIDTH)),
            out_whole((1, FF)),
            out_whole((8, 128)),
        ],
        (ids, dealt, *weights, perm),
        "attention_forward",
        22 * 10**9,
        22 * 10**6,
        ATTENTION_SCRATCH + [pltpu.VMEM((32, PACKED - 3 * WIDTH), f32), pltpu.SemaphoreType.DMA((8,))],
        58,
    )


def halves(block, shape, where):
    return [(pl.BlockSpec(block, lambda s, ids: where(s)), jax.ShapeDtypeStruct(shape, bf16))] * 2


def call_ffn(ids, dealt, dealt_c, ctx_t, inner, outer, vec, bias_in):
    outer_rows = FF // GROUP
    inner_rows = WIDTH // GROUP
    first = SEQ_DEV
    second = first + RING
    return run(
        feed_forward,
        (second + FF_STEPS + 1,),
        [DEALT_SPEC] * 2
        + [whole((WIDTH, ROWS))]
        + [ANYWHERE] * 8
        + [whole((8, WIDTH)), whole((1, FF))],
        [out_rows(WIDTH, bf16), out_rows(WIDTH, f32), out_rows(WIDTH, bf16)]
        + halves(
            (1, outer_rows, WIDTH), (RING, outer_rows, WIDTH), lambda s: (jnp.clip(s - first, 0, RING - 1), 0, 0)
        )
        + halves(
            (RING, inner_rows, FF_STEP),
            (RING, inner_rows, FF),
            lambda s: (0, 0, jnp.clip(s - second, 0, FF_STEPS - 1)),
        )
        + halves((RING, inner_rows, WIDTH + 128), (RING, inner_rows, WIDTH + 128), lambda s: (0, 0, 0)),
        (ids, dealt, dealt_c, ctx_t, *inner, *outer, vec, bias_in),
        "feed_forward",
        50 * 10**9,
        40 * 10**6,
        [
            pltpu.VMEM((SLOT, FF), bf16),
            pltpu.VMEM((8, WIDTH), f32),
            pltpu.VMEM((1, FF), f32),
            pltpu.VMEM((RING, CORES, 2, 48, MIXED), bf16),
            pltpu.VMEM((RING, CORES, RING, 2, 48, WIDTH), bf16),
            pltpu.VMEM((SEQ_DEV, WIDTH, SLOT), bf16),
            pltpu.VMEM((SEQ_DEV, FF, SLOT), bf16),
            pltpu.VMEM((SEQ_DEV, SLOT, WIDTH), bf16),
            pltpu.VMEM((SEQ_DEV, FF_STEPS, SLOT, FF_STEP), bf16),
            pltpu.VMEM((SEQ_DEV, SLOT, WIDTH), bf16),
            pltpu.SemaphoreType.DMA((RING, RING)),
            pltpu.SemaphoreType.DMA((RING, RING, RING)),
        ],
        58,
    )


def call_backward(ids, dsum, dattn, qkv, expo, norm, ctx_t, x_t, dealt_c, layer, weights, inner):
    block = (RING, WIDTH // GROUP, 3 * WIDTH + 128)
    return run(
        attention_backward,
        (SEQ_DEV + 1,),
        [by_rows(WIDTH), by_rows(WIDTH), by_rows(3 * WIDTH), EXP_SPEC, NORM_SPEC, by_columns(WIDTH)]
        + [whole((WIDTH, ROWS)), DEALT_SPEC, by_rows(WIDTH)]
        + [ANYWHERE] * 12,
        [(RETURN_SPEC, RETURN_SHAPE)] + halves(block, block, lambda s: (0, 0, 0)),
        (ids, dsum, dattn, qkv, expo, norm, ctx_t, x_t, dealt_c, layer, *weights, *inner),
        "attention_backward",
        28 * 10**9,
        30 * 10**6,
        ATTENTION_SCRATCH
        + [
            pltpu.VMEM((RING, CORES, 2, 48, WIDTH), bf16),
            pltpu.VMEM((8, WIDTH), f32),
            pltpu.VMEM((SEQ_DEV, 3, SLOT, WIDTH), bf16),
            pltpu.SemaphoreType.DMA((8,)),
            pltpu.SemaphoreType.DMA((RING, RING)),
        ],
        58,
    )


def call_by_x(kernel, name, ids, pieces, at, out_shapes, out_at, scratch):
    count = len(out_shapes)

    def every_x(ids, *refs):
        ins, outs, rest = refs[: len(pieces)], refs[len(pieces) :][:count], refs[len(pieces) + count :]
        for x in range(RING):
            one = (pl.ds(x, 1),)
            kernel(
                ids,
                *[ref.at[(slice(None),) * at + one] for ref in ins],
                *[ref.at[(slice(None),) * out_at + one] for ref in outs],
                *rest,
            )

    return call_small(every_x, name, ids, pieces, *out_shapes, scratch=scratch)


def call_small(kernel, name, ids, pieces, *out_shapes, kind=bf16, scratch=()):
    def full(shape):
        return pl.BlockSpec(shape, lambda i, ids: (0,) * len(shape))

    return run(
        kernel,
        (1,),
        [full(piece.shape) for piece in pieces],
        [(full(shape), jax.ShapeDtypeStruct(shape, kind)) for shape in out_shapes],
        (ids, *pieces),
        name,
        10**6,
        6 * 10**6,
        [pltpu.VMEM(shape, f32) for shape in scratch],
        30,
    )


def shift(value, axis, step):
    size = CORES if axis == "core" else RING
    return lax.ppermute(value, axis, [(i, (i + step) % size) for i in range(size)])


def swap(value, axis):
    return lax.ppermute(value, axis, [(i, i ^ 1) for i in range(RING)])


def arrivals(value, axis):
    return [value] + [shift(value, axis, step) for step in (1, 2, 3)]


def both_cores(pieces):
    return [part for piece in pieces for part in (piece, shift(piece, "core", 1))]


def paired(value, axis):
    return in_half(value, swap(value, axis), axis)


def in_half(value, other, axis):
    even = lax.rem(lax.axis_index(axis), 2) == 0
    return jnp.where(even, value, other), jnp.where(even, other, value)


def hold(value, *others):
    return lax.optimization_barrier((value, *others))[0]


def send_ring(parts, axis):
    return [parts[0]] + [shift(parts[step], axis, step) for step in (1, 2, 3)]


def over(value, axis):
    return lax.all_to_all(value, axis, split_axis=0, concat_axis=0, tiled=True)


def body(
    tokens,
    cotangent,
    perm,
    lengths,
    drop,
    w_query,
    b_query,
    w_key,
    w_value,
    b_value,
    w_out,
    b_out,
    norm1_gain,
    norm1_bias,
    w_inner,
    b_inner,
    w_outer,
    b_outer,
    norm2_gain,
    norm2_bias,
):
    me_x = lax.axis_index("x")
    me_c = lax.axis_index("core")
    me_z = lax.axis_index("z")
    me_y = lax.axis_index("y")
    first = ((me_z * RING + me_y) * 8 + me_x * CORES + me_c) * SEQ_DEV
    places = jnp.stack([me_x, me_c, first, me_z, me_y]).astype(jnp.int32)
    places = jnp.pad(places, (8, 3))

    vectors = [b_query, b_value, b_out, norm1_gain, norm1_bias, b_outer, norm2_gain, norm2_bias, b_inner]
    vectors += [lengths.astype(bf16), drop.astype(bf16)]
    row = jnp.zeros((WIDTH,), bf16)
    start = 0
    for vector in vectors:
        end = start + vector.shape[0]
        row += jnp.pad(vector, (start, WIDTH - end))
        start = end
    (piece,) = call_small(
        pack_rows, "pack_rows", places, (w_query, w_key, w_value, w_out, w_inner, row[None]), (8, 4 * WIDTH + FF)
    )
    pieces_y = arrivals(piece, "y")
    dp = ("x", "core")
    dealt = (GROUP, SEQ_DEV, PIECE, WIDTH)
    dealt_x = over(tokens.reshape(dealt), dp)
    attn_y, inner_y = call_small(merge_rows, "merge_rows", places, pieces_y, (24, PACKED), (24, MIXED))
    (attn_zy,) = call_small(
        stack_rows, "stack_rows", places, arrivals(attn_y, "z"), (RING, 24, PACKED)
    )

    outer_pair = paired(w_outer, "y")
    ffn_x = arrivals(jnp.concatenate([hold(inner_y, dealt_x), *outer_pair], axis=1), "x")
    ffn_x[0] = hold(ffn_x[0], attn_zy)
    inner_x, outer_x = call_small(
        split_ffn, "split_ffn", places, ffn_x, (RING, 24, MIXED), (RING, 48, WIDTH)
    )
    attn_x = arrivals(hold(attn_zy, dealt_x).reshape(96, PACKED), "x")
    attn_pieces = both_cores(attn_x)
    inner_z = swap(inner_x, "z")
    outer_z = over(jnp.broadcast_to(outer_x[None], (RING, RING, 48, WIDTH)), "z")
    inner_z = jnp.concatenate(in_half(inner_x, hold(inner_z, attn_x[1]), "z"), axis=1)
    inner_far = shift(inner_z, "z", 2)
    outer_z = hold(outer_z, attn_x[1])
    outer_far = shift(outer_z, "y", 2)
    dealt_c = over(hold(cotangent, attn_x[1]).reshape(dealt), dp)

    x_t, qkv, expo, norm, ctx_t, vec, inner_bias, info = call_forward(
        places, dealt_x, attn_pieces, perm.reshape(32, 16)
    )
    ids = jnp.concatenate([info[:, 0].astype(jnp.int32), places[8:]])

    inner_pieces = both_cores([hold(inner_z, ctx_t, dealt_c), hold(inner_far, ctx_t)])
    outer_pieces = both_cores([hold(outer_z, ctx_t), hold(outer_far, ctx_t)])
    (
        layer, d_sum1, d_attn, outer_away, outer_mine, inner_away, inner_mine, out_away, out_mine
    ) = call_ffn(ids, dealt_x, dealt_c, ctx_t, inner_pieces, outer_pieces, vec, inner_bias)

    inner_core = shift(inner_away, "core", 1)
    out_core = shift(out_away, "core", 1)
    outer_core = shift(hold(outer_away, out_core), "core", 1)
    inner_width = FF + WIDTH + 128
    inner_parts = call_by_x(
        sum_blocks, "sum_blocks", places, (inner_mine, inner_core, out_mine, out_core), 0,
        [(RING, 24, inner_width)] * RING, 0, [(96, inner_width)],
    )
    (outer_sum,) = call_by_x(
        sum_outer, "sum_outer", hold(places, inner_parts[0]), (outer_mine, outer_core), 0,
        [(RING, RING, RING, 24, WIDTH)], 1, [],
    )
    inner_parts = send_ring(inner_parts, "z")
    outer_y = over(outer_sum, "y")

    d_sum1, d_attn = lax.optimization_barrier((d_sum1, d_attn, inner_parts[0], outer_sum))[:2]
    back, attn_away, attn_mine = call_backward(
        ids, d_sum1, d_attn, qkv, expo, norm, ctx_t, x_t, dealt_c, layer, attn_pieces, inner_pieces
    )

    attn_core = shift(hold(attn_away, outer_y, *inner_parts[1:]), "core", 1)
    (outer_z,) = call_by_x(
        sum_first, "sum_first", hold(places, attn_away), (hold(outer_y, attn_away),), 1,
        [(RING, RING, 24, WIDTH)], 0, [],
    )
    attn_width = 3 * WIDTH + 128
    attn_parts = call_by_x(
        sum_attention, "sum_attention", places, (outer_z, attn_mine, attn_core), 0,
        [(RING, 24, attn_width + WIDTH)] * RING, 0, [(96, attn_width)],
    )
    attn_first = attn_parts[0]
    attn_parts = send_ring(attn_parts, "z")
    back = over(hold(back, outer_z), dp)

    inner_parts = [hold(p, attn_first) for p in inner_parts]
    inner_parts = call_by_x(
        split_rows, "split_rows", places, inner_parts, 0,
        [(RING, 8, FF + WIDTH)] * RING, 0, [(RING, 8, FF + WIDTH)],
    )
    *attn_parts, outer_z = call_by_x(
        split_rows, "split_rows", hold(places, inner_parts[0]), attn_parts, 0,
        [(RING, 8, 3 * WIDTH)] * RING + [(RING, 24, WIDTH)], 0, [(RING, 8, 3 * WIDTH)],
    )
    inner_parts = send_ring(inner_parts, "y")
    attn_parts = send_ring(attn_parts, "y")
    last = call_small(
        join_flows, "join_flows", places, [*inner_parts, *attn_parts, outer_z], *[(8, LAST)] * 4,
        scratch=[(RING, 8, LAST)],
    )
    back = hold(back, last[0])
    layer_final = back[:, 0].reshape(GROUP * SEQ_DEV, PIECE, WIDTH)
    grad_final = back[:, 1].reshape(GROUP * SEQ_DEV, PIECE, WIDTH)
    square = (6, WIDTH)
    grad_query, grad_key, grad_value, grad_out, grad_inner, grad_outer, vectors = call_small(
        write_grads, "write_grads", hold(places, layer_final), send_ring(last, "x"),
        square, square, square, square, (6, FF), (24, WIDTH), (2, 128), kind=f32,
    )
    ffn_vectors = [vectors[0, 6 * i : 6 * i + 6] for i in range(6)]
    return (
        layer_final,
        grad_final,
        grad_query,
        vectors[1, :6],
        grad_key,
        grad_value,
        vectors[1, 6:12],
        grad_out,
        ffn_vectors[5],
        ffn_vectors[3],
        ffn_vectors[4],
        grad_inner,
        vectors[0, 36:60],
        grad_outer,
        ffn_vectors[0],
        ffn_vectors[1],
        ffn_vectors[2],
    )


def solution(mesh):
    chips = Mesh(mesh.devices.reshape(RING, CORES, RING, RING), ("x", "core", "z", "y"))
    dp = ("x", "core")
    fsdp = ("z", "y")
    every = P(dp + fsdp)
    rows = P(dp + fsdp, None)
    whole_rows = P(fsdp, dp, None)
    return jax.shard_map(
        body,
        mesh=chips,
        in_specs=(
            whole_rows, whole_rows, P(), every, every,
            rows, every, rows, rows, every, rows, every, every, every,
            rows, every, rows, every, every, every,
        ),
        out_specs=(
            whole_rows, whole_rows,
            rows, every, rows, rows, every, rows, every, every, every,
            rows, every, rows, every, every, every,
        ),
        check_vma=False,
    )
```

```python
import functools
import jax
import jax.numpy as jnp
from jax import lax
from jax.experimental import pallas as pl
from jax.experimental.pallas import tpu as pltpu
from jax.sharding import Mesh
from jax.sharding import PartitionSpec as P

HEADS = 12
HEAD = 64
WIDTH = 768
FF = 3072
SLOT = 256
SEQ_DEV = 4
RING = 4
CORES = 2
PIECE = 32
GROUP = RING * CORES
ROWS = SEQ_DEV * SLOT
PAIR = 2 * HEAD
PACKED = 3 * WIDTH + 512
MIXED = WIDTH + FF

epsilon = 1e-05
bf16 = jnp.bfloat16
f32 = jnp.float32
MIB = 1024 * 1024

TN = (((0,), (0,)), ((), ()))
NT = (((1,), (1,)), ((), ()))


def mm(a, b):
    return jnp.dot(a, b, preferred_element_type=f32)


def mm_nt(a, b):
    return lax.dot_general(a, b, NT, preferred_element_type=f32)


def mm_tn(a, b):
    return lax.dot_general(a, b, TN, preferred_element_type=f32)


def joined(ref):
    return ref[...].reshape(SLOT, WIDTH)


def spread(extras, start, width):
    total = 128 * width
    group = lax.broadcasted_iota(jnp.int32, (32, total), 0)
    owner = lax.broadcasted_iota(jnp.int32, (32, total), 1) // width
    pick = lax.broadcasted_iota(jnp.int32, (width, total), 0)
    within = lax.rem(lax.broadcasted_iota(jnp.int32, (width, total), 1), width)
    chosen = (pick == within).astype(bf16)
    out = jnp.zeros((32, total), f32)
    for y in range(RING):
        values = extras[:, 128 * y + start : 128 * y + start + width].astype(bf16)
        out += jnp.where(owner == group * RING + y, mm(values, chosen), 0.0)
    return jnp.sum(out, axis=0, keepdims=True)


def gather_back(vectors):
    values = jnp.zeros((128, 128), f32)
    start = 0
    for vector in vectors:
        total = vector.shape[1]
        width = total // 128
        owner = lax.broadcasted_iota(jnp.int32, (128, total), 1) // width
        mine = owner == lax.broadcasted_iota(jnp.int32, (128, total), 0)
        within = lax.rem(lax.broadcasted_iota(jnp.int32, (total, 128), 0), width)
        column = lax.broadcasted_iota(jnp.int32, (total, 128), 1)
        spots = (column == within + start).astype(bf16)
        values += mm(jnp.where(mine, vector, 0.0).astype(bf16), spots)
        start += width
    row = lax.broadcasted_iota(jnp.int32, (WIDTH, 128), 0)
    device = lax.broadcasted_iota(jnp.int32, (WIDTH, 128), 1)
    within = lax.rem(row, 24)
    picks = (within < RING) & (row // 24 * RING + within == device)
    return mm(picks.astype(bf16), values.astype(bf16)).astype(bf16)


def attention_copies(ids, pieces, w, sems):
    copies = []
    for i, piece in enumerate(pieces):
        x = lax.rem(ids[8] + RING - i // 2, RING)
        c = ids[9] if i % 2 == 0 else 1 - ids[9]
        copies.append(pltpu.make_async_copy(piece, w.at[x, c], sems.at[i]))
    return copies


def half_of(ids, i):
    c = ids[9] if i % 2 == 0 else 1 - ids[9]
    return c, ids[11] // 2 if i // 2 == 0 else 1 - ids[11] // 2


def columns(w, start, end):
    return w[:, :, :, start:end].reshape(WIDTH, end - start)


def attention_forward(
    ids, x_in, p0, p1, p2, p3, p4, p5, p6, p7, perm,
    xt_out, qkv_out, exp_out, norm_out, ctxt_out, vec, bias_out, info,
    w, extras, sems,
):
    s = pl.program_id(0)

    @pl.when(s == 0)
    def _():
        copies = attention_copies(ids, (p0, p1, p2, p3, p4, p5, p6, p7), w, sems)
        for copy in copies:
            copy.start()
        for copy in copies:
            copy.wait()
        rows = columns(w, 3 * WIDTH, PACKED).astype(f32).reshape(32, 24, PACKED - 3 * WIDTH)
        extras[...] = jnp.sum(rows, axis=1)
        for i in range(8):
            vec[i : i + 1] = spread(extras, 6 * i, 6)
        bias_out[...] = spread(extras, 48, 24)

    length = jnp.zeros((1, 1), f32)
    dropped = jnp.zeros((1, 1), f32)
    for y in range(RING):
        hit = perm[:, RING * y : RING * y + 4] == ids[10] + s
        length += jnp.sum(jnp.where(hit, extras[:, 128 * y + 72 : 128 * y + 76], 0.0), keepdims=True)
        dropped += jnp.sum(jnp.where(hit, extras[:, 128 * y + 76 : 128 * y + 80], 0.0), keepdims=True)
    line = lax.broadcasted_iota(jnp.int32, (8, 128), 0)
    info[...] = jnp.where(line == s, length, jnp.where(line == s + 4, dropped, info[...]))

    x = joined(x_in)
    xt_out[...] = x.T
    q = ((mm(x, columns(w, 0, WIDTH)) + vec[0:1]).astype(bf16).astype(f32) * HEAD**-0.5).astype(bf16)
    k = mm(x, columns(w, WIDTH, 2 * WIDTH)).astype(bf16)
    v = (mm(x, columns(w, 2 * WIDTH, 3 * WIDTH)) + vec[1:2]).astype(bf16)
    qkv_out[:, :WIDTH] = q
    qkv_out[:, WIDTH : 2 * WIDTH] = k
    qkv_out[:, 2 * WIDTH :] = v
    q_t = q.T
    v_t = v.T
    keys = lax.broadcasted_iota(jnp.int32, (SLOT, 1), 0).astype(f32)
    bias = jnp.where(keys < length, 0.0, -1e30)
    low = lax.broadcasted_iota(jnp.int32, (SLOT, PAIR), 1) < HEAD
    ctx_t = []
    for h in range(HEADS):
        p = h // 2 * PAIR
        k_pair = k[:, p : p + PAIR]
        k_one = jnp.where(low if h % 2 == 0 else ~low, k_pair, jnp.zeros_like(k_pair))
        scores = mm(k_one, q_t[p : p + PAIR]) + bias
        top = jnp.max(scores, axis=0, keepdims=True)
        expo = jnp.exp(scores - top)
        inverse = 1.0 / jnp.sum(expo, axis=0, keepdims=True)
        norm_out[0, h : h + 1, :] = inverse
        expo = expo.astype(bf16)
        exp_out[0, h] = expo
        ctx_t.append(mm(v_t[h * HEAD : (h + 1) * HEAD], expo) * inverse)
    ctx_t = jnp.concatenate(ctx_t, axis=0).astype(bf16)
    ctxt_out[...] = ctx_t


def row_mean(v):
    return jnp.mean(v, axis=-1, keepdims=True)


def normalised(z):
    center = z - row_mean(z)
    r = lax.rsqrt(row_mean(center * center) + epsilon)
    return center * r, r


def norm_back(dy, zhat, r, gain):
    e = dy * gain
    return r * (e - row_mean(e) - zhat * row_mean(e * zhat))


def col_sum(v):
    return jnp.sum(v, axis=0, keepdims=True)


FF_STEP = 768
FF_STEPS = FF // FF_STEP


def cut_cores(ids, value, away, mine):
    blocks, rows, _ = away.shape
    first = ids[9] == 0
    for x in range(blocks):
        even = value[2 * x * rows : (2 * x + 1) * rows]
        odd = value[(2 * x + 1) * rows : (2 * x + 2) * rows]
        away[x] = jnp.where(first, odd, even)
        mine[x] = jnp.where(first, even, odd)


def feed_forward(
    ids, x_in, c_in, ctx_t, i0, i1, i2, i3, j0, j1, j2, j3, vec, bias_in,
    layer_out, dsum_out, dattn_out, outer_away, outer_mine, inner_away, inner_mine, out_away, out_mine,
    slope, vec_grad, bias_grad, w_in, w_out, hid_t, act_t, d_branches, d_inners, d_attns, in_sems, out_sems,
):
    s = pl.program_id(0)

    @pl.when(s == 0)
    def _():
        vec_grad[...] = jnp.zeros_like(vec_grad)
        bias_grad[...] = jnp.zeros_like(bias_grad)
        copies = []
        for i, (piece, late) in enumerate(zip((i0, i1, i2, i3), (j0, j1, j2, j3))):
            c, z_half = half_of(ids, i)
            y_half = ids[12] // 2 if i // 2 == 0 else 1 - ids[12] // 2
            for d in range(RING):
                x = lax.rem(ids[8] + RING - d, RING)
                copies.append(pltpu.make_async_copy(piece.at[d], w_in.at[x, c, z_half], in_sems.at[i, d]))
                for n in range(RING):
                    target = w_out.at[x, c, n, y_half]
                    copies.append(pltpu.make_async_copy(late.at[n, d], target, out_sems.at[i, d, n]))
        for copy in copies:
            copy.start()
        for copy in copies:
            copy.wait()

    def inner_columns(n):
        return w_in[:, :, :, :, WIDTH + n * FF_STEP : WIDTH + (n + 1) * FF_STEP].reshape(WIDTH, FF_STEP)

    def outer_rows(n):
        return w_out[n].reshape(FF_STEP, WIDTH)

    @pl.when(s < SEQ_DEV)
    def _():
        x = joined(x_in).astype(f32)
        context = ctx_t[:, pl.ds(pl.multiple_of(s * SLOT, SLOT), SLOT)].T
        attn_out = mm(context, w_in[:, :, :, :, :WIDTH].reshape(WIDTH, WIDTH)) + vec[2:3]
        zhat1, r1 = normalised(x + attn_out)
        hidden = zhat1 * vec[3:4] + vec[4:5]
        hid_low = hidden.astype(bf16)
        hid_t[s] = hid_low.T
        branch = jnp.broadcast_to(vec[5:6], (SLOT, WIDTH))
        for n in range(FF_STEPS):
            cols = slice(n * FF_STEP, (n + 1) * FF_STEP)
            inner = mm(hid_low, inner_columns(n)) + bias_in[0:1, cols]
            half = 0.5 * lax.erf(inner * 0.7071067811865476) + 0.5
            bell = 0.3989422804014327 * jnp.exp(-0.5 * (inner * inner))
            act = (inner * half).astype(bf16)
            act_t[s, cols, :] = act.T
            slope[:, cols] = (half + inner * bell).astype(bf16)
            branch += mm(act, outer_rows(n))
        zhat2, r2 = normalised(hidden + branch)
        gain2 = vec[6:7]
        normed = zhat2 * gain2 + vec[7:8]
        valid = (lax.broadcasted_iota(jnp.int32, (SLOT, 1), 0) < ids[s]).astype(f32)
        keep = ids[4 + s] == 0
        layer_out[...] = (jnp.where(keep, normed, x) * valid).astype(bf16)
        dy = joined(c_in).astype(f32) * jnp.where(keep, valid, 0.0)
        vec_grad[1:2] += col_sum(dy * zhat2)
        vec_grad[2:3] += col_sum(dy)
        d_sum2 = norm_back(dy, zhat2, r2, gain2)
        d_branch = d_sum2.astype(bf16)
        d_branches[s] = d_branch
        vec_grad[0:1] += col_sum(d_branch.astype(f32))
        d_hidden = d_sum2
        for n in range(FF_STEPS):
            cols = slice(n * FF_STEP, (n + 1) * FF_STEP)
            d_act = mm_nt(d_branch, outer_rows(n))
            d_inner = (d_act * slope[:, cols].astype(f32)).astype(bf16)
            d_inners[s, n] = d_inner
            bias_grad[0:1, cols] += col_sum(d_inner.astype(f32))
            d_hidden += mm_nt(d_inner, inner_columns(n))
        vec_grad[3:4] += col_sum(d_hidden * zhat1)
        vec_grad[4:5] += col_sum(d_hidden)
        d_sum1 = norm_back(d_hidden, zhat1, r1, vec[3:4])
        dsum_out[...] = d_sum1
        d_attn = d_sum1.astype(bf16)
        dattn_out[...] = d_attn
        d_attns[s] = d_attn
        vec_grad[5:6] += col_sum(d_attn.astype(f32))

    @pl.when((s >= SEQ_DEV) & (s < SEQ_DEV + RING))
    def _():
        rows = pl.ds(pl.multiple_of((s - SEQ_DEV) * FF_STEP, FF_STEP), FF_STEP)
        value = mm(act_t[0, rows, :], d_branches[0])
        for i in range(1, SEQ_DEV):
            value += mm(act_t[i, rows, :], d_branches[i])
        cut_cores(ids, value.astype(bf16), outer_away, outer_mine)

    @pl.when((s >= SEQ_DEV + RING) & (s < SEQ_DEV + RING + FF_STEPS))
    def _():
        n = s - SEQ_DEV - RING
        value = mm(hid_t[0], d_inners[0, n])
        for i in range(1, SEQ_DEV):
            value += mm(hid_t[i], d_inners[i, n])
        cut_cores(ids, value.astype(bf16), inner_away, inner_mine)

    @pl.when(s == SEQ_DEV + RING + FF_STEPS)
    def _():
        value = mm(ctx_t[:, :SLOT], d_attns[0])
        for i in range(1, SEQ_DEV):
            value += mm(ctx_t[:, i * SLOT : (i + 1) * SLOT], d_attns[i])
        block = gather_back([vec_grad[i : i + 1] for i in range(6)] + [bias_grad[...]])
        cut_cores(ids, jnp.concatenate([value.astype(bf16), block], axis=1), out_away, out_mine)


def attention_backward(
    ids, dsum, dattn, qkv, exp_in, norm_in, ctxt_in, x_t, c_in, layer_in, p0, p1, p2, p3, p4, p5, p6, p7, i0, i1, i2, i3,
    back_out, attn_away, attn_mine,
    w, w_out, vec_grad, d_qkv, sems, out_sems,
):
    s = pl.program_id(0)

    @pl.when(s == 0)
    def _():
        vec_grad[...] = jnp.zeros_like(vec_grad)
        copies = attention_copies(ids, (p0, p1, p2, p3, p4, p5, p6, p7), w, sems)
        for i, piece in enumerate((i0, i1, i2, i3)):
            c, z_half = half_of(ids, i)
            for d in range(RING):
                x = lax.rem(ids[8] + RING - d, RING)
                source = piece.at[d, :, pl.ds(0, WIDTH)]
                copies.append(pltpu.make_async_copy(source, w_out.at[x, c, z_half], out_sems.at[i, d]))
        for copy in copies:
            copy.start()
        for copy in copies:
            copy.wait()

    @pl.when(s < SEQ_DEV)
    def _():
        d_sum1 = dsum[...]
        dctx_t = mm_nt(dattn[...], w_out[...].reshape(WIDTH, WIDTH)).T
        ctx_t = ctxt_in[...].astype(f32)
        k_t = qkv[:, WIDTH : 2 * WIDTH].T
        scaled = []
        deltas = []
        for h in range(HEADS):
            rows = slice(h * HEAD, (h + 1) * HEAD)
            one = (dctx_t[rows] * norm_in[0, h : h + 1, :]).astype(bf16)
            scaled.append(one)
            deltas.append(col_sum(one.astype(f32) * ctx_t[rows]))
        dctx_t = jnp.concatenate(scaled, axis=0)
        dctx = dctx_t.T
        low = lax.broadcasted_iota(jnp.int32, (SLOT, PAIR), 1) < HEAD
        dq_t = []
        for p in range(0, WIDTH, PAIR):
            cols = slice(p, p + PAIR)
            q_pair = qkv[:, cols]
            v_pair = qkv[:, 2 * WIDTH + p : 2 * WIDTH + p + PAIR]
            dks = []
            dvs = []
            for half in range(2):
                h = p // HEAD + half
                v_one = jnp.where(low if half == 0 else ~low, v_pair, jnp.zeros_like(v_pair))
                d_probs = mm(v_one, dctx_t[cols]) - deltas[h]
                expo = exp_in[0, h]
                d_scores = (expo.astype(f32) * d_probs).astype(bf16)
                dvs.append(mm(expo, dctx[:, cols]))
                dks.append(mm(d_scores, q_pair))
                dq_t.append(mm(k_t[h * HEAD : (h + 1) * HEAD], d_scores))
            d_qkv[s, 1, :, cols] = jnp.where(low, dks[0], dks[1]).astype(bf16)
            d_qkv[s, 2, :, cols] = jnp.where(low, dvs[0], dvs[1]).astype(bf16)
        dq = (jnp.concatenate(dq_t, axis=0).T * HEAD**-0.5).astype(bf16)
        d_qkv[s, 0] = dq
        vec_grad[0:1] += col_sum(dq.astype(f32))
        vec_grad[1:2] += col_sum(d_qkv[s, 2].astype(f32))
        d_in = d_sum1
        for n in range(3):
            d_in += mm_nt(d_qkv[s, n], columns(w, n * WIDTH, (n + 1) * WIDTH))
        valid = (lax.broadcasted_iota(jnp.int32, (SLOT, 1), 0) < ids[s]).astype(f32)
        upstream = joined(c_in).astype(f32) * valid
        keep = ids[4 + s] == 0
        grad = jnp.where(keep, d_in, upstream).astype(bf16)
        back_out[:, 0, 0] = layer_in[...].reshape(GROUP, PIECE, WIDTH)
        back_out[:, 1, 0] = grad.reshape(GROUP, PIECE, WIDTH)

    @pl.when(s == SEQ_DEV)
    def _():
        values = []
        for n in range(3):
            value = mm(x_t[:, :SLOT], d_qkv[0, n])
            for i in range(1, SEQ_DEV):
                value += mm(x_t[:, i * SLOT : (i + 1) * SLOT], d_qkv[i, n])
            values.append(value.astype(bf16))
        values.append(gather_back([vec_grad[0:1], vec_grad[1:2]]))
        cut_cores(ids, jnp.concatenate(values, axis=1), attn_away, attn_mine)


def in_order(values, me):
    ordered = []
    for j in range(RING):
        step = lax.rem(me + RING - j, RING)
        value = values[0]
        for d in (1, 2, 3):
            value = jnp.where(step == d, values[d], value)
        ordered.append(value)
    return ordered


def pack_rows(ids, query, key, value, out, inner, row, packed):
    for i, ref in enumerate((query, key, value, out)):
        block = jnp.concatenate([ref[...].astype(f32), jnp.zeros((2, WIDTH), f32)], axis=0)
        if i == 0:
            line = lax.broadcasted_iota(jnp.int32, (8, WIDTH), 0)
            block = jnp.where(line == 6, row[...].astype(f32), block)
        packed[:, i * WIDTH : (i + 1) * WIDTH] = block.astype(bf16)
    block = jnp.concatenate([inner[...].astype(f32), jnp.zeros((2, FF), f32)], axis=0)
    packed[:, 4 * WIDTH :] = block.astype(bf16)


def merge_rows(ids, own, r1, r2, r3, attn_out, inner_out):
    ordered = in_order([v[...].astype(f32) for v in (own, r1, r2, r3)], ids[12])
    width = 3 * WIDTH
    rows = jnp.concatenate([v[:6] for v in ordered], axis=0).astype(bf16)
    attn_out[:, :width] = rows[:, :width]
    inner_out[...] = rows[:, width:]
    row = jnp.concatenate([v[6:7, :128] for v in ordered], axis=1)
    first = lax.broadcasted_iota(jnp.int32, (24, 4 * 128), 0) == 0
    attn_out[:, width:] = jnp.where(first, jnp.broadcast_to(row, (24, 4 * 128)), 0.0).astype(bf16)


def stack_rows(ids, own, r1, r2, r3, out):
    for d, piece in enumerate((own, r1, r2, r3)):
        out[lax.rem(ids[11] + RING - d, RING)] = piece[...]


def ahead(ids, axis, step):
    return lax.rem(ids[axis] + step, RING)


def sum_of(refs):
    total = refs[0][...].astype(f32)
    for ref in refs[1:]:
        total += ref[...].astype(f32)
    return total


def sum_blocks(ids, *refs):
    *parts, o0, o1, o2, o3, scratch = refs
    start = 0
    for mine, core in zip(parts[::2], parts[1::2]):
        end = start + mine.shape[2]
        scratch[:, start:end] = mine[0].astype(f32) + core[0].astype(f32)
        start = end
    for d, out in enumerate((o0, o1, o2, o3)):
        first = pl.multiple_of(ahead(ids, 11, d) * 24, 8)
        out[0] = scratch[pl.ds(first, 24), :].astype(bf16)


def sum_attention(ids, outer, mine, core, o0, o1, o2, o3, scratch):
    scratch[...] = mine[0].astype(f32) + core[0].astype(f32)
    for d, out in enumerate((o0, o1, o2, o3)):
        z = ahead(ids, 11, d)
        first = pl.multiple_of(z * 24, 8)
        out[0, :, : scratch.shape[1]] = scratch[pl.ds(first, 24), :].astype(bf16)
        out[0, :, scratch.shape[1] :] = outer[0, z]


def sum_outer(ids, mine, core, out):
    total = mine[0].astype(f32) + core[0].astype(f32)
    for z in range(RING):
        for y in range(RING):
            first = 96 * z + 24 * y
            out[y, 0, z] = total[first : first + 24].astype(bf16)


def sum_first(ids, value, out):
    for z in range(RING):
        out[0, z] = sum_of([value.at[y, 0, z] for y in range(RING)]).astype(bf16)


def split_rows(ids, p0, p1, p2, p3, o0, o1, o2, o3, *refs):
    *rest, scratch = refs
    width = o0.shape[2]
    total = sum_of([p.at[0] for p in (p0, p1, p2, p3)])
    if rest:
        rest[0][0] = total[:, width + 128 :].astype(bf16)
    for y in range(RING):
        vectors = total[y : y + 1, width : width + 128]
        row = jnp.concatenate([vectors, jnp.zeros((1, width - 128), f32)], axis=1)
        rows = total[6 * y : 6 * y + 6, :width]
        scratch[y] = jnp.concatenate([rows, row, jnp.zeros((1, width), f32)], axis=0)
    for d, out in enumerate((o0, o1, o2, o3)):
        out[0] = scratch[ahead(ids, 12, d)].astype(bf16)


LAST = FF + WIDTH + 3 * WIDTH + 3 * WIDTH


def join_flows(ids, i0, i1, i2, i3, a0, a1, a2, a3, outer, o0, o1, o2, o3, scratch):
    scratch[:, :, : FF + WIDTH] = sum_of((i0, i1, i2, i3))
    scratch[:, :, FF + WIDTH : FF + 4 * WIDTH] = sum_of((a0, a1, a2, a3))
    for x in range(RING):
        total = outer[x].astype(f32)
        for k in range(3):
            start = FF + (4 + k) * WIDTH
            scratch[x, :, start : start + WIDTH] = total[8 * k : 8 * k + 8]
    for d, out in enumerate((o0, o1, o2, o3)):
        out[...] = scratch[ahead(ids, 8, d)].astype(bf16)


def split_ffn(ids, p0, p1, p2, p3, inner, outer):
    for d, piece in enumerate((p0, p1, p2, p3)):
        inner[d] = piece[:, :MIXED]
        halves = [piece[:, MIXED + i * WIDTH : MIXED + (i + 1) * WIDTH].astype(f32) for i in range(2)]
        outer[d] = jnp.concatenate(halves, axis=0).astype(bf16)


def write_grads(ids, p0, p1, p2, p3, query, key, value, out, inner, outer, vectors):
    total = sum_of((p0, p1, p2, p3))
    inner[...] = total[:6, :FF]
    out[...] = total[:6, FF : FF + WIDTH]
    start = FF + WIDTH
    query[...] = total[:6, start : start + WIDTH]
    key[...] = total[:6, start + WIDTH : start + 2 * WIDTH]
    value[...] = total[:6, start + 2 * WIDTH : start + 3 * WIDTH]
    vectors[...] = jnp.concatenate([total[6:7, :128], total[6:7, start : start + 128]], axis=0)
    start += 3 * WIDTH
    for k in range(3):
        outer[8 * k : 8 * k + 8] = total[:, start + k * WIDTH : start + (k + 1) * WIDTH]


def whole(shape):
    return pl.BlockSpec(shape, lambda s, ids: (0,) * len(shape), pipeline_mode=pl.Buffered(1))


def sequence(s):
    return jnp.minimum(s, SEQ_DEV - 1)


DEALT_SPEC = pl.BlockSpec((GROUP, 1, PIECE, WIDTH), lambda s, ids: (0, sequence(s), 0, 0))


def by_rows(width):
    return pl.BlockSpec((SLOT, width), lambda s, ids: (sequence(s), 0))


def rows_of(width, kind):
    return jax.ShapeDtypeStruct((ROWS, width), kind)


EXP_SPEC = pl.BlockSpec((1, HEADS, SLOT, SLOT), lambda s, ids: (sequence(s), 0, 0, 0))
NORM_SPEC = pl.BlockSpec((1, 16, SLOT), lambda s, ids: (sequence(s), 0, 0))
RETURN_SPEC = pl.BlockSpec((GROUP, 2, 1, PIECE, WIDTH), lambda s, ids: (0, 0, sequence(s), 0, 0))
RETURN_SHAPE = jax.ShapeDtypeStruct((GROUP, 2, SEQ_DEV, PIECE, WIDTH), bf16)


def by_columns(height):
    return pl.BlockSpec((height, SLOT), lambda s, ids: (0, sequence(s)))


def columns_of(height):
    return jax.ShapeDtypeStruct((height, ROWS), bf16)


def run(kernel, grid, ins, outs, operands, name, flops, moved, scratch, limit):
    return pl.pallas_call(
        kernel,
        grid_spec=pltpu.PrefetchScalarGridSpec(
            num_scalar_prefetch=1,
            grid=grid,
            in_specs=ins,
            out_specs=[spec for spec, _ in outs],
            scratch_shapes=list(scratch),
        ),
        out_shape=[shape for _, shape in outs],
        compiler_params=pltpu.CompilerParams(
            vmem_limit_bytes=limit * MIB, dimension_semantics=("arbitrary",) * len(grid)
        ),
        cost_estimate=pl.CostEstimate(flops=flops, bytes_accessed=moved, transcendentals=0),
        name=name,
    )(*operands)


def out_rows(width, kind):
    return (by_rows(width), rows_of(width, kind))


def out_columns(height):
    return (by_columns(height), columns_of(height))


def out_whole(shape):
    return (whole(shape), jax.ShapeDtypeStruct(shape, f32))


ANYWHERE = pl.BlockSpec(memory_space=pl.ANY)
ATTENTION_SCRATCH = [pltpu.VMEM((RING, CORES, 96, PACKED), bf16)]


def call_forward(ids, dealt, weights, perm):
    return run(
        attention_forward,
        (SEQ_DEV,),
        [DEALT_SPEC] + [ANYWHERE] * 8 + [whole((32, 16))],
        [
            out_columns(WIDTH),
            out_rows(3 * WIDTH, bf16),
            (EXP_SPEC, jax.ShapeDtypeStruct((SEQ_DEV, HEADS, SLOT, SLOT), bf16)),
            (NORM_SPEC, jax.ShapeDtypeStruct((SEQ_DEV, 16, SLOT), f32)),
            out_columns(WIDTH),
            out_whole((8, WIDTH)),
            out_whole((1, FF)),
            out_whole((8, 128)),
        ],
        (ids, dealt, *weights, perm),
        "attention_forward",
        8 * 10**9,
        5 * 10**6,
        ATTENTION_SCRATCH + [pltpu.VMEM((32, PACKED - 3 * WIDTH), f32), pltpu.SemaphoreType.DMA((8,))],
        58,
    )


def halves(block, shape, where):
    return [(pl.BlockSpec(block, lambda s, ids: where(s)), jax.ShapeDtypeStruct(shape, bf16))] * 2


def call_ffn(ids, dealt, dealt_c, ctx_t, inner, outer, vec, bias_in):
    outer_rows = FF // GROUP
    inner_rows = WIDTH // GROUP
    first = SEQ_DEV
    second = first + RING
    return run(
        feed_forward,
        (second + FF_STEPS + 1,),
        [DEALT_SPEC] * 2
        + [whole((WIDTH, ROWS))]
        + [ANYWHERE] * 8
        + [whole((8, WIDTH)), whole((1, FF))],
        [out_rows(WIDTH, bf16), out_rows(WIDTH, f32), out_rows(WIDTH, bf16)]
        + halves(
            (1, outer_rows, WIDTH), (RING, outer_rows, WIDTH), lambda s: (jnp.clip(s - first, 0, RING - 1), 0, 0)
        )
        + halves(
            (RING, inner_rows, FF_STEP),
            (RING, inner_rows, FF),
            lambda s: (0, 0, jnp.clip(s - second, 0, FF_STEPS - 1)),
        )
        + halves((RING, inner_rows, WIDTH + 128), (RING, inner_rows, WIDTH + 128), lambda s: (0, 0, 0)),
        (ids, dealt, dealt_c, ctx_t, *inner, *outer, vec, bias_in),
        "feed_forward",
        50 * 10**9,
        40 * 10**6,
        [
            pltpu.VMEM((SLOT, FF), bf16),
            pltpu.VMEM((8, WIDTH), f32),
            pltpu.VMEM((1, FF), f32),
            pltpu.VMEM((RING, CORES, 2, 48, MIXED), bf16),
            pltpu.VMEM((RING, CORES, RING, 2, 48, WIDTH), bf16),
            pltpu.VMEM((SEQ_DEV, WIDTH, SLOT), bf16),
            pltpu.VMEM((SEQ_DEV, FF, SLOT), bf16),
            pltpu.VMEM((SEQ_DEV, SLOT, WIDTH), bf16),
            pltpu.VMEM((SEQ_DEV, FF_STEPS, SLOT, FF_STEP), bf16),
            pltpu.VMEM((SEQ_DEV, SLOT, WIDTH), bf16),
            pltpu.SemaphoreType.DMA((RING, RING)),
            pltpu.SemaphoreType.DMA((RING, RING, RING)),
        ],
        58,
    )


def call_backward(ids, dsum, dattn, qkv, expo, norm, ctx_t, x_t, dealt_c, layer, weights, inner):
    block = (RING, WIDTH // GROUP, 3 * WIDTH + 128)
    return run(
        attention_backward,
        (SEQ_DEV + 1,),
        [by_rows(WIDTH), by_rows(WIDTH), by_rows(3 * WIDTH), EXP_SPEC, NORM_SPEC, by_columns(WIDTH)]
        + [whole((WIDTH, ROWS)), DEALT_SPEC, by_rows(WIDTH)]
        + [ANYWHERE] * 12,
        [(RETURN_SPEC, RETURN_SHAPE)] + halves(block, block, lambda s: (0, 0, 0)),
        (ids, dsum, dattn, qkv, expo, norm, ctx_t, x_t, dealt_c, layer, *weights, *inner),
        "attention_backward",
        28 * 10**9,
        30 * 10**6,
        ATTENTION_SCRATCH
        + [
            pltpu.VMEM((RING, CORES, 2, 48, WIDTH), bf16),
            pltpu.VMEM((8, WIDTH), f32),
            pltpu.VMEM((SEQ_DEV, 3, SLOT, WIDTH), bf16),
            pltpu.SemaphoreType.DMA((8,)),
            pltpu.SemaphoreType.DMA((RING, RING)),
        ],
        58,
    )


def call_by_x(kernel, name, ids, pieces, at, out_shapes, out_at, scratch):
    count = len(out_shapes)

    def every_x(ids, *refs):
        ins, outs, rest = refs[: len(pieces)], refs[len(pieces) :][:count], refs[len(pieces) + count :]
        for x in range(RING):
            one = (pl.ds(x, 1),)
            kernel(
                ids,
                *[ref.at[(slice(None),) * at + one] for ref in ins],
                *[ref.at[(slice(None),) * out_at + one] for ref in outs],
                *rest,
            )

    return call_small(every_x, name, ids, pieces, *out_shapes, scratch=scratch)


def call_small(kernel, name, ids, pieces, *out_shapes, kind=bf16, scratch=()):
    def full(shape):
        return pl.BlockSpec(shape, lambda i, ids: (0,) * len(shape))

    return run(
        kernel,
        (1,),
        [full(piece.shape) for piece in pieces],
        [(full(shape), jax.ShapeDtypeStruct(shape, kind)) for shape in out_shapes],
        (ids, *pieces),
        name,
        10**6,
        6 * 10**6,
        [pltpu.VMEM(shape, f32) for shape in scratch],
        30,
    )


def shift(value, axis, step):
    size = CORES if axis == "core" else RING
    return lax.ppermute(value, axis, [(i, (i + step) % size) for i in range(size)])


def swap(value, axis):
    return lax.ppermute(value, axis, [(i, i ^ 1) for i in range(RING)])


def arrivals(value, axis):
    return [value] + [shift(value, axis, step) for step in (1, 2, 3)]


def both_cores(pieces):
    return [part for piece in pieces for part in (piece, shift(piece, "core", 1))]


def paired(value, axis):
    return in_half(value, swap(value, axis), axis)


def in_half(value, other, axis):
    even = lax.rem(lax.axis_index(axis), 2) == 0
    return jnp.where(even, value, other), jnp.where(even, other, value)


def hold(value, *others):
    return lax.optimization_barrier((value, *others))[0]


def send_ring(parts, axis):
    return [parts[0]] + [shift(parts[step], axis, step) for step in (1, 2, 3)]


def over(value, axis):
    return lax.all_to_all(value, axis, split_axis=0, concat_axis=0, tiled=True)


def body(
    tokens,
    cotangent,
    perm,
    lengths,
    drop,
    w_query,
    b_query,
    w_key,
    w_value,
    b_value,
    w_out,
    b_out,
    norm1_gain,
    norm1_bias,
    w_inner,
    b_inner,
    w_outer,
    b_outer,
    norm2_gain,
    norm2_bias,
):
    me_x = lax.axis_index("x")
    me_c = lax.axis_index("core")
    me_z = lax.axis_index("z")
    me_y = lax.axis_index("y")
    first = ((me_z * RING + me_y) * 8 + me_x * CORES + me_c) * SEQ_DEV
    places = jnp.stack([me_x, me_c, first, me_z, me_y]).astype(jnp.int32)
    places = jnp.pad(places, (8, 3))

    vectors = [b_query, b_value, b_out, norm1_gain, norm1_bias, b_outer, norm2_gain, norm2_bias, b_inner]
    vectors += [lengths.astype(bf16), drop.astype(bf16)]
    row = jnp.zeros((WIDTH,), bf16)
    start = 0
    for vector in vectors:
        end = start + vector.shape[0]
        row += jnp.pad(vector, (start, WIDTH - end))
        start = end
    (piece,) = call_small(
        pack_rows, "pack_rows", places, (w_query, w_key, w_value, w_out, w_inner, row[None]), (8, 4 * WIDTH + FF)
    )
    pieces_y = arrivals(piece, "y")
    dp = ("x", "core")
    dealt = (GROUP, SEQ_DEV, PIECE, WIDTH)
    dealt_x = over(tokens.reshape(dealt), dp)
    attn_y, inner_y = call_small(merge_rows, "merge_rows", places, pieces_y, (24, PACKED), (24, MIXED))
    (attn_zy,) = call_small(
        stack_rows, "stack_rows", places, arrivals(attn_y, "z"), (RING, 24, PACKED)
    )

    outer_pair = paired(w_outer, "y")
    ffn_x = arrivals(jnp.concatenate([hold(inner_y, dealt_x), *outer_pair], axis=1), "x")
    ffn_x[0] = hold(ffn_x[0], attn_zy)
    inner_x, outer_x = call_small(
        split_ffn, "split_ffn", places, ffn_x, (RING, 24, MIXED), (RING, 48, WIDTH)
    )
    attn_x = arrivals(hold(attn_zy, dealt_x).reshape(96, PACKED), "x")
    inner_z = swap(inner_x, "z")
    outer_z = over(jnp.broadcast_to(outer_x[None], (RING, RING, 48, WIDTH)), "z")
    inner_z = jnp.concatenate(in_half(inner_x, inner_z, "z"), axis=1)
    attn_pieces = both_cores([attn_x[0]] + [hold(p, inner_z) for p in attn_x[1:]])
    inner_far = shift(inner_z, "z", 2)
    outer_z = hold(outer_z, inner_z)
    outer_far = shift(outer_z, "y", 2)
    dealt_c = over(hold(cotangent, inner_z).reshape(dealt), dp)

    x_t, qkv, expo, norm, ctx_t, vec, inner_bias, info = call_forward(
        places, dealt_x, attn_pieces, perm.reshape(32, 16)
    )
    ids = jnp.concatenate([info[:, 0].astype(jnp.int32), places[8:]])

    inner_pieces = both_cores([hold(inner_z, ctx_t, dealt_c), hold(inner_far, ctx_t)])
    outer_pieces = both_cores([hold(outer_z, ctx_t), hold(outer_far, ctx_t)])
    (
        layer, d_sum1, d_attn, outer_away, outer_mine, inner_away, inner_mine, out_away, out_mine
    ) = call_ffn(ids, dealt_x, dealt_c, ctx_t, inner_pieces, outer_pieces, vec, inner_bias)

    inner_core = shift(inner_away, "core", 1)
    out_core = shift(out_away, "core", 1)
    outer_core = shift(hold(outer_away, out_core), "core", 1)
    inner_width = FF + WIDTH + 128
    inner_parts = call_by_x(
        sum_blocks, "sum_blocks", places, (inner_mine, inner_core, out_mine, out_core), 0,
        [(RING, 24, inner_width)] * RING, 0, [(96, inner_width)],
    )
    (outer_sum,) = call_by_x(
        sum_outer, "sum_outer", hold(places, inner_parts[0]), (outer_mine, outer_core), 0,
        [(RING, RING, RING, 24, WIDTH)], 1, [],
    )
    inner_parts = send_ring(inner_parts, "z")
    outer_y = over(outer_sum, "y")

    d_sum1, d_attn = lax.optimization_barrier((d_sum1, d_attn, inner_parts[0], outer_sum))[:2]
    back, attn_away, attn_mine = call_backward(
        ids, d_sum1, d_attn, qkv, expo, norm, ctx_t, x_t, dealt_c, layer, attn_pieces, inner_pieces
    )

    attn_core = shift(hold(attn_away, outer_y, *inner_parts[1:]), "core", 1)
    (outer_z,) = call_by_x(
        sum_first, "sum_first", hold(places, attn_away), (hold(outer_y, attn_away),), 1,
        [(RING, RING, 24, WIDTH)], 0, [],
    )
    attn_width = 3 * WIDTH + 128
    attn_parts = call_by_x(
        sum_attention, "sum_attention", places, (outer_z, attn_mine, attn_core), 0,
        [(RING, 24, attn_width + WIDTH)] * RING, 0, [(96, attn_width)],
    )
    attn_first = attn_parts[0]
    attn_parts = send_ring(attn_parts, "z")
    back = over(hold(back, outer_z), dp)

    inner_parts = [hold(p, attn_first) for p in inner_parts]
    inner_parts = call_by_x(
        split_rows, "split_rows", places, inner_parts, 0,
        [(RING, 8, FF + WIDTH)] * RING, 0, [(RING, 8, FF + WIDTH)],
    )
    *attn_parts, outer_z = call_by_x(
        split_rows, "split_rows", hold(places, inner_parts[0]), attn_parts, 0,
        [(RING, 8, 3 * WIDTH)] * RING + [(RING, 24, WIDTH)], 0, [(RING, 8, 3 * WIDTH)],
    )
    inner_parts = send_ring(inner_parts, "y")
    attn_parts = send_ring(attn_parts, "y")
    last = call_small(
        join_flows, "join_flows", places, [*inner_parts, *attn_parts, outer_z], *[(8, LAST)] * 4,
        scratch=[(RING, 8, LAST)],
    )
    back = hold(back, last[0])
    layer_final = back[:, 0].reshape(GROUP * SEQ_DEV, PIECE, WIDTH)
    grad_final = back[:, 1].reshape(GROUP * SEQ_DEV, PIECE, WIDTH)
    square = (6, WIDTH)
    grad_query, grad_key, grad_value, grad_out, grad_inner, grad_outer, vectors = call_small(
        write_grads, "write_grads", hold(places, layer_final), send_ring(last, "x"),
        square, square, square, square, (6, FF), (24, WIDTH), (2, 128), kind=f32,
    )
    ffn_vectors = [vectors[0, 6 * i : 6 * i + 6] for i in range(6)]
    return (
        layer_final,
        grad_final,
        grad_query,
        vectors[1, :6],
        grad_key,
        grad_value,
        vectors[1, 6:12],
        grad_out,
        ffn_vectors[5],
        ffn_vectors[3],
        ffn_vectors[4],
        grad_inner,
        vectors[0, 36:60],
        grad_outer,
        ffn_vectors[0],
        ffn_vectors[1],
        ffn_vectors[2],
    )


def solution(mesh):
    chips = Mesh(mesh.devices.reshape(RING, CORES, RING, RING), ("x", "core", "z", "y"))
    dp = ("x", "core")
    fsdp = ("z", "y")
    every = P(dp + fsdp)
    rows = P(dp + fsdp, None)
    whole_rows = P(fsdp, dp, None)
    return jax.shard_map(
        body,
        mesh=chips,
        in_specs=(
            whole_rows, whole_rows, P(), every, every,
            rows, every, rows, rows, every, rows, every, every, every,
            rows, every, rows, every, every, every,
        ),
        out_specs=(
            whole_rows, whole_rows,
            rows, every, rows, rows, every, rows, every, every, every,
            rows, every, rows, every, every, every,
        ),
        check_vma=False,
    )
```

```python
import functools
import jax
import jax.numpy as jnp
from jax import lax
from jax.experimental import pallas as pl
from jax.experimental.pallas import tpu as pltpu
from jax.sharding import Mesh
from jax.sharding import PartitionSpec as P

HEADS = 12
HEAD = 64
WIDTH = 768
FF = 3072
SLOT = 256
SEQ_DEV = 4
RING = 4
CORES = 2
PIECE = 32
GROUP = RING * CORES
ROWS = SEQ_DEV * SLOT
PAIR = 2 * HEAD
PACKED = 3 * WIDTH + 512
MIXED = WIDTH + FF

epsilon = 1e-05
bf16 = jnp.bfloat16
f32 = jnp.float32
MIB = 1024 * 1024

TN = (((0,), (0,)), ((), ()))
NT = (((1,), (1,)), ((), ()))


def mm(a, b):
    return jnp.dot(a, b, preferred_element_type=f32)


def mm_nt(a, b):
    return lax.dot_general(a, b, NT, preferred_element_type=f32)


def mm_tn(a, b):
    return lax.dot_general(a, b, TN, preferred_element_type=f32)


def joined(ref):
    return ref[...].reshape(SLOT, WIDTH)


def spread(extras, start, width):
    total = 128 * width
    group = lax.broadcasted_iota(jnp.int32, (32, total), 0)
    owner = lax.broadcasted_iota(jnp.int32, (32, total), 1) // width
    pick = lax.broadcasted_iota(jnp.int32, (width, total), 0)
    within = lax.rem(lax.broadcasted_iota(jnp.int32, (width, total), 1), width)
    chosen = (pick == within).astype(bf16)
    out = jnp.zeros((32, total), f32)
    for y in range(RING):
        values = extras[:, 128 * y + start : 128 * y + start + width].astype(bf16)
        out += jnp.where(owner == group * RING + y, mm(values, chosen), 0.0)
    return jnp.sum(out, axis=0, keepdims=True)


def gather_back(vectors):
    values = jnp.zeros((128, 128), f32)
    start = 0
    for vector in vectors:
        total = vector.shape[1]
        width = total // 128
        owner = lax.broadcasted_iota(jnp.int32, (128, total), 1) // width
        mine = owner == lax.broadcasted_iota(jnp.int32, (128, total), 0)
        within = lax.rem(lax.broadcasted_iota(jnp.int32, (total, 128), 0), width)
        column = lax.broadcasted_iota(jnp.int32, (total, 128), 1)
        spots = (column == within + start).astype(bf16)
        values += mm(jnp.where(mine, vector, 0.0).astype(bf16), spots)
        start += width
    row = lax.broadcasted_iota(jnp.int32, (WIDTH, 128), 0)
    device = lax.broadcasted_iota(jnp.int32, (WIDTH, 128), 1)
    within = lax.rem(row, 24)
    picks = (within < RING) & (row // 24 * RING + within == device)
    return mm(picks.astype(bf16), values.astype(bf16)).astype(bf16)


def attention_copies(ids, pieces, w, sems):
    copies = []
    for i, piece in enumerate(pieces):
        x = lax.rem(ids[8] + RING - i // 2, RING)
        c = ids[9] if i % 2 == 0 else 1 - ids[9]
        copies.append(pltpu.make_async_copy(piece, w.at[x, c], sems.at[i]))
    return copies


def half_of(ids, i):
    c = ids[9] if i % 2 == 0 else 1 - ids[9]
    return c, ids[11] // 2 if i // 2 == 0 else 1 - ids[11] // 2


def columns(w, start, end):
    return w[:, :, :, start:end].reshape(WIDTH, end - start)


def attention_forward(
    ids, x_in, p0, p1, p2, p3, p4, p5, p6, p7, perm,
    xt_out, qkv_out, exp_out, norm_out, ctxt_out, vec, bias_out, info,
    w, extras, sems,
):
    s = pl.program_id(0)

    @pl.when(s == 0)
    def _():
        copies = attention_copies(ids, (p0, p1, p2, p3, p4, p5, p6, p7), w, sems)
        for copy in copies:
            copy.start()
        for copy in copies:
            copy.wait()
        rows = columns(w, 3 * WIDTH, PACKED).astype(f32).reshape(32, 24, PACKED - 3 * WIDTH)
        extras[...] = jnp.sum(rows, axis=1)
        for i in range(8):
            vec[i : i + 1] = spread(extras, 6 * i, 6)
        bias_out[...] = spread(extras, 48, 24)

    length = jnp.zeros((1, 1), f32)
    dropped = jnp.zeros((1, 1), f32)
    for y in range(RING):
        hit = perm[:, RING * y : RING * y + 4] == ids[10] + s
        length += jnp.sum(jnp.where(hit, extras[:, 128 * y + 72 : 128 * y + 76], 0.0), keepdims=True)
        dropped += jnp.sum(jnp.where(hit, extras[:, 128 * y + 76 : 128 * y + 80], 0.0), keepdims=True)
    line = lax.broadcasted_iota(jnp.int32, (8, 128), 0)
    info[...] = jnp.where(line == s, length, jnp.where(line == s + 4, dropped, info[...]))

    x = joined(x_in)
    xt_out[...] = x.T
    q = ((mm(x, columns(w, 0, WIDTH)) + vec[0:1]).astype(bf16).astype(f32) * HEAD**-0.5).astype(bf16)
    k = mm(x, columns(w, WIDTH, 2 * WIDTH)).astype(bf16)
    v = (mm(x, columns(w, 2 * WIDTH, 3 * WIDTH)) + vec[1:2]).astype(bf16)
    qkv_out[:, :WIDTH] = q
    qkv_out[:, WIDTH : 2 * WIDTH] = k
    qkv_out[:, 2 * WIDTH :] = v
    q_t = q.T
    v_t = v.T
    keys = lax.broadcasted_iota(jnp.int32, (SLOT, 1), 0).astype(f32)
    bias = jnp.where(keys < length, 0.0, -1e30)
    low = lax.broadcasted_iota(jnp.int32, (SLOT, PAIR), 1) < HEAD
    ctx_t = []
    for h in range(HEADS):
        p = h // 2 * PAIR
        k_pair = k[:, p : p + PAIR]
        k_one = jnp.where(low if h % 2 == 0 else ~low, k_pair, jnp.zeros_like(k_pair))
        scores = mm(k_one, q_t[p : p + PAIR]) + bias
        top = jnp.max(scores, axis=0, keepdims=True)
        expo = jnp.exp(scores - top)
        inverse = 1.0 / jnp.sum(expo, axis=0, keepdims=True)
        norm_out[0, h : h + 1, :] = inverse
        expo = expo.astype(bf16)
        exp_out[0, h] = expo
        ctx_t.append(mm(v_t[h * HEAD : (h + 1) * HEAD], expo) * inverse)
    ctx_t = jnp.concatenate(ctx_t, axis=0).astype(bf16)
    ctxt_out[...] = ctx_t


def row_mean(v):
    return jnp.mean(v, axis=-1, keepdims=True)


def normalised(z):
    center = z - row_mean(z)
    r = lax.rsqrt(row_mean(center * center) + epsilon)
    return center * r, r


def norm_back(dy, zhat, r, gain):
    e = dy * gain
    return r * (e - row_mean(e) - zhat * row_mean(e * zhat))


def col_sum(v):
    return jnp.sum(v, axis=0, keepdims=True)


FF_STEP = 768
FF_STEPS = FF // FF_STEP


def cut_cores(ids, value, away, mine):
    blocks, rows, _ = away.shape
    first = ids[9] == 0
    for x in range(blocks):
        even = value[2 * x * rows : (2 * x + 1) * rows]
        odd = value[(2 * x + 1) * rows : (2 * x + 2) * rows]
        away[x] = jnp.where(first, odd, even)
        mine[x] = jnp.where(first, even, odd)


def feed_forward(
    ids, x_in, c_in, ctx_t, i0, i1, i2, i3, j0, j1, j2, j3, vec, bias_in,
    layer_out, dsum_out, dattn_out, outer_away, outer_mine, inner_away, inner_mine, out_away, out_mine,
    slope, vec_grad, bias_grad, w_in, w_out, hid_t, act_t, d_branches, d_inners, d_attns, in_sems, out_sems,
):
    s = pl.program_id(0)

    def weight_copies():
        ins = []
        outs = []
        for i, (piece, late) in enumerate(zip((i0, i1, i2, i3), (j0, j1, j2, j3))):
            c, z_half = half_of(ids, i)
            y_half = ids[12] // 2 if i // 2 == 0 else 1 - ids[12] // 2
            for d in range(RING):
                x = lax.rem(ids[8] + RING - d, RING)
                ins.append(pltpu.make_async_copy(piece.at[d], w_in.at[x, c, z_half], in_sems.at[i, d]))
                for n in range(RING):
                    target = w_out.at[x, c, n, y_half]
                    outs.append(pltpu.make_async_copy(late.at[n, d], target, out_sems.at[i, d, n]))
        return ins, outs

    @pl.when(s == 0)
    def _():
        vec_grad[...] = jnp.zeros_like(vec_grad)
        bias_grad[...] = jnp.zeros_like(bias_grad)
        ins, outs = weight_copies()
        for copy in ins + outs:
            copy.start()
        for copy in ins:
            copy.wait()

    def inner_columns(n):
        return w_in[:, :, :, :, WIDTH + n * FF_STEP : WIDTH + (n + 1) * FF_STEP].reshape(WIDTH, FF_STEP)

    def outer_rows(n):
        return w_out[n].reshape(FF_STEP, WIDTH)

    @pl.when(s < SEQ_DEV)
    def _():
        x = joined(x_in).astype(f32)
        context = ctx_t[:, pl.ds(pl.multiple_of(s * SLOT, SLOT), SLOT)].T
        attn_out = mm(context, w_in[:, :, :, :, :WIDTH].reshape(WIDTH, WIDTH)) + vec[2:3]
        zhat1, r1 = normalised(x + attn_out)
        hidden = zhat1 * vec[3:4] + vec[4:5]
        hid_low = hidden.astype(bf16)
        hid_t[s] = hid_low.T

        @pl.when(s == 0)
        def _():
            for copy in weight_copies()[1]:
                copy.wait()

        branch = jnp.broadcast_to(vec[5:6], (SLOT, WIDTH))
        for n in range(FF_STEPS):
            cols = slice(n * FF_STEP, (n + 1) * FF_STEP)
            inner = mm(hid_low, inner_columns(n)) + bias_in[0:1, cols]
            half = 0.5 * lax.erf(inner * 0.7071067811865476) + 0.5
            bell = 0.3989422804014327 * jnp.exp(-0.5 * (inner * inner))
            act = (inner * half).astype(bf16)
            act_t[s, cols, :] = act.T
            slope[:, cols] = (half + inner * bell).astype(bf16)
            branch += mm(act, outer_rows(n))
        zhat2, r2 = normalised(hidden + branch)
        gain2 = vec[6:7]
        normed = zhat2 * gain2 + vec[7:8]
        valid = (lax.broadcasted_iota(jnp.int32, (SLOT, 1), 0) < ids[s]).astype(f32)
        keep = ids[4 + s] == 0
        layer_out[...] = (jnp.where(keep, normed, x) * valid).astype(bf16)
        dy = joined(c_in).astype(f32) * jnp.where(keep, valid, 0.0)
        vec_grad[1:2] += col_sum(dy * zhat2)
        vec_grad[2:3] += col_sum(dy)
        d_sum2 = norm_back(dy, zhat2, r2, gain2)
        d_branch = d_sum2.astype(bf16)
        d_branches[s] = d_branch
        vec_grad[0:1] += col_sum(d_branch.astype(f32))
        d_hidden = d_sum2
        for n in range(FF_STEPS):
            cols = slice(n * FF_STEP, (n + 1) * FF_STEP)
            d_act = mm_nt(d_branch, outer_rows(n))
            d_inner = (d_act * slope[:, cols].astype(f32)).astype(bf16)
            d_inners[s, n] = d_inner
            bias_grad[0:1, cols] += col_sum(d_inner.astype(f32))
            d_hidden += mm_nt(d_inner, inner_columns(n))
        vec_grad[3:4] += col_sum(d_hidden * zhat1)
        vec_grad[4:5] += col_sum(d_hidden)
        d_sum1 = norm_back(d_hidden, zhat1, r1, vec[3:4])
        dsum_out[...] = d_sum1
        d_attn = d_sum1.astype(bf16)
        dattn_out[...] = d_attn
        d_attns[s] = d_attn
        vec_grad[5:6] += col_sum(d_attn.astype(f32))

    @pl.when((s >= SEQ_DEV) & (s < SEQ_DEV + RING))
    def _():
        rows = pl.ds(pl.multiple_of((s - SEQ_DEV) * FF_STEP, FF_STEP), FF_STEP)
        value = mm(act_t[0, rows, :], d_branches[0])
        for i in range(1, SEQ_DEV):
            value += mm(act_t[i, rows, :], d_branches[i])
        cut_cores(ids, value.astype(bf16), outer_away, outer_mine)

    @pl.when((s >= SEQ_DEV + RING) & (s < SEQ_DEV + RING + FF_STEPS))
    def _():
        n = s - SEQ_DEV - RING
        value = mm(hid_t[0], d_inners[0, n])
        for i in range(1, SEQ_DEV):
            value += mm(hid_t[i], d_inners[i, n])
        cut_cores(ids, value.astype(bf16), inner_away, inner_mine)

    @pl.when(s == SEQ_DEV + RING + FF_STEPS)
    def _():
        value = mm(ctx_t[:, :SLOT], d_attns[0])
        for i in range(1, SEQ_DEV):
            value += mm(ctx_t[:, i * SLOT : (i + 1) * SLOT], d_attns[i])
        block = gather_back([vec_grad[i : i + 1] for i in range(6)] + [bias_grad[...]])
        cut_cores(ids, jnp.concatenate([value.astype(bf16), block], axis=1), out_away, out_mine)


def attention_backward(
    ids, dsum, dattn, qkv, exp_in, norm_in, ctxt_in, x_t, c_in, layer_in, p0, p1, p2, p3, p4, p5, p6, p7, i0, i1, i2, i3,
    back_out, attn_away, attn_mine,
    w, w_out, vec_grad, d_qkv, sems, out_sems,
):
    s = pl.program_id(0)

    @pl.when(s == 0)
    def _():
        vec_grad[...] = jnp.zeros_like(vec_grad)
        copies = attention_copies(ids, (p0, p1, p2, p3, p4, p5, p6, p7), w, sems)
        for i, piece in enumerate((i0, i1, i2, i3)):
            c, z_half = half_of(ids, i)
            for d in range(RING):
                x = lax.rem(ids[8] + RING - d, RING)
                source = piece.at[d, :, pl.ds(0, WIDTH)]
                copies.append(pltpu.make_async_copy(source, w_out.at[x, c, z_half], out_sems.at[i, d]))
        for copy in copies:
            copy.start()
        for copy in copies:
            copy.wait()

    @pl.when(s < SEQ_DEV)
    def _():
        d_sum1 = dsum[...]
        dctx_t = mm_nt(dattn[...], w_out[...].reshape(WIDTH, WIDTH)).T
        ctx_t = ctxt_in[...].astype(f32)
        k_t = qkv[:, WIDTH : 2 * WIDTH].T
        scaled = []
        deltas = []
        for h in range(HEADS):
            rows = slice(h * HEAD, (h + 1) * HEAD)
            one = (dctx_t[rows] * norm_in[0, h : h + 1, :]).astype(bf16)
            scaled.append(one)
            deltas.append(col_sum(one.astype(f32) * ctx_t[rows]))
        dctx_t = jnp.concatenate(scaled, axis=0)
        dctx = dctx_t.T
        low = lax.broadcasted_iota(jnp.int32, (SLOT, PAIR), 1) < HEAD
        dq_t = []
        for p in range(0, WIDTH, PAIR):
            cols = slice(p, p + PAIR)
            q_pair = qkv[:, cols]
            v_pair = qkv[:, 2 * WIDTH + p : 2 * WIDTH + p + PAIR]
            dks = []
            dvs = []
            for half in range(2):
                h = p // HEAD + half
                v_one = jnp.where(low if half == 0 else ~low, v_pair, jnp.zeros_like(v_pair))
                d_probs = mm(v_one, dctx_t[cols]) - deltas[h]
                expo = exp_in[0, h]
                d_scores = (expo.astype(f32) * d_probs).astype(bf16)
                dvs.append(mm(expo, dctx[:, cols]))
                dks.append(mm(d_scores, q_pair))
                dq_t.append(mm(k_t[h * HEAD : (h + 1) * HEAD], d_scores))
            d_qkv[s, 1, :, cols] = jnp.where(low, dks[0], dks[1]).astype(bf16)
            d_qkv[s, 2, :, cols] = jnp.where(low, dvs[0], dvs[1]).astype(bf16)
        dq = (jnp.concatenate(dq_t, axis=0).T * HEAD**-0.5).astype(bf16)
        d_qkv[s, 0] = dq
        vec_grad[0:1] += col_sum(dq.astype(f32))
        vec_grad[1:2] += col_sum(d_qkv[s, 2].astype(f32))
        d_in = d_sum1
        for n in range(3):
            d_in += mm_nt(d_qkv[s, n], columns(w, n * WIDTH, (n + 1) * WIDTH))
        valid = (lax.broadcasted_iota(jnp.int32, (SLOT, 1), 0) < ids[s]).astype(f32)
        upstream = joined(c_in).astype(f32) * valid
        keep = ids[4 + s] == 0
        grad = jnp.where(keep, d_in, upstream).astype(bf16)
        back_out[:, 0, 0] = layer_in[...].reshape(GROUP, PIECE, WIDTH)
        back_out[:, 1, 0] = grad.reshape(GROUP, PIECE, WIDTH)

    @pl.when(s == SEQ_DEV)
    def _():
        values = []
        for n in range(3):
            value = mm(x_t[:, :SLOT], d_qkv[0, n])
            for i in range(1, SEQ_DEV):
                value += mm(x_t[:, i * SLOT : (i + 1) * SLOT], d_qkv[i, n])
            values.append(value.astype(bf16))
        values.append(gather_back([vec_grad[0:1], vec_grad[1:2]]))
        cut_cores(ids, jnp.concatenate(values, axis=1), attn_away, attn_mine)


def in_order(values, me):
    ordered = []
    for j in range(RING):
        step = lax.rem(me + RING - j, RING)
        value = values[0]
        for d in (1, 2, 3):
            value = jnp.where(step == d, values[d], value)
        ordered.append(value)
    return ordered


def pack_rows(ids, query, key, value, out, inner, row, packed):
    for i, ref in enumerate((query, key, value, out)):
        block = jnp.concatenate([ref[...].astype(f32), jnp.zeros((2, WIDTH), f32)], axis=0)
        if i == 0:
            line = lax.broadcasted_iota(jnp.int32, (8, WIDTH), 0)
            block = jnp.where(line == 6, row[...].astype(f32), block)
        packed[:, i * WIDTH : (i + 1) * WIDTH] = block.astype(bf16)
    block = jnp.concatenate([inner[...].astype(f32), jnp.zeros((2, FF), f32)], axis=0)
    packed[:, 4 * WIDTH :] = block.astype(bf16)


def merge_rows(ids, own, r1, r2, r3, attn_out, inner_out):
    ordered = in_order([v[...].astype(f32) for v in (own, r1, r2, r3)], ids[12])
    width = 3 * WIDTH
    rows = jnp.concatenate([v[:6] for v in ordered], axis=0).astype(bf16)
    attn_out[:, :width] = rows[:, :width]
    inner_out[...] = rows[:, width:]
    row = jnp.concatenate([v[6:7, :128] for v in ordered], axis=1)
    first = lax.broadcasted_iota(jnp.int32, (24, 4 * 128), 0) == 0
    attn_out[:, width:] = jnp.where(first, jnp.broadcast_to(row, (24, 4 * 128)), 0.0).astype(bf16)


def stack_rows(ids, own, r1, r2, r3, out):
    for d, piece in enumerate((own, r1, r2, r3)):
        out[lax.rem(ids[11] + RING - d, RING)] = piece[...]


def ahead(ids, axis, step):
    return lax.rem(ids[axis] + step, RING)


def sum_of(refs):
    total = refs[0][...].astype(f32)
    for ref in refs[1:]:
        total += ref[...].astype(f32)
    return total


def sum_blocks(ids, *refs):
    *parts, o0, o1, o2, o3, scratch = refs
    start = 0
    for mine, core in zip(parts[::2], parts[1::2]):
        end = start + mine.shape[2]
        scratch[:, start:end] = mine[0].astype(f32) + core[0].astype(f32)
        start = end
    for d, out in enumerate((o0, o1, o2, o3)):
        first = pl.multiple_of(ahead(ids, 11, d) * 24, 8)
        out[0] = scratch[pl.ds(first, 24), :].astype(bf16)


def sum_attention(ids, outer, mine, core, o0, o1, o2, o3, scratch):
    scratch[...] = mine[0].astype(f32) + core[0].astype(f32)
    for d, out in enumerate((o0, o1, o2, o3)):
        z = ahead(ids, 11, d)
        first = pl.multiple_of(z * 24, 8)
        out[0, :, : scratch.shape[1]] = scratch[pl.ds(first, 24), :].astype(bf16)
        out[0, :, scratch.shape[1] :] = outer[0, z]


def sum_outer(ids, mine, core, out):
    total = mine[0].astype(f32) + core[0].astype(f32)
    for z in range(RING):
        for y in range(RING):
            first = 96 * z + 24 * y
            out[y, 0, z] = total[first : first + 24].astype(bf16)


def sum_first(ids, value, out):
    for z in range(RING):
        out[0, z] = sum_of([value.at[y, 0, z] for y in range(RING)]).astype(bf16)


def split_rows(ids, p0, p1, p2, p3, o0, o1, o2, o3, *refs):
    *rest, scratch = refs
    width = o0.shape[2]
    total = sum_of([p.at[0] for p in (p0, p1, p2, p3)])
    if rest:
        rest[0][0] = total[:, width + 128 :].astype(bf16)
    for y in range(RING):
        vectors = total[y : y + 1, width : width + 128]
        row = jnp.concatenate([vectors, jnp.zeros((1, width - 128), f32)], axis=1)
        rows = total[6 * y : 6 * y + 6, :width]
        scratch[y] = jnp.concatenate([rows, row, jnp.zeros((1, width), f32)], axis=0)
    for d, out in enumerate((o0, o1, o2, o3)):
        out[0] = scratch[ahead(ids, 12, d)].astype(bf16)


LAST = FF + WIDTH + 3 * WIDTH + 3 * WIDTH


def join_flows(ids, i0, i1, i2, i3, a0, a1, a2, a3, outer, o0, o1, o2, o3, scratch):
    scratch[:, :, : FF + WIDTH] = sum_of((i0, i1, i2, i3))
    scratch[:, :, FF + WIDTH : FF + 4 * WIDTH] = sum_of((a0, a1, a2, a3))
    for x in range(RING):
        total = outer[x].astype(f32)
        for k in range(3):
            start = FF + (4 + k) * WIDTH
            scratch[x, :, start : start + WIDTH] = total[8 * k : 8 * k + 8]
    for d, out in enumerate((o0, o1, o2, o3)):
        out[...] = scratch[ahead(ids, 8, d)].astype(bf16)


def split_ffn(ids, p0, p1, p2, p3, inner, outer):
    for d, piece in enumerate((p0, p1, p2, p3)):
        inner[d] = piece[:, :MIXED]
        halves = [piece[:, MIXED + i * WIDTH : MIXED + (i + 1) * WIDTH].astype(f32) for i in range(2)]
        outer[d] = jnp.concatenate(halves, axis=0).astype(bf16)


def write_grads(ids, p0, p1, p2, p3, query, key, value, out, inner, outer, vectors):
    total = sum_of((p0, p1, p2, p3))
    inner[...] = total[:6, :FF]
    out[...] = total[:6, FF : FF + WIDTH]
    start = FF + WIDTH
    query[...] = total[:6, start : start + WIDTH]
    key[...] = total[:6, start + WIDTH : start + 2 * WIDTH]
    value[...] = total[:6, start + 2 * WIDTH : start + 3 * WIDTH]
    vectors[...] = jnp.concatenate([total[6:7, :128], total[6:7, start : start + 128]], axis=0)
    start += 3 * WIDTH
    for k in range(3):
        outer[8 * k : 8 * k + 8] = total[:, start + k * WIDTH : start + (k + 1) * WIDTH]


def whole(shape):
    return pl.BlockSpec(shape, lambda s, ids: (0,) * len(shape), pipeline_mode=pl.Buffered(1))


def sequence(s):
    return jnp.minimum(s, SEQ_DEV - 1)


DEALT_SPEC = pl.BlockSpec((GROUP, 1, PIECE, WIDTH), lambda s, ids: (0, sequence(s), 0, 0))


def by_rows(width):
    return pl.BlockSpec((SLOT, width), lambda s, ids: (sequence(s), 0))


def rows_of(width, kind):
    return jax.ShapeDtypeStruct((ROWS, width), kind)


EXP_SPEC = pl.BlockSpec((1, HEADS, SLOT, SLOT), lambda s, ids: (sequence(s), 0, 0, 0))
NORM_SPEC = pl.BlockSpec((1, 16, SLOT), lambda s, ids: (sequence(s), 0, 0))
RETURN_SPEC = pl.BlockSpec((GROUP, 2, 1, PIECE, WIDTH), lambda s, ids: (0, 0, sequence(s), 0, 0))
RETURN_SHAPE = jax.ShapeDtypeStruct((GROUP, 2, SEQ_DEV, PIECE, WIDTH), bf16)


def by_columns(height):
    return pl.BlockSpec((height, SLOT), lambda s, ids: (0, sequence(s)))


def columns_of(height):
    return jax.ShapeDtypeStruct((height, ROWS), bf16)


def run(kernel, grid, ins, outs, operands, name, flops, moved, scratch, limit):
    return pl.pallas_call(
        kernel,
        grid_spec=pltpu.PrefetchScalarGridSpec(
            num_scalar_prefetch=1,
            grid=grid,
            in_specs=ins,
            out_specs=[spec for spec, _ in outs],
            scratch_shapes=list(scratch),
        ),
        out_shape=[shape for _, shape in outs],
        compiler_params=pltpu.CompilerParams(
            vmem_limit_bytes=limit * MIB, dimension_semantics=("arbitrary",) * len(grid)
        ),
        cost_estimate=pl.CostEstimate(flops=flops, bytes_accessed=moved, transcendentals=0),
        name=name,
    )(*operands)


def out_rows(width, kind):
    return (by_rows(width), rows_of(width, kind))


def out_columns(height):
    return (by_columns(height), columns_of(height))


def out_whole(shape):
    return (whole(shape), jax.ShapeDtypeStruct(shape, f32))


ANYWHERE = pl.BlockSpec(memory_space=pl.ANY)
ATTENTION_SCRATCH = [pltpu.VMEM((RING, CORES, 96, PACKED), bf16)]


def call_forward(ids, dealt, weights, perm):
    return run(
        attention_forward,
        (SEQ_DEV,),
        [DEALT_SPEC] + [ANYWHERE] * 8 + [whole((32, 16))],
        [
            out_columns(WIDTH),
            out_rows(3 * WIDTH, bf16),
            (EXP_SPEC, jax.ShapeDtypeStruct((SEQ_DEV, HEADS, SLOT, SLOT), bf16)),
            (NORM_SPEC, jax.ShapeDtypeStruct((SEQ_DEV, 16, SLOT), f32)),
            out_columns(WIDTH),
            out_whole((8, WIDTH)),
            out_whole((1, FF)),
            out_whole((8, 128)),
        ],
        (ids, dealt, *weights, perm),
        "attention_forward",
        8 * 10**9,
        5 * 10**6,
        ATTENTION_SCRATCH + [pltpu.VMEM((32, PACKED - 3 * WIDTH), f32), pltpu.SemaphoreType.DMA((8,))],
        58,
    )


def halves(block, shape, where):
    return [(pl.BlockSpec(block, lambda s, ids: where(s)), jax.ShapeDtypeStruct(shape, bf16))] * 2


def call_ffn(ids, dealt, dealt_c, ctx_t, inner, outer, vec, bias_in):
    outer_rows = FF // GROUP
    inner_rows = WIDTH // GROUP
    first = SEQ_DEV
    second = first + RING
    return run(
        feed_forward,
        (second + FF_STEPS + 1,),
        [DEALT_SPEC] * 2
        + [whole((WIDTH, ROWS))]
        + [ANYWHERE] * 8
        + [whole((8, WIDTH)), whole((1, FF))],
        [out_rows(WIDTH, bf16), out_rows(WIDTH, f32), out_rows(WIDTH, bf16)]
        + halves(
            (1, outer_rows, WIDTH), (RING, outer_rows, WIDTH), lambda s: (jnp.clip(s - first, 0, RING - 1), 0, 0)
        )
        + halves(
            (RING, inner_rows, FF_STEP),
            (RING, inner_rows, FF),
            lambda s: (0, 0, jnp.clip(s - second, 0, FF_STEPS - 1)),
        )
        + halves((RING, inner_rows, WIDTH + 128), (RING, inner_rows, WIDTH + 128), lambda s: (0, 0, 0)),
        (ids, dealt, dealt_c, ctx_t, *inner, *outer, vec, bias_in),
        "feed_forward",
        50 * 10**9,
        40 * 10**6,
        [
            pltpu.VMEM((SLOT, FF), bf16),
            pltpu.VMEM((8, WIDTH), f32),
            pltpu.VMEM((1, FF), f32),
            pltpu.VMEM((RING, CORES, 2, 48, MIXED), bf16),
            pltpu.VMEM((RING, CORES, RING, 2, 48, WIDTH), bf16),
            pltpu.VMEM((SEQ_DEV, WIDTH, SLOT), bf16),
            pltpu.VMEM((SEQ_DEV, FF, SLOT), bf16),
            pltpu.VMEM((SEQ_DEV, SLOT, WIDTH), bf16),
            pltpu.VMEM((SEQ_DEV, FF_STEPS, SLOT, FF_STEP), bf16),
            pltpu.VMEM((SEQ_DEV, SLOT, WIDTH), bf16),
            pltpu.SemaphoreType.DMA((RING, RING)),
            pltpu.SemaphoreType.DMA((RING, RING, RING)),
        ],
        58,
    )


def call_backward(ids, dsum, dattn, qkv, expo, norm, ctx_t, x_t, dealt_c, layer, weights, inner):
    block = (RING, WIDTH // GROUP, 3 * WIDTH + 128)
    return run(
        attention_backward,
        (SEQ_DEV + 1,),
        [by_rows(WIDTH), by_rows(WIDTH), by_rows(3 * WIDTH), EXP_SPEC, NORM_SPEC, by_columns(WIDTH)]
        + [whole((WIDTH, ROWS)), DEALT_SPEC, by_rows(WIDTH)]
        + [ANYWHERE] * 12,
        [(RETURN_SPEC, RETURN_SHAPE)] + halves(block, block, lambda s: (0, 0, 0)),
        (ids, dsum, dattn, qkv, expo, norm, ctx_t, x_t, dealt_c, layer, *weights, *inner),
        "attention_backward",
        28 * 10**9,
        30 * 10**6,
        ATTENTION_SCRATCH
        + [
            pltpu.VMEM((RING, CORES, 2, 48, WIDTH), bf16),
            pltpu.VMEM((8, WIDTH), f32),
            pltpu.VMEM((SEQ_DEV, 3, SLOT, WIDTH), bf16),
            pltpu.SemaphoreType.DMA((8,)),
            pltpu.SemaphoreType.DMA((RING, RING)),
        ],
        58,
    )


def call_by_x(kernel, name, ids, pieces, at, out_shapes, out_at, scratch):
    count = len(out_shapes)

    def every_x(ids, *refs):
        ins, outs, rest = refs[: len(pieces)], refs[len(pieces) :][:count], refs[len(pieces) + count :]
        for x in range(RING):
            one = (pl.ds(x, 1),)
            kernel(
                ids,
                *[ref.at[(slice(None),) * at + one] for ref in ins],
                *[ref.at[(slice(None),) * out_at + one] for ref in outs],
                *rest,
            )

    return call_small(every_x, name, ids, pieces, *out_shapes, scratch=scratch)


def call_small(kernel, name, ids, pieces, *out_shapes, kind=bf16, scratch=()):
    def full(shape):
        return pl.BlockSpec(shape, lambda i, ids: (0,) * len(shape))

    return run(
        kernel,
        (1,),
        [full(piece.shape) for piece in pieces],
        [(full(shape), jax.ShapeDtypeStruct(shape, kind)) for shape in out_shapes],
        (ids, *pieces),
        name,
        10**6,
        6 * 10**6,
        [pltpu.VMEM(shape, f32) for shape in scratch],
        30,
    )


def shift(value, axis, step):
    size = CORES if axis == "core" else RING
    return lax.ppermute(value, axis, [(i, (i + step) % size) for i in range(size)])


def swap(value, axis):
    return lax.ppermute(value, axis, [(i, i ^ 1) for i in range(RING)])


def arrivals(value, axis):
    return [value] + [shift(value, axis, step) for step in (1, 2, 3)]


def both_cores(pieces):
    return [part for piece in pieces for part in (piece, shift(piece, "core", 1))]


def paired(value, axis):
    return in_half(value, swap(value, axis), axis)


def in_half(value, other, axis):
    even = lax.rem(lax.axis_index(axis), 2) == 0
    return jnp.where(even, value, other), jnp.where(even, other, value)


def hold(value, *others):
    return lax.optimization_barrier((value, *others))[0]


def send_ring(parts, axis):
    return [parts[0]] + [shift(parts[step], axis, step) for step in (1, 2, 3)]


def over(value, axis):
    return lax.all_to_all(value, axis, split_axis=0, concat_axis=0, tiled=True)


def body(
    tokens,
    cotangent,
    perm,
    lengths,
    drop,
    w_query,
    b_query,
    w_key,
    w_value,
    b_value,
    w_out,
    b_out,
    norm1_gain,
    norm1_bias,
    w_inner,
    b_inner,
    w_outer,
    b_outer,
    norm2_gain,
    norm2_bias,
):
    me_x = lax.axis_index("x")
    me_c = lax.axis_index("core")
    me_z = lax.axis_index("z")
    me_y = lax.axis_index("y")
    first = ((me_z * RING + me_y) * 8 + me_x * CORES + me_c) * SEQ_DEV
    places = jnp.stack([me_x, me_c, first, me_z, me_y]).astype(jnp.int32)
    places = jnp.pad(places, (8, 3))

    vectors = [b_query, b_value, b_out, norm1_gain, norm1_bias, b_outer, norm2_gain, norm2_bias, b_inner]
    vectors += [lengths.astype(bf16), drop.astype(bf16)]
    row = jnp.zeros((WIDTH,), bf16)
    start = 0
    for vector in vectors:
        end = start + vector.shape[0]
        row += jnp.pad(vector, (start, WIDTH - end))
        start = end
    (piece,) = call_small(
        pack_rows, "pack_rows", places, (w_query, w_key, w_value, w_out, w_inner, row[None]), (8, 4 * WIDTH + FF)
    )
    pieces_y = arrivals(piece, "y")
    dp = ("x", "core")
    dealt = (GROUP, SEQ_DEV, PIECE, WIDTH)
    dealt_x = over(tokens.reshape(dealt), dp)
    attn_y, inner_y = call_small(merge_rows, "merge_rows", places, pieces_y, (24, PACKED), (24, MIXED))
    (attn_zy,) = call_small(
        stack_rows, "stack_rows", places, arrivals(attn_y, "z"), (RING, 24, PACKED)
    )

    outer_pair = paired(w_outer, "y")
    ffn_x = arrivals(jnp.concatenate([hold(inner_y, dealt_x), *outer_pair], axis=1), "x")
    ffn_x[0] = hold(ffn_x[0], attn_zy)
    inner_x, outer_x = call_small(
        split_ffn, "split_ffn", places, ffn_x, (RING, 24, MIXED), (RING, 48, WIDTH)
    )
    attn_x = arrivals(hold(attn_zy, dealt_x).reshape(96, PACKED), "x")
    inner_z = swap(inner_x, "z")
    outer_z = over(jnp.broadcast_to(outer_x[None], (RING, RING, 48, WIDTH)), "z")
    inner_z = jnp.concatenate(in_half(inner_x, inner_z, "z"), axis=1)
    attn_pieces = both_cores([attn_x[0]] + [hold(p, inner_z) for p in attn_x[1:]])
    inner_far = shift(hold(inner_z, outer_z), "z", 2)
    outer_far = shift(outer_z, "y", 2)
    dealt_c = over(hold(cotangent, inner_z).reshape(dealt), dp)

    x_t, qkv, expo, norm, ctx_t, vec, inner_bias, info = call_forward(
        places, dealt_x, attn_pieces, perm.reshape(32, 16)
    )
    ids = jnp.concatenate([info[:, 0].astype(jnp.int32), places[8:]])

    inner_pieces = both_cores([hold(inner_z, ctx_t, dealt_c), hold(inner_far, ctx_t)])
    outer_pieces = both_cores([hold(outer_z, ctx_t), hold(outer_far, ctx_t)])
    (
        layer, d_sum1, d_attn, outer_away, outer_mine, inner_away, inner_mine, out_away, out_mine
    ) = call_ffn(ids, dealt_x, dealt_c, ctx_t, inner_pieces, outer_pieces, vec, inner_bias)

    inner_core = shift(inner_away, "core", 1)
    out_core = shift(out_away, "core", 1)
    outer_core = shift(hold(outer_away, out_core), "core", 1)
    inner_width = FF + WIDTH + 128
    inner_parts = call_by_x(
        sum_blocks, "sum_blocks", places, (inner_mine, inner_core, out_mine, out_core), 0,
        [(RING, 24, inner_width)] * RING, 0, [(96, inner_width)],
    )
    (outer_sum,) = call_by_x(
        sum_outer, "sum_outer", hold(places, inner_parts[0]), (outer_mine, outer_core), 0,
        [(RING, RING, RING, 24, WIDTH)], 1, [],
    )
    inner_parts = send_ring(inner_parts, "z")
    outer_y = over(outer_sum, "y")

    d_sum1, d_attn = lax.optimization_barrier((d_sum1, d_attn, inner_parts[0], outer_sum))[:2]
    back, attn_away, attn_mine = call_backward(
        ids, d_sum1, d_attn, qkv, expo, norm, ctx_t, x_t, dealt_c, layer, attn_pieces, inner_pieces
    )

    attn_core = shift(hold(attn_away, outer_y, *inner_parts[1:]), "core", 1)
    (outer_z,) = call_by_x(
        sum_first, "sum_first", hold(places, attn_away), (hold(outer_y, attn_away),), 1,
        [(RING, RING, 24, WIDTH)], 0, [],
    )
    attn_width = 3 * WIDTH + 128
    attn_parts = call_by_x(
        sum_attention, "sum_attention", places, (outer_z, attn_mine, attn_core), 0,
        [(RING, 24, attn_width + WIDTH)] * RING, 0, [(96, attn_width)],
    )
    attn_first = attn_parts[0]
    attn_parts = send_ring(attn_parts, "z")
    back = over(hold(back, outer_z), dp)

    inner_parts = [hold(p, attn_first) for p in inner_parts]
    inner_parts = call_by_x(
        split_rows, "split_rows", places, inner_parts, 0,
        [(RING, 8, FF + WIDTH)] * RING, 0, [(RING, 8, FF + WIDTH)],
    )
    *attn_parts, outer_z = call_by_x(
        split_rows, "split_rows", hold(places, inner_parts[0]), attn_parts, 0,
        [(RING, 8, 3 * WIDTH)] * RING + [(RING, 24, WIDTH)], 0, [(RING, 8, 3 * WIDTH)],
    )
    inner_parts = send_ring(inner_parts, "y")
    attn_parts = send_ring(attn_parts, "y")
    last = call_small(
        join_flows, "join_flows", places, [*inner_parts, *attn_parts, outer_z], *[(8, LAST)] * 4,
        scratch=[(RING, 8, LAST)],
    )
    back = hold(back, last[0])
    layer_final = back[:, 0].reshape(GROUP * SEQ_DEV, PIECE, WIDTH)
    grad_final = back[:, 1].reshape(GROUP * SEQ_DEV, PIECE, WIDTH)
    square = (6, WIDTH)
    grad_query, grad_key, grad_value, grad_out, grad_inner, grad_outer, vectors = call_small(
        write_grads, "write_grads", hold(places, layer_final), send_ring(last, "x"),
        square, square, square, square, (6, FF), (24, WIDTH), (2, 128), kind=f32,
    )
    ffn_vectors = [vectors[0, 6 * i : 6 * i + 6] for i in range(6)]
    return (
        layer_final,
        grad_final,
        grad_query,
        vectors[1, :6],
        grad_key,
        grad_value,
        vectors[1, 6:12],
        grad_out,
        ffn_vectors[5],
        ffn_vectors[3],
        ffn_vectors[4],
        grad_inner,
        vectors[0, 36:60],
        grad_outer,
        ffn_vectors[0],
        ffn_vectors[1],
        ffn_vectors[2],
    )


def solution(mesh):
    chips = Mesh(mesh.devices.reshape(RING, CORES, RING, RING), ("x", "core", "z", "y"))
    dp = ("x", "core")
    fsdp = ("z", "y")
    every = P(dp + fsdp)
    rows = P(dp + fsdp, None)
    whole_rows = P(fsdp, dp, None)
    return jax.shard_map(
        body,
        mesh=chips,
        in_specs=(
            whole_rows, whole_rows, P(), every, every,
            rows, every, rows, rows, every, rows, every, every, every,
            rows, every, rows, every, every, every,
        ),
        out_specs=(
            whole_rows, whole_rows,
            rows, every, rows, rows, every, rows, every, every, every,
            rows, every, rows, every, every, every,
        ),
        check_vma=False,
    )
```

```python
import functools
import jax
import jax.numpy as jnp
from jax import lax
from jax.experimental import pallas as pl
from jax.experimental.pallas import tpu as pltpu
from jax.sharding import Mesh
from jax.sharding import PartitionSpec as P

HEADS = 12
HEAD = 64
WIDTH = 768
FF = 3072
SLOT = 256
SEQ_DEV = 4
RING = 4
CORES = 2
PIECE = 32
GROUP = RING * CORES
ROWS = SEQ_DEV * SLOT
PAIR = 2 * HEAD
PACKED = 3 * WIDTH + 512
MIXED = WIDTH + FF

epsilon = 1e-05
bf16 = jnp.bfloat16
f32 = jnp.float32
MIB = 1024 * 1024

TN = (((0,), (0,)), ((), ()))
NT = (((1,), (1,)), ((), ()))


def mm(a, b):
    return jnp.dot(a, b, preferred_element_type=f32)


def mm_nt(a, b):
    return lax.dot_general(a, b, NT, preferred_element_type=f32)


def mm_tn(a, b):
    return lax.dot_general(a, b, TN, preferred_element_type=f32)


def joined(ref):
    return ref[...].reshape(SLOT, WIDTH)


def spread(extras, start, width):
    total = 128 * width
    group = lax.broadcasted_iota(jnp.int32, (32, total), 0)
    owner = lax.broadcasted_iota(jnp.int32, (32, total), 1) // width
    pick = lax.broadcasted_iota(jnp.int32, (width, total), 0)
    within = lax.rem(lax.broadcasted_iota(jnp.int32, (width, total), 1), width)
    chosen = (pick == within).astype(bf16)
    out = jnp.zeros((32, total), f32)
    for y in range(RING):
        values = extras[:, 128 * y + start : 128 * y + start + width].astype(bf16)
        out += jnp.where(owner == group * RING + y, mm(values, chosen), 0.0)
    return jnp.sum(out, axis=0, keepdims=True)


def gather_back(vectors):
    values = jnp.zeros((128, 128), f32)
    start = 0
    for vector in vectors:
        total = vector.shape[1]
        width = total // 128
        owner = lax.broadcasted_iota(jnp.int32, (128, total), 1) // width
        mine = owner == lax.broadcasted_iota(jnp.int32, (128, total), 0)
        within = lax.rem(lax.broadcasted_iota(jnp.int32, (total, 128), 0), width)
        column = lax.broadcasted_iota(jnp.int32, (total, 128), 1)
        spots = (column == within + start).astype(bf16)
        values += mm(jnp.where(mine, vector, 0.0).astype(bf16), spots)
        start += width
    row = lax.broadcasted_iota(jnp.int32, (WIDTH, 128), 0)
    device = lax.broadcasted_iota(jnp.int32, (WIDTH, 128), 1)
    within = lax.rem(row, 24)
    picks = (within < RING) & (row // 24 * RING + within == device)
    return mm(picks.astype(bf16), values.astype(bf16)).astype(bf16)


def attention_copies(ids, pieces, w, sems):
    copies = []
    for i, piece in enumerate(pieces):
        x = lax.rem(ids[8] + RING - i // 2, RING)
        c = ids[9] if i % 2 == 0 else 1 - ids[9]
        copies.append(pltpu.make_async_copy(piece, w.at[x, c], sems.at[i]))
    return copies


def half_of(ids, i):
    c = ids[9] if i % 2 == 0 else 1 - ids[9]
    return c, ids[11] // 2 if i // 2 == 0 else 1 - ids[11] // 2


def columns(w, start, end):
    return w[:, :, :, start:end].reshape(WIDTH, end - start)


def attention_forward(
    ids, x_in, p0, p1, p2, p3, p4, p5, p6, p7, perm,
    xt_out, qkv_out, exp_out, norm_out, ctxt_out, vec, bias_out, info,
    w, extras, sems,
):
    s = pl.program_id(0)

    @pl.when(s == 0)
    def _():
        copies = attention_copies(ids, (p0, p1, p2, p3, p4, p5, p6, p7), w, sems)
        for copy in copies:
            copy.start()
        for copy in copies:
            copy.wait()
        rows = columns(w, 3 * WIDTH, PACKED).astype(f32).reshape(32, 24, PACKED - 3 * WIDTH)
        extras[...] = jnp.sum(rows, axis=1)
        for i in range(8):
            vec[i : i + 1] = spread(extras, 6 * i, 6)
        bias_out[...] = spread(extras, 48, 24)

    length = jnp.zeros((1, 1), f32)
    dropped = jnp.zeros((1, 1), f32)
    for y in range(RING):
        hit = perm[:, RING * y : RING * y + 4] == ids[10] + s
        length += jnp.sum(jnp.where(hit, extras[:, 128 * y + 72 : 128 * y + 76], 0.0), keepdims=True)
        dropped += jnp.sum(jnp.where(hit, extras[:, 128 * y + 76 : 128 * y + 80], 0.0), keepdims=True)
    line = lax.broadcasted_iota(jnp.int32, (8, 128), 0)
    info[...] = jnp.where(line == s, length, jnp.where(line == s + 4, dropped, info[...]))

    x = joined(x_in)
    xt_out[...] = x.T
    q = ((mm(x, columns(w, 0, WIDTH)) + vec[0:1]).astype(bf16).astype(f32) * HEAD**-0.5).astype(bf16)
    k = mm(x, columns(w, WIDTH, 2 * WIDTH)).astype(bf16)
    v = (mm(x, columns(w, 2 * WIDTH, 3 * WIDTH)) + vec[1:2]).astype(bf16)
    qkv_out[:, :WIDTH] = q
    qkv_out[:, WIDTH : 2 * WIDTH] = k
    qkv_out[:, 2 * WIDTH :] = v
    q_t = q.T
    v_t = v.T
    keys = lax.broadcasted_iota(jnp.int32, (SLOT, 1), 0).astype(f32)
    bias = jnp.where(keys < length, 0.0, -1e30)
    low = lax.broadcasted_iota(jnp.int32, (SLOT, PAIR), 1) < HEAD
    ctx_t = []
    for h in range(HEADS):
        p = h // 2 * PAIR
        k_pair = k[:, p : p + PAIR]
        k_one = jnp.where(low if h % 2 == 0 else ~low, k_pair, jnp.zeros_like(k_pair))
        scores = mm(k_one, q_t[p : p + PAIR]) + bias
        top = jnp.max(scores, axis=0, keepdims=True)
        expo = jnp.exp(scores - top)
        inverse = 1.0 / jnp.sum(expo, axis=0, keepdims=True)
        norm_out[0, h : h + 1, :] = inverse
        expo = expo.astype(bf16)
        exp_out[0, h] = expo
        ctx_t.append(mm(v_t[h * HEAD : (h + 1) * HEAD], expo) * inverse)
    ctx_t = jnp.concatenate(ctx_t, axis=0).astype(bf16)
    ctxt_out[...] = ctx_t


def row_mean(v):
    return jnp.mean(v, axis=-1, keepdims=True)


def normalised(z):
    center = z - row_mean(z)
    r = lax.rsqrt(row_mean(center * center) + epsilon)
    return center * r, r


def norm_back(dy, zhat, r, gain):
    e = dy * gain
    return r * (e - row_mean(e) - zhat * row_mean(e * zhat))


def col_sum(v):
    return jnp.sum(v, axis=0, keepdims=True)


FF_STEP = 768
FF_STEPS = FF // FF_STEP


def cut_cores(ids, value, away, mine):
    blocks, rows, _ = away.shape
    first = ids[9] == 0
    for x in range(blocks):
        even = value[2 * x * rows : (2 * x + 1) * rows]
        odd = value[(2 * x + 1) * rows : (2 * x + 2) * rows]
        away[x] = jnp.where(first, odd, even)
        mine[x] = jnp.where(first, even, odd)


def feed_forward(
    ids, x_in, c_in, ctx_t, i0, i1, i2, i3, j0, j1, j2, j3, vec, bias_in,
    layer_out, dsum_out, dattn_out, outer_away, outer_mine, inner_away, inner_mine, out_away, out_mine,
    slope, vec_grad, bias_grad, w_in, w_out, hid_t, act_t, d_branches, d_inners, d_attns, in_sems, out_sems,
):
    s = pl.program_id(0)

    @pl.when(s == 0)
    def _():
        vec_grad[...] = jnp.zeros_like(vec_grad)
        bias_grad[...] = jnp.zeros_like(bias_grad)
        copies = []
        for i, (piece, late) in enumerate(zip((i0, i1, i2, i3), (j0, j1, j2, j3))):
            c, z_half = half_of(ids, i)
            y_half = ids[12] // 2 if i // 2 == 0 else 1 - ids[12] // 2
            for d in range(RING):
                x = lax.rem(ids[8] + RING - d, RING)
                copies.append(pltpu.make_async_copy(piece.at[d], w_in.at[x, c, z_half], in_sems.at[i, d]))
                for n in range(RING):
                    target = w_out.at[x, c, n, y_half]
                    copies.append(pltpu.make_async_copy(late.at[n, d], target, out_sems.at[i, d, n]))
        for copy in copies:
            copy.start()
        for copy in copies:
            copy.wait()

    def inner_columns(n):
        return w_in[:, :, :, :, WIDTH + n * FF_STEP : WIDTH + (n + 1) * FF_STEP].reshape(WIDTH, FF_STEP)

    def outer_rows(n):
        return w_out[n].reshape(FF_STEP, WIDTH)

    @pl.when(s < SEQ_DEV)
    def _():
        x = joined(x_in).astype(f32)
        context = ctx_t[:, pl.ds(pl.multiple_of(s * SLOT, SLOT), SLOT)].T
        attn_out = mm(context, w_in[:, :, :, :, :WIDTH].reshape(WIDTH, WIDTH)) + vec[2:3]
        zhat1, r1 = normalised(x + attn_out)
        hidden = zhat1 * vec[3:4] + vec[4:5]
        hid_low = hidden.astype(bf16)
        hid_t[s] = hid_low.T
        branch = jnp.broadcast_to(vec[5:6], (SLOT, WIDTH))
        for n in range(FF_STEPS):
            cols = slice(n * FF_STEP, (n + 1) * FF_STEP)
            inner = mm(hid_low, inner_columns(n)) + bias_in[0:1, cols]
            half = 0.5 * lax.erf(inner * 0.7071067811865476) + 0.5
            bell = 0.3989422804014327 * jnp.exp(-0.5 * (inner * inner))
            act = (inner * half).astype(bf16)
            act_t[s, cols, :] = act.T
            slope[:, cols] = (half + inner * bell).astype(bf16)
            branch += mm(act, outer_rows(n))
        zhat2, r2 = normalised(hidden + branch)
        gain2 = vec[6:7]
        normed = zhat2 * gain2 + vec[7:8]
        valid = (lax.broadcasted_iota(jnp.int32, (SLOT, 1), 0) < ids[s]).astype(f32)
        keep = ids[4 + s] == 0
        layer_out[...] = (jnp.where(keep, normed, x) * valid).astype(bf16)
        dy = joined(c_in).astype(f32) * jnp.where(keep, valid, 0.0)
        vec_grad[1:2] += col_sum(dy * zhat2)
        vec_grad[2:3] += col_sum(dy)
        d_sum2 = norm_back(dy, zhat2, r2, gain2)
        d_branch = d_sum2.astype(bf16)
        d_branches[s] = d_branch
        vec_grad[0:1] += col_sum(d_branch.astype(f32))
        d_hidden = d_sum2
        for n in range(FF_STEPS):
            cols = slice(n * FF_STEP, (n + 1) * FF_STEP)
            d_act = mm_nt(d_branch, outer_rows(n))
            d_inner = (d_act * slope[:, cols].astype(f32)).astype(bf16)
            d_inners[s, n] = d_inner
            bias_grad[0:1, cols] += col_sum(d_inner.astype(f32))
            d_hidden += mm_nt(d_inner, inner_columns(n))
        vec_grad[3:4] += col_sum(d_hidden * zhat1)
        vec_grad[4:5] += col_sum(d_hidden)
        d_sum1 = norm_back(d_hidden, zhat1, r1, vec[3:4])
        dsum_out[...] = d_sum1
        d_attn = d_sum1.astype(bf16)
        dattn_out[...] = d_attn
        d_attns[s] = d_attn
        vec_grad[5:6] += col_sum(d_attn.astype(f32))

    @pl.when((s >= SEQ_DEV) & (s < SEQ_DEV + RING))
    def _():
        rows = pl.ds(pl.multiple_of((s - SEQ_DEV) * FF_STEP, FF_STEP), FF_STEP)
        value = mm(act_t[0, rows, :], d_branches[0])
        for i in range(1, SEQ_DEV):
            value += mm(act_t[i, rows, :], d_branches[i])
        cut_cores(ids, value.astype(bf16), outer_away, outer_mine)

    @pl.when((s >= SEQ_DEV + RING) & (s < SEQ_DEV + RING + FF_STEPS))
    def _():
        n = s - SEQ_DEV - RING
        value = mm(hid_t[0], d_inners[0, n])
        for i in range(1, SEQ_DEV):
            value += mm(hid_t[i], d_inners[i, n])
        cut_cores(ids, value.astype(bf16), inner_away, inner_mine)

    @pl.when(s == SEQ_DEV + RING + FF_STEPS)
    def _():
        value = mm(ctx_t[:, :SLOT], d_attns[0])
        for i in range(1, SEQ_DEV):
            value += mm(ctx_t[:, i * SLOT : (i + 1) * SLOT], d_attns[i])
        block = gather_back([vec_grad[i : i + 1] for i in range(6)] + [bias_grad[...]])
        cut_cores(ids, jnp.concatenate([value.astype(bf16), block], axis=1), out_away, out_mine)


def attention_backward(
    ids, dsum, dattn, qkv, exp_in, norm_in, ctxt_in, x_t, c_in, layer_in, p0, p1, p2, p3, p4, p5, p6, p7, i0, i1, i2, i3,
    back_out, attn_away, attn_mine,
    w, w_out, vec_grad, d_qkv, sems, out_sems,
):
    s = pl.program_id(0)

    @pl.when(s == 0)
    def _():
        vec_grad[...] = jnp.zeros_like(vec_grad)
        copies = attention_copies(ids, (p0, p1, p2, p3, p4, p5, p6, p7), w, sems)
        for i, piece in enumerate((i0, i1, i2, i3)):
            c, z_half = half_of(ids, i)
            for d in range(RING):
                x = lax.rem(ids[8] + RING - d, RING)
                source = piece.at[d, :, pl.ds(0, WIDTH)]
                copies.append(pltpu.make_async_copy(source, w_out.at[x, c, z_half], out_sems.at[i, d]))
        for copy in copies:
            copy.start()
        for copy in copies:
            copy.wait()

    @pl.when(s < SEQ_DEV)
    def _():
        d_sum1 = dsum[...]
        dctx_t = mm_nt(dattn[...], w_out[...].reshape(WIDTH, WIDTH)).T
        ctx_t = ctxt_in[...].astype(f32)
        k_t = qkv[:, WIDTH : 2 * WIDTH].T
        scaled = []
        deltas = []
        for h in range(HEADS):
            rows = slice(h * HEAD, (h + 1) * HEAD)
            one = (dctx_t[rows] * norm_in[0, h : h + 1, :]).astype(bf16)
            scaled.append(one)
            deltas.append(col_sum(one.astype(f32) * ctx_t[rows]))
        dctx_t = jnp.concatenate(scaled, axis=0)
        dctx = dctx_t.T
        low = lax.broadcasted_iota(jnp.int32, (SLOT, PAIR), 1) < HEAD
        dq_t = []
        for p in range(0, WIDTH, PAIR):
            cols = slice(p, p + PAIR)
            q_pair = qkv[:, cols]
            v_pair = qkv[:, 2 * WIDTH + p : 2 * WIDTH + p + PAIR]
            dks = []
            dvs = []
            for half in range(2):
                h = p // HEAD + half
                v_one = jnp.where(low if half == 0 else ~low, v_pair, jnp.zeros_like(v_pair))
                d_probs = mm(v_one, dctx_t[cols]) - deltas[h]
                expo = exp_in[0, h]
                d_scores = (expo.astype(f32) * d_probs).astype(bf16)
                dvs.append(mm(expo, dctx[:, cols]))
                dks.append(mm(d_scores, q_pair))
                dq_t.append(mm(k_t[h * HEAD : (h + 1) * HEAD], d_scores))
            d_qkv[s, 1, :, cols] = jnp.where(low, dks[0], dks[1]).astype(bf16)
            d_qkv[s, 2, :, cols] = jnp.where(low, dvs[0], dvs[1]).astype(bf16)
        dq = (jnp.concatenate(dq_t, axis=0).T * HEAD**-0.5).astype(bf16)
        d_qkv[s, 0] = dq
        vec_grad[0:1] += col_sum(dq.astype(f32))
        vec_grad[1:2] += col_sum(d_qkv[s, 2].astype(f32))
        d_in = d_sum1
        for n in range(3):
            d_in += mm_nt(d_qkv[s, n], columns(w, n * WIDTH, (n + 1) * WIDTH))
        valid = (lax.broadcasted_iota(jnp.int32, (SLOT, 1), 0) < ids[s]).astype(f32)
        upstream = joined(c_in).astype(f32) * valid
        keep = ids[4 + s] == 0
        grad = jnp.where(keep, d_in, upstream).astype(bf16)
        back_out[:, 0, 0] = layer_in[...].reshape(GROUP, PIECE, WIDTH)
        back_out[:, 1, 0] = grad.reshape(GROUP, PIECE, WIDTH)

    @pl.when(s == SEQ_DEV)
    def _():
        values = []
        for n in range(3):
            value = mm(x_t[:, :SLOT], d_qkv[0, n])
            for i in range(1, SEQ_DEV):
                value += mm(x_t[:, i * SLOT : (i + 1) * SLOT], d_qkv[i, n])
            values.append(value.astype(bf16))
        values.append(gather_back([vec_grad[0:1], vec_grad[1:2]]))
        cut_cores(ids, jnp.concatenate(values, axis=1), attn_away, attn_mine)


def in_order(values, me):
    ordered = []
    for j in range(RING):
        step = lax.rem(me + RING - j, RING)
        value = values[0]
        for d in (1, 2, 3):
            value = jnp.where(step == d, values[d], value)
        ordered.append(value)
    return ordered


def pack_rows(ids, query, key, value, out, inner, row, packed):
    for i, ref in enumerate((query, key, value, out)):
        block = jnp.concatenate([ref[...].astype(f32), jnp.zeros((2, WIDTH), f32)], axis=0)
        if i == 0:
            line = lax.broadcasted_iota(jnp.int32, (8, WIDTH), 0)
            block = jnp.where(line == 6, row[...].astype(f32), block)
        packed[:, i * WIDTH : (i + 1) * WIDTH] = block.astype(bf16)
    block = jnp.concatenate([inner[...].astype(f32), jnp.zeros((2, FF), f32)], axis=0)
    packed[:, 4 * WIDTH :] = block.astype(bf16)


def merge_rows(ids, own, r1, r2, r3, attn_out, inner_out):
    ordered = in_order([v[...].astype(f32) for v in (own, r1, r2, r3)], ids[12])
    width = 3 * WIDTH
    rows = jnp.concatenate([v[:6] for v in ordered], axis=0).astype(bf16)
    attn_out[:, :width] = rows[:, :width]
    inner_out[...] = rows[:, width:]
    row = jnp.concatenate([v[6:7, :128] for v in ordered], axis=1)
    first = lax.broadcasted_iota(jnp.int32, (24, 4 * 128), 0) == 0
    attn_out[:, width:] = jnp.where(first, jnp.broadcast_to(row, (24, 4 * 128)), 0.0).astype(bf16)


def stack_rows(ids, own, r1, r2, r3, out):
    for d, piece in enumerate((own, r1, r2, r3)):
        out[lax.rem(ids[11] + RING - d, RING)] = piece[...]


def ahead(ids, axis, step):
    return lax.rem(ids[axis] + step, RING)


def sum_of(refs):
    total = refs[0][...].astype(f32)
    for ref in refs[1:]:
        total += ref[...].astype(f32)
    return total


def sum_blocks(ids, *refs):
    *parts, o0, o1, o2, o3, scratch = refs
    start = 0
    for mine, core in zip(parts[::2], parts[1::2]):
        end = start + mine.shape[2]
        scratch[:, start:end] = mine[0].astype(f32) + core[0].astype(f32)
        start = end
    for d, out in enumerate((o0, o1, o2, o3)):
        first = pl.multiple_of(ahead(ids, 11, d) * 24, 8)
        out[0] = scratch[pl.ds(first, 24), :].astype(bf16)


def sum_attention(ids, outer, mine, core, o0, o1, o2, o3, scratch):
    scratch[...] = mine[0].astype(f32) + core[0].astype(f32)
    for d, out in enumerate((o0, o1, o2, o3)):
        z = ahead(ids, 11, d)
        first = pl.multiple_of(z * 24, 8)
        out[0, :, : scratch.shape[1]] = scratch[pl.ds(first, 24), :].astype(bf16)
        out[0, :, scratch.shape[1] :] = outer[0, z]


def sum_outer(ids, mine, core, out):
    total = mine[0].astype(f32) + core[0].astype(f32)
    for z in range(RING):
        for y in range(RING):
            first = 96 * z + 24 * y
            out[y, 0, z] = total[first : first + 24].astype(bf16)


def sum_first(ids, value, out):
    for z in range(RING):
        out[0, z] = sum_of([value.at[y, 0, z] for y in range(RING)]).astype(bf16)


def split_rows(ids, p0, p1, p2, p3, o0, o1, o2, o3, *refs):
    *rest, scratch = refs
    width = o0.shape[2]
    total = sum_of([p.at[0] for p in (p0, p1, p2, p3)])
    if rest:
        rest[0][0] = total[:, width + 128 :].astype(bf16)
    for y in range(RING):
        vectors = total[y : y + 1, width : width + 128]
        row = jnp.concatenate([vectors, jnp.zeros((1, width - 128), f32)], axis=1)
        rows = total[6 * y : 6 * y + 6, :width]
        scratch[y] = jnp.concatenate([rows, row, jnp.zeros((1, width), f32)], axis=0)
    for d, out in enumerate((o0, o1, o2, o3)):
        out[0] = scratch[ahead(ids, 12, d)].astype(bf16)


LAST = FF + WIDTH + 3 * WIDTH + 3 * WIDTH


def join_flows(ids, i0, i1, i2, i3, a0, a1, a2, a3, outer, o0, o1, o2, o3, scratch):
    scratch[:, :, : FF + WIDTH] = sum_of((i0, i1, i2, i3))
    scratch[:, :, FF + WIDTH : FF + 4 * WIDTH] = sum_of((a0, a1, a2, a3))
    for x in range(RING):
        total = outer[x].astype(f32)
        for k in range(3):
            start = FF + (4 + k) * WIDTH
            scratch[x, :, start : start + WIDTH] = total[8 * k : 8 * k + 8]
    for d, out in enumerate((o0, o1, o2, o3)):
        out[...] = scratch[ahead(ids, 8, d)].astype(bf16)


def split_ffn(ids, p0, p1, p2, p3, inner, outer):
    for d, piece in enumerate((p0, p1, p2, p3)):
        inner[d] = piece[:, :MIXED]
        halves = [piece[:, MIXED + i * WIDTH : MIXED + (i + 1) * WIDTH].astype(f32) for i in range(2)]
        outer[d] = jnp.concatenate(halves, axis=0).astype(bf16)


def write_grads(ids, p0, p1, p2, p3, query, key, value, out, inner, outer, vectors):
    total = sum_of((p0, p1, p2, p3))
    inner[...] = total[:6, :FF]
    out[...] = total[:6, FF : FF + WIDTH]
    start = FF + WIDTH
    query[...] = total[:6, start : start + WIDTH]
    key[...] = total[:6, start + WIDTH : start + 2 * WIDTH]
    value[...] = total[:6, start + 2 * WIDTH : start + 3 * WIDTH]
    vectors[...] = jnp.concatenate([total[6:7, :128], total[6:7, start : start + 128]], axis=0)
    start += 3 * WIDTH
    for k in range(3):
        outer[8 * k : 8 * k + 8] = total[:, start + k * WIDTH : start + (k + 1) * WIDTH]


def whole(shape):
    return pl.BlockSpec(shape, lambda s, ids: (0,) * len(shape), pipeline_mode=pl.Buffered(1))


def sequence(s):
    return jnp.minimum(s, SEQ_DEV - 1)


DEALT_SPEC = pl.BlockSpec((GROUP, 1, PIECE, WIDTH), lambda s, ids: (0, sequence(s), 0, 0))


def by_rows(width):
    return pl.BlockSpec((SLOT, width), lambda s, ids: (sequence(s), 0))


def rows_of(width, kind):
    return jax.ShapeDtypeStruct((ROWS, width), kind)


EXP_SPEC = pl.BlockSpec((1, HEADS, SLOT, SLOT), lambda s, ids: (sequence(s), 0, 0, 0))
NORM_SPEC = pl.BlockSpec((1, 16, SLOT), lambda s, ids: (sequence(s), 0, 0))
RETURN_SPEC = pl.BlockSpec((GROUP, 2, 1, PIECE, WIDTH), lambda s, ids: (0, 0, sequence(s), 0, 0))
RETURN_SHAPE = jax.ShapeDtypeStruct((GROUP, 2, SEQ_DEV, PIECE, WIDTH), bf16)


def by_columns(height):
    return pl.BlockSpec((height, SLOT), lambda s, ids: (0, sequence(s)))


def columns_of(height):
    return jax.ShapeDtypeStruct((height, ROWS), bf16)


def run(kernel, grid, ins, outs, operands, name, flops, moved, scratch, limit):
    return pl.pallas_call(
        kernel,
        grid_spec=pltpu.PrefetchScalarGridSpec(
            num_scalar_prefetch=1,
            grid=grid,
            in_specs=ins,
            out_specs=[spec for spec, _ in outs],
            scratch_shapes=list(scratch),
        ),
        out_shape=[shape for _, shape in outs],
        compiler_params=pltpu.CompilerParams(
            vmem_limit_bytes=limit * MIB, dimension_semantics=("arbitrary",) * len(grid)
        ),
        cost_estimate=pl.CostEstimate(flops=flops, bytes_accessed=moved, transcendentals=0),
        name=name,
    )(*operands)


def out_rows(width, kind):
    return (by_rows(width), rows_of(width, kind))


def out_columns(height):
    return (by_columns(height), columns_of(height))


def out_whole(shape):
    return (whole(shape), jax.ShapeDtypeStruct(shape, f32))


ANYWHERE = pl.BlockSpec(memory_space=pl.ANY)
ATTENTION_SCRATCH = [pltpu.VMEM((RING, CORES, 96, PACKED), bf16)]


def call_forward(ids, dealt, weights, perm):
    return run(
        attention_forward,
        (SEQ_DEV,),
        [DEALT_SPEC] + [ANYWHERE] * 8 + [whole((32, 16))],
        [
            out_columns(WIDTH),
            out_rows(3 * WIDTH, bf16),
            (EXP_SPEC, jax.ShapeDtypeStruct((SEQ_DEV, HEADS, SLOT, SLOT), bf16)),
            (NORM_SPEC, jax.ShapeDtypeStruct((SEQ_DEV, 16, SLOT), f32)),
            out_columns(WIDTH),
            out_whole((8, WIDTH)),
            out_whole((1, FF)),
            out_whole((8, 128)),
        ],
        (ids, dealt, *weights, perm),
        "attention_forward",
        8 * 10**9,
        5 * 10**6,
        ATTENTION_SCRATCH + [pltpu.VMEM((32, PACKED - 3 * WIDTH), f32), pltpu.SemaphoreType.DMA((8,))],
        58,
    )


def halves(block, shape, where):
    return [(pl.BlockSpec(block, lambda s, ids: where(s)), jax.ShapeDtypeStruct(shape, bf16))] * 2


def call_ffn(ids, dealt, dealt_c, ctx_t, inner, outer, vec, bias_in):
    outer_rows = FF // GROUP
    inner_rows = WIDTH // GROUP
    first = SEQ_DEV
    second = first + RING
    return run(
        feed_forward,
        (second + FF_STEPS + 1,),
        [DEALT_SPEC] * 2
        + [whole((WIDTH, ROWS))]
        + [ANYWHERE] * 8
        + [whole((8, WIDTH)), whole((1, FF))],
        [out_rows(WIDTH, bf16), out_rows(WIDTH, f32), out_rows(WIDTH, bf16)]
        + halves(
            (1, outer_rows, WIDTH), (RING, outer_rows, WIDTH), lambda s: (jnp.clip(s - first, 0, RING - 1), 0, 0)
        )
        + halves(
            (RING, inner_rows, FF_STEP),
            (RING, inner_rows, FF),
            lambda s: (0, 0, jnp.clip(s - second, 0, FF_STEPS - 1)),
        )
        + halves((RING, inner_rows, WIDTH + 128), (RING, inner_rows, WIDTH + 128), lambda s: (0, 0, 0)),
        (ids, dealt, dealt_c, ctx_t, *inner, *outer, vec, bias_in),
        "feed_forward",
        50 * 10**9,
        40 * 10**6,
        [
            pltpu.VMEM((SLOT, FF), bf16),
            pltpu.VMEM((8, WIDTH), f32),
            pltpu.VMEM((1, FF), f32),
            pltpu.VMEM((RING, CORES, 2, 48, MIXED), bf16),
            pltpu.VMEM((RING, CORES, RING, 2, 48, WIDTH), bf16),
            pltpu.VMEM((SEQ_DEV, WIDTH, SLOT), bf16),
            pltpu.VMEM((SEQ_DEV, FF, SLOT), bf16),
            pltpu.VMEM((SEQ_DEV, SLOT, WIDTH), bf16),
            pltpu.VMEM((SEQ_DEV, FF_STEPS, SLOT, FF_STEP), bf16),
            pltpu.VMEM((SEQ_DEV, SLOT, WIDTH), bf16),
            pltpu.SemaphoreType.DMA((RING, RING)),
            pltpu.SemaphoreType.DMA((RING, RING, RING)),
        ],
        58,
    )


def call_backward(ids, dsum, dattn, qkv, expo, norm, ctx_t, x_t, dealt_c, layer, weights, inner):
    block = (RING, WIDTH // GROUP, 3 * WIDTH + 128)
    return run(
        attention_backward,
        (SEQ_DEV + 1,),
        [by_rows(WIDTH), by_rows(WIDTH), by_rows(3 * WIDTH), EXP_SPEC, NORM_SPEC, by_columns(WIDTH)]
        + [whole((WIDTH, ROWS)), DEALT_SPEC, by_rows(WIDTH)]
        + [ANYWHERE] * 12,
        [(RETURN_SPEC, RETURN_SHAPE)] + halves(block, block, lambda s: (0, 0, 0)),
        (ids, dsum, dattn, qkv, expo, norm, ctx_t, x_t, dealt_c, layer, *weights, *inner),
        "attention_backward",
        28 * 10**9,
        30 * 10**6,
        ATTENTION_SCRATCH
        + [
            pltpu.VMEM((RING, CORES, 2, 48, WIDTH), bf16),
            pltpu.VMEM((8, WIDTH), f32),
            pltpu.VMEM((SEQ_DEV, 3, SLOT, WIDTH), bf16),
            pltpu.SemaphoreType.DMA((8,)),
            pltpu.SemaphoreType.DMA((RING, RING)),
        ],
        58,
    )


def call_by_x(kernel, name, ids, pieces, at, out_shapes, out_at, scratch):
    count = len(out_shapes)

    def every_x(ids, *refs):
        ins, outs, rest = refs[: len(pieces)], refs[len(pieces) :][:count], refs[len(pieces) + count :]
        for x in range(RING):
            one = (pl.ds(x, 1),)
            kernel(
                ids,
                *[ref.at[(slice(None),) * at + one] for ref in ins],
                *[ref.at[(slice(None),) * out_at + one] for ref in outs],
                *rest,
            )

    return call_small(every_x, name, ids, pieces, *out_shapes, scratch=scratch)


def call_small(kernel, name, ids, pieces, *out_shapes, kind=bf16, scratch=()):
    def full(shape):
        return pl.BlockSpec(shape, lambda i, ids: (0,) * len(shape))

    return run(
        kernel,
        (1,),
        [full(piece.shape) for piece in pieces],
        [(full(shape), jax.ShapeDtypeStruct(shape, kind)) for shape in out_shapes],
        (ids, *pieces),
        name,
        10**6,
        6 * 10**6,
        [pltpu.VMEM(shape, f32) for shape in scratch],
        30,
    )


def shift(value, axis, step):
    size = CORES if axis == "core" else RING
    return lax.ppermute(value, axis, [(i, (i + step) % size) for i in range(size)])


def swap(value, axis):
    return lax.ppermute(value, axis, [(i, i ^ 1) for i in range(RING)])


def arrivals(value, axis):
    return [value] + [shift(value, axis, step) for step in (1, 2, 3)]


def both_cores(pieces):
    return [part for piece in pieces for part in (piece, shift(piece, "core", 1))]


def paired(value, axis):
    return in_half(value, swap(value, axis), axis)


def in_half(value, other, axis):
    even = lax.rem(lax.axis_index(axis), 2) == 0
    return jnp.where(even, value, other), jnp.where(even, other, value)


def hold(value, *others):
    return lax.optimization_barrier((value, *others))[0]


def send_ring(parts, axis):
    return [parts[0]] + [shift(parts[step], axis, step) for step in (1, 2, 3)]


def over(value, axis):
    return lax.all_to_all(value, axis, split_axis=0, concat_axis=0, tiled=True)


def body(
    tokens,
    cotangent,
    perm,
    lengths,
    drop,
    w_query,
    b_query,
    w_key,
    w_value,
    b_value,
    w_out,
    b_out,
    norm1_gain,
    norm1_bias,
    w_inner,
    b_inner,
    w_outer,
    b_outer,
    norm2_gain,
    norm2_bias,
):
    me_x = lax.axis_index("x")
    me_c = lax.axis_index("core")
    me_z = lax.axis_index("z")
    me_y = lax.axis_index("y")
    first = ((me_z * RING + me_y) * 8 + me_x * CORES + me_c) * SEQ_DEV
    places = jnp.stack([me_x, me_c, first, me_z, me_y]).astype(jnp.int32)
    places = jnp.pad(places, (8, 3))

    vectors = [b_query, b_value, b_out, norm1_gain, norm1_bias, b_outer, norm2_gain, norm2_bias, b_inner]
    vectors += [lengths.astype(bf16), drop.astype(bf16)]
    row = jnp.zeros((WIDTH,), bf16)
    start = 0
    for vector in vectors:
        end = start + vector.shape[0]
        row += jnp.pad(vector, (start, WIDTH - end))
        start = end
    (piece,) = call_small(
        pack_rows, "pack_rows", places, (w_query, w_key, w_value, w_out, w_inner, row[None]), (8, 4 * WIDTH + FF)
    )
    pieces_y = arrivals(piece, "y")
    dp = ("x", "core")
    dealt = (GROUP, SEQ_DEV, PIECE, WIDTH)
    dealt_x = over(tokens.reshape(dealt), dp)
    attn_y, inner_y = call_small(merge_rows, "merge_rows", places, pieces_y, (24, PACKED), (24, MIXED))
    (attn_zy,) = call_small(
        stack_rows, "stack_rows", places, arrivals(attn_y, "z"), (RING, 24, PACKED)
    )

    outer_pair = paired(w_outer, "y")
    ffn_x = arrivals(jnp.concatenate([hold(inner_y, dealt_x), *outer_pair], axis=1), "x")
    ffn_x[0] = hold(ffn_x[0], attn_zy)
    inner_x, outer_x = call_small(
        split_ffn, "split_ffn", places, ffn_x, (RING, 24, MIXED), (RING, 48, WIDTH)
    )
    attn_x = arrivals(hold(attn_zy, dealt_x).reshape(96, PACKED), "x")
    inner_z = swap(inner_x, "z")
    outer_z = over(jnp.broadcast_to(outer_x[None], (RING, RING, 48, WIDTH)), "z")
    inner_z = jnp.concatenate(in_half(inner_x, inner_z, "z"), axis=1)
    attn_pieces = both_cores([attn_x[0]] + [hold(p, inner_z) for p in attn_x[1:]])
    inner_far = shift(inner_z, "z", 2)
    outer_z = hold(outer_z, inner_z)
    outer_far = shift(outer_z, "y", 2)
    dealt_c = over(hold(cotangent, inner_z).reshape(dealt), dp)

    x_t, qkv, expo, norm, ctx_t, vec, inner_bias, info = call_forward(
        places, dealt_x, attn_pieces, perm.reshape(32, 16)
    )
    ids = jnp.concatenate([info[:, 0].astype(jnp.int32), places[8:]])

    inner_pieces = both_cores([hold(inner_z, ctx_t, dealt_c), hold(inner_far, ctx_t)])
    outer_pieces = both_cores([hold(outer_z, ctx_t), hold(outer_far, ctx_t)])
    (
        layer, d_sum1, d_attn, outer_away, outer_mine, inner_away, inner_mine, out_away, out_mine
    ) = call_ffn(ids, dealt_x, dealt_c, ctx_t, inner_pieces, outer_pieces, vec, inner_bias)

    inner_core = shift(inner_away, "core", 1)
    out_core = shift(out_away, "core", 1)
    outer_core = shift(hold(outer_away, out_core), "core", 1)
    inner_width = FF + WIDTH + 128
    inner_parts = call_by_x(
        sum_blocks, "sum_blocks", places, (inner_mine, inner_core, out_mine, out_core), 0,
        [(RING, 24, inner_width)] * RING, 0, [(96, inner_width)],
    )
    (outer_sum,) = call_by_x(
        sum_outer, "sum_outer", hold(places, inner_parts[0]), (outer_mine, outer_core), 0,
        [(RING, RING, RING, 24, WIDTH)], 1, [],
    )
    inner_parts = send_ring(inner_parts, "z")
    outer_y = over(outer_sum, "y")

    d_sum1, d_attn = lax.optimization_barrier((d_sum1, d_attn, inner_parts[0], outer_sum))[:2]
    back, attn_away, attn_mine = call_backward(
        ids, d_sum1, d_attn, qkv, expo, norm, ctx_t, x_t, dealt_c, layer, attn_pieces, inner_pieces
    )

    attn_core = shift(hold(attn_away, outer_y, *inner_parts[1:]), "core", 1)
    (outer_z,) = call_by_x(
        sum_first, "sum_first", hold(places, attn_away), (hold(outer_y, attn_away),), 1,
        [(RING, RING, 24, WIDTH)], 0, [],
    )
    attn_width = 3 * WIDTH + 128
    attn_parts = call_by_x(
        sum_attention, "sum_attention", places, (outer_z, attn_mine, attn_core), 0,
        [(RING, 24, attn_width + WIDTH)] * RING, 0, [(96, attn_width)],
    )
    attn_first = attn_parts[0]
    attn_parts = send_ring(attn_parts, "z")
    back = over(hold(back, outer_z), dp)

    inner_parts = [hold(p, attn_away) for p in inner_parts]
    inner_parts = call_by_x(
        split_rows, "split_rows", places, inner_parts, 0,
        [(RING, 8, FF + WIDTH)] * RING, 0, [(RING, 8, FF + WIDTH)],
    )
    *attn_parts, outer_z = call_by_x(
        split_rows, "split_rows", hold(places, inner_parts[0]), attn_parts, 0,
        [(RING, 8, 3 * WIDTH)] * RING + [(RING, 24, WIDTH)], 0, [(RING, 8, 3 * WIDTH)],
    )
    inner_parts = send_ring(inner_parts, "y")
    attn_parts = send_ring(attn_parts, "y")
    last = call_small(
        join_flows, "join_flows", places, [*inner_parts, *attn_parts, outer_z], *[(8, LAST)] * 4,
        scratch=[(RING, 8, LAST)],
    )
    back = hold(back, last[0])
    layer_final = back[:, 0].reshape(GROUP * SEQ_DEV, PIECE, WIDTH)
    grad_final = back[:, 1].reshape(GROUP * SEQ_DEV, PIECE, WIDTH)
    square = (6, WIDTH)
    grad_query, grad_key, grad_value, grad_out, grad_inner, grad_outer, vectors = call_small(
        write_grads, "write_grads", hold(places, layer_final), send_ring(last, "x"),
        square, square, square, square, (6, FF), (24, WIDTH), (2, 128), kind=f32,
    )
    ffn_vectors = [vectors[0, 6 * i : 6 * i + 6] for i in range(6)]
    return (
        layer_final,
        grad_final,
        grad_query,
        vectors[1, :6],
        grad_key,
        grad_value,
        vectors[1, 6:12],
        grad_out,
        ffn_vectors[5],
        ffn_vectors[3],
        ffn_vectors[4],
        grad_inner,
        vectors[0, 36:60],
        grad_outer,
        ffn_vectors[0],
        ffn_vectors[1],
        ffn_vectors[2],
    )


def solution(mesh):
    chips = Mesh(mesh.devices.reshape(RING, CORES, RING, RING), ("x", "core", "z", "y"))
    dp = ("x", "core")
    fsdp = ("z", "y")
    every = P(dp + fsdp)
    rows = P(dp + fsdp, None)
    whole_rows = P(fsdp, dp, None)
    return jax.shard_map(
        body,
        mesh=chips,
        in_specs=(
            whole_rows, whole_rows, P(), every, every,
            rows, every, rows, rows, every, rows, every, every, every,
            rows, every, rows, every, every, every,
        ),
        out_specs=(
            whole_rows, whole_rows,
            rows, every, rows, rows, every, rows, every, every, every,
            rows, every, rows, every, every, every,
        ),
        check_vma=False,
    )
```
